32 devices in a mesh: blk: 8 (over z, y), rep: 4 (over x, core).
Axes of the slice: x: 2, y: 2, z: 4, core: 2. Of those that a mesh axis runs over, the one named last changes fastest.
Arguments:
- features: bfloat16 [8192, 256], P(('blk', 'rep')), may hold values from -6 to 6
- node_type: int32 [8192], P(('blk', 'rep')), may hold values from 0 to 3, as said below
- time_gap: int32 [8192], P(('blk', 'rep')), may hold values from 0 to 15
- node_valid: int32 [8192], P(('blk', 'rep')), may hold values from 0 to 1, as said below
- edge_codes: int32 [8192, 2048], P(('blk', 'rep')), may hold values from 0 to 2, as said below
- query_w: bfloat16 [4, 256, 256], replicated, may hold values from -0.375 to 0.375
- key_w: bfloat16 [4, 256, 256], replicated, may hold values from -0.375 to 0.375
- value_w: bfloat16 [4, 256, 256], replicated, may hold values from -0.375 to 0.375
- out_w: bfloat16 [4, 256, 256], replicated, may hold values from -1.5 to 1.5
- rel_att: bfloat16 [8, 8, 32, 32], replicated, may hold values from -1 to 1
- rel_msg: bfloat16 [8, 8, 32, 32], replicated, may hold values from -1 to 1
- rel_prior: float32 [8, 8], replicated, may hold values from 0.5 to 2
- skip_logit: float32 [4], replicated, may hold values from -1.5 to 1.5
- rte_w: bfloat16 [256, 256], replicated, may hold values from -0.375 to 0.375
- ln_gain: float32 [256], replicated, may hold values from 0.5 to 1.5
- ln_bias: float32 [256], replicated, may hold values from -3 to 3
- cotangent: bfloat16 [8192, 256], P(('blk', 'rep')), may hold values from -6 to 6
Outputs:
- layer_out: bfloat16 [8192, 256], P(('blk', 'rep'))
- input_grad: bfloat16 [8192, 256], P(('blk', 'rep'))
- query_grad: float32 [4, 256, 256], replicated
- key_grad: float32 [4, 256, 256], replicated
- value_grad: float32 [4, 256, 256], replicated
- out_grad: float32 [4, 256, 256], replicated
- att_grad: float32 [8, 8, 32, 32], replicated
- msg_grad: float32 [8, 8, 32, 32], replicated
- prior_grad: float32 [8, 8], replicated
- skip_grad: float32 [4], replicated
- rte_grad: float32 [256, 256], replicated
- gain_grad: float32 [256], replicated
- bias_grad: float32 [256], replicated
The draws below stay inside these ranges and needn't reach their ends.
Inputs may be any that keep to these rules, and one draw needn't show every extreme that they name: `node_type`: 0 paper, 1 author, 2 field, 3 institution. `node_valid`: each device's 256 rows hold its real nodes first and its padding after them. `edge_codes`: 0 no edge, 1 an edge whose relation follows from the two types, 2 a cited_by edge between two papers; edges join only real nodes and only the type pairs of the relation list.
All inputs are finite; a program needn't handle non-finite values.
Results may differ from the reference program's by a relative error of at most 0.022.
The reference program's roundings to bfloat16 on the way count: a program that leaves them out, or rounds other values in their place, can miss the bound.
Values may be sent and summed in bfloat16 or wider, within the bound.
A program may use at most 128 MiB of HBM per device.

```python
import math
import jax
import jax.numpy as jnp
import numpy as np
from jax import lax

HID = 256
HEADS = 8
TYPES = 4
RELS = 8
HEAD_DIM = 32
LEVELS = 16
NODE_DEV = 256
GROUP = 2048
NODES = 8192
N_BLK = 8
N_REP = 4


def node_kinds(key):
    key = jax.random.fold_in(key, 101)
    nodes_all = NODE_DEV * N_BLK * N_REP
    roll_kind = jax.random.randint(key, (nodes_all,), 0, 10)
    return (roll_kind >= 5).astype(jnp.int32) + (roll_kind >= 8).astype(jnp.int32) + (roll_kind >= 9).astype(jnp.int32)


def node_keep(key):
    key = jax.random.fold_in(key, 202)
    kept_rows = jax.random.randint(key, (N_BLK * N_REP, 1), 3 * NODE_DEV // 4, NODE_DEV + 1)
    local_idx = jnp.arange(NODE_DEV)[None, :]
    return (local_idx < kept_rows).astype(jnp.int32).reshape(-1)


def draw_node_type(key, part):
    return node_kinds(key)


def draw_node_valid(key, part):
    return node_keep(key)


def draw_edge_codes(key, part):
    kinds = node_kinds(key)
    keep = node_keep(key)
    key = jax.random.fold_in(key, 3)
    key_rate, key_active, key_edge, key_cite, key_dev = jax.random.split(key, 5)
    group_nodes = NODE_DEV * N_BLK
    nodes_all = NODE_DEV * N_BLK * N_REP
    dev_rate = jax.random.randint(key_dev, (N_BLK, N_REP, 1), 250, 1001)
    roll_active = jax.random.randint(key_active, (N_BLK, N_REP, N_BLK), 0, 1000)
    tgt_blk = jnp.arange(N_BLK)[:, None, None]
    src_blk = jnp.arange(N_BLK)[None, None, :]
    forced = (src_blk == tgt_blk) | (src_blk == (tgt_blk + 1) % N_BLK) | (src_blk == (tgt_blk + N_BLK - 1) % N_BLK) | (src_blk == N_BLK - 1 - tgt_blk)
    active = (roll_active < dev_rate) | forced
    row_idx = jnp.arange(nodes_all)
    row_blk = row_idx // (N_REP * NODE_DEV)
    row_rep = row_idx // NODE_DEV % N_REP
    col_idx = jnp.arange(group_nodes)
    col_blk = col_idx // NODE_DEV
    col_loc = col_idx % NODE_DEV
    src_node = (col_blk[None, :] * N_REP + row_rep[:, None]) * NODE_DEV + col_loc[None, :]
    src_kind = kinds[src_node]
    src_keep = keep[src_node]
    allowed_tab = jnp.asarray(np.array([[1, 1, 1, 0], [1, 0, 0, 1], [1, 0, 0, 0], [0, 1, 0, 0]], np.int32)).reshape(-1)
    allowed = allowed_tab[kinds[:, None] * 4 + src_kind]
    block_on = active[row_blk[:, None], row_rep[:, None], col_blk[None, :]]
    edge_rate = jax.random.randint(key_rate, (nodes_all, 1), 10, 80)
    roll_edge = jax.random.randint(key_edge, (nodes_all, group_nodes), 0, 1000)
    present = (roll_edge < edge_rate) & (allowed > 0) & block_on & (keep[:, None] > 0) & (src_keep > 0)
    cite_bit = jax.random.randint(key_cite, (nodes_all, group_nodes), 0, 2)
    both_paper = ((kinds[:, None] == 0) & (src_kind == 0)).astype(jnp.int32)
    return present.astype(jnp.int32) * (1 + cite_bit * both_paper)


def plant(values, key, low, top_value):
    shape = values.shape
    spot = [jax.random.randint(jax.random.fold_in(key, axis), (), 0, shape[axis]) for axis in range(len(shape))]
    values = values.at[tuple(spot)].set(low)
    longest = shape.index(max(shape))
    spot[longest] = (spot[longest] + 1) % shape[longest]
    return values.at[tuple(spot)].set(top_value)


def block_levels(own_key, dims, shards, low, top_value):
    loudness, own = 1.0, jax.random.fold_in(own_key, 6)
    for axis_at, blocks in shards:
        draws = jnp.exp(jax.random.uniform(jax.random.fold_in(own, axis_at), (blocks,), jnp.float32, low / len(shards), top_value / len(shards)))
        loudness = loudness * jnp.repeat(draws, dims[axis_at] // blocks).reshape([-1 if axis == axis_at else 1 for axis in range(len(dims))])
    return loudness


def bell_draw(own_key, shape, width, limit, cuts=(), held_as=jnp.bfloat16):
    loudness = block_levels(own_key, shape, cuts, -0.22, 0.18) if cuts else 1.0
    values = jax.random.normal(own_key, shape, jnp.float32) * width * loudness
    return jnp.minimum(jnp.maximum(values, -limit), limit).astype(held_as)


def setup_inputs(seed: int = 0) -> dict:
    arg_keys = jax.random.split(jax.random.key(seed), 18)
    features = bell_draw(arg_keys[0], (NODES, HID), 1.0, 6.0, ((0, 32),))
    node_type = draw_node_type(jax.random.fold_in(arg_keys[17], 71), 0)
    time_gap = plant(jax.random.randint(arg_keys[2], (NODES,), 0, LEVELS), jax.random.fold_in(arg_keys[2], 1), 0, LEVELS - 1).astype(jnp.int32)
    node_valid = draw_node_valid(jax.random.fold_in(arg_keys[17], 71), 0)
    edge_codes = draw_edge_codes(jax.random.fold_in(arg_keys[17], 71), 0)
    query_w = bell_draw(arg_keys[5], (TYPES, HID, HID), HID ** -0.5, 0.375)
    key_w = bell_draw(arg_keys[6], (TYPES, HID, HID), HID ** -0.5, 0.375)
    value_w = bell_draw(arg_keys[7], (TYPES, HID, HID), HID ** -0.5, 0.375)
    out_w = bell_draw(arg_keys[8], (TYPES, HID, HID), (HID // 16) ** -0.5, 1.5)
    rel_att = bell_draw(arg_keys[9], (RELS, HEADS, HEAD_DIM, HEAD_DIM), HEAD_DIM ** -0.5, 1.0)
    rel_msg = bell_draw(arg_keys[10], (RELS, HEADS, HEAD_DIM, HEAD_DIM), HEAD_DIM ** -0.5, 1.0)
    rel_prior = jnp.clip(jnp.exp(jax.random.uniform(arg_keys[11], (RELS, HEADS), jnp.float32, math.log(0.5), math.log(2.0))), 0.5, 2.0)
    skip_logit = jnp.clip(jax.random.uniform(arg_keys[12], (TYPES,), jnp.float32, -1.5, 1.5), -1.5, 1.5)
    rte_w = bell_draw(arg_keys[13], (HID, HID), HID ** -0.5, 0.375)
    ln_gain = jnp.clip(1.0 + 0.1 * jax.random.normal(arg_keys[14], (HID,), jnp.float32), 0.5, 1.5)
    ln_bias = bell_draw(arg_keys[15], (HID,), 0.5, 3.0, (), jnp.float32)
    cotangent = bell_draw(arg_keys[16], (NODES, HID), 1.0, 6.0, ((0, 32),))
    return dict(features=features, node_type=node_type, time_gap=time_gap, node_valid=node_valid, edge_codes=edge_codes, query_w=query_w, key_w=key_w, value_w=value_w, out_w=out_w, rel_att=rel_att, rel_msg=rel_msg, rel_prior=rel_prior, skip_logit=skip_logit, rte_w=rte_w, ln_gain=ln_gain, ln_bias=ln_bias, cotangent=cotangent)


NEG_FILL = -1e+30
LN_EPS = 1e-05
HIGH = lax.Precision.HIGHEST

@jax.custom_vjp
def low(v):
    return lax.optimization_barrier(v.astype(jnp.bfloat16)).astype(jnp.float32)

@jax.custom_vjp
def low_back(v):
    return v

def low_keep(v):
    return (low(v), None)

def low_pass(kept, grad):
    return (grad,)

def back_keep(v):
    return (v, None)

def back_low(kept, grad):
    return (low(grad),)
low.defvjp(low_keep, low_pass)
low_back.defvjp(back_keep, back_low)

def relation_table():
    rel_tab = np.zeros((4, 4, 8), np.float32)
    rel_tab[0, 1, 0] = 1.0
    rel_tab[1, 0, 1] = 1.0
    rel_tab[0, 0, 2] = 1.0
    rel_tab[2, 0, 4] = 1.0
    rel_tab[0, 2, 5] = 1.0
    rel_tab[3, 1, 6] = 1.0
    rel_tab[1, 3, 7] = 1.0
    return rel_tab

def time_table(level_count, feat_width):
    positions = jnp.arange(level_count, dtype=jnp.float32)[:, None]
    freq_idx = jnp.arange(feat_width // 2, dtype=jnp.float32)[None, :]
    phases = positions / jnp.power(10000.0, 2.0 * freq_idx / feat_width)
    return jnp.stack([jnp.sin(phases), jnp.cos(phases)], axis=2).reshape(level_count, feat_width)

def slot_spread(heads_arr, kind_hot):
    spread_out = heads_arr[..., None, :] * kind_hot[..., :, None, :, None]
    return spread_out.reshape(heads_arr.shape[:-1] + (-1,))

def attend_group(q_four, q_cite, k_four, k_heads, v_four, v_heads, code_grid):
    group_rows = q_four.shape[0]
    block_rows = min(512, group_rows)
    block_count = group_rows // block_rows

    def one_block(pieces):
        qf_blk, qc_blk, code_blk = pieces
        slot_dot = jnp.einsum('thc,shc->hts', qf_blk, k_four, precision=HIGH)
        cite_dot = jnp.einsum('thd,shd->hts', qc_blk, k_heads, precision=HIGH)
        is_one = (code_blk == 1)[None]
        is_two = (code_blk == 2)[None]
        scores = jnp.where(is_one, slot_dot, jnp.where(is_two, cite_dot, NEG_FILL))
        scores = low_back(scores)
        run_max = lax.optimization_barrier(jnp.max(scores, axis=2, keepdims=True))
        expd = jnp.where((code_blk > 0)[None], jnp.exp(scores - run_max), 0.0)
        denom = jnp.maximum(lax.optimization_barrier(jnp.sum(expd, axis=2, keepdims=True)), 1.0)
        prob_low = low(expd / denom)
        u_four = jnp.einsum('hts,shc->thc', jnp.where(is_one, prob_low, 0.0), v_four, precision=HIGH)
        u_cite = jnp.einsum('hts,shd->thd', jnp.where(is_two, prob_low, 0.0), v_heads, precision=HIGH)
        return (u_four, u_cite)
    outs = lax.map(jax.checkpoint(one_block), (q_four.reshape((block_count, block_rows) + q_four.shape[1:]), q_cite.reshape((block_count, block_rows) + q_cite.shape[1:]), code_grid.reshape(block_count, block_rows, group_rows)))
    return (outs[0].reshape((group_rows,) + outs[0].shape[2:]), outs[1].reshape((group_rows,) + outs[1].shape[2:]))

def reference(features, node_type, time_gap, node_valid, edge_codes, query_w, key_w, value_w, out_w, rel_att, rel_msg, rel_prior, skip_logit, rte_w, ln_gain, ln_bias, cotangent):

    def grouped(array_in):
        tail_dims = array_in.shape[1:]
        return array_in.reshape((N_BLK, N_REP, NODE_DEV) + tail_dims).swapaxes(0, 1).reshape((N_REP, N_BLK * NODE_DEV) + tail_dims)

    def ungrouped(array_in):
        tail_dims = array_in.shape[2:]
        return array_in.reshape((N_REP, N_BLK, NODE_DEV) + tail_dims).swapaxes(0, 1).reshape((N_REP * N_BLK * NODE_DEV,) + tail_dims)
    kinds_g = grouped(node_type)
    gaps_g = grouped(time_gap)
    valid_g = grouped(node_valid).astype(jnp.float32)[..., None]
    codes_g = grouped(edge_codes)
    type_hot = (kinds_g[..., None] == jnp.arange(TYPES)).astype(jnp.float32)
    gap_hot = (gaps_g[..., None] == jnp.arange(LEVELS)).astype(jnp.float32)
    cite_hot = (jnp.arange(RELS) == 3).astype(jnp.float32)
    time_raw = time_table(LEVELS, HID)

    def typed(inp, weights):
        parts = jnp.einsum('gnh,khd->gnkd', inp, weights, precision=HIGH)
        return lax.optimization_barrier(jnp.sum(parts * type_hot[..., None], axis=2))

    def forward(x_f, qw, kw, vw, ow, att, msg, prior, skipl, rtew, gain, bias):
        select = jnp.einsum('gnk,ksr->gnsr', type_hot, jnp.asarray(relation_table()), precision=HIGH)
        time_low = low(time_raw)
        rte_table = jnp.dot(time_low, rtew, precision=HIGH)
        shifted = x_f + jnp.einsum('gnl,lh->gnh', gap_hot, rte_table, precision=HIGH)
        shifted_low = low(shifted)
        query = low(low_back(typed(x_f, qw)))
        key_full = low(low_back(typed(shifted_low, kw)))
        value_full = low(low_back(typed(shifted_low, vw)))
        q_heads = query.reshape(N_REP, GROUP, HEADS, HEAD_DIM)
        k_heads = key_full.reshape(N_REP, GROUP, HEADS, HEAD_DIM)
        v_heads = value_full.reshape(N_REP, GROUP, HEADS, HEAD_DIM)
        factor = prior / math.sqrt(HEAD_DIM)
        rel_query = jnp.einsum('gthj,rhjk->rgthk', q_heads, att, precision=HIGH) * factor[:, None, None, :, None]
        rel_query = low(low_back(rel_query))
        q_four = jnp.einsum('gtsr,rgthd->gthsd', select, rel_query, precision=HIGH).reshape(N_REP, GROUP, HEADS, TYPES * HEAD_DIM)
        q_cite = rel_query[3]
        k_four = slot_spread(k_heads, type_hot)
        v_four = slot_spread(v_heads, type_hot)
        results = [attend_group(q_four[item], q_cite[item], k_four[item], k_heads[item], v_four[item], v_heads[item], codes_g[item]) for item in range(N_REP)]
        u_four = jnp.stack([res[0] for res in results])
        u_cite = jnp.stack([res[1] for res in results])
        u_rel = jnp.einsum('gtsr,gthsd->rgthd', select, u_four.reshape(N_REP, GROUP, HEADS, TYPES, HEAD_DIM), precision=HIGH)
        u_rel = u_rel + cite_hot[:, None, None, None, None] * u_cite[None]
        u_rel = low(low_back(u_rel))
        agg_sum = jnp.einsum('rgthd,rhde->gthe', u_rel, msg, precision=HIGH).reshape(N_REP, GROUP, HID)
        agg_sum = low_back(agg_sum)
        act_low = low(jax.nn.gelu(agg_sum))
        branch = low_back(typed(act_low, ow))
        skip_gate = lax.optimization_barrier(jnp.sum(type_hot * jax.nn.sigmoid(skipl), axis=-1, keepdims=True))
        mixed_sum = skip_gate * branch + (1.0 - skip_gate) * x_f
        centered = mixed_sum - lax.optimization_barrier(jnp.mean(mixed_sum, axis=-1, keepdims=True))
        normed = centered * lax.rsqrt(lax.optimization_barrier(jnp.mean(centered * centered, axis=-1, keepdims=True)) + LN_EPS)
        return valid_g * (normed * gain + bias)
    x_f = grouped(features).astype(jnp.float32)
    result, pullback = jax.vjp(forward, x_f, query_w.astype(jnp.float32), key_w.astype(jnp.float32), value_w.astype(jnp.float32), out_w.astype(jnp.float32), rel_att.astype(jnp.float32), rel_msg.astype(jnp.float32), rel_prior.astype(jnp.float32), skip_logit.astype(jnp.float32), rte_w.astype(jnp.float32), ln_gain.astype(jnp.float32), ln_bias.astype(jnp.float32))
    grads = pullback(grouped(cotangent).astype(jnp.float32))
    layer_out = ungrouped(result).astype(jnp.bfloat16)
    input_grad = ungrouped(grads[0]).astype(jnp.bfloat16)
    return (layer_out, input_grad, grads[1], grads[2], grads[3], grads[4], grads[5], grads[6], grads[7], grads[8], grads[9], grads[10], grads[11])
```

```python
import math

import jax
import jax.numpy as jnp
import numpy as np
from jax import lax
from jax.experimental import pallas as pl
from jax.experimental.pallas import tpu as pltpu
from jax.sharding import PartitionSpec as P

LEVELS = 16


NEG_FILL = -1e30
LN_EPS = 1e-05
HIGH = lax.Precision.HIGHEST


def from_behind(block, axis, distance):
    devices = range(lax.axis_size(axis))
    route = [((i - distance) % len(devices), i) for i in devices]
    return lax.ppermute(block, axis, route)


def relation_table():
    rel_tab = np.zeros((4, 4, 8), np.float32)
    rel_tab[0, 1, 0] = 1.0
    rel_tab[1, 0, 1] = 1.0
    rel_tab[0, 0, 2] = 1.0
    rel_tab[2, 0, 4] = 1.0
    rel_tab[0, 2, 5] = 1.0
    rel_tab[3, 1, 6] = 1.0
    rel_tab[1, 3, 7] = 1.0
    return rel_tab


def time_table(level_count, feat_width):
    positions = jnp.arange(level_count, dtype=jnp.float32)[:, None]
    freq_idx = jnp.arange(feat_width // 2, dtype=jnp.float32)[None, :]
    phases = positions / jnp.power(10000.0, 2.0 * freq_idx / feat_width)
    return jnp.stack([jnp.sin(phases), jnp.cos(phases)], axis=2).reshape(level_count, feat_width)


def slot_spread(heads_arr, kind_hot):
    spread_out = heads_arr[:, :, None, :] * kind_hot[:, None, :, None]
    return spread_out.reshape(heads_arr.shape[0], heads_arr.shape[1], -1)


def slot_collapse(slot_arr, kind_hot):
    src_rows, head_count = (slot_arr.shape[0], slot_arr.shape[1])
    kind_count = kind_hot.shape[1]
    shaped = slot_arr.reshape(src_rows, head_count, kind_count, -1)
    return jnp.sum(shaped * kind_hot.astype(jnp.float32)[:, None, :, None], axis=2)


def block_scores(kv_blk, q_four, q_cite, code_blk, kind_count):
    key_blk, value_blk, kind_blk = kv_blk
    src_rows = key_blk.shape[0]
    head_count = q_four.shape[1]
    key_heads = key_blk.reshape(src_rows, head_count, -1)
    value_heads = value_blk.reshape(src_rows, head_count, -1)
    kind_hot = (kind_blk[:, None] == jnp.arange(kind_count).astype(jnp.bfloat16)[None, :]).astype(
        jnp.bfloat16
    )
    key_four = slot_spread(key_heads, kind_hot)
    value_four = slot_spread(value_heads, kind_hot)
    is_one = (code_blk == 1)[None]
    is_two = (code_blk == 2)[None]
    slot_dot = jnp.einsum("thc,shc->hts", q_four, key_four, preferred_element_type=jnp.float32)
    cite_dot = jnp.einsum("thd,shd->hts", q_cite, key_heads, preferred_element_type=jnp.float32)
    scores = jnp.where(is_one, slot_dot, jnp.where(is_two, cite_dot, NEG_FILL))
    return (scores, is_one, is_two, key_heads, value_heads, key_four, value_four, kind_hot)


def attend_block(run_state, kv_blk, q_four, q_cite, code_blk, kind_count):
    run_max, run_sum, acc_four, acc_cite = run_state
    scores, is_one, is_two, key_heads, value_heads, key_four, value_four, kind_hot = block_scores(
        kv_blk, q_four, q_cite, code_blk, kind_count
    )
    new_max = jnp.maximum(run_max, jnp.max(scores, axis=2))
    expd = jnp.where((code_blk > 0)[None], jnp.exp(scores - new_max[:, :, None]), 0.0)
    rescale = jnp.exp(run_max - new_max)
    run_sum = run_sum * rescale + jnp.sum(expd, axis=2)
    prob_low = expd.astype(jnp.bfloat16)
    zero_low = jnp.zeros_like(prob_low)
    p_one = jnp.where(is_one, prob_low, zero_low)
    p_two = jnp.where(is_two, prob_low, zero_low)
    rescale_t = rescale.T[:, :, None]
    acc_four = acc_four * rescale_t + jnp.einsum(
        "hts,shc->thc", p_one, value_four, preferred_element_type=jnp.float32
    )
    acc_cite = acc_cite * rescale_t + jnp.einsum(
        "hts,shd->thd", p_two, value_heads, preferred_element_type=jnp.float32
    )
    return (new_max, run_sum, acc_four, acc_cite)


def back_block(
    kv_blk, q_four, q_cite, grad_four, grad_cite, log_total, row_delta, code_blk, kind_count
):
    scores, is_one, is_two, key_heads, value_heads, key_four, value_four, kind_hot = block_scores(
        kv_blk, q_four, q_cite, code_blk, kind_count
    )
    prob_full = jnp.where((code_blk > 0)[None], jnp.exp(scores - log_total[:, :, None]), 0.0)
    prob_low = prob_full.astype(jnp.bfloat16)
    zero_low = jnp.zeros_like(prob_low)
    p_one = jnp.where(is_one, prob_low, zero_low)
    p_two = jnp.where(is_two, prob_low, zero_low)
    grad_slot = jnp.einsum(
        "thc,shc->hts", grad_four, value_four, preferred_element_type=jnp.float32
    )
    grad_other = jnp.einsum(
        "thd,shd->hts", grad_cite, value_heads, preferred_element_type=jnp.float32
    )
    grad_probs = jnp.where(is_one, grad_slot, jnp.where(is_two, grad_other, 0.0))
    grad_scores = (prob_full * (grad_probs - row_delta[:, :, None])).astype(jnp.bfloat16)
    d_one = jnp.where(is_one, grad_scores, zero_low)
    d_two = jnp.where(is_two, grad_scores, zero_low)
    qf_grad = jnp.einsum("hts,shc->thc", d_one, key_four, preferred_element_type=jnp.float32)
    qc_grad = jnp.einsum("hts,shd->thd", d_two, key_heads, preferred_element_type=jnp.float32)
    k_grad = slot_collapse(
        jnp.einsum("hts,thc->shc", d_one, q_four, preferred_element_type=jnp.float32), kind_hot
    )
    k_grad = k_grad + jnp.einsum("hts,thd->shd", d_two, q_cite, preferred_element_type=jnp.float32)
    v_grad = slot_collapse(
        jnp.einsum("hts,thc->shc", p_one, grad_four, preferred_element_type=jnp.float32), kind_hot
    )
    v_grad = v_grad + jnp.einsum(
        "hts,thd->shd", p_two, grad_cite, preferred_element_type=jnp.float32
    )
    src_rows = k_grad.shape[0]
    return (k_grad.reshape(src_rows, -1), v_grad.reshape(src_rows, -1), qf_grad, qc_grad)


def body(
    features,
    node_type,
    time_gap,
    node_valid,
    edge_codes,
    query_w,
    key_w,
    value_w,
    out_w,
    rel_att,
    rel_msg,
    rel_prior,
    skip_logit,
    rte_w,
    ln_gain,
    ln_bias,
    cotangent,
):
    tgt_rows, feat_dim = features.shape
    kind_count = query_w.shape[0]
    rel_count = rel_att.shape[0]
    head_count = rel_att.shape[1]
    head_size = rel_att.shape[2]
    n_blk = lax.axis_size("blk")
    my_blk = lax.axis_index("blk")
    type_hot = (node_type[:, None] == jnp.arange(kind_count)[None, :]).astype(jnp.float32)
    type_low = type_hot.astype(jnp.bfloat16)
    gap_hot = (time_gap[:, None] == jnp.arange(LEVELS)[None, :]).astype(jnp.float32)
    time_low = time_table(LEVELS, feat_dim).astype(jnp.bfloat16).astype(jnp.float32)
    rte_table = jnp.dot(time_low, rte_w.astype(jnp.float32), precision=HIGH)
    x_f = features.astype(jnp.float32)
    shifted = x_f + jnp.dot(gap_hot, rte_table, precision=HIGH)
    shifted_b = shifted.astype(jnp.bfloat16)

    def typed(inp, weights):
        parts = jnp.einsum("th,khd->tkd", inp, weights, preferred_element_type=jnp.float32)
        return jnp.sum(parts * type_hot[:, :, None], axis=1)

    def typed_grad(inp, grad_low):
        masked = inp[:, None, :] * type_low[:, :, None]
        return jnp.einsum("tkh,td->khd", masked, grad_low, preferred_element_type=jnp.float32)

    def typed_back(grad_low, weights):
        parts = jnp.einsum("td,khd->tkh", grad_low, weights, preferred_element_type=jnp.float32)
        return jnp.sum(parts * type_hot[:, :, None], axis=1)

    q_low = typed(features, query_w).astype(jnp.bfloat16)
    key_low = typed(shifted_b, key_w).astype(jnp.bfloat16)
    value_low = typed(shifted_b, value_w).astype(jnp.bfloat16)
    kind_low = node_type.astype(jnp.bfloat16)
    q_heads = q_low.reshape(tgt_rows, head_count, head_size).astype(jnp.float32)
    att_f = rel_att.astype(jnp.float32)
    factor = rel_prior / math.sqrt(head_size)
    rel_raw = jnp.einsum("thj,rhjk->rthk", q_heads, att_f, precision=HIGH)
    rel_query = (rel_raw * factor[:, None, :, None]).astype(jnp.bfloat16)
    select = jnp.einsum("tk,ksr->tsr", type_hot, jnp.asarray(relation_table()), precision=HIGH)
    select_low = select.astype(jnp.bfloat16)
    cite_hot = (jnp.arange(rel_count) == 3).astype(jnp.float32)
    q_four = (
        jnp.einsum("tsr,rthd->thsd", select_low, rel_query, preferred_element_type=jnp.float32)
        .astype(jnp.bfloat16)
        .reshape(tgt_rows, head_count, kind_count * head_size)
    )
    q_cite = rel_query[3]

    def block_codes(source):
        return lax.dynamic_slice_in_dim(edge_codes, source * tgt_rows, tgt_rows, 1)

    def forward_block(run_state, kv_blk, qf_part, qc_part, code_blk):
        result = attend_block(run_state, kv_blk, qf_part, qc_part, code_blk, kind_count)
        return result

    def backward_block(kv_blk, qf_part, qc_part, gf_part, gc_part, lse_part, delta_part, code_blk):
        return back_block(
            kv_blk, qf_part, qc_part, gf_part, gc_part, lse_part, delta_part, code_blk, kind_count
        )

    whole_kv = (key_low, value_low, kind_low)

    def forward_turn(step_idx, loop_state):
        run_state, kv_blk = loop_state
        run_state = forward_block(
            run_state, kv_blk, q_four, q_cite, block_codes((my_blk - step_idx) % n_blk)
        )
        kv_blk = from_behind((kv_blk[0], kv_blk[1], kv_blk[2]), "blk", 1)
        return (run_state, kv_blk)

    run_state, kv_last = lax.fori_loop(
        0,
        n_blk,
        forward_turn,
        (
            (
                jnp.full((head_count, tgt_rows), NEG_FILL, jnp.float32),
                jnp.zeros((head_count, tgt_rows), jnp.float32),
                jnp.zeros((tgt_rows, head_count, kind_count * head_size), jnp.float32),
                jnp.zeros((tgt_rows, head_count, head_size), jnp.float32),
            ),
            whole_kv,
        ),
    )
    run_max, run_sum, acc_four, acc_cite = run_state
    floor_sum = jnp.maximum(run_sum, 1.0)
    log_total = run_max + jnp.log(floor_sum)
    norm_t = floor_sum.T[:, :, None]
    u_four = acc_four / norm_t
    u_cite = acc_cite / norm_t
    u_rel = jnp.einsum(
        "tsr,thsd->rthd",
        select,
        u_four.reshape(tgt_rows, head_count, kind_count, head_size),
        precision=HIGH,
    )
    u_rel = u_rel + cite_hot[:, None, None, None] * u_cite[None]
    u_rel_b = u_rel.astype(jnp.bfloat16)
    agg_sum = jnp.einsum(
        "rthd,rhde->the", u_rel_b, rel_msg, preferred_element_type=jnp.float32
    ).reshape(tgt_rows, feat_dim)
    act_full, gelu_back = jax.vjp(jax.nn.gelu, agg_sum)
    act_low = act_full.astype(jnp.bfloat16)
    branch = typed(act_low, out_w)
    skip_all = jax.nn.sigmoid(skip_logit)
    skip_gate = jnp.sum(type_hot * skip_all[None, :], axis=1)[:, None]
    mixed_sum = skip_gate * branch + (1.0 - skip_gate) * x_f
    centered = mixed_sum - jnp.mean(mixed_sum, axis=1, keepdims=True)
    inv_std = lax.rsqrt(jnp.mean(centered * centered, axis=1, keepdims=True) + LN_EPS)
    normed = centered * inv_std
    valid_col = node_valid.astype(jnp.float32)[:, None]
    layer_out = (valid_col * (normed * ln_gain + ln_bias)).astype(jnp.bfloat16)
    grad_y = cotangent.astype(jnp.float32) * valid_col
    gain_grad = jnp.sum(grad_y * normed, axis=0)
    bias_grad = jnp.sum(grad_y, axis=0)
    grad_norm = grad_y * ln_gain
    grad_mix = inv_std * (
        grad_norm
        - jnp.mean(grad_norm, axis=1, keepdims=True)
        - normed * jnp.mean(grad_norm * normed, axis=1, keepdims=True)
    )
    grad_branch = (skip_gate * grad_mix).astype(jnp.bfloat16)
    gate_term = (
        jnp.sum(grad_mix * (branch - x_f), axis=1, keepdims=True) * skip_gate * (1.0 - skip_gate)
    )
    skip_grad = jnp.sum(type_hot * gate_term, axis=0)
    out_grad = typed_grad(act_low, grad_branch)
    grad_agg = gelu_back(typed_back(grad_branch, out_w))[0].astype(jnp.bfloat16)
    grad_agg_heads = grad_agg.reshape(tgt_rows, head_count, head_size)
    msg_grad = jnp.einsum(
        "rthd,the->rhde", u_rel_b, grad_agg_heads, preferred_element_type=jnp.float32
    )
    grad_urel = jnp.einsum(
        "the,rhde->rthd", grad_agg_heads, rel_msg, preferred_element_type=jnp.float32
    ).astype(jnp.bfloat16)
    grad_four = (
        jnp.einsum("tsr,rthd->thsd", select_low, grad_urel, preferred_element_type=jnp.float32)
        .astype(jnp.bfloat16)
        .reshape(tgt_rows, head_count, kind_count * head_size)
    )
    grad_cite = grad_urel[3]
    row_delta = (
        jnp.sum(grad_four.astype(jnp.float32) * u_four, axis=2)
        + jnp.sum(grad_cite.astype(jnp.float32) * u_cite, axis=2)
    ).T
    zero_four = jnp.zeros((tgt_rows, head_count, kind_count * head_size), jnp.float32)
    zero_cite = jnp.zeros((tgt_rows, head_count, head_size), jnp.float32)

    def back_turn(step_idx, loop_state):
        kv_blk, travel, acc_qf, acc_qc = loop_state
        k_grad, v_grad, qf_grad, qc_grad = backward_block(
            kv_blk,
            q_four,
            q_cite,
            grad_four,
            grad_cite,
            log_total,
            row_delta,
            block_codes((my_blk - step_idx) % n_blk),
        )
        travel = (
            from_behind((travel[0] + k_grad).astype(jnp.bfloat16), "blk", 1).astype(jnp.float32),
            from_behind((travel[1] + v_grad).astype(jnp.bfloat16), "blk", 1).astype(jnp.float32),
        )
        kv_blk = from_behind((kv_blk[0], kv_blk[1], kv_blk[2]), "blk", 1)
        return (kv_blk, travel, acc_qf + qf_grad, acc_qc + qc_grad)

    zero_kv = jnp.zeros((tgt_rows, feat_dim), jnp.float32)
    loop_state = lax.fori_loop(
        0, n_blk, back_turn, (whole_kv, (zero_kv, zero_kv), zero_four, zero_cite)
    )
    key_acc, value_acc = loop_state[1]
    acc_qf, acc_qc = (loop_state[2], loop_state[3])
    grad_key = key_acc.astype(jnp.bfloat16)
    grad_value = value_acc.astype(jnp.bfloat16)
    grad_relq = jnp.einsum(
        "tsr,thsd->rthd",
        select,
        acc_qf.reshape(tgt_rows, head_count, kind_count, head_size),
        precision=HIGH,
    )
    grad_relq = (
        (grad_relq + cite_hot[:, None, None, None] * acc_qc[None])
        .astype(jnp.bfloat16)
        .astype(jnp.float32)
    )
    prior_grad = jnp.sum(grad_relq * rel_raw, axis=(1, 3)) / math.sqrt(head_size)
    grad_raw = grad_relq * factor[:, None, :, None]
    att_grad = jnp.einsum("thj,rthk->rhjk", q_heads, grad_raw, precision=HIGH)
    grad_query = (
        jnp.einsum("rthk,rhjk->thj", grad_raw, att_f, precision=HIGH)
        .reshape(tgt_rows, feat_dim)
        .astype(jnp.bfloat16)
    )
    query_grad = typed_grad(features, grad_query)
    key_grad = typed_grad(shifted_b, grad_key)
    value_grad = typed_grad(shifted_b, grad_value)
    grad_shift = typed_back(grad_key, key_w) + typed_back(grad_value, value_w)
    table_grad = jnp.dot(gap_hot.T, grad_shift, precision=HIGH)
    rte_grad = jnp.dot(time_low.T, table_grad, precision=HIGH)
    input_grad = (
        (1.0 - skip_gate) * grad_mix + typed_back(grad_query, query_w) + grad_shift
    ).astype(jnp.bfloat16)
    summed = lax.psum(
        (
            query_grad,
            key_grad,
            value_grad,
            out_grad,
            att_grad,
            msg_grad,
            prior_grad,
            skip_grad,
            rte_grad,
            gain_grad,
            bias_grad,
        ),
        ("blk", "rep"),
    )
    return (
        layer_out,
        input_grad,
        summed[0],
        summed[1],
        summed[2],
        summed[3],
        summed[4],
        summed[5],
        summed[6],
        summed[7],
        summed[8],
        summed[9],
        summed[10],
    )


REL_TAB = relation_table()
HALF = 128
F32 = jnp.float32
LOW = jnp.bfloat16
VMEM_CAP = 65000 * 2**10


def nn(a, b):
    return lax.dot_general(a, b, (((1,), (0,)), ((), ())), preferred_element_type=F32)


def nt(a, b):
    return lax.dot_general(a, b, (((1,), (1,)), ((), ())), preferred_element_type=F32)


def tn(a, b):
    return lax.dot_general(a, b, (((0,), (0,)), ((), ())), preferred_element_type=F32)


def pick(kinds, kind, value):
    return jnp.where(kinds == kind, value, jnp.zeros_like(value))


def relation_of(kind, slot):
    hit = np.nonzero(REL_TAB[kind, slot])[0]
    return int(hit[0]) if len(hit) else None


def to_slots(rel_rows, kinds, kind_count):
    slots = []
    for slot in range(kind_count):
        rows = jnp.zeros(kinds.shape, F32)
        for kind in range(kind_count):
            rel = relation_of(kind, slot)
            if rel is not None:
                rows = jnp.where(kinds == kind, rel_rows(rel), rows)
        slots.append(rows)
    return slots, pick(kinds, 0, rel_rows(3))


def to_relations(slot_rows, cite_rows, kinds, kind_count, rel_count):
    out = []
    for rel in range(rel_count):
        if rel == 3:
            out.append(pick(kinds, 0, cite_rows))
            continue
        (kind, slot) = [
            (k, s) for k in range(kind_count) for s in range(kind_count) if relation_of(k, s) == rel
        ][0]
        out.append(pick(kinds, kind, slot_rows(slot)))
    return out


def prep_kernel(x_ref, meta_ref, rte_ref, time_ref, shifted_ref, xt_ref):
    levels = time_ref.shape[1]
    x_t = x_ref[...].astype(F32).T
    xt_ref[...] = x_t.astype(LOW)
    table = tn(rte_ref[...], time_ref[...])
    table_hi = table.astype(LOW)
    table_lo = (table - table_hi.astype(F32)).astype(LOW)
    gaps = jnp.broadcast_to(meta_ref[1:2, :], (levels, x_t.shape[1]))
    hot = (lax.broadcasted_iota(jnp.int32, gaps.shape, 0) == gaps).astype(F32).astype(LOW)
    shifted_ref[...] = (x_t + nn(table_hi, hot) + nn(table_lo, hot)).astype(LOW)


def layer_kernel(
    xt_ref,
    shifted_ref,
    meta_ref,
    metas_ref,
    codes_ref,
    cot_ref,
    qw_ref,
    kw_ref,
    vw_ref,
    ow_ref,
    att_ref,
    msg_ref,
    factor_ref,
    gate_ref,
    gain_ref,
    bias_ref,
    out_ref,
    base_ref,
    gsh_ref,
    qg_ref,
    kg_ref,
    vg_ref,
    og_ref,
    atta_ref,
    msga_ref,
    pack_ref,
    kt,
    vx,
    sbuf,
    probs,
    mx,
    sm,
    qs,
    qt2,
    qh,
    gs,
    gt2,
    acc,
    urel,
    dka,
    dva,
    two,
    wkt,
    wvt,
    agg,
):
    feat, rows = xt_ref.shape
    n_blk = shifted_ref.shape[0]
    kind_count = qw_ref.shape[0]
    heads, size = qh.shape[0], qh.shape[1]
    rel_count = att_ref.shape[1] // size
    kinds = jnp.broadcast_to(meta_ref[0:1, :], (size, rows))
    kinds_f = jnp.broadcast_to(meta_ref[0:1, :], (feat, rows))
    valid_f = jnp.broadcast_to(meta_ref[2:3, :], (feat, rows)).astype(F32)
    lane = lax.broadcasted_iota(jnp.int32, (rows, HALF), 1)
    ones_pad = (lax.broadcasted_iota(jnp.int32, (16, rows), 0) < 2).astype(F32).astype(LOW)

    def cols(j):
        return pl.ds(pl.multiple_of(j * rows, rows), rows)

    for k in range(kind_count):
        wkt[pl.ds(k * feat, feat), :] = kw_ref[k].astype(F32).T.astype(LOW)
        wvt[pl.ds(k * feat, feat), :] = vw_ref[k].astype(F32).T.astype(LOW)

    x_t = xt_ref[...]
    q_full = jnp.zeros((feat, rows), F32)
    for k in range(kind_count):
        q_full = jnp.where(kinds_f == k, tn(qw_ref[k], x_t), q_full)
    for h in range(heads):
        qh[h] = q_full[h * size : (h + 1) * size].astype(LOW)

    def query_head(h, carry):
        raw = nn(att_ref[h], qh[h])

        def rel_rows(r):
            return (raw[r * size : (r + 1) * size] * factor_ref[r, h]).astype(LOW).astype(F32)

        slots, cite = to_slots(rel_rows, kinds, kind_count)
        slot_t = jnp.concatenate(slots, axis=0)
        cite_t = jnp.concatenate([cite, jnp.zeros((HALF - size, rows), F32)], axis=0)
        qt2[h, :, 0:rows] = slot_t.astype(LOW)
        qt2[h, :, rows:] = cite_t.astype(LOW)
        qs[h, 0:rows, :] = slot_t.T.astype(LOW)
        qs[h, rows:, :] = cite_t.T.astype(LOW)
        return carry

    lax.fori_loop(0, heads, query_head, 0)

    def expand(j, carry):
        src = jnp.broadcast_to(metas_ref[j, 0:1, :], (size, rows))
        block = shifted_ref[j]
        for k in range(kind_count):
            key = nn(wkt[pl.ds(k * feat, feat), :], block)
            value = nn(wvt[pl.ds(k * feat, feat), :], block)
            for h in range(heads):
                part = slice(h * size, (h + 1) * size)
                kt[j, h, pl.ds(k * size, size), :] = pick(src, k, key[part]).astype(LOW)
                vx[j, h, pl.ds(k * size, size), :] = pick(src, k, value[part]).astype(LOW)
        for h in range(heads):
            vx[j, h, pl.ds(HALF, 16), :] = ones_pad
        two[j] = (codes_ref[:, cols(j)] == 2).astype(F32).astype(LOW)
        return carry

    lax.fori_loop(0, n_blk, expand, 0)

    def score_block(h, j):
        both = nn(qs[h], kt[j, h])
        code = codes_ref[:, cols(j)]
        val = jnp.where(code == 2, both[rows:], both[:rows])
        val = jnp.where(code > 0, val, NEG_FILL)
        sbuf[h % 2, j] = val
        top = jnp.maximum(val[:, :HALF], val[:, HALF:])
        for c in range(2 * HALF, rows, HALF):
            top = jnp.maximum(top, val[:, c : c + HALF])
        mx[h % 2] = jnp.maximum(mx[h % 2], top)

    def prob_block(h, j):
        top = sm[h % 2]
        val = jnp.exp(sbuf[h % 2, j] - jnp.concatenate([top] * (rows // HALF), axis=1))
        total = val[:, :HALF]
        for c in range(HALF, rows, HALF):
            total = total + val[:, c : c + HALF]
        mx[2 + h % 2] = mx[2 + h % 2] + total
        low = val.astype(LOW)
        second = low * two[j]
        probs[j, h, 0:rows, :] = low - second
        probs[j, h, rows:, :] = second
        acc[h] = acc[h] + nt(vx[j, h, 0:HALF, :], probs[j, h])

    def open_head(h):
        mx[h % 2] = jnp.full((rows, HALF), NEG_FILL, F32)

    def close_scores(h):
        top = jnp.max(mx[h % 2], axis=1, keepdims=True)
        sm[h % 2] = jnp.broadcast_to(jnp.maximum(top, 0.1 * NEG_FILL), (rows, HALF))
        mx[2 + h % 2] = jnp.zeros((rows, HALF), F32)
        acc[h] = jnp.zeros(acc.shape[1:], F32)

    def close_probs(h):
        total = jnp.sum(mx[2 + h % 2], axis=1, keepdims=True)
        sm[2] = jnp.where(lane == h, jnp.broadcast_to(total, (rows, HALF)), sm[2])

    sm[2] = jnp.zeros((rows, HALF), F32)
    open_head(0)

    def first(j, carry):
        score_block(0, j)
        return carry

    lax.fori_loop(0, n_blk, first, 0)

    def forward_head(h, carry):
        close_scores(h)
        open_head(h + 1)

        def step(j, carry):
            score_block(h + 1, j)
            prob_block(h, j)
            return carry

        lax.fori_loop(0, n_blk, step, 0)
        close_probs(h)
        return carry

    lax.fori_loop(0, heads - 1, forward_head, 0)
    close_scores(heads - 1)

    def last(j, carry):
        prob_block(heads - 1, j)
        return carry

    lax.fori_loop(0, n_blk, last, 0)
    close_probs(heads - 1)

    denom = jnp.maximum(sm[2].T, 1.0)
    inverse = 1.0 / denom
    sm[2, 0:HALF, :] = inverse[:, 0:HALF]
    sm[2, HALF : 2 * HALF, :] = inverse[:, HALF : 2 * HALF]

    def inv_row(h, count):
        row = jnp.concatenate([sm[2, pl.ds(h, 1), :], sm[2, pl.ds(HALF + h, 1), :]], axis=1)
        return jnp.broadcast_to(row, (count, rows))

    for h in range(heads):
        inv = inv_row(h, HALF)
        u_slot = acc[h, :, 0:rows] * inv
        u_cite = acc[h, 0:size, rows:] * inv[0:size]
        acc[h, :, 0:rows] = u_slot
        acc[h, 0:size, rows:] = u_cite
        rel = to_relations(
            lambda s: u_slot[s * size : (s + 1) * size], u_cite, kinds, kind_count, rel_count
        )
        urel[h] = jnp.concatenate(rel, axis=0).astype(LOW)
        agg[pl.ds(h * size, size), :] = tn(msg_ref[h], urel[h])
    agg_t = agg[...]
    slope = 0.7978845608028654
    inner = jnp.tanh(slope * (agg_t + 0.044715 * agg_t * agg_t * agg_t))
    act_t = (0.5 * agg_t * (1.0 + inner)).astype(LOW)
    gelu_back = 0.5 * (1.0 + inner) + 0.5 * agg_t * (1.0 - inner * inner) * slope * (
        1.0 + 3.0 * 0.044715 * agg_t * agg_t
    )
    x_f = x_t.astype(F32)
    gate = jnp.zeros((feat, rows), F32)
    branch = jnp.zeros((feat, rows), F32)
    for k in range(kind_count):
        gate = jnp.where(kinds_f == k, gate_ref[k], gate)
        branch = jnp.where(kinds_f == k, tn(ow_ref[k], act_t), branch)
    mixed = gate * branch + (1.0 - gate) * x_f
    centered = mixed - jnp.mean(mixed, axis=0, keepdims=True)
    inv_std = lax.rsqrt(jnp.mean(centered * centered, axis=0, keepdims=True) + LN_EPS)
    normed = centered * inv_std
    gain = gain_ref[...]
    out_t = valid_f * (normed * gain + bias_ref[...])
    out_ref[...] = out_t.T.astype(LOW)
    grad_y = cot_ref[...].astype(F32).T * valid_f
    gain_col = jnp.sum(grad_y * normed, axis=1, keepdims=True)
    bias_col = jnp.sum(grad_y, axis=1, keepdims=True)
    grad_norm = grad_y * gain
    grad_mix = inv_std * (
        grad_norm
        - jnp.mean(grad_norm, axis=0, keepdims=True)
        - normed * jnp.mean(grad_norm * normed, axis=0, keepdims=True)
    )
    gate_row = gate[0:1]
    skip_row = (
        jnp.sum(grad_mix * (branch - x_f), axis=0, keepdims=True) * gate_row * (1.0 - gate_row)
    )
    base_ref[...] = (1.0 - gate) * grad_mix
    grad_branch = (gate * grad_mix).astype(LOW)
    grad_act = jnp.zeros((feat, rows), F32)
    for k in range(kind_count):
        masked = pick(kinds_f, k, grad_branch.astype(F32)).astype(LOW)
        og_ref[k] = nt(act_t, masked)
        grad_act = grad_act + nn(ow_ref[k], masked)
    agg[...] = gelu_back * grad_act

    def grad_head(h, carry):
        grad_agg = agg[pl.ds(pl.multiple_of(h * size, size), size), :].astype(LOW)
        msga_ref[pl.ds(pl.multiple_of(h * size, size), size), :] = nt(grad_agg, urel[h])
        inv = inv_row(h, size)
        grad_u = nn(msg_ref[h], grad_agg)

        def rel_rows(r):
            return grad_u[r * size : (r + 1) * size] * inv

        slots, cite = to_slots(rel_rows, kinds, kind_count)
        slot_t = jnp.concatenate(slots, axis=0).astype(LOW)
        cite_t = jnp.concatenate([cite, jnp.zeros((HALF - size, rows), F32)], axis=0).astype(LOW)
        gt2[h, :, 0:rows] = slot_t
        gt2[h, :, rows:] = cite_t
        slot_f = slot_t.astype(F32)
        cite_f = cite_t.astype(F32)
        delta = -(
            jnp.sum(slot_f * acc[h, :, 0:rows], axis=0, keepdims=True)
            + jnp.sum(cite_f[0:size] * acc[h, 0:size, rows:], axis=0, keepdims=True)
        )
        delta_hi = delta.astype(LOW).astype(F32)
        tail = jnp.concatenate(
            [delta_hi, delta - delta_hi, jnp.zeros((HALF - 2, rows), F32)], axis=0
        )
        tail_t = tail.T.astype(LOW)
        gs[h, 0:rows, 0:HALF] = slot_f.T.astype(LOW)
        gs[h, rows:, 0:HALF] = cite_f.T.astype(LOW)
        gs[h, 0:rows, HALF:] = tail_t[:, 0:16]
        gs[h, rows:, HALF:] = tail_t[:, 0:16]
        acc[h] = jnp.zeros(acc.shape[1:], F32)
        return carry

    lax.fori_loop(0, heads, grad_head, 0)

    slot_id = lax.broadcasted_iota(jnp.int32, (HALF, rows), 0) // size

    def back_block(j, carry):
        src = jnp.broadcast_to(metas_ref[j, 0:1, :], (HALF, rows))
        own = slot_id == src

        def back_head(h, carry):
            pair = probs[j, h]
            grad = pair * nn(gs[h], vx[j, h]).astype(LOW)
            d_key = jnp.where(own, nn(qt2[h], grad), 0.0).astype(LOW)
            d_value = jnp.where(own, nn(gt2[h], pair), 0.0).astype(LOW)
            for k in range(kind_count):
                at = pl.ds(pl.multiple_of(k * feat + h * size, size), size)
                dka[at, cols(j)] = d_key[k * size : (k + 1) * size]
                dva[at, cols(j)] = d_value[k * size : (k + 1) * size]
            acc[h] = acc[h] + nt(kt[j, h], grad)
            return carry

        lax.fori_loop(0, heads, back_head, 0)
        return carry

    lax.fori_loop(0, n_blk, back_block, 0)

    level_count = 16
    table = jnp.zeros((feat, level_count), F32)
    for k in range(kind_count):
        at = pl.ds(k * feat, feat)
        k_sum = jnp.zeros((feat, feat), F32)
        v_sum = jnp.zeros((feat, feat), F32)
        for j in range(n_blk):
            k_sum = k_sum + nt(shifted_ref[j], dka[at, pl.ds(j * rows, rows)])
            v_sum = v_sum + nt(shifted_ref[j], dva[at, pl.ds(j * rows, rows)])
        kg_ref[k] = k_sum
        vg_ref[k] = v_sum
    pack_ref[...] = jnp.zeros_like(pack_ref)

    def shift_block(j, carry):
        total = jnp.zeros((feat, rows), F32)
        for k in range(kind_count):
            at = pl.ds(k * feat, feat)
            total = total + nn(kw_ref[k], dka[at, cols(j)]) + nn(vw_ref[k], dva[at, cols(j)])
        low = total.astype(LOW)
        gsh_ref[j] = low
        gaps = jnp.broadcast_to(metas_ref[j, 1:2, :], (level_count, rows))
        hot = (lax.broadcasted_iota(jnp.int32, gaps.shape, 0) == gaps).astype(F32).astype(LOW)
        pack_ref[:, 0:level_count] = pack_ref[:, 0:level_count] + nt(low, hot)
        return carry

    lax.fori_loop(0, n_blk, shift_block, 0)
    wide = lax.broadcasted_iota(jnp.int32, (feat, HALF), 1)
    row_at = lax.broadcasted_iota(jnp.int32, (feat, HALF), 0)
    pack = pack_ref[...]
    pack = jnp.where(wide == level_count, jnp.broadcast_to(gain_col, (feat, HALF)), pack)
    pack = jnp.where(wide == level_count + 1, jnp.broadcast_to(bias_col, (feat, HALF)), pack)
    for k in range(kind_count):
        mine = jnp.sum(pick(kinds[0:1], k, skip_row), axis=1, keepdims=True)
        pack = jnp.where(
            (wide == level_count + 2) & (row_at == k), jnp.broadcast_to(mine, (feat, HALF)), pack
        )
    pack_ref[...] = pack

    def query_back(h, carry):
        slot = acc[h, :, 0:rows]
        rel = to_relations(
            lambda s: slot[s * size : (s + 1) * size],
            acc[h, 0:size, rows:],
            kinds,
            kind_count,
            rel_count,
        )
        rel = [part.astype(LOW) for part in rel]
        at = pl.ds(pl.multiple_of(h * size, size), size)
        atta_ref[at, :] = nt(qh[h], jnp.concatenate(rel, axis=0))
        raw = [(part.astype(F32) * factor_ref[r, h]).astype(LOW) for r, part in enumerate(rel)]
        agg[at, :] = tn(att_ref[h], jnp.concatenate(raw, axis=0))
        return carry

    lax.fori_loop(0, heads, query_back, 0)
    grad_q = agg[...].astype(LOW).astype(F32)
    base = base_ref[...]
    for k in range(kind_count):
        masked = pick(kinds_f, k, grad_q).astype(LOW)
        qg_ref[k] = nt(x_t, masked)
        base = base + nn(qw_ref[k], masked)
    base_ref[...] = base


def fast_body(
    features,
    node_type,
    time_gap,
    node_valid,
    edge_codes,
    query_w,
    key_w,
    value_w,
    out_w,
    rel_att,
    rel_msg,
    rel_prior,
    skip_logit,
    rte_w,
    ln_gain,
    ln_bias,
    cotangent,
):
    rows, feat = features.shape
    n_blk = lax.axis_size("blk")
    kind_count = query_w.shape[0]
    rel_count, heads, size = rel_att.shape[:3]
    time_low = time_table(LEVELS, feat).astype(LOW)
    meta = jnp.concatenate(
        [node_type[None], time_gap[None], node_valid[None], jnp.zeros((5, rows), jnp.int32)], axis=0
    )
    vmem = pl.BlockSpec(memory_space=pltpu.VMEM)
    smem = pl.BlockSpec(memory_space=pltpu.SMEM)
    shifted, x_t = pl.pallas_call(
        prep_kernel,
        out_shape=[jax.ShapeDtypeStruct((feat, rows), LOW)] * 2,
        in_specs=[vmem] * 4,
        out_specs=[vmem] * 2,
        name="prep",
    )(features, meta, rte_w, time_low.T)
    shifted_all = lax.all_gather(shifted, "blk")
    meta_all = lax.all_gather(meta, "blk")
    att_rows = rel_att.transpose(1, 0, 3, 2).reshape(heads, rel_count * size, size)
    msg_rows = rel_msg.transpose(1, 0, 2, 3).reshape(heads, rel_count * size, size)
    factor = rel_prior / math.sqrt(size)
    gate = jax.nn.sigmoid(skip_logit)

    def shape(dims, kind):
        return jax.ShapeDtypeStruct(dims, kind)

    square = (feat, feat)
    outs = pl.pallas_call(
        layer_kernel,
        out_shape=[
            shape((rows, feat), LOW),
            shape((feat, rows), F32),
            shape((n_blk, feat, rows), LOW),
        ]
        + [shape((kind_count,) + square, F32)] * 4
        + [shape(square, F32)] * 2
        + [shape((feat, HALF), F32)],
        in_specs=[vmem] * 12 + [smem] * 2 + [vmem] * 2,
        out_specs=[vmem] * 10,
        scratch_shapes=[
            pltpu.VMEM((n_blk, heads, HALF, rows), LOW),
            pltpu.VMEM((n_blk, heads, HALF + 16, rows), LOW),
            pltpu.VMEM((2, n_blk, rows, rows), F32),
            pltpu.VMEM((n_blk, heads, 2 * rows, rows), LOW),
            pltpu.VMEM((4, rows, HALF), F32),
            pltpu.VMEM((3, rows, HALF), F32),
            pltpu.VMEM((heads, 2 * rows, HALF), LOW),
            pltpu.VMEM((heads, HALF, 2 * rows), LOW),
            pltpu.VMEM((heads, size, rows), LOW),
            pltpu.VMEM((heads, 2 * rows, HALF + 16), LOW),
            pltpu.VMEM((heads, HALF, 2 * rows), LOW),
            pltpu.VMEM((heads, HALF, 2 * rows), F32),
            pltpu.VMEM((heads, rel_count * size, rows), LOW),
            pltpu.VMEM((kind_count * feat, n_blk * rows), LOW),
            pltpu.VMEM((kind_count * feat, n_blk * rows), LOW),
            pltpu.VMEM((n_blk, rows, rows), LOW),
            pltpu.VMEM((kind_count * feat, feat), LOW),
            pltpu.VMEM((kind_count * feat, feat), LOW),
            pltpu.VMEM(square, F32),
        ],
        compiler_params=pltpu.CompilerParams(vmem_limit_bytes=VMEM_CAP),
        name="layer",
    )(
        x_t,
        shifted_all,
        meta,
        meta_all,
        edge_codes,
        cotangent,
        query_w,
        key_w,
        value_w,
        out_w,
        att_rows,
        msg_rows,
        factor,
        gate,
        ln_gain[:, None],
        ln_bias[:, None],
    )
    layer_out, base, gsh, qg, kg, vg, og, att_a, msg_a, pack = outs
    own = lax.psum_scatter(gsh.astype(F32), "blk", scatter_dimension=0)
    input_grad = (base + own).T.astype(LOW)
    qg, kg, vg, og, att_a, msg_a, pack = lax.psum(
        (qg, kg, vg, og, att_a, msg_a, pack), ("blk", "rep")
    )
    att_grad = att_a.reshape(heads, size, rel_count, size).transpose(2, 0, 1, 3)
    prior_grad = jnp.sum(att_grad * rel_att.astype(F32), axis=(2, 3)) / math.sqrt(size)
    att_grad = att_grad * factor[:, :, None, None]
    msg_grad = msg_a.reshape(heads, size, rel_count, size).transpose(2, 0, 3, 1)
    rte_grad = jnp.dot(time_low.astype(F32).T, pack[:, :LEVELS].T, precision=HIGH)
    return (
        layer_out,
        input_grad,
        qg,
        kg,
        vg,
        og,
        att_grad,
        msg_grad,
        prior_grad,
        pack[:kind_count, LEVELS + 2],
        rte_grad,
        pack[:, LEVELS],
        pack[:, LEVELS + 1],
    )


def solution(mesh):
    in_specs = (
        P(("blk", "rep"), None),
        P(("blk", "rep")),
        P(("blk", "rep")),
        P(("blk", "rep")),
        P(("blk", "rep"), None),
        P(),
        P(),
        P(),
        P(),
        P(),
        P(),
        P(),
        P(),
        P(),
        P(),
        P(),
        P(("blk", "rep"), None),
    )
    out_specs = (
        P(("blk", "rep"), None),
        P(("blk", "rep"), None),
        P(),
        P(),
        P(),
        P(),
        P(),
        P(),
        P(),
        P(),
        P(),
        P(),
        P(),
    )
    plan = fast_body if mesh.shape["blk"] <= 8 else body
    return jax.shard_map(plan, mesh=mesh, in_specs=in_specs, out_specs=out_specs, check_vma=False)
```

```python
import math

import jax
import jax.numpy as jnp
import numpy as np
from jax import lax
from jax.experimental import pallas as pl
from jax.experimental.pallas import tpu as pltpu
from jax.sharding import PartitionSpec as P

LEVELS = 16


NEG_FILL = -1e30
LN_EPS = 1e-05
HIGH = lax.Precision.HIGHEST


def from_behind(block, axis, distance):
    devices = range(lax.axis_size(axis))
    route = [((i - distance) % len(devices), i) for i in devices]
    return lax.ppermute(block, axis, route)


def relation_table():
    rel_tab = np.zeros((4, 4, 8), np.float32)
    rel_tab[0, 1, 0] = 1.0
    rel_tab[1, 0, 1] = 1.0
    rel_tab[0, 0, 2] = 1.0
    rel_tab[2, 0, 4] = 1.0
    rel_tab[0, 2, 5] = 1.0
    rel_tab[3, 1, 6] = 1.0
    rel_tab[1, 3, 7] = 1.0
    return rel_tab


def time_table(level_count, feat_width):
    positions = jnp.arange(level_count, dtype=jnp.float32)[:, None]
    freq_idx = jnp.arange(feat_width // 2, dtype=jnp.float32)[None, :]
    phases = positions / jnp.power(10000.0, 2.0 * freq_idx / feat_width)
    return jnp.stack([jnp.sin(phases), jnp.cos(phases)], axis=2).reshape(level_count, feat_width)


def slot_spread(heads_arr, kind_hot):
    spread_out = heads_arr[:, :, None, :] * kind_hot[:, None, :, None]
    return spread_out.reshape(heads_arr.shape[0], heads_arr.shape[1], -1)


def slot_collapse(slot_arr, kind_hot):
    src_rows, head_count = (slot_arr.shape[0], slot_arr.shape[1])
    kind_count = kind_hot.shape[1]
    shaped = slot_arr.reshape(src_rows, head_count, kind_count, -1)
    return jnp.sum(shaped * kind_hot.astype(jnp.float32)[:, None, :, None], axis=2)


def block_scores(kv_blk, q_four, q_cite, code_blk, kind_count):
    key_blk, value_blk, kind_blk = kv_blk
    src_rows = key_blk.shape[0]
    head_count = q_four.shape[1]
    key_heads = key_blk.reshape(src_rows, head_count, -1)
    value_heads = value_blk.reshape(src_rows, head_count, -1)
    kind_hot = (kind_blk[:, None] == jnp.arange(kind_count).astype(jnp.bfloat16)[None, :]).astype(
        jnp.bfloat16
    )
    key_four = slot_spread(key_heads, kind_hot)
    value_four = slot_spread(value_heads, kind_hot)
    is_one = (code_blk == 1)[None]
    is_two = (code_blk == 2)[None]
    slot_dot = jnp.einsum("thc,shc->hts", q_four, key_four, preferred_element_type=jnp.float32)
    cite_dot = jnp.einsum("thd,shd->hts", q_cite, key_heads, preferred_element_type=jnp.float32)
    scores = jnp.where(is_one, slot_dot, jnp.where(is_two, cite_dot, NEG_FILL))
    return (scores, is_one, is_two, key_heads, value_heads, key_four, value_four, kind_hot)


def attend_block(run_state, kv_blk, q_four, q_cite, code_blk, kind_count):
    run_max, run_sum, acc_four, acc_cite = run_state
    scores, is_one, is_two, key_heads, value_heads, key_four, value_four, kind_hot = block_scores(
        kv_blk, q_four, q_cite, code_blk, kind_count
    )
    new_max = jnp.maximum(run_max, jnp.max(scores, axis=2))
    expd = jnp.where((code_blk > 0)[None], jnp.exp(scores - new_max[:, :, None]), 0.0)
    rescale = jnp.exp(run_max - new_max)
    run_sum = run_sum * rescale + jnp.sum(expd, axis=2)
    prob_low = expd.astype(jnp.bfloat16)
    zero_low = jnp.zeros_like(prob_low)
    p_one = jnp.where(is_one, prob_low, zero_low)
    p_two = jnp.where(is_two, prob_low, zero_low)
    rescale_t = rescale.T[:, :, None]
    acc_four = acc_four * rescale_t + jnp.einsum(
        "hts,shc->thc", p_one, value_four, preferred_element_type=jnp.float32
    )
    acc_cite = acc_cite * rescale_t + jnp.einsum(
        "hts,shd->thd", p_two, value_heads, preferred_element_type=jnp.float32
    )
    return (new_max, run_sum, acc_four, acc_cite)


def back_block(
    kv_blk, q_four, q_cite, grad_four, grad_cite, log_total, row_delta, code_blk, kind_count
):
    scores, is_one, is_two, key_heads, value_heads, key_four, value_four, kind_hot = block_scores(
        kv_blk, q_four, q_cite, code_blk, kind_count
    )
    prob_full = jnp.where((code_blk > 0)[None], jnp.exp(scores - log_total[:, :, None]), 0.0)
    prob_low = prob_full.astype(jnp.bfloat16)
    zero_low = jnp.zeros_like(prob_low)
    p_one = jnp.where(is_one, prob_low, zero_low)
    p_two = jnp.where(is_two, prob_low, zero_low)
    grad_slot = jnp.einsum(
        "thc,shc->hts", grad_four, value_four, preferred_element_type=jnp.float32
    )
    grad_other = jnp.einsum(
        "thd,shd->hts", grad_cite, value_heads, preferred_element_type=jnp.float32
    )
    grad_probs = jnp.where(is_one, grad_slot, jnp.where(is_two, grad_other, 0.0))
    grad_scores = (prob_full * (grad_probs - row_delta[:, :, None])).astype(jnp.bfloat16)
    d_one = jnp.where(is_one, grad_scores, zero_low)
    d_two = jnp.where(is_two, grad_scores, zero_low)
    qf_grad = jnp.einsum("hts,shc->thc", d_one, key_four, preferred_element_type=jnp.float32)
    qc_grad = jnp.einsum("hts,shd->thd", d_two, key_heads, preferred_element_type=jnp.float32)
    k_grad = slot_collapse(
        jnp.einsum("hts,thc->shc", d_one, q_four, preferred_element_type=jnp.float32), kind_hot
    )
    k_grad = k_grad + jnp.einsum("hts,thd->shd", d_two, q_cite, preferred_element_type=jnp.float32)
    v_grad = slot_collapse(
        jnp.einsum("hts,thc->shc", p_one, grad_four, preferred_element_type=jnp.float32), kind_hot
    )
    v_grad = v_grad + jnp.einsum(
        "hts,thd->shd", p_two, grad_cite, preferred_element_type=jnp.float32
    )
    src_rows = k_grad.shape[0]
    return (k_grad.reshape(src_rows, -1), v_grad.reshape(src_rows, -1), qf_grad, qc_grad)


def body(
    features,
    node_type,
    time_gap,
    node_valid,
    edge_codes,
    query_w,
    key_w,
    value_w,
    out_w,
    rel_att,
    rel_msg,
    rel_prior,
    skip_logit,
    rte_w,
    ln_gain,
    ln_bias,
    cotangent,
):
    tgt_rows, feat_dim = features.shape
    kind_count = query_w.shape[0]
    rel_count = rel_att.shape[0]
    head_count = rel_att.shape[1]
    head_size = rel_att.shape[2]
    n_blk = lax.axis_size("blk")
    my_blk = lax.axis_index("blk")
    type_hot = (node_type[:, None] == jnp.arange(kind_count)[None, :]).astype(jnp.float32)
    type_low = type_hot.astype(jnp.bfloat16)
    gap_hot = (time_gap[:, None] == jnp.arange(LEVELS)[None, :]).astype(jnp.float32)
    time_low = time_table(LEVELS, feat_dim).astype(jnp.bfloat16).astype(jnp.float32)
    rte_table = jnp.dot(time_low, rte_w.astype(jnp.float32), precision=HIGH)
    x_f = features.astype(jnp.float32)
    shifted = x_f + jnp.dot(gap_hot, rte_table, precision=HIGH)
    shifted_b = shifted.astype(jnp.bfloat16)

    def typed(inp, weights):
        parts = jnp.einsum("th,khd->tkd", inp, weights, preferred_element_type=jnp.float32)
        return jnp.sum(parts * type_hot[:, :, None], axis=1)

    def typed_grad(inp, grad_low):
        masked = inp[:, None, :] * type_low[:, :, None]
        return jnp.einsum("tkh,td->khd", masked, grad_low, preferred_element_type=jnp.float32)

    def typed_back(grad_low, weights):
        parts = jnp.einsum("td,khd->tkh", grad_low, weights, preferred_element_type=jnp.float32)
        return jnp.sum(parts * type_hot[:, :, None], axis=1)

    q_low = typed(features, query_w).astype(jnp.bfloat16)
    key_low = typed(shifted_b, key_w).astype(jnp.bfloat16)
    value_low = typed(shifted_b, value_w).astype(jnp.bfloat16)
    kind_low = node_type.astype(jnp.bfloat16)
    q_heads = q_low.reshape(tgt_rows, head_count, head_size).astype(jnp.float32)
    att_f = rel_att.astype(jnp.float32)
    factor = rel_prior / math.sqrt(head_size)
    rel_raw = jnp.einsum("thj,rhjk->rthk", q_heads, att_f, precision=HIGH)
    rel_query = (rel_raw * factor[:, None, :, None]).astype(jnp.bfloat16)
    select = jnp.einsum("tk,ksr->tsr", type_hot, jnp.asarray(relation_table()), precision=HIGH)
    select_low = select.astype(jnp.bfloat16)
    cite_hot = (jnp.arange(rel_count) == 3).astype(jnp.float32)
    q_four = (
        jnp.einsum("tsr,rthd->thsd", select_low, rel_query, preferred_element_type=jnp.float32)
        .astype(jnp.bfloat16)
        .reshape(tgt_rows, head_count, kind_count * head_size)
    )
    q_cite = rel_query[3]

    def block_codes(source):
        return lax.dynamic_slice_in_dim(edge_codes, source * tgt_rows, tgt_rows, 1)

    def forward_block(run_state, kv_blk, qf_part, qc_part, code_blk):
        result = attend_block(run_state, kv_blk, qf_part, qc_part, code_blk, kind_count)
        return result

    def backward_block(kv_blk, qf_part, qc_part, gf_part, gc_part, lse_part, delta_part, code_blk):
        return back_block(
            kv_blk, qf_part, qc_part, gf_part, gc_part, lse_part, delta_part, code_blk, kind_count
        )

    whole_kv = (key_low, value_low, kind_low)

    def forward_turn(step_idx, loop_state):
        run_state, kv_blk = loop_state
        run_state = forward_block(
            run_state, kv_blk, q_four, q_cite, block_codes((my_blk - step_idx) % n_blk)
        )
        kv_blk = from_behind((kv_blk[0], kv_blk[1], kv_blk[2]), "blk", 1)
        return (run_state, kv_blk)

    run_state, kv_last = lax.fori_loop(
        0,
        n_blk,
        forward_turn,
        (
            (
                jnp.full((head_count, tgt_rows), NEG_FILL, jnp.float32),
                jnp.zeros((head_count, tgt_rows), jnp.float32),
                jnp.zeros((tgt_rows, head_count, kind_count * head_size), jnp.float32),
                jnp.zeros((tgt_rows, head_count, head_size), jnp.float32),
            ),
            whole_kv,
        ),
    )
    run_max, run_sum, acc_four, acc_cite = run_state
    floor_sum = jnp.maximum(run_sum, 1.0)
    log_total = run_max + jnp.log(floor_sum)
    norm_t = floor_sum.T[:, :, None]
    u_four = acc_four / norm_t
    u_cite = acc_cite / norm_t
    u_rel = jnp.einsum(
        "tsr,thsd->rthd",
        select,
        u_four.reshape(tgt_rows, head_count, kind_count, head_size),
        precision=HIGH,
    )
    u_rel = u_rel + cite_hot[:, None, None, None] * u_cite[None]
    u_rel_b = u_rel.astype(jnp.bfloat16)
    agg_sum = jnp.einsum(
        "rthd,rhde->the", u_rel_b, rel_msg, preferred_element_type=jnp.float32
    ).reshape(tgt_rows, feat_dim)
    act_full, gelu_back = jax.vjp(jax.nn.gelu, agg_sum)
    act_low = act_full.astype(jnp.bfloat16)
    branch = typed(act_low, out_w)
    skip_all = jax.nn.sigmoid(skip_logit)
    skip_gate = jnp.sum(type_hot * skip_all[None, :], axis=1)[:, None]
    mixed_sum = skip_gate * branch + (1.0 - skip_gate) * x_f
    centered = mixed_sum - jnp.mean(mixed_sum, axis=1, keepdims=True)
    inv_std = lax.rsqrt(jnp.mean(centered * centered, axis=1, keepdims=True) + LN_EPS)
    normed = centered * inv_std
    valid_col = node_valid.astype(jnp.float32)[:, None]
    layer_out = (valid_col * (normed * ln_gain + ln_bias)).astype(jnp.bfloat16)
    grad_y = cotangent.astype(jnp.float32) * valid_col
    gain_grad = jnp.sum(grad_y * normed, axis=0)
    bias_grad = jnp.sum(grad_y, axis=0)
    grad_norm = grad_y * ln_gain
    grad_mix = inv_std * (
        grad_norm
        - jnp.mean(grad_norm, axis=1, keepdims=True)
        - normed * jnp.mean(grad_norm * normed, axis=1, keepdims=True)
    )
    grad_branch = (skip_gate * grad_mix).astype(jnp.bfloat16)
    gate_term = (
        jnp.sum(grad_mix * (branch - x_f), axis=1, keepdims=True) * skip_gate * (1.0 - skip_gate)
    )
    skip_grad = jnp.sum(type_hot * gate_term, axis=0)
    out_grad = typed_grad(act_low, grad_branch)
    grad_agg = gelu_back(typed_back(grad_branch, out_w))[0].astype(jnp.bfloat16)
    grad_agg_heads = grad_agg.reshape(tgt_rows, head_count, head_size)
    msg_grad = jnp.einsum(
        "rthd,the->rhde", u_rel_b, grad_agg_heads, preferred_element_type=jnp.float32
    )
    grad_urel = jnp.einsum(
        "the,rhde->rthd", grad_agg_heads, rel_msg, preferred_element_type=jnp.float32
    ).astype(jnp.bfloat16)
    grad_four = (
        jnp.einsum("tsr,rthd->thsd", select_low, grad_urel, preferred_element_type=jnp.float32)
        .astype(jnp.bfloat16)
        .reshape(tgt_rows, head_count, kind_count * head_size)
    )
    grad_cite = grad_urel[3]
    row_delta = (
        jnp.sum(grad_four.astype(jnp.float32) * u_four, axis=2)
        + jnp.sum(grad_cite.astype(jnp.float32) * u_cite, axis=2)
    ).T
    zero_four = jnp.zeros((tgt_rows, head_count, kind_count * head_size), jnp.float32)
    zero_cite = jnp.zeros((tgt_rows, head_count, head_size), jnp.float32)

    def back_turn(step_idx, loop_state):
        kv_blk, travel, acc_qf, acc_qc = loop_state
        k_grad, v_grad, qf_grad, qc_grad = backward_block(
            kv_blk,
            q_four,
            q_cite,
            grad_four,
            grad_cite,
            log_total,
            row_delta,
            block_codes((my_blk - step_idx) % n_blk),
        )
        travel = (
            from_behind((travel[0] + k_grad).astype(jnp.bfloat16), "blk", 1).astype(jnp.float32),
            from_behind((travel[1] + v_grad).astype(jnp.bfloat16), "blk", 1).astype(jnp.float32),
        )
        kv_blk = from_behind((kv_blk[0], kv_blk[1], kv_blk[2]), "blk", 1)
        return (kv_blk, travel, acc_qf + qf_grad, acc_qc + qc_grad)

    zero_kv = jnp.zeros((tgt_rows, feat_dim), jnp.float32)
    loop_state = lax.fori_loop(
        0, n_blk, back_turn, (whole_kv, (zero_kv, zero_kv), zero_four, zero_cite)
    )
    key_acc, value_acc = loop_state[1]
    acc_qf, acc_qc = (loop_state[2], loop_state[3])
    grad_key = key_acc.astype(jnp.bfloat16)
    grad_value = value_acc.astype(jnp.bfloat16)
    grad_relq = jnp.einsum(
        "tsr,thsd->rthd",
        select,
        acc_qf.reshape(tgt_rows, head_count, kind_count, head_size),
        precision=HIGH,
    )
    grad_relq = (
        (grad_relq + cite_hot[:, None, None, None] * acc_qc[None])
        .astype(jnp.bfloat16)
        .astype(jnp.float32)
    )
    prior_grad = jnp.sum(grad_relq * rel_raw, axis=(1, 3)) / math.sqrt(head_size)
    grad_raw = grad_relq * factor[:, None, :, None]
    att_grad = jnp.einsum("thj,rthk->rhjk", q_heads, grad_raw, precision=HIGH)
    grad_query = (
        jnp.einsum("rthk,rhjk->thj", grad_raw, att_f, precision=HIGH)
        .reshape(tgt_rows, feat_dim)
        .astype(jnp.bfloat16)
    )
    query_grad = typed_grad(features, grad_query)
    key_grad = typed_grad(shifted_b, grad_key)
    value_grad = typed_grad(shifted_b, grad_value)
    grad_shift = typed_back(grad_key, key_w) + typed_back(grad_value, value_w)
    table_grad = jnp.dot(gap_hot.T, grad_shift, precision=HIGH)
    rte_grad = jnp.dot(time_low.T, table_grad, precision=HIGH)
    input_grad = (
        (1.0 - skip_gate) * grad_mix + typed_back(grad_query, query_w) + grad_shift
    ).astype(jnp.bfloat16)
    summed = lax.psum(
        (
            query_grad,
            key_grad,
            value_grad,
            out_grad,
            att_grad,
            msg_grad,
            prior_grad,
            skip_grad,
            rte_grad,
            gain_grad,
            bias_grad,
        ),
        ("blk", "rep"),
    )
    return (
        layer_out,
        input_grad,
        summed[0],
        summed[1],
        summed[2],
        summed[3],
        summed[4],
        summed[5],
        summed[6],
        summed[7],
        summed[8],
        summed[9],
        summed[10],
    )


REL_TAB = relation_table()
HALF = 128
F32 = jnp.float32
LOW = jnp.bfloat16
VMEM_CAP = 65000 * 2**10


def nn(a, b):
    return lax.dot_general(a, b, (((1,), (0,)), ((), ())), preferred_element_type=F32)


def nt(a, b):
    return lax.dot_general(a, b, (((1,), (1,)), ((), ())), preferred_element_type=F32)


def tn(a, b):
    return lax.dot_general(a, b, (((0,), (0,)), ((), ())), preferred_element_type=F32)


def pick(kinds, kind, value):
    return jnp.where(kinds == kind, value, jnp.zeros_like(value))


def relation_of(kind, slot):
    hit = np.nonzero(REL_TAB[kind, slot])[0]
    return int(hit[0]) if len(hit) else None


def to_slots(rel_rows, kinds, kind_count):
    slots = []
    for slot in range(kind_count):
        rows = jnp.zeros(kinds.shape, F32)
        for kind in range(kind_count):
            rel = relation_of(kind, slot)
            if rel is not None:
                rows = jnp.where(kinds == kind, rel_rows(rel), rows)
        slots.append(rows)
    return slots, pick(kinds, 0, rel_rows(3))


def to_relations(slot_rows, cite_rows, kinds, kind_count, rel_count):
    out = []
    for rel in range(rel_count):
        if rel == 3:
            out.append(pick(kinds, 0, cite_rows))
            continue
        (kind, slot) = [
            (k, s) for k in range(kind_count) for s in range(kind_count) if relation_of(k, s) == rel
        ][0]
        out.append(pick(kinds, kind, slot_rows(slot)))
    return out


def flip(index, mask):
    return sum(((index // bit + mask // bit) % 2) * bit for bit in (1, 2, 4))


def gap_hot(gap_row, levels):
    gaps = jnp.broadcast_to(gap_row, (levels, gap_row.shape[1]))
    return (lax.broadcasted_iota(jnp.int32, gaps.shape, 0) == gaps).astype(F32).astype(LOW)


def remote(src, dst, sends, recvs, send_at, recv_at, device):
    return pltpu.make_async_remote_copy(
        src_ref=src,
        dst_ref=dst,
        send_sem=sends.at[send_at],
        recv_sem=recvs.at[recv_at],
        device_id=device,
        device_id_type=pl.DeviceIdType.MESH,
    )


def greet(devices):
    barrier = pltpu.get_barrier_semaphore()
    for device in devices:
        pl.semaphore_signal(
            barrier, inc=1, device_id=device, device_id_type=pl.DeviceIdType.MESH
        )
    pl.semaphore_wait(barrier, len(devices))


def layer_kernel(
    x_ref,
    meta_ref,
    rte_ref,
    time_ref,
    codes_ref,
    cot_ref,
    qw_ref,
    kw_ref,
    vw_ref,
    ow_ref,
    att_ref,
    msg_ref,
    factor_ref,
    gate_ref,
    gain_ref,
    bias_ref,
    out_ref,
    input_ref,
    grads_ref,
    pack_ref,
    shifted,
    xt,
    base,
    shift_out,
    shift_in,
    gather_send,
    gather_recv,
    back_send,
    back_recv,
    kt,
    vx,
    sbuf,
    probs,
    mx,
    sm,
    qs,
    qt2,
    qh,
    gt2,
    acc,
    urel,
    dka,
    dva,
    two,
    wkt,
    wvt,
    agg,
):
    rows, feat = x_ref.shape
    n_blk = shifted.shape[0]
    levels = time_ref.shape[1]
    me = lax.axis_index("blk")
    rep = lax.axis_index("rep")
    greet([(flip(me, mask), rep) for mask in range(1, n_blk)])
    x_f = x_ref[...].astype(F32).T
    x_t = x_f.astype(LOW)
    xt[...] = x_t
    table = tn(rte_ref[...], time_ref[...])
    table_hi = table.astype(LOW)
    table_lo = (table - table_hi.astype(F32)).astype(LOW)
    hot = gap_hot(meta_ref[1:2, :], levels)
    shifted[me, 0:feat, :] = (x_f + nn(table_hi, hot) + nn(table_lo, hot)).astype(LOW)
    shifted[me, feat:, :] = jnp.concatenate(
        [meta_ref[...].astype(F32), jnp.zeros((8, rows), F32)], axis=0
    ).astype(LOW)

    def hand_on(block, mask, send_at):
        return remote(
            shifted.at[block],
            shifted.at[block],
            gather_send,
            gather_recv,
            send_at,
            block,
            (flip(me, mask), rep),
        )

    for mask in (1, 2, 6, 4):
        hand_on(me, mask, mask).start()

    def source_row(j, row):
        return shifted[j, feat : feat + 16, :].astype(F32)[row : row + 1].astype(jnp.int32)
    kind_count = qw_ref.shape[0]
    heads, size = qh.shape[0], qh.shape[1]
    rel_count = att_ref.shape[2] // size
    kinds = jnp.broadcast_to(meta_ref[0:1, :], (size, rows))
    kinds_f = jnp.broadcast_to(meta_ref[0:1, :], (feat, rows))
    valid_f = jnp.broadcast_to(meta_ref[2:3, :], (feat, rows)).astype(F32)
    lane = lax.broadcasted_iota(jnp.int32, (rows, HALF), 1)
    ones_pad = (lax.broadcasted_iota(jnp.int32, (16, rows), 0) < 2).astype(F32).astype(LOW)

    def cols(j):
        return pl.ds(pl.multiple_of(j * rows, rows), rows)

    def store_grad(at, value):
        for part in range(feat // HALF):
            start = (at * (feat // HALF) + part) * feat
            grads_ref[pl.ds(start, feat), :] = value[:, part * HALF : (part + 1) * HALF].astype(LOW)

    def store_rows(at, h, value):
        for part in range(feat // HALF):
            start = (at * (feat // HALF) + part) * feat + h * size
            grads_ref[pl.ds(pl.multiple_of(start, size), size), :] = value[
                :, part * HALF : (part + 1) * HALF
            ].astype(LOW)

    for k in range(kind_count):
        wkt[pl.ds(k * feat, feat), :] = kw_ref[k].astype(F32).T.astype(LOW)
        wvt[pl.ds(k * feat, feat), :] = vw_ref[k].astype(F32).T.astype(LOW)

    q_full = jnp.zeros((feat, rows), F32)
    for k in range(kind_count):
        q_full = jnp.where(kinds_f == k, tn(qw_ref[k], x_t), q_full)
    for h in range(heads):
        qh[h] = q_full[h * size : (h + 1) * size].astype(LOW)

    def query_head(h, carry):
        raw = tn(att_ref[h], qh[h])

        def rel_rows(r):
            return (raw[r * size : (r + 1) * size] * factor_ref[r, h]).astype(LOW).astype(F32)

        slots, cite = to_slots(rel_rows, kinds, kind_count)
        slot_t = jnp.concatenate(slots, axis=0)
        cite_t = jnp.concatenate([cite, jnp.zeros((HALF - size, rows), F32)], axis=0)
        qt2[h, :, 0:rows] = slot_t.astype(LOW)
        qt2[h, :, rows:] = cite_t.astype(LOW)
        qs[h, 0:rows, 0:HALF] = slot_t.T.astype(LOW)
        qs[h, rows:, 0:HALF] = cite_t.T.astype(LOW)
        return carry

    lax.fori_loop(0, heads, query_head, 0)

    def expand(i, carry):
        j = flip(me, i)

        @pl.when(i > 0)
        def _():
            hand_on(j, 1, 0).wait_recv()

        @pl.when((i > 0) & (i % 2 == 0))
        def _():
            hand_on(j, 1, i + 1).start()

        src = jnp.broadcast_to(source_row(j, 0), (size, rows))
        block = shifted[j, 0:feat, :]
        for k in range(kind_count):
            key = nn(wkt[pl.ds(k * feat, feat), :], block)
            value = nn(wvt[pl.ds(k * feat, feat), :], block)
            for h in range(heads):
                part = slice(h * size, (h + 1) * size)
                kt[j, h, pl.ds(k * size, size), :] = pick(src, k, key[part]).astype(LOW)
                vx[j, h, pl.ds(k * size, size), :] = pick(src, k, value[part]).astype(LOW)
        for h in range(heads):
            vx[j, h, pl.ds(HALF, 16), :] = ones_pad
        two[j] = (codes_ref[:, cols(j)] == 2).astype(F32).astype(LOW)
        return carry

    lax.fori_loop(0, n_blk, expand, 0)
    for send_at in range(1, n_blk):
        hand_on(me, 1, send_at).wait_send()

    def score_block(h, j):
        both = nn(qs[h, :, 0:HALF], kt[j, h])
        code = codes_ref[:, cols(j)]
        val = jnp.where(code == 2, both[rows:], both[:rows])
        val = jnp.where(code > 0, val, NEG_FILL)
        sbuf[h % 2, j] = val
        top = jnp.maximum(val[:, :HALF], val[:, HALF:])
        for c in range(2 * HALF, rows, HALF):
            top = jnp.maximum(top, val[:, c : c + HALF])
        mx[h % 2] = jnp.maximum(mx[h % 2], top)

    def prob_block(h, j):
        top = sm[h % 2]
        val = jnp.exp(sbuf[h % 2, j] - jnp.concatenate([top] * (rows // HALF), axis=1))
        total = val[:, :HALF]
        for c in range(HALF, rows, HALF):
            total = total + val[:, c : c + HALF]
        mx[2 + h % 2] = mx[2 + h % 2] + total
        low = val.astype(LOW)
        second = low * two[j]
        probs[j, h, 0:rows, :] = low - second
        probs[j, h, rows:, :] = second
        acc[h] = acc[h] + nt(vx[j, h, 0:HALF, :], probs[j, h])

    def open_head(h):
        mx[h % 2] = jnp.full((rows, HALF), NEG_FILL, F32)

    def close_scores(h):
        top = jnp.max(mx[h % 2], axis=1, keepdims=True)
        sm[h % 2] = jnp.broadcast_to(jnp.maximum(top, 0.1 * NEG_FILL), (rows, HALF))
        mx[2 + h % 2] = jnp.zeros((rows, HALF), F32)
        acc[h] = jnp.zeros(acc.shape[1:], F32)

    def close_probs(h):
        total = jnp.sum(mx[2 + h % 2], axis=1, keepdims=True)
        sm[2] = jnp.where(lane == h, jnp.broadcast_to(total, (rows, HALF)), sm[2])

    sm[2] = jnp.zeros((rows, HALF), F32)
    open_head(0)

    def first(j, carry):
        score_block(0, j)
        return carry

    lax.fori_loop(0, n_blk, first, 0)

    def forward_head(h, carry):
        close_scores(h)
        open_head(h + 1)

        def step(j, carry):
            score_block(h + 1, j)
            prob_block(h, j)
            return carry

        lax.fori_loop(0, n_blk, step, 0)
        close_probs(h)
        return carry

    lax.fori_loop(0, heads - 1, forward_head, 0)
    close_scores(heads - 1)

    def last(j, carry):
        prob_block(heads - 1, j)
        return carry

    lax.fori_loop(0, n_blk, last, 0)
    close_probs(heads - 1)

    denom = jnp.maximum(sm[2].T, 1.0)
    inverse = 1.0 / denom
    sm[2, 0:HALF, :] = inverse[:, 0:HALF]
    sm[2, HALF : 2 * HALF, :] = inverse[:, HALF : 2 * HALF]

    def inv_row(h, count):
        row = jnp.concatenate([sm[2, pl.ds(h, 1), :], sm[2, pl.ds(HALF + h, 1), :]], axis=1)
        return jnp.broadcast_to(row, (count, rows))

    for h in range(heads):
        inv = inv_row(h, HALF)
        u_slot = acc[h, :, 0:rows] * inv
        u_cite = acc[h, 0:size, rows:] * inv[0:size]
        acc[h, :, 0:rows] = u_slot
        acc[h, 0:size, rows:] = u_cite
        rel = to_relations(
            lambda s: u_slot[s * size : (s + 1) * size], u_cite, kinds, kind_count, rel_count
        )
        urel[h] = jnp.concatenate(rel, axis=0).astype(LOW)
        agg[pl.ds(h * size, size), :] = nn(msg_ref[h], urel[h])
    agg_t = agg[...]
    slope = 0.7978845608028654
    inner = jnp.tanh(slope * (agg_t + 0.044715 * agg_t * agg_t * agg_t))
    act_t = (0.5 * agg_t * (1.0 + inner)).astype(LOW)
    gelu_back = 0.5 * (1.0 + inner) + 0.5 * agg_t * (1.0 - inner * inner) * slope * (
        1.0 + 3.0 * 0.044715 * agg_t * agg_t
    )
    gate = jnp.zeros((feat, rows), F32)
    branch = jnp.zeros((feat, rows), F32)
    for k in range(kind_count):
        gate = jnp.where(kinds_f == k, gate_ref[k], gate)
        branch = jnp.where(kinds_f == k, tn(ow_ref[k], act_t), branch)
    mixed = gate * branch + (1.0 - gate) * x_f
    centered = mixed - jnp.mean(mixed, axis=0, keepdims=True)
    inv_std = lax.rsqrt(jnp.mean(centered * centered, axis=0, keepdims=True) + LN_EPS)
    normed = centered * inv_std
    gain = gain_ref[...]
    out_t = valid_f * (normed * gain + bias_ref[...])
    out_ref[...] = out_t.T.astype(LOW)
    grad_y = cot_ref[...].astype(F32).T * valid_f
    gain_col = jnp.sum(grad_y * normed, axis=1, keepdims=True)
    bias_col = jnp.sum(grad_y, axis=1, keepdims=True)
    grad_norm = grad_y * gain
    grad_mix = inv_std * (
        grad_norm
        - jnp.mean(grad_norm, axis=0, keepdims=True)
        - normed * jnp.mean(grad_norm * normed, axis=0, keepdims=True)
    )
    gate_row = gate[0:1]
    skip_row = (
        jnp.sum(grad_mix * (branch - x_f), axis=0, keepdims=True) * gate_row * (1.0 - gate_row)
    )
    base[...] = (1.0 - gate) * grad_mix
    grad_branch = (gate * grad_mix).astype(LOW)
    grad_act = jnp.zeros((feat, rows), F32)
    for k in range(kind_count):
        masked = pick(kinds_f, k, grad_branch.astype(F32)).astype(LOW)
        store_grad(3 * kind_count + k, nt(act_t, masked))
        grad_act = grad_act + nn(ow_ref[k], masked)
    agg[...] = gelu_back * grad_act

    def grad_head(h, carry):
        grad_agg = agg[pl.ds(pl.multiple_of(h * size, size), size), :].astype(LOW)
        store_rows(4 * kind_count + 1, h, nt(grad_agg, urel[h]))
        inv = inv_row(h, size)
        grad_u = tn(msg_ref[h], grad_agg)

        def rel_rows(r):
            return grad_u[r * size : (r + 1) * size] * inv

        slots, cite = to_slots(rel_rows, kinds, kind_count)
        slot_t = jnp.concatenate(slots, axis=0).astype(LOW)
        cite_t = jnp.concatenate([cite, jnp.zeros((HALF - size, rows), F32)], axis=0).astype(LOW)
        gt2[h, :, 0:rows] = slot_t
        gt2[h, :, rows:] = cite_t
        slot_f = slot_t.astype(F32)
        cite_f = cite_t.astype(F32)
        delta = -(
            jnp.sum(slot_f * acc[h, :, 0:rows], axis=0, keepdims=True)
            + jnp.sum(cite_f[0:size] * acc[h, 0:size, rows:], axis=0, keepdims=True)
        )
        delta_hi = delta.astype(LOW).astype(F32)
        tail = jnp.concatenate(
            [delta_hi, delta - delta_hi, jnp.zeros((HALF - 2, rows), F32)], axis=0
        )
        tail_t = tail.T.astype(LOW)
        qs[h, 0:rows, 0:HALF] = slot_f.T.astype(LOW)
        qs[h, rows:, 0:HALF] = cite_f.T.astype(LOW)
        qs[h, 0:rows, HALF:] = tail_t[:, 0:16]
        qs[h, rows:, HALF:] = tail_t[:, 0:16]
        acc[h] = jnp.zeros(acc.shape[1:], F32)
        return carry

    lax.fori_loop(0, heads, grad_head, 0)

    slot_id = lax.broadcasted_iota(jnp.int32, (HALF, rows), 0) // size

    pack_ref[...] = jnp.zeros_like(pack_ref)

    def send_back(j):
        return remote(
            shift_out.at[j], shift_in.at[me], back_send, back_recv, j, me, (j, rep)
        )

    def back_block(i, carry):
        j = flip(me, n_blk - 1 - i)
        src = jnp.broadcast_to(source_row(j, 0), (HALF, rows))
        own = slot_id == src

        def back_head(h, carry):
            pair = probs[j, h]
            grad = pair * nn(qs[h], vx[j, h]).astype(LOW)
            d_key = jnp.where(own, nn(qt2[h], grad), 0.0).astype(LOW)
            d_value = jnp.where(own, nn(gt2[h], pair), 0.0).astype(LOW)
            for k in range(kind_count):
                at = pl.ds(pl.multiple_of(k * feat + h * size, size), size)
                dka[at, cols(j)] = d_key[k * size : (k + 1) * size]
                dva[at, cols(j)] = d_value[k * size : (k + 1) * size]
            acc[h] = acc[h] + nt(kt[j, h], grad)
            return carry

        lax.fori_loop(0, heads, back_head, 0)
        total = jnp.zeros((feat, rows), F32)
        for k in range(kind_count):
            at = pl.ds(k * feat, feat)
            total = total + nn(kw_ref[k], dka[at, cols(j)]) + nn(vw_ref[k], dva[at, cols(j)])
        low = total.astype(LOW)
        shift_out[j] = low

        @pl.when(i < n_blk - 1)
        def _():
            send_back(j).start()

        pack_ref[0:levels, :] = pack_ref[0:levels, :] + nt(gap_hot(source_row(j, 1), levels), low)
        return carry

    lax.fori_loop(0, n_blk, back_block, 0)

    for k in range(kind_count):
        at = pl.ds(k * feat, feat)
        k_sum = jnp.zeros((feat, feat), F32)
        v_sum = jnp.zeros((feat, feat), F32)
        for j in range(n_blk):
            k_sum = k_sum + nt(shifted[j, 0:feat, :], dka[at, pl.ds(j * rows, rows)])
            v_sum = v_sum + nt(shifted[j, 0:feat, :], dva[at, pl.ds(j * rows, rows)])
        store_grad(kind_count + k, k_sum)
        store_grad(2 * kind_count + k, v_sum)
    pair = jnp.where(
        lane == 0,
        jnp.broadcast_to(gain_col, (feat, HALF)),
        jnp.where(lane == 1, jnp.broadcast_to(bias_col, (feat, HALF)), 0.0),
    ).T
    spot = lax.broadcasted_iota(jnp.int32, (1, rows), 1)
    skips = jnp.zeros((1, rows), F32)
    for k in range(kind_count):
        skips = jnp.where(
            spot == k, jnp.sum(pick(kinds[0:1], k, skip_row), axis=1, keepdims=True), skips
        )
    pack_ref[levels : levels + 8, :] = jnp.concatenate(
        [pair[0:2], skips, jnp.zeros((5, rows), F32)], axis=0
    )

    def query_back(h, carry):
        slot = acc[h, :, 0:rows]
        rel = to_relations(
            lambda s: slot[s * size : (s + 1) * size],
            acc[h, 0:size, rows:],
            kinds,
            kind_count,
            rel_count,
        )
        rel = [part.astype(LOW) for part in rel]
        at = pl.ds(pl.multiple_of(h * size, size), size)
        store_rows(4 * kind_count, h, nt(qh[h], jnp.concatenate(rel, axis=0)))
        raw = [(part.astype(F32) * factor_ref[r, h]).astype(LOW) for r, part in enumerate(rel)]
        agg[at, :] = nn(att_ref[h], jnp.concatenate(raw, axis=0))
        return carry

    lax.fori_loop(0, heads, query_back, 0)
    grad_q = agg[...].astype(LOW).astype(F32)
    total = base[...] + shift_out[me].astype(F32)
    for k in range(kind_count):
        masked = pick(kinds_f, k, grad_q).astype(LOW)
        store_grad(k, nt(x_t, masked))
        total = total + nn(qw_ref[k], masked)
    for mask in range(1, n_blk):
        j = flip(me, mask)
        send_back(j).wait_send()
        remote(shift_in.at[j], shift_in.at[j], back_send, back_recv, j, j, (j, rep)).wait_recv()
        total = total + shift_in[j].astype(F32)
    input_ref[...] = total.T.astype(LOW)


def reduce_kernel(
    grads_ref,
    pack_ref,
    att_ref,
    time_ref,
    factor_ref,
    qg_ref,
    kg_ref,
    vg_ref,
    og_ref,
    attg_ref,
    msgg_ref,
    prior_ref,
    rte_ref,
    small_ref,
    work,
    full,
    core_in,
    plane_in,
    line_in,
    pack_in,
    pack_work,
    sends,
    recvs,
):
    me = lax.axis_index("blk")
    rep = lax.axis_index("rep")
    z, y, x, core = me // 2, me % 2, rep // 2, rep % 2
    by_core = (me, rep + 1 - 2 * core)
    by_x = (me, rep + 2 - 4 * x)
    by_y = (me + 1 - 2 * y, rep)
    by_z = [(((z + step) % 4) * 2 + y, rep) for step in (1, 2, 3)]
    greet([by_core, by_x, by_y] + by_z)
    total = grads_ref.shape[0]
    half, quarter = total // 2, total // 4
    count = iter(range(sends.shape[0]))

    def send(src, dst, device):
        at = next(count)
        copy = remote(src, dst, sends, recvs, at, at, device)
        copy.start()
        return copy

    def rows_of(ref, start, size):
        return ref.at[pl.ds(pl.multiple_of(start, 16), size), :]

    def load(ref, start, size):
        return ref[pl.ds(pl.multiple_of(start, 16), size), :].astype(F32)

    def add_in(start, size, *parts):
        value = load(work, start, size)
        for part in parts:
            value = value + part
        work[pl.ds(pl.multiple_of(start, 16), size), :] = value.astype(LOW)

    mine = core * half
    a = send(rows_of(grads_ref, half - mine, half), core_in, by_core)
    b = send(pack_ref, pack_in.at[0], by_core)
    a.wait()
    b.wait()
    work[...] = (load(grads_ref, mine, half) + core_in[...].astype(F32)).astype(LOW)
    pack_work[0] = pack_ref[...] + pack_in[0]
    size = quarter // 2
    starts = [x * size, quarter + y * size]
    away = [size - x * size, quarter + size - y * size]
    copies = [
        send(rows_of(work, away[0], size), plane_in.at[0], by_x),
        send(rows_of(work, away[1], size), plane_in.at[1], by_y),
        send(pack_work.at[0], pack_in.at[1], by_x),
    ]
    for copy in copies:
        copy.wait()
    for s in range(2):
        add_in(starts[s], size, plane_in[s].astype(F32))
    pack_work[1] = pack_work[0] + pack_in[1]
    size = size // 2
    turn = [y, x]
    copies = [
        send(
            rows_of(work, starts[s] + size - turn[s] * size, size),
            plane_in.at[2 + s, pl.ds(0, size), :],
            (by_y, by_x)[s],
        )
        for s in range(2)
    ]
    copies.append(send(pack_work.at[1], pack_in.at[2], by_y))
    for copy in copies:
        copy.wait()
    starts = [starts[s] + turn[s] * size for s in range(2)]
    for s in range(2):
        add_in(starts[s], size, plane_in[2 + s, 0:size, :].astype(F32))
    pack_work[2] = pack_work[1] + pack_in[2]
    size = size // 4
    copies = []
    for step in (2, 3, 1):
        for s in range(2):
            there = starts[s] + ((z + step) % 4) * size
            copies.append(
                send(rows_of(work, there, size), line_in.at[s, step - 1], by_z[step - 1])
            )
        copies.append(send(pack_work.at[2], pack_in.at[2 + step], by_z[step - 1]))
    for copy in copies:
        copy.wait()
    small = pack_work[2] + pack_in[3] + pack_in[4] + pack_in[5]
    starts = [starts[s] + z * size for s in range(2)]
    for s in range(2):
        value = load(work, starts[s], size)
        for step in range(3):
            value = value + line_in[s, step].astype(F32)
        full[pl.ds(pl.multiple_of(mine + starts[s], 16), size), :] = value.astype(LOW)

    def share(start, size, device):
        return send(rows_of(full, start, size), rows_of(full, start, size), device)

    copies = [
        share(mine + starts[s], size, by_z[step - 1]) for step in (2, 3, 1) for s in range(2)
    ]
    for copy in copies:
        copy.wait()
    starts = [starts[s] - z * size for s in range(2)]
    size = size * 4
    copies = [share(mine + starts[s], size, (by_y, by_x)[s]) for s in range(2)]
    for copy in copies:
        copy.wait()
    starts = [starts[s] - turn[s] * size for s in range(2)]
    size = size * 2
    copies = [share(mine + starts[s], size, (by_x, by_y)[s]) for s in range(2)]
    early = [share(mine + starts[s], size, by_core) for s in range(2)]
    for copy in copies:
        copy.wait()
    late = [share(mine + away[s], size, by_core) for s in range(2)]
    for copy in early + late:
        copy.wait()

    kind_count, feat = qg_ref.shape[:2]
    rel_count, heads, width = attg_ref.shape[:3]
    parts = feat // HALF

    def whole(at):
        return jnp.concatenate(
            [full[pl.ds((at * parts + p) * feat, feat), :].astype(F32) for p in range(parts)],
            axis=1,
        )

    for m, ref in enumerate((qg_ref, kg_ref, vg_ref, og_ref)):
        for k in range(kind_count):
            ref[k] = whole(m * kind_count + k)
    att = whole(4 * kind_count)
    msg = whole(4 * kind_count + 1).T
    for r in range(rel_count):
        for h in range(heads):
            block = (slice(h * width, (h + 1) * width), slice(r * width, (r + 1) * width))
            attg_ref[r, h] = att[block] * factor_ref[r, h]
            msgg_ref[r, h] = msg[block[::-1]]
    prod = (att * att_ref[...].astype(F32)).reshape(heads, width, feat)
    prod = jnp.sum(prod, axis=1)
    spread = (
        lax.broadcasted_iota(jnp.int32, (feat, rel_count), 0) // width
        == lax.broadcasted_iota(jnp.int32, (feat, rel_count), 1)
    ).astype(F32).astype(LOW)
    prior = jnp.zeros((rel_count, heads), F32)
    for _ in range(3):
        low = prod.astype(LOW)
        prior = prior + lax.dot_general(
            spread, low, (((0,), (1,)), ((), ())), preferred_element_type=F32
        )
        prod = prod - low.astype(F32)
    prior_ref[...] = prior * (1.0 / math.sqrt(width))
    levels = time_ref.shape[1]
    rte = jnp.zeros(rte_ref.shape, F32)
    rest = small[0:levels]
    for _ in range(3):
        low = rest.astype(LOW)
        rte = rte + nn(time_ref[...], low)
        rest = rest - low.astype(F32)
    rte_ref[...] = rte
    small_ref[...] = small[levels:]


def fast_body(
    features,
    node_type,
    time_gap,
    node_valid,
    edge_codes,
    query_w,
    key_w,
    value_w,
    out_w,
    rel_att,
    rel_msg,
    rel_prior,
    skip_logit,
    rte_w,
    ln_gain,
    ln_bias,
    cotangent,
):
    rows, feat = features.shape
    n_blk = lax.axis_size("blk")
    kind_count = query_w.shape[0]
    rel_count, heads, size = rel_att.shape[:3]
    time_low = time_table(LEVELS, feat).astype(LOW)
    meta = jnp.concatenate(
        [node_type[None], time_gap[None], node_valid[None], jnp.zeros((5, rows), jnp.int32)], axis=0
    )
    vmem = pl.BlockSpec(memory_space=pltpu.VMEM)
    smem = pl.BlockSpec(memory_space=pltpu.SMEM)
    att_flat = rel_att.transpose(1, 2, 0, 3).reshape(feat, rel_count * size)
    msg_flat = rel_msg.transpose(1, 3, 0, 2).reshape(feat, rel_count * size)
    factor = rel_prior / math.sqrt(size)
    gate = jax.nn.sigmoid(skip_logit)
    square = (feat, feat)
    grad_rows = (4 * kind_count + 2) * (feat // HALF) * feat

    def shape(dims, kind):
        return jax.ShapeDtypeStruct(dims, kind)

    layer_out, input_grad, grads, pack = pl.pallas_call(
        layer_kernel,
        out_shape=[
            shape((rows, feat), LOW),
            shape((rows, feat), LOW),
            shape((grad_rows, HALF), LOW),
            shape((LEVELS + 8, feat), F32),
        ],
        in_specs=[vmem] * 12 + [smem] * 2 + [vmem] * 2,
        out_specs=[vmem] * 4,
        scratch_shapes=[
            pltpu.VMEM((n_blk, feat + 16, rows), LOW),
            pltpu.VMEM((feat, rows), LOW),
            pltpu.VMEM((feat, rows), F32),
            pltpu.VMEM((n_blk, feat, rows), LOW),
            pltpu.VMEM((n_blk, feat, rows), LOW),
            pltpu.SemaphoreType.DMA((n_blk,)),
            pltpu.SemaphoreType.DMA((n_blk,)),
            pltpu.SemaphoreType.DMA((n_blk,)),
            pltpu.SemaphoreType.DMA((n_blk,)),
            pltpu.VMEM((n_blk, heads, HALF, rows), LOW),
            pltpu.VMEM((n_blk, heads, HALF + 16, rows), LOW),
            pltpu.VMEM((2, n_blk, rows, rows), F32),
            pltpu.VMEM((n_blk, heads, 2 * rows, rows), LOW),
            pltpu.VMEM((4, rows, HALF), F32),
            pltpu.VMEM((3, rows, HALF), F32),
            pltpu.VMEM((heads, 2 * rows, HALF + 16), LOW),
            pltpu.VMEM((heads, HALF, 2 * rows), LOW),
            pltpu.VMEM((heads, size, rows), LOW),
            pltpu.VMEM((heads, HALF, 2 * rows), LOW),
            pltpu.VMEM((heads, HALF, 2 * rows), F32),
            pltpu.VMEM((heads, rel_count * size, rows), LOW),
            pltpu.VMEM((kind_count * feat, n_blk * rows), LOW),
            pltpu.VMEM((kind_count * feat, n_blk * rows), LOW),
            pltpu.VMEM((n_blk, rows, rows), LOW),
            pltpu.VMEM((kind_count * feat, feat), LOW),
            pltpu.VMEM((kind_count * feat, feat), LOW),
            pltpu.VMEM(square, F32),
        ],
        compiler_params=pltpu.CompilerParams(
            vmem_limit_bytes=VMEM_CAP, collective_id=0, has_side_effects=True
        ),
        name="layer",
    )(
        features,
        meta,
        rte_w,
        time_low.T,
        edge_codes,
        cotangent,
        query_w,
        key_w,
        value_w,
        out_w,
        att_flat.reshape(heads, size, rel_count * size),
        msg_flat.reshape(heads, size, rel_count * size),
        factor,
        gate,
        ln_gain[:, None],
        ln_bias[:, None],
    )
    quarter = grad_rows // 4
    outs = pl.pallas_call(
        reduce_kernel,
        out_shape=[shape((kind_count,) + square, F32)] * 4
        + [shape(rel_att.shape, F32)] * 2
        + [shape(rel_prior.shape, F32), shape(square, F32), shape((8, feat), F32)],
        in_specs=[vmem] * 4 + [smem],
        out_specs=[vmem] * 9,
        scratch_shapes=[
            pltpu.VMEM((grad_rows // 2, HALF), LOW),
            pltpu.VMEM((grad_rows, HALF), LOW),
            pltpu.VMEM((grad_rows // 2, HALF), LOW),
            pltpu.VMEM((4, quarter // 2, HALF), LOW),
            pltpu.VMEM((2, 3, quarter // 16, HALF), LOW),
            pltpu.VMEM((6, LEVELS + 8, feat), F32),
            pltpu.VMEM((3, LEVELS + 8, feat), F32),
            pltpu.SemaphoreType.DMA((40,)),
            pltpu.SemaphoreType.DMA((40,)),
        ],
        compiler_params=pltpu.CompilerParams(
            vmem_limit_bytes=VMEM_CAP, collective_id=1, has_side_effects=True
        ),
        name="reduce",
    )(grads, pack, att_flat, time_low.T, factor)
    small = outs[8]
    return (
        layer_out,
        input_grad,
        *outs[:7],
        small[2, :kind_count],
        outs[7],
        small[0],
        small[1],
    )


def solution(mesh):
    in_specs = (
        P(("blk", "rep"), None),
        P(("blk", "rep")),
        P(("blk", "rep")),
        P(("blk", "rep")),
        P(("blk", "rep"), None),
        P(),
        P(),
        P(),
        P(),
        P(),
        P(),
        P(),
        P(),
        P(),
        P(),
        P(),
        P(("blk", "rep"), None),
    )
    out_specs = (
        P(("blk", "rep"), None),
        P(("blk", "rep"), None),
        P(),
        P(),
        P(),
        P(),
        P(),
        P(),
        P(),
        P(),
        P(),
        P(),
        P(),
    )
    plan = fast_body if tuple(mesh.shape.values()) == (8, 4) else body
    return jax.shard_map(plan, mesh=mesh, in_specs=in_specs, out_specs=out_specs, check_vma=False)
```

```python
import math

import jax
import jax.numpy as jnp
import numpy as np
from jax import lax
from jax.experimental import pallas as pl
from jax.experimental.pallas import tpu as pltpu
from jax.sharding import PartitionSpec as P

LEVELS = 16


NEG_FILL = -1e30
LN_EPS = 1e-05
HIGH = lax.Precision.HIGHEST


def from_behind(block, axis, distance):
    devices = range(lax.axis_size(axis))
    route = [((i - distance) % len(devices), i) for i in devices]
    return lax.ppermute(block, axis, route)


def relation_table():
    rel_tab = np.zeros((4, 4, 8), np.float32)
    rel_tab[0, 1, 0] = 1.0
    rel_tab[1, 0, 1] = 1.0
    rel_tab[0, 0, 2] = 1.0
    rel_tab[2, 0, 4] = 1.0
    rel_tab[0, 2, 5] = 1.0
    rel_tab[3, 1, 6] = 1.0
    rel_tab[1, 3, 7] = 1.0
    return rel_tab


def time_table(level_count, feat_width):
    positions = jnp.arange(level_count, dtype=jnp.float32)[:, None]
    freq_idx = jnp.arange(feat_width // 2, dtype=jnp.float32)[None, :]
    phases = positions / jnp.power(10000.0, 2.0 * freq_idx / feat_width)
    return jnp.stack([jnp.sin(phases), jnp.cos(phases)], axis=2).reshape(level_count, feat_width)


def slot_spread(heads_arr, kind_hot):
    spread_out = heads_arr[:, :, None, :] * kind_hot[:, None, :, None]
    return spread_out.reshape(heads_arr.shape[0], heads_arr.shape[1], -1)


def slot_collapse(slot_arr, kind_hot):
    src_rows, head_count = (slot_arr.shape[0], slot_arr.shape[1])
    kind_count = kind_hot.shape[1]
    shaped = slot_arr.reshape(src_rows, head_count, kind_count, -1)
    return jnp.sum(shaped * kind_hot.astype(jnp.float32)[:, None, :, None], axis=2)


def block_scores(kv_blk, q_four, q_cite, code_blk, kind_count):
    key_blk, value_blk, kind_blk = kv_blk
    src_rows = key_blk.shape[0]
    head_count = q_four.shape[1]
    key_heads = key_blk.reshape(src_rows, head_count, -1)
    value_heads = value_blk.reshape(src_rows, head_count, -1)
    kind_hot = (kind_blk[:, None] == jnp.arange(kind_count).astype(jnp.bfloat16)[None, :]).astype(
        jnp.bfloat16
    )
    key_four = slot_spread(key_heads, kind_hot)
    value_four = slot_spread(value_heads, kind_hot)
    is_one = (code_blk == 1)[None]
    is_two = (code_blk == 2)[None]
    slot_dot = jnp.einsum("thc,shc->hts", q_four, key_four, preferred_element_type=jnp.float32)
    cite_dot = jnp.einsum("thd,shd->hts", q_cite, key_heads, preferred_element_type=jnp.float32)
    scores = jnp.where(is_one, slot_dot, jnp.where(is_two, cite_dot, NEG_FILL))
    return (scores, is_one, is_two, key_heads, value_heads, key_four, value_four, kind_hot)


def attend_block(run_state, kv_blk, q_four, q_cite, code_blk, kind_count):
    run_max, run_sum, acc_four, acc_cite = run_state
    scores, is_one, is_two, key_heads, value_heads, key_four, value_four, kind_hot = block_scores(
        kv_blk, q_four, q_cite, code_blk, kind_count
    )
    new_max = jnp.maximum(run_max, jnp.max(scores, axis=2))
    expd = jnp.where((code_blk > 0)[None], jnp.exp(scores - new_max[:, :, None]), 0.0)
    rescale = jnp.exp(run_max - new_max)
    run_sum = run_sum * rescale + jnp.sum(expd, axis=2)
    prob_low = expd.astype(jnp.bfloat16)
    zero_low = jnp.zeros_like(prob_low)
    p_one = jnp.where(is_one, prob_low, zero_low)
    p_two = jnp.where(is_two, prob_low, zero_low)
    rescale_t = rescale.T[:, :, None]
    acc_four = acc_four * rescale_t + jnp.einsum(
        "hts,shc->thc", p_one, value_four, preferred_element_type=jnp.float32
    )
    acc_cite = acc_cite * rescale_t + jnp.einsum(
        "hts,shd->thd", p_two, value_heads, preferred_element_type=jnp.float32
    )
    return (new_max, run_sum, acc_four, acc_cite)


def back_block(
    kv_blk, q_four, q_cite, grad_four, grad_cite, log_total, row_delta, code_blk, kind_count
):
    scores, is_one, is_two, key_heads, value_heads, key_four, value_four, kind_hot = block_scores(
        kv_blk, q_four, q_cite, code_blk, kind_count
    )
    prob_full = jnp.where((code_blk > 0)[None], jnp.exp(scores - log_total[:, :, None]), 0.0)
    prob_low = prob_full.astype(jnp.bfloat16)
    zero_low = jnp.zeros_like(prob_low)
    p_one = jnp.where(is_one, prob_low, zero_low)
    p_two = jnp.where(is_two, prob_low, zero_low)
    grad_slot = jnp.einsum(
        "thc,shc->hts", grad_four, value_four, preferred_element_type=jnp.float32
    )
    grad_other = jnp.einsum(
        "thd,shd->hts", grad_cite, value_heads, preferred_element_type=jnp.float32
    )
    grad_probs = jnp.where(is_one, grad_slot, jnp.where(is_two, grad_other, 0.0))
    grad_scores = (prob_full * (grad_probs - row_delta[:, :, None])).astype(jnp.bfloat16)
    d_one = jnp.where(is_one, grad_scores, zero_low)
    d_two = jnp.where(is_two, grad_scores, zero_low)
    qf_grad = jnp.einsum("hts,shc->thc", d_one, key_four, preferred_element_type=jnp.float32)
    qc_grad = jnp.einsum("hts,shd->thd", d_two, key_heads, preferred_element_type=jnp.float32)
    k_grad = slot_collapse(
        jnp.einsum("hts,thc->shc", d_one, q_four, preferred_element_type=jnp.float32), kind_hot
    )
    k_grad = k_grad + jnp.einsum("hts,thd->shd", d_two, q_cite, preferred_element_type=jnp.float32)
    v_grad = slot_collapse(
        jnp.einsum("hts,thc->shc", p_one, grad_four, preferred_element_type=jnp.float32), kind_hot
    )
    v_grad = v_grad + jnp.einsum(
        "hts,thd->shd", p_two, grad_cite, preferred_element_type=jnp.float32
    )
    src_rows = k_grad.shape[0]
    return (k_grad.reshape(src_rows, -1), v_grad.reshape(src_rows, -1), qf_grad, qc_grad)


def body(
    features,
    node_type,
    time_gap,
    node_valid,
    edge_codes,
    query_w,
    key_w,
    value_w,
    out_w,
    rel_att,
    rel_msg,
    rel_prior,
    skip_logit,
    rte_w,
    ln_gain,
    ln_bias,
    cotangent,
):
    tgt_rows, feat_dim = features.shape
    kind_count = query_w.shape[0]
    rel_count = rel_att.shape[0]
    head_count = rel_att.shape[1]
    head_size = rel_att.shape[2]
    n_blk = lax.axis_size("blk")
    my_blk = lax.axis_index("blk")
    type_hot = (node_type[:, None] == jnp.arange(kind_count)[None, :]).astype(jnp.float32)
    type_low = type_hot.astype(jnp.bfloat16)
    gap_hot = (time_gap[:, None] == jnp.arange(LEVELS)[None, :]).astype(jnp.float32)
    time_low = time_table(LEVELS, feat_dim).astype(jnp.bfloat16).astype(jnp.float32)
    rte_table = jnp.dot(time_low, rte_w.astype(jnp.float32), precision=HIGH)
    x_f = features.astype(jnp.float32)
    shifted = x_f + jnp.dot(gap_hot, rte_table, precision=HIGH)
    shifted_b = shifted.astype(jnp.bfloat16)

    def typed(inp, weights):
        parts = jnp.einsum("th,khd->tkd", inp, weights, preferred_element_type=jnp.float32)
        return jnp.sum(parts * type_hot[:, :, None], axis=1)

    def typed_grad(inp, grad_low):
        masked = inp[:, None, :] * type_low[:, :, None]
        return jnp.einsum("tkh,td->khd", masked, grad_low, preferred_element_type=jnp.float32)

    def typed_back(grad_low, weights):
        parts = jnp.einsum("td,khd->tkh", grad_low, weights, preferred_element_type=jnp.float32)
        return jnp.sum(parts * type_hot[:, :, None], axis=1)

    q_low = typed(features, query_w).astype(jnp.bfloat16)
    key_low = typed(shifted_b, key_w).astype(jnp.bfloat16)
    value_low = typed(shifted_b, value_w).astype(jnp.bfloat16)
    kind_low = node_type.astype(jnp.bfloat16)
    q_heads = q_low.reshape(tgt_rows, head_count, head_size).astype(jnp.float32)
    att_f = rel_att.astype(jnp.float32)
    factor = rel_prior / math.sqrt(head_size)
    rel_raw = jnp.einsum("thj,rhjk->rthk", q_heads, att_f, precision=HIGH)
    rel_query = (rel_raw * factor[:, None, :, None]).astype(jnp.bfloat16)
    select = jnp.einsum("tk,ksr->tsr", type_hot, jnp.asarray(relation_table()), precision=HIGH)
    select_low = select.astype(jnp.bfloat16)
    cite_hot = (jnp.arange(rel_count) == 3).astype(jnp.float32)
    q_four = (
        jnp.einsum("tsr,rthd->thsd", select_low, rel_query, preferred_element_type=jnp.float32)
        .astype(jnp.bfloat16)
        .reshape(tgt_rows, head_count, kind_count * head_size)
    )
    q_cite = rel_query[3]

    def block_codes(source):
        return lax.dynamic_slice_in_dim(edge_codes, source * tgt_rows, tgt_rows, 1)

    def forward_block(run_state, kv_blk, qf_part, qc_part, code_blk):
        result = attend_block(run_state, kv_blk, qf_part, qc_part, code_blk, kind_count)
        return result

    def backward_block(kv_blk, qf_part, qc_part, gf_part, gc_part, lse_part, delta_part, code_blk):
        return back_block(
            kv_blk, qf_part, qc_part, gf_part, gc_part, lse_part, delta_part, code_blk, kind_count
        )

    whole_kv = (key_low, value_low, kind_low)

    def forward_turn(step_idx, loop_state):
        run_state, kv_blk = loop_state
        run_state = forward_block(
            run_state, kv_blk, q_four, q_cite, block_codes((my_blk - step_idx) % n_blk)
        )
        kv_blk = from_behind((kv_blk[0], kv_blk[1], kv_blk[2]), "blk", 1)
        return (run_state, kv_blk)

    run_state, kv_last = lax.fori_loop(
        0,
        n_blk,
        forward_turn,
        (
            (
                jnp.full((head_count, tgt_rows), NEG_FILL, jnp.float32),
                jnp.zeros((head_count, tgt_rows), jnp.float32),
                jnp.zeros((tgt_rows, head_count, kind_count * head_size), jnp.float32),
                jnp.zeros((tgt_rows, head_count, head_size), jnp.float32),
            ),
            whole_kv,
        ),
    )
    run_max, run_sum, acc_four, acc_cite = run_state
    floor_sum = jnp.maximum(run_sum, 1.0)
    log_total = run_max + jnp.log(floor_sum)
    norm_t = floor_sum.T[:, :, None]
    u_four = acc_four / norm_t
    u_cite = acc_cite / norm_t
    u_rel = jnp.einsum(
        "tsr,thsd->rthd",
        select,
        u_four.reshape(tgt_rows, head_count, kind_count, head_size),
        precision=HIGH,
    )
    u_rel = u_rel + cite_hot[:, None, None, None] * u_cite[None]
    u_rel_b = u_rel.astype(jnp.bfloat16)
    agg_sum = jnp.einsum(
        "rthd,rhde->the", u_rel_b, rel_msg, preferred_element_type=jnp.float32
    ).reshape(tgt_rows, feat_dim)
    act_full, gelu_back = jax.vjp(jax.nn.gelu, agg_sum)
    act_low = act_full.astype(jnp.bfloat16)
    branch = typed(act_low, out_w)
    skip_all = jax.nn.sigmoid(skip_logit)
    skip_gate = jnp.sum(type_hot * skip_all[None, :], axis=1)[:, None]
    mixed_sum = skip_gate * branch + (1.0 - skip_gate) * x_f
    centered = mixed_sum - jnp.mean(mixed_sum, axis=1, keepdims=True)
    inv_std = lax.rsqrt(jnp.mean(centered * centered, axis=1, keepdims=True) + LN_EPS)
    normed = centered * inv_std
    valid_col = node_valid.astype(jnp.float32)[:, None]
    layer_out = (valid_col * (normed * ln_gain + ln_bias)).astype(jnp.bfloat16)
    grad_y = cotangent.astype(jnp.float32) * valid_col
    gain_grad = jnp.sum(grad_y * normed, axis=0)
    bias_grad = jnp.sum(grad_y, axis=0)
    grad_norm = grad_y * ln_gain
    grad_mix = inv_std * (
        grad_norm
        - jnp.mean(grad_norm, axis=1, keepdims=True)
        - normed * jnp.mean(grad_norm * normed, axis=1, keepdims=True)
    )
    grad_branch = (skip_gate * grad_mix).astype(jnp.bfloat16)
    gate_term = (
        jnp.sum(grad_mix * (branch - x_f), axis=1, keepdims=True) * skip_gate * (1.0 - skip_gate)
    )
    skip_grad = jnp.sum(type_hot * gate_term, axis=0)
    out_grad = typed_grad(act_low, grad_branch)
    grad_agg = gelu_back(typed_back(grad_branch, out_w))[0].astype(jnp.bfloat16)
    grad_agg_heads = grad_agg.reshape(tgt_rows, head_count, head_size)
    msg_grad = jnp.einsum(
        "rthd,the->rhde", u_rel_b, grad_agg_heads, preferred_element_type=jnp.float32
    )
    grad_urel = jnp.einsum(
        "the,rhde->rthd", grad_agg_heads, rel_msg, preferred_element_type=jnp.float32
    ).astype(jnp.bfloat16)
    grad_four = (
        jnp.einsum("tsr,rthd->thsd", select_low, grad_urel, preferred_element_type=jnp.float32)
        .astype(jnp.bfloat16)
        .reshape(tgt_rows, head_count, kind_count * head_size)
    )
    grad_cite = grad_urel[3]
    row_delta = (
        jnp.sum(grad_four.astype(jnp.float32) * u_four, axis=2)
        + jnp.sum(grad_cite.astype(jnp.float32) * u_cite, axis=2)
    ).T
    zero_four = jnp.zeros((tgt_rows, head_count, kind_count * head_size), jnp.float32)
    zero_cite = jnp.zeros((tgt_rows, head_count, head_size), jnp.float32)

    def back_turn(step_idx, loop_state):
        kv_blk, travel, acc_qf, acc_qc = loop_state
        k_grad, v_grad, qf_grad, qc_grad = backward_block(
            kv_blk,
            q_four,
            q_cite,
            grad_four,
            grad_cite,
            log_total,
            row_delta,
            block_codes((my_blk - step_idx) % n_blk),
        )
        travel = (
            from_behind((travel[0] + k_grad).astype(jnp.bfloat16), "blk", 1).astype(jnp.float32),
            from_behind((travel[1] + v_grad).astype(jnp.bfloat16), "blk", 1).astype(jnp.float32),
        )
        kv_blk = from_behind((kv_blk[0], kv_blk[1], kv_blk[2]), "blk", 1)
        return (kv_blk, travel, acc_qf + qf_grad, acc_qc + qc_grad)

    zero_kv = jnp.zeros((tgt_rows, feat_dim), jnp.float32)
    loop_state = lax.fori_loop(
        0, n_blk, back_turn, (whole_kv, (zero_kv, zero_kv), zero_four, zero_cite)
    )
    key_acc, value_acc = loop_state[1]
    acc_qf, acc_qc = (loop_state[2], loop_state[3])
    grad_key = key_acc.astype(jnp.bfloat16)
    grad_value = value_acc.astype(jnp.bfloat16)
    grad_relq = jnp.einsum(
        "tsr,thsd->rthd",
        select,
        acc_qf.reshape(tgt_rows, head_count, kind_count, head_size),
        precision=HIGH,
    )
    grad_relq = (
        (grad_relq + cite_hot[:, None, None, None] * acc_qc[None])
        .astype(jnp.bfloat16)
        .astype(jnp.float32)
    )
    prior_grad = jnp.sum(grad_relq * rel_raw, axis=(1, 3)) / math.sqrt(head_size)
    grad_raw = grad_relq * factor[:, None, :, None]
    att_grad = jnp.einsum("thj,rthk->rhjk", q_heads, grad_raw, precision=HIGH)
    grad_query = (
        jnp.einsum("rthk,rhjk->thj", grad_raw, att_f, precision=HIGH)
        .reshape(tgt_rows, feat_dim)
        .astype(jnp.bfloat16)
    )
    query_grad = typed_grad(features, grad_query)
    key_grad = typed_grad(shifted_b, grad_key)
    value_grad = typed_grad(shifted_b, grad_value)
    grad_shift = typed_back(grad_key, key_w) + typed_back(grad_value, value_w)
    table_grad = jnp.dot(gap_hot.T, grad_shift, precision=HIGH)
    rte_grad = jnp.dot(time_low.T, table_grad, precision=HIGH)
    input_grad = (
        (1.0 - skip_gate) * grad_mix + typed_back(grad_query, query_w) + grad_shift
    ).astype(jnp.bfloat16)
    summed = lax.psum(
        (
            query_grad,
            key_grad,
            value_grad,
            out_grad,
            att_grad,
            msg_grad,
            prior_grad,
            skip_grad,
            rte_grad,
            gain_grad,
            bias_grad,
        ),
        ("blk", "rep"),
    )
    return (
        layer_out,
        input_grad,
        summed[0],
        summed[1],
        summed[2],
        summed[3],
        summed[4],
        summed[5],
        summed[6],
        summed[7],
        summed[8],
        summed[9],
        summed[10],
    )


REL_TAB = relation_table()
HALF = 128
F32 = jnp.float32
LOW = jnp.bfloat16
VMEM_CAP = 65000 * 2**10


def nn(a, b):
    return lax.dot_general(a, b, (((1,), (0,)), ((), ())), preferred_element_type=F32)


def nt(a, b):
    return lax.dot_general(a, b, (((1,), (1,)), ((), ())), preferred_element_type=F32)


def tn(a, b):
    return lax.dot_general(a, b, (((0,), (0,)), ((), ())), preferred_element_type=F32)


def pick(kinds, kind, value):
    return jnp.where(kinds == kind, value, jnp.zeros_like(value))


def relation_of(kind, slot):
    hit = np.nonzero(REL_TAB[kind, slot])[0]
    return int(hit[0]) if len(hit) else None


def to_slots(rel_rows, kinds, kind_count):
    slots = []
    for slot in range(kind_count):
        rows = jnp.zeros(kinds.shape, F32)
        for kind in range(kind_count):
            rel = relation_of(kind, slot)
            if rel is not None:
                rows = jnp.where(kinds == kind, rel_rows(rel), rows)
        slots.append(rows)
    return slots, pick(kinds, 0, rel_rows(3))


def to_relations(slot_rows, cite_rows, kinds, kind_count, rel_count):
    out = []
    for rel in range(rel_count):
        if rel == 3:
            out.append(pick(kinds, 0, cite_rows))
            continue
        (kind, slot) = [
            (k, s) for k in range(kind_count) for s in range(kind_count) if relation_of(k, s) == rel
        ][0]
        out.append(pick(kinds, kind, slot_rows(slot)))
    return out


def flip(index, mask):
    return sum(((index // bit + mask // bit) % 2) * bit for bit in (1, 2, 4))


def gap_hot(gap_row, levels):
    gaps = jnp.broadcast_to(gap_row, (levels, gap_row.shape[1]))
    return (lax.broadcasted_iota(jnp.int32, gaps.shape, 0) == gaps).astype(F32).astype(LOW)


def remote(src, dst, sends, recvs, send_at, recv_at, device):
    return pltpu.make_async_remote_copy(
        src_ref=src,
        dst_ref=dst,
        send_sem=sends.at[send_at],
        recv_sem=recvs.at[recv_at],
        device_id=device,
        device_id_type=pl.DeviceIdType.MESH,
    )


def greet(devices):
    barrier = pltpu.get_barrier_semaphore()
    for device in devices:
        pl.semaphore_signal(
            barrier, inc=1, device_id=device, device_id_type=pl.DeviceIdType.MESH
        )
    pl.semaphore_wait(barrier, len(devices))


def layer_kernel(
    x_ref,
    kind_ref,
    gap_ref,
    valid_ref,
    rte_ref,
    time_ref,
    codes_hbm,
    cot_ref,
    qw_hbm,
    kw_hbm,
    vw_hbm,
    ow_hbm,
    att_ref,
    msg_ref,
    prior_ref,
    skip_ref,
    gain_ref,
    bias_ref,
    out_ref,
    input_ref,
    grads_ref,
    pack_ref,
    att_flat,
    codes,
    qw,
    kw,
    vw,
    ow,
    msg_flat,
    shifted,
    xt,
    base,
    shift_out,
    shift_in,
    load_sem,
    gather_send,
    gather_recv,
    back_send,
    back_recv,
    kt,
    vx,
    sbuf,
    probs,
    mx,
    sm,
    qs,
    qt2,
    qh,
    gt2,
    acc,
    two,
    agg,
    flat,
    grad_even,
    grad_odd,
):
    rows, feat = x_ref.shape
    n_blk = shifted.shape[0]
    levels = time_ref.shape[1]
    kind_count = qw.shape[0]
    rel_count, heads, size = att_ref.shape[:3]
    group = heads // 2
    me = lax.axis_index("blk")
    rep = lax.axis_index("rep")
    loads = [
        pltpu.make_async_copy(src, dst, load_sem.at[at])
        for at, (src, dst) in enumerate(
            ((kw_hbm, kw), (vw_hbm, vw), (qw_hbm, qw), (codes_hbm, codes), (ow_hbm, ow))
        )
    ]
    for load in loads:
        load.start()
    greet([(flip(me, mask), rep) for mask in range(1, n_blk)])

    x_f = x_ref[...].astype(F32).T
    x_t = x_f.astype(LOW)
    xt[...] = x_t
    table = tn(rte_ref[...], time_ref[...])
    table_hi = table.astype(LOW)
    table_lo = (table - table_hi.astype(F32)).astype(LOW)
    hot = gap_hot(gap_ref[...], levels)
    shifted[me, 0:feat, :] = (x_f + nn(table_hi, hot) + nn(table_lo, hot)).astype(LOW)
    shifted[me, feat:, :] = jnp.concatenate(
        [kind_ref[...].astype(F32), gap_ref[...].astype(F32), jnp.zeros((14, rows), F32)], axis=0
    ).astype(LOW)

    def hand_on(block, mask, send_at):
        return remote(
            shifted.at[block],
            shifted.at[block],
            gather_send,
            gather_recv,
            send_at,
            block,
            (flip(me, mask), rep),
        )

    for mask in (1, 2, 6, 4):
        hand_on(me, mask, mask).start()

    def source_row(j, row):
        return shifted[j, feat : feat + 16, :].astype(F32)[row : row + 1].astype(jnp.int32)

    kinds = jnp.broadcast_to(kind_ref[...], (size, rows))
    kinds_f = jnp.broadcast_to(kind_ref[...], (feat, rows))
    valid_f = jnp.broadcast_to(valid_ref[...], (feat, rows)).astype(F32)
    lane = lax.broadcasted_iota(jnp.int32, (rows, HALF), 1)
    ones_pad = (lax.broadcasted_iota(jnp.int32, (16, rows), 0) < 2).astype(F32).astype(LOW)
    scale = 1.0 / math.sqrt(size)

    def cols(j):
        return pl.ds(pl.multiple_of(j * rows, rows), rows)

    def store_part(start, value):
        grads_ref[pl.ds(start, value.shape[0]), :] = value.astype(LOW)

    for r in range(rel_count):
        for h in range(heads):
            flat[h * size : (h + 1) * size, r * size : (r + 1) * size] = att_ref[r, h].astype(F32)
    att_flat[...] = flat[...].astype(LOW)
    for r in range(rel_count):
        for h in range(heads):
            flat[r * size : (r + 1) * size, h * size : (h + 1) * size] = msg_ref[r, h].astype(F32)
    msg_flat[...] = flat[...].T.astype(LOW)

    def turned(m, k):
        return probs.at[0, 2 * m + k // 2, pl.ds((k % 2) * feat, feat), :]

    for m, (load, ref) in enumerate(((loads[0], kw), (loads[1], vw))):
        load.wait()
        for k in range(kind_count):
            turned(m, k)[...] = ref[k].astype(F32).T.astype(LOW)

    loads[2].wait()
    q_full = jnp.zeros((feat, rows), F32)
    for k in range(kind_count):
        q_full = jnp.where(kinds_f == k, tn(qw[k], x_t), q_full)
    for h in range(heads):
        qh[h] = q_full[h * size : (h + 1) * size].astype(LOW)

    def head_rows(ref, h):
        return ref[pl.ds(pl.multiple_of(h * size, size), size), :]

    def query_head(h, carry):
        raw = tn(head_rows(att_flat, h), qh[h])

        def rel_rows(r):
            part = raw[r * size : (r + 1) * size] * (prior_ref[r, h] * scale)
            return part.astype(LOW).astype(F32)

        slots, cite = to_slots(rel_rows, kinds, kind_count)
        slot_t = jnp.concatenate(slots, axis=0)
        cite_t = jnp.concatenate([cite, jnp.zeros((HALF - size, rows), F32)], axis=0)
        qt2[h, :, 0:rows] = slot_t.astype(LOW)
        qt2[h, :, rows:] = cite_t.astype(LOW)
        qs[h, 0:rows, 0:HALF] = slot_t.T.astype(LOW)
        qs[h, rows:, 0:HALF] = cite_t.T.astype(LOW)
        return carry

    lax.fori_loop(0, heads, query_head, 0, unroll=2)
    loads[3].wait()
    mx[...] = jnp.full(mx.shape, NEG_FILL, F32)

    def keep_scores(h, j, both, second, edge):
        val = jnp.where(second, both[rows:], both[:rows])
        val = jnp.where(edge, val, NEG_FILL)
        if h < group:
            sbuf[j, pl.ds(h * rows, rows), :] = val
        else:
            high = val.astype(LOW)
            probs[j, h, 0:rows, :] = high
            probs[j, h, rows:, :] = (val - high.astype(F32)).astype(LOW)
        mx[h] = jnp.maximum(mx[h], jnp.maximum(val[:, :HALF], val[:, HALF:]))

    def arrive(i, carry):
        j = flip(me, i)

        @pl.when(i > 0)
        def _():
            hand_on(j, 1, 0).wait_recv()

        @pl.when((i > 0) & (i % 2 == 0))
        def _():
            hand_on(j, 1, i + 1).start()

        src = jnp.broadcast_to(source_row(j, 0), (size, rows))
        block = shifted[j, 0:feat, :]
        for k in range(kind_count):
            key = nn(turned(0, k)[...], block)
            value = nn(turned(1, k)[...], block)
            for h in range(heads):
                part = slice(h * size, (h + 1) * size)
                kt[j, h, pl.ds(k * size, size), :] = pick(src, k, key[part]).astype(LOW)
                vx[j, h, pl.ds(k * size, size), :] = pick(src, k, value[part]).astype(LOW)
        for h in range(heads):
            vx[j, h, pl.ds(HALF, 16), :] = ones_pad
        code = codes[:, cols(j)]
        second = code == 2
        edge = code > 0
        two[j] = second.astype(F32).astype(LOW)
        before = None
        for h in range(heads + 1):
            both = nn(qs[h, :, 0:HALF], kt[j, h]) if h < heads else None
            if h > 0:
                keep_scores(h - 1, j, before, second, edge)
            before = both
        return carry

    lax.fori_loop(0, n_blk, arrive, 0)
    for send_at in range(1, n_blk):
        hand_on(me, 1, send_at).wait_send()

    def prob_block(h, j, top):
        if h < group:
            val = sbuf[j, pl.ds(h * rows, rows), :]
        else:
            val = probs[j, h, 0:rows, :].astype(F32) + probs[j, h, rows:, :].astype(F32)
        val = jnp.exp(val - top)
        low = val.astype(LOW)
        second = low * two[j]
        probs[j, h, 0:rows, :] = low - second
        probs[j, h, rows:, :] = second
        return val[:, :HALF] + val[:, HALF:]

    totals = jnp.zeros((rows, HALF), F32)
    for h in range(heads):
        top = jnp.max(mx[h], axis=1, keepdims=True)
        top = jnp.broadcast_to(jnp.maximum(top, 0.1 * NEG_FILL), (rows, rows))
        value_sum = None
        total = None
        for j in range(n_blk + 1):
            if j < n_blk:
                part = prob_block(h, j, top)
                total = part if total is None else total + part
            if j > 0:
                part = nt(vx[j - 1, h, 0:HALF, :], probs[j - 1, h])
                value_sum = part if value_sum is None else value_sum + part
        acc[h] = value_sum
        total = jnp.sum(total, axis=1, keepdims=True)
        totals = jnp.where(lane == h, jnp.broadcast_to(total, (rows, HALF)), totals)

    inverse = 1.0 / jnp.maximum(totals.T, 1.0)
    sm[...] = inverse[0:heads]

    def inv_row(h, count):
        return jnp.broadcast_to(sm[pl.ds(h, 1), :], (count, rows))

    def rel_part(h):
        return sbuf[h // group, pl.ds((h % group) * feat, feat), :].astype(LOW)

    for h in range(heads):
        inv = inv_row(h, HALF)
        u_slot = acc[h, :, 0:rows] * inv
        u_cite = acc[h, 0:size, rows:] * inv[0:size]
        acc[h, :, 0:rows] = u_slot
        acc[h, 0:size, rows:] = u_cite
        rel = to_relations(
            lambda s: u_slot[s * size : (s + 1) * size], u_cite, kinds, kind_count, rel_count
        )
        rel = jnp.concatenate(rel, axis=0)
        sbuf[h // group, pl.ds((h % group) * feat, feat), :] = rel
        agg[pl.ds(h * size, size), :] = nn(head_rows(msg_flat, h), rel.astype(LOW))
    loads[4].wait()
    agg_t = agg[...]
    slope = 0.7978845608028654
    inner = jnp.tanh(slope * (agg_t + 0.044715 * agg_t * agg_t * agg_t))
    act_t = (0.5 * agg_t * (1.0 + inner)).astype(LOW)
    gelu_back = 0.5 * (1.0 + inner) + 0.5 * agg_t * (1.0 - inner * inner) * slope * (
        1.0 + 3.0 * 0.044715 * agg_t * agg_t
    )
    skip = jnp.zeros((1, rows), F32)
    branch = jnp.zeros((feat, rows), F32)
    for k in range(kind_count):
        skip = jnp.where(kinds[0:1] == k, skip_ref[k], skip)
        branch = jnp.where(kinds_f == k, tn(ow[k], act_t), branch)
    gate_row = 1.0 / (1.0 + jnp.exp(-skip))
    gate = jnp.broadcast_to(gate_row, (feat, rows))
    mixed = gate * branch + (1.0 - gate) * x_f
    centered = mixed - jnp.mean(mixed, axis=0, keepdims=True)
    inv_std = lax.rsqrt(jnp.mean(centered * centered, axis=0, keepdims=True) + LN_EPS)
    normed = centered * inv_std
    affine = jnp.concatenate([gain_ref[...], bias_ref[...], jnp.zeros((HALF - 2, feat), F32)], axis=0).T
    gain = jnp.broadcast_to(affine[:, 0:1], (feat, rows))
    bias = jnp.broadcast_to(affine[:, 1:2], (feat, rows))
    out_ref[...] = (valid_f * (normed * gain + bias)).T.astype(LOW)
    grad_y = cot_ref[...].astype(F32).T * valid_f
    gain_col = jnp.sum(grad_y * normed, axis=1, keepdims=True)
    bias_col = jnp.sum(grad_y, axis=1, keepdims=True)
    grad_norm = grad_y * gain
    grad_mix = inv_std * (
        grad_norm
        - jnp.mean(grad_norm, axis=0, keepdims=True)
        - normed * jnp.mean(grad_norm * normed, axis=0, keepdims=True)
    )
    skip_row = (
        jnp.sum(grad_mix * (branch - x_f), axis=0, keepdims=True) * gate_row * (1.0 - gate_row)
    )
    base[...] = (1.0 - gate) * grad_mix
    grad_branch = gate * grad_mix
    grad_act = jnp.zeros((feat, rows), F32)
    for k in range(kind_count):
        masked = pick(kinds_f, k, grad_branch).astype(LOW)
        out_grad = nt(act_t, masked)
        store_part(out_at(k, 0), out_grad[:, :HALF])
        store_part(out_at(k, 1), out_grad[:, HALF:])
        grad_act = grad_act + nn(ow[k], masked)
    agg[...] = gelu_back * grad_act

    for h in range(heads):
        grad_agg = agg[pl.ds(h * size, size), :].astype(LOW)
        msg_grad = nt(grad_agg, rel_part(h))
        store_part(msg_at(0) + h * size, msg_grad[:, :HALF])
        store_part(msg_at(1) + h * size, msg_grad[:, HALF:])
        inv = inv_row(h, size)
        grad_u = tn(head_rows(msg_flat, h), grad_agg)

        def rel_rows(r):
            return grad_u[r * size : (r + 1) * size] * inv

        slots, cite = to_slots(rel_rows, kinds, kind_count)
        slot_t = jnp.concatenate(slots, axis=0).astype(LOW)
        cite_t = jnp.concatenate([cite, jnp.zeros((HALF - size, rows), F32)], axis=0).astype(LOW)
        gt2[h, :, 0:rows] = slot_t
        gt2[h, :, rows:] = cite_t
        slot_f = slot_t.astype(F32)
        cite_f = cite_t.astype(F32)
        delta = -(
            jnp.sum(slot_f * acc[h, :, 0:rows], axis=0, keepdims=True)
            + jnp.sum(cite_f[0:size] * acc[h, 0:size, rows:], axis=0, keepdims=True)
        )
        delta_hi = delta.astype(LOW).astype(F32)
        tail = jnp.concatenate(
            [delta_hi, delta - delta_hi, jnp.zeros((HALF - 2, rows), F32)], axis=0
        )
        tail_t = tail.T.astype(LOW)
        qs[h, 0:rows, 0:HALF] = slot_f.T.astype(LOW)
        qs[h, rows:, 0:HALF] = cite_f.T.astype(LOW)
        qs[h, 0:rows, HALF:] = tail_t[:, 0:16]
        qs[h, rows:, HALF:] = tail_t[:, 0:16]
        acc[h] = jnp.zeros(acc.shape[1:], F32)

    slot_id = lax.broadcasted_iota(jnp.int32, (HALF, rows), 0) // size

    def own_slots(j):
        return slot_id == jnp.broadcast_to(source_row(j, 0), (HALF, rows))

    def value_block(j, carry):
        own = own_slots(j)
        for h in range(heads):
            part = jnp.where(own, nn(gt2[h], probs[j, h]), 0.0)
            for k in range(kind_count):
                sbuf[j, pl.ds(k * feat + h * size, size), :] = part[k * size : (k + 1) * size]
        total = None
        for k in range(kind_count):
            part = nn(vw[k], sbuf[j, pl.ds(k * feat, feat), :].astype(LOW))
            total = part if total is None else total + part
        shift_out[j] = total.astype(LOW)
        return carry

    lax.fori_loop(0, n_blk, value_block, 0, unroll=2)
    for k in range(kind_count):
        total = None
        for j in range(n_blk):
            part = nt(shifted[j, 0:feat, :], sbuf[j, pl.ds(k * feat, feat), :].astype(LOW))
            total = part if total is None else total + part
        store_part(value_at(k, 0), total[:, :HALF])
        store_part(value_at(k, 1), total[:, HALF:])

    pack_ref[...] = jnp.zeros_like(pack_ref)

    def send_back(j):
        return remote(
            shift_out.at[j], shift_in.at[me], back_send, back_recv, j, me, (j, rep)
        )

    grad_bufs = (grad_even, grad_odd)
    for g in range(2):
        half = slice(g * HALF, (g + 1) * HALF)
        key_cat = jnp.concatenate([kw[k, :, half] for k in range(kind_count)], axis=1)

        def score_grads(i, carry, g=g, key_cat=key_cat):
            j = flip(me, n_blk - 1 - i)
            own = own_slots(j)
            for u in range(group + 1):
                h = g * group + u
                if u < group:
                    grad_bufs[h % 2][...] = probs[j, h] * nn(qs[h], vx[j, h]).astype(LOW)
                if u > 0:
                    grad = grad_bufs[(h - 1) % 2][...]
                    part = jnp.where(own, nn(qt2[h - 1], grad), 0.0)
                    for k in range(kind_count):
                        at = pl.ds(k * HALF + (u - 1) * size, size)
                        sbuf[j, at, :] = part[k * size : (k + 1) * size]
                    acc[h - 1] = acc[h - 1] + nt(kt[j, h - 1], grad)
            total = shift_out[j].astype(F32) + nn(
                key_cat, sbuf[j, pl.ds(0, kind_count * HALF), :].astype(LOW)
            )
            low = total.astype(LOW)
            shift_out[j] = low
            if g == 1:

                @pl.when(i < n_blk - 1)
                def _():
                    send_back(j).start()

                gaps = gap_hot(source_row(j, 1), levels)
                pack_ref[0:levels, :] = pack_ref[0:levels, :] + nt(gaps, low)
            return carry

        lax.fori_loop(0, n_blk, score_grads, 0)
        total = None
        for j in range(n_blk):
            part = nt(
                shifted[j, 0:feat, :], sbuf[j, pl.ds(0, kind_count * HALF), :].astype(LOW)
            )
            total = part if total is None else total + part
        for k in range(kind_count):
            store_part(key_at(k, g), total[:, k * HALF : (k + 1) * HALF])
        grad_q = []
        for h in range(g * group, (g + 1) * group):
            slot = acc[h, :, 0:rows]
            rel = to_relations(
                lambda s: slot[s * size : (s + 1) * size],
                acc[h, 0:size, rows:],
                kinds,
                kind_count,
                rel_count,
            )
            rel = [part.astype(LOW) for part in rel]
            att_grad = nt(qh[h], jnp.concatenate(rel, axis=0))
            store_part(att_at(0) + h * size, att_grad[:, :HALF])
            store_part(att_at(1) + h * size, att_grad[:, HALF:])
            raw = [
                (part.astype(F32) * (prior_ref[r, h] * scale)).astype(LOW)
                for r, part in enumerate(rel)
            ]
            grad_q.append(nn(head_rows(att_flat, h), jnp.concatenate(raw, axis=0)))
        grad_q = jnp.concatenate(grad_q, axis=0).astype(LOW).astype(F32)
        total = base[...]
        for k in range(kind_count):
            masked = pick(kinds_f[0:HALF], k, grad_q).astype(LOW)
            store_part(query_at(k, g), nt(xt[...], masked))
            total = total + nn(qw[k, :, half], masked)
        base[...] = total

    pair = jnp.where(
        lane == 0,
        jnp.broadcast_to(gain_col, (feat, HALF)),
        jnp.where(lane == 1, jnp.broadcast_to(bias_col, (feat, HALF)), 0.0),
    ).T
    spot = lax.broadcasted_iota(jnp.int32, (1, rows), 1)
    skips = jnp.zeros((1, rows), F32)
    for k in range(kind_count):
        skips = jnp.where(
            spot == k, jnp.sum(pick(kinds[0:1], k, skip_row), axis=1, keepdims=True), skips
        )
    pack_ref[levels : levels + 8, :] = jnp.concatenate(
        [pair[0:2], skips, jnp.zeros((5, rows), F32)], axis=0
    )
    total = base[...] + shift_out[me].astype(F32)
    for mask in range(1, n_blk):
        j = flip(me, mask)
        send_back(j).wait_send()
        remote(shift_in.at[j], shift_in.at[j], back_send, back_recv, j, j, (j, rep)).wait_recv()
        total = total + shift_in[j].astype(F32)
    input_ref[...] = total.T.astype(LOW)


def out_at(k, half):
    return (2 * k + half) * 256


def msg_at(half):
    return 2048 + half * 256


def value_at(k, half):
    return 2560 + (2 * k + half) * 256


def query_at(k, half):
    return 4608 + (8 * half + k) * 256


def key_at(k, half):
    return 4608 + (8 * half + 4 + k) * 256


def att_at(half):
    return 8704 + half * 256


GRAD_ROWS = 9216


def reduce_kernel(
    grads_ref,
    pack_ref,
    full,
    small_ref,
    work,
    core_in,
    plane_in,
    line_in,
    pack_in,
    pack_work,
    sends,
    recvs,
):
    me = lax.axis_index("blk")
    rep = lax.axis_index("rep")
    z, y, x, core = me // 2, me % 2, rep // 2, rep % 2
    by_core = (me, rep + 1 - 2 * core)
    by_x = (me, rep + 2 - 4 * x)
    by_y = (me + 1 - 2 * y, rep)
    by_z = [(((z + step) % 4) * 2 + y, rep) for step in (1, 2, 3)]
    greet([by_core, by_x, by_y] + by_z)
    total = grads_ref.shape[0]
    half, quarter = total // 2, total // 4
    count = iter(range(sends.shape[0]))

    def send(src, dst, device):
        at = next(count)
        copy = remote(src, dst, sends, recvs, at, at, device)
        copy.start()
        return copy

    def rows_of(ref, start, size):
        return ref.at[pl.ds(pl.multiple_of(start, 16), size), :]

    def load(ref, start, size):
        return ref[pl.ds(pl.multiple_of(start, 16), size), :].astype(F32)

    def add_in(start, size, *parts):
        value = load(work, start, size)
        for part in parts:
            value = value + part
        work[pl.ds(pl.multiple_of(start, 16), size), :] = value.astype(LOW)

    mine = core * half
    a = send(rows_of(grads_ref, half - mine, half), core_in, by_core)
    b = send(pack_ref, pack_in.at[0], by_core)
    a.wait()
    b.wait()
    work[...] = (load(grads_ref, mine, half) + core_in[...].astype(F32)).astype(LOW)
    pack_work[0] = pack_ref[...] + pack_in[0]
    size = quarter // 2
    starts = [x * size, quarter + y * size]
    away = [size - x * size, quarter + size - y * size]
    copies = [
        send(rows_of(work, away[0], size), plane_in.at[0], by_x),
        send(rows_of(work, away[1], size), plane_in.at[1], by_y),
        send(pack_work.at[0], pack_in.at[1], by_x),
    ]
    for copy in copies:
        copy.wait()
    for s in range(2):
        add_in(starts[s], size, plane_in[s].astype(F32))
    pack_work[1] = pack_work[0] + pack_in[1]
    size = size // 2
    turn = [y, x]
    copies = [
        send(
            rows_of(work, starts[s] + size - turn[s] * size, size),
            plane_in.at[2 + s, pl.ds(0, size), :],
            (by_y, by_x)[s],
        )
        for s in range(2)
    ]
    copies.append(send(pack_work.at[1], pack_in.at[2], by_y))
    for copy in copies:
        copy.wait()
    starts = [starts[s] + turn[s] * size for s in range(2)]
    for s in range(2):
        add_in(starts[s], size, plane_in[2 + s, 0:size, :].astype(F32))
    pack_work[2] = pack_work[1] + pack_in[2]
    size = size // 4
    copies = []
    for step in (2, 3, 1):
        for s in range(2):
            there = starts[s] + ((z + step) % 4) * size
            copies.append(
                send(rows_of(work, there, size), line_in.at[s, step - 1], by_z[step - 1])
            )
        copies.append(send(pack_work.at[2], pack_in.at[2 + step], by_z[step - 1]))
    for copy in copies:
        copy.wait()
    small = pack_work[2] + pack_in[3] + pack_in[4] + pack_in[5]
    starts = [starts[s] + z * size for s in range(2)]
    for s in range(2):
        value = load(work, starts[s], size)
        for step in range(3):
            value = value + line_in[s, step].astype(F32)
        full[pl.ds(pl.multiple_of(mine + starts[s], 16), size), :] = value.astype(LOW)

    def share(start, size, device):
        return send(rows_of(full, start, size), rows_of(full, start, size), device)

    copies = [
        share(mine + starts[s], size, by_z[step - 1]) for step in (2, 3, 1) for s in range(2)
    ]
    for copy in copies:
        copy.wait()
    starts = [starts[s] - z * size for s in range(2)]
    size = size * 4
    copies = [share(mine + starts[s], size, (by_y, by_x)[s]) for s in range(2)]
    for copy in copies:
        copy.wait()
    starts = [starts[s] - turn[s] * size for s in range(2)]
    size = size * 2
    copies = [share(mine + starts[s], size, (by_x, by_y)[s]) for s in range(2)]
    early = [share(mine + starts[s], size, by_core) for s in range(2)]
    for copy in copies:
        copy.wait()
    late = [share(mine + away[s], size, by_core) for s in range(2)]
    for copy in early + late:
        copy.wait()
    small_ref[...] = small


def finish_kernel(
    full,
    small_ref,
    att_flat,
    time_ref,
    prior_ref,
    out_in,
    input_in,
    out_ref,
    input_ref,
    qg_ref,
    kg_ref,
    vg_ref,
    og_ref,
    attg_ref,
    msgg_ref,
    priorg_ref,
    skip_ref,
    rte_ref,
    gain_ref,
    bias_ref,
):
    out_ref[...] = out_in[...]
    input_ref[...] = input_in[...]
    kind_count, feat = qg_ref.shape[:2]
    rel_count, heads, width = attg_ref.shape[:3]
    scale = 1.0 / math.sqrt(width)

    def part(start):
        return full[pl.ds(start, feat), :].astype(F32)

    for ref, at in ((qg_ref, query_at), (kg_ref, key_at), (vg_ref, value_at), (og_ref, out_at)):
        for k in range(kind_count):
            for half in range(2):
                ref[k, :, half * HALF : (half + 1) * HALF] = part(at(k, half))
    att = jnp.concatenate([part(att_at(0)), part(att_at(1))], axis=1)
    msg = jnp.concatenate([part(msg_at(0)), part(msg_at(1))], axis=1).T
    for r in range(rel_count):
        for h in range(heads):
            block = (slice(h * width, (h + 1) * width), slice(r * width, (r + 1) * width))
            attg_ref[r, h] = att[block] * (prior_ref[r, h] * scale)
            msgg_ref[r, h] = msg[block[::-1]]
    prod = (att * att_flat[...].astype(F32)).reshape(heads, width, feat)
    prod = jnp.sum(prod, axis=1)
    spread = (
        lax.broadcasted_iota(jnp.int32, (feat, rel_count), 0) // width
        == lax.broadcasted_iota(jnp.int32, (feat, rel_count), 1)
    ).astype(F32).astype(LOW)
    prior = jnp.zeros((rel_count, heads), F32)
    for _ in range(3):
        low = prod.astype(LOW)
        prior = prior + lax.dot_general(
            spread, low, (((0,), (1,)), ((), ())), preferred_element_type=F32
        )
        prod = prod - low.astype(F32)
    priorg_ref[...] = prior * scale
    levels = time_ref.shape[1]
    small = small_ref[...]
    rte = jnp.zeros(rte_ref.shape, F32)
    rest = small[0:levels]
    for _ in range(3):
        low = rest.astype(LOW)
        rte = rte + nn(time_ref[...], low)
        rest = rest - low.astype(F32)
    rte_ref[...] = rte
    gain_ref[...] = small[levels : levels + 1]
    bias_ref[...] = small[levels + 1 : levels + 2]
    skip_ref[...] = small[levels + 2 : levels + 3, 0:kind_count]


def layer_call(n_blk, *args):
    rows, feat = args[0].shape
    kind_count = args[8].shape[0]
    rel_count, heads, size = args[12].shape[:3]
    vmem = pl.BlockSpec(memory_space=pltpu.VMEM)
    smem = pl.BlockSpec(memory_space=pltpu.SMEM)
    hbm = pl.BlockSpec(memory_space=pl.ANY)
    square = (feat, feat)
    weight = pltpu.VMEM((kind_count,) + square, LOW)

    def shape(dims, kind):
        return jax.ShapeDtypeStruct(dims, kind)

    return pl.pallas_call(
        layer_kernel,
        out_shape=[
            shape((rows, feat), LOW),
            shape((rows, feat), LOW),
            shape((GRAD_ROWS, HALF), LOW),
            shape((LEVELS + 8, feat), F32),
            shape(square, LOW),
        ],
        in_specs=[vmem] * 6 + [hbm, vmem] + [hbm] * 4 + [vmem] * 2 + [smem] * 2 + [vmem] * 2,
        out_specs=[vmem] * 5,
        scratch_shapes=[
            pltpu.VMEM((rows, n_blk * rows), jnp.int32),
            weight,
            weight,
            weight,
            weight,
            pltpu.VMEM(square, LOW),
            pltpu.VMEM((n_blk, feat + 16, rows), LOW),
            pltpu.VMEM((feat, rows), LOW),
            pltpu.VMEM((feat, rows), F32),
            pltpu.VMEM((n_blk, feat, rows), LOW),
            pltpu.VMEM((n_blk, feat, rows), LOW),
            pltpu.SemaphoreType.DMA((5,)),
            pltpu.SemaphoreType.DMA((n_blk,)),
            pltpu.SemaphoreType.DMA((n_blk,)),
            pltpu.SemaphoreType.DMA((n_blk,)),
            pltpu.SemaphoreType.DMA((n_blk,)),
            pltpu.VMEM((n_blk, heads, HALF, rows), LOW),
            pltpu.VMEM((n_blk, heads, HALF + 16, rows), LOW),
            pltpu.VMEM((n_blk, heads // 2 * rows, rows), F32),
            pltpu.VMEM((n_blk, heads, 2 * rows, rows), LOW),
            pltpu.VMEM((heads, rows, HALF), F32),
            pltpu.VMEM((heads, rows), F32),
            pltpu.VMEM((heads, 2 * rows, HALF + 16), LOW),
            pltpu.VMEM((heads, HALF, 2 * rows), LOW),
            pltpu.VMEM((heads, size, rows), LOW),
            pltpu.VMEM((heads, HALF, 2 * rows), LOW),
            pltpu.VMEM((heads, HALF, 2 * rows), F32),
            pltpu.VMEM((n_blk, rows, rows), LOW),
            pltpu.VMEM(square, F32),
            pltpu.VMEM(square, F32),
            pltpu.VMEM((2 * rows, rows), LOW),
            pltpu.VMEM((2 * rows, rows), LOW),
        ],
        compiler_params=pltpu.CompilerParams(
            vmem_limit_bytes=VMEM_CAP, collective_id=0, has_side_effects=True
        ),
        name="layer",
    )(*args)


def time_columns(level_count, feat_width):
    positions = np.arange(level_count, dtype=np.float32)[:, None]
    steps = np.arange(feat_width // 2, dtype=np.float32)[None, :]
    phases = positions / np.power(np.float32(10000.0), np.float32(2.0) * steps / feat_width)
    table = np.stack([np.sin(phases), np.cos(phases)], axis=2).reshape(level_count, feat_width)
    return jnp.asarray(np.ascontiguousarray(table.T), LOW)


def fast_body(
    features,
    node_type,
    time_gap,
    node_valid,
    edge_codes,
    query_w,
    key_w,
    value_w,
    out_w,
    rel_att,
    rel_msg,
    rel_prior,
    skip_logit,
    rte_w,
    ln_gain,
    ln_bias,
    cotangent,
):
    rows, feat = features.shape
    n_blk = lax.axis_size("blk")
    kind_count = query_w.shape[0]
    time_low = time_columns(LEVELS, feat)
    vmem = pl.BlockSpec(memory_space=pltpu.VMEM)
    smem = pl.BlockSpec(memory_space=pltpu.SMEM)
    square = (feat, feat)

    def shape(dims, kind):
        return jax.ShapeDtypeStruct(dims, kind)

    layer_out, input_grad, grads, pack, att_flat = layer_call(
        n_blk,
        features,
        node_type[None],
        time_gap[None],
        node_valid[None],
        rte_w,
        time_low,
        edge_codes,
        cotangent,
        query_w,
        key_w,
        value_w,
        out_w,
        rel_att,
        rel_msg,
        rel_prior,
        skip_logit,
        ln_gain[None],
        ln_bias[None],
    )
    quarter = GRAD_ROWS // 4
    full, small = pl.pallas_call(
        reduce_kernel,
        out_shape=[shape(grads.shape, LOW), shape(pack.shape, F32)],
        in_specs=[vmem] * 2,
        out_specs=[vmem] * 2,
        scratch_shapes=[
            pltpu.VMEM((GRAD_ROWS // 2, HALF), LOW),
            pltpu.VMEM((GRAD_ROWS // 2, HALF), LOW),
            pltpu.VMEM((4, quarter // 2, HALF), LOW),
            pltpu.VMEM((2, 3, quarter // 16, HALF), LOW),
            pltpu.VMEM((6, LEVELS + 8, feat), F32),
            pltpu.VMEM((3, LEVELS + 8, feat), F32),
            pltpu.SemaphoreType.DMA((40,)),
            pltpu.SemaphoreType.DMA((40,)),
        ],
        compiler_params=pltpu.CompilerParams(
            vmem_limit_bytes=VMEM_CAP, collective_id=1, has_side_effects=True
        ),
        name="reduce",
    )(grads, pack)
    outs = pl.pallas_call(
        finish_kernel,
        out_shape=[shape(layer_out.shape, LOW), shape(input_grad.shape, LOW)]
        + [shape((kind_count,) + square, F32)] * 4
        + [shape(rel_att.shape, F32)] * 2
        + [
            shape(rel_prior.shape, F32),
            shape((1, kind_count), F32),
            shape(square, F32),
            shape((1, feat), F32),
            shape((1, feat), F32),
        ],
        in_specs=[vmem] * 4 + [smem] + [vmem] * 2,
        out_specs=[vmem] * 13,
        compiler_params=pltpu.CompilerParams(vmem_limit_bytes=VMEM_CAP),
        name="finish",
    )(full, small, att_flat, time_low, rel_prior, layer_out, input_grad)
    return (*outs[:9], outs[9][0], outs[10], outs[11][0], outs[12][0])


def solution(mesh):
    in_specs = (
        P(("blk", "rep"), None),
        P(("blk", "rep")),
        P(("blk", "rep")),
        P(("blk", "rep")),
        P(("blk", "rep"), None),
        P(),
        P(),
        P(),
        P(),
        P(),
        P(),
        P(),
        P(),
        P(),
        P(),
        P(),
        P(("blk", "rep"), None),
    )
    out_specs = (
        P(("blk", "rep"), None),
        P(("blk", "rep"), None),
        P(),
        P(),
        P(),
        P(),
        P(),
        P(),
        P(),
        P(),
        P(),
        P(),
        P(),
    )
    plan = fast_body if tuple(mesh.shape.values()) == (8, 4) else body
    return jax.shard_map(plan, mesh=mesh, in_specs=in_specs, out_specs=out_specs, check_vma=False)
```

```python
import math

import jax
import jax.numpy as jnp
import numpy as np
from jax import lax
from jax.experimental import pallas as pl
from jax.experimental.pallas import tpu as pltpu
from jax.sharding import PartitionSpec as P

LEVELS = 16


NEG_FILL = -1e30
LN_EPS = 1e-05
HIGH = lax.Precision.HIGHEST


def from_behind(block, axis, distance):
    devices = range(lax.axis_size(axis))
    route = [((i - distance) % len(devices), i) for i in devices]
    return lax.ppermute(block, axis, route)


def relation_table():
    rel_tab = np.zeros((4, 4, 8), np.float32)
    rel_tab[0, 1, 0] = 1.0
    rel_tab[1, 0, 1] = 1.0
    rel_tab[0, 0, 2] = 1.0
    rel_tab[2, 0, 4] = 1.0
    rel_tab[0, 2, 5] = 1.0
    rel_tab[3, 1, 6] = 1.0
    rel_tab[1, 3, 7] = 1.0
    return rel_tab


def time_table(level_count, feat_width):
    positions = jnp.arange(level_count, dtype=jnp.float32)[:, None]
    freq_idx = jnp.arange(feat_width // 2, dtype=jnp.float32)[None, :]
    phases = positions / jnp.power(10000.0, 2.0 * freq_idx / feat_width)
    return jnp.stack([jnp.sin(phases), jnp.cos(phases)], axis=2).reshape(level_count, feat_width)


def slot_spread(heads_arr, kind_hot):
    spread_out = heads_arr[:, :, None, :] * kind_hot[:, None, :, None]
    return spread_out.reshape(heads_arr.shape[0], heads_arr.shape[1], -1)


def slot_collapse(slot_arr, kind_hot):
    src_rows, head_count = (slot_arr.shape[0], slot_arr.shape[1])
    kind_count = kind_hot.shape[1]
    shaped = slot_arr.reshape(src_rows, head_count, kind_count, -1)
    return jnp.sum(shaped * kind_hot.astype(jnp.float32)[:, None, :, None], axis=2)


def block_scores(kv_blk, q_four, q_cite, code_blk, kind_count):
    key_blk, value_blk, kind_blk = kv_blk
    src_rows = key_blk.shape[0]
    head_count = q_four.shape[1]
    key_heads = key_blk.reshape(src_rows, head_count, -1)
    value_heads = value_blk.reshape(src_rows, head_count, -1)
    kind_hot = (kind_blk[:, None] == jnp.arange(kind_count).astype(jnp.bfloat16)[None, :]).astype(
        jnp.bfloat16
    )
    key_four = slot_spread(key_heads, kind_hot)
    value_four = slot_spread(value_heads, kind_hot)
    is_one = (code_blk == 1)[None]
    is_two = (code_blk == 2)[None]
    slot_dot = jnp.einsum("thc,shc->hts", q_four, key_four, preferred_element_type=jnp.float32)
    cite_dot = jnp.einsum("thd,shd->hts", q_cite, key_heads, preferred_element_type=jnp.float32)
    scores = jnp.where(is_one, slot_dot, jnp.where(is_two, cite_dot, NEG_FILL))
    return (scores, is_one, is_two, key_heads, value_heads, key_four, value_four, kind_hot)


def attend_block(run_state, kv_blk, q_four, q_cite, code_blk, kind_count):
    run_max, run_sum, acc_four, acc_cite = run_state
    scores, is_one, is_two, key_heads, value_heads, key_four, value_four, kind_hot = block_scores(
        kv_blk, q_four, q_cite, code_blk, kind_count
    )
    new_max = jnp.maximum(run_max, jnp.max(scores, axis=2))
    expd = jnp.where((code_blk > 0)[None], jnp.exp(scores - new_max[:, :, None]), 0.0)
    rescale = jnp.exp(run_max - new_max)
    run_sum = run_sum * rescale + jnp.sum(expd, axis=2)
    prob_low = expd.astype(jnp.bfloat16)
    zero_low = jnp.zeros_like(prob_low)
    p_one = jnp.where(is_one, prob_low, zero_low)
    p_two = jnp.where(is_two, prob_low, zero_low)
    rescale_t = rescale.T[:, :, None]
    acc_four = acc_four * rescale_t + jnp.einsum(
        "hts,shc->thc", p_one, value_four, preferred_element_type=jnp.float32
    )
    acc_cite = acc_cite * rescale_t + jnp.einsum(
        "hts,shd->thd", p_two, value_heads, preferred_element_type=jnp.float32
    )
    return (new_max, run_sum, acc_four, acc_cite)


def back_block(
    kv_blk, q_four, q_cite, grad_four, grad_cite, log_total, row_delta, code_blk, kind_count
):
    scores, is_one, is_two, key_heads, value_heads, key_four, value_four, kind_hot = block_scores(
        kv_blk, q_four, q_cite, code_blk, kind_count
    )
    prob_full = jnp.where((code_blk > 0)[None], jnp.exp(scores - log_total[:, :, None]), 0.0)
    prob_low = prob_full.astype(jnp.bfloat16)
    zero_low = jnp.zeros_like(prob_low)
    p_one = jnp.where(is_one, prob_low, zero_low)
    p_two = jnp.where(is_two, prob_low, zero_low)
    grad_slot = jnp.einsum(
        "thc,shc->hts", grad_four, value_four, preferred_element_type=jnp.float32
    )
    grad_other = jnp.einsum(
        "thd,shd->hts", grad_cite, value_heads, preferred_element_type=jnp.float32
    )
    grad_probs = jnp.where(is_one, grad_slot, jnp.where(is_two, grad_other, 0.0))
    grad_scores = (prob_full * (grad_probs - row_delta[:, :, None])).astype(jnp.bfloat16)
    d_one = jnp.where(is_one, grad_scores, zero_low)
    d_two = jnp.where(is_two, grad_scores, zero_low)
    qf_grad = jnp.einsum("hts,shc->thc", d_one, key_four, preferred_element_type=jnp.float32)
    qc_grad = jnp.einsum("hts,shd->thd", d_two, key_heads, preferred_element_type=jnp.float32)
    k_grad = slot_collapse(
        jnp.einsum("hts,thc->shc", d_one, q_four, preferred_element_type=jnp.float32), kind_hot
    )
    k_grad = k_grad + jnp.einsum("hts,thd->shd", d_two, q_cite, preferred_element_type=jnp.float32)
    v_grad = slot_collapse(
        jnp.einsum("hts,thc->shc", p_one, grad_four, preferred_element_type=jnp.float32), kind_hot
    )
    v_grad = v_grad + jnp.einsum(
        "hts,thd->shd", p_two, grad_cite, preferred_element_type=jnp.float32
    )
    src_rows = k_grad.shape[0]
    return (k_grad.reshape(src_rows, -1), v_grad.reshape(src_rows, -1), qf_grad, qc_grad)


def body(
    features,
    node_type,
    time_gap,
    node_valid,
    edge_codes,
    query_w,
    key_w,
    value_w,
    out_w,
    rel_att,
    rel_msg,
    rel_prior,
    skip_logit,
    rte_w,
    ln_gain,
    ln_bias,
    cotangent,
):
    tgt_rows, feat_dim = features.shape
    kind_count = query_w.shape[0]
    rel_count = rel_att.shape[0]
    head_count = rel_att.shape[1]
    head_size = rel_att.shape[2]
    n_blk = lax.axis_size("blk")
    my_blk = lax.axis_index("blk")
    type_hot = (node_type[:, None] == jnp.arange(kind_count)[None, :]).astype(jnp.float32)
    type_low = type_hot.astype(jnp.bfloat16)
    gap_hot = (time_gap[:, None] == jnp.arange(LEVELS)[None, :]).astype(jnp.float32)
    time_low = time_table(LEVELS, feat_dim).astype(jnp.bfloat16).astype(jnp.float32)
    rte_table = jnp.dot(time_low, rte_w.astype(jnp.float32), precision=HIGH)
    x_f = features.astype(jnp.float32)
    shifted = x_f + jnp.dot(gap_hot, rte_table, precision=HIGH)
    shifted_b = shifted.astype(jnp.bfloat16)

    def typed(inp, weights):
        parts = jnp.einsum("th,khd->tkd", inp, weights, preferred_element_type=jnp.float32)
        return jnp.sum(parts * type_hot[:, :, None], axis=1)

    def typed_grad(inp, grad_low):
        masked = inp[:, None, :] * type_low[:, :, None]
        return jnp.einsum("tkh,td->khd", masked, grad_low, preferred_element_type=jnp.float32)

    def typed_back(grad_low, weights):
        parts = jnp.einsum("td,khd->tkh", grad_low, weights, preferred_element_type=jnp.float32)
        return jnp.sum(parts * type_hot[:, :, None], axis=1)

    q_low = typed(features, query_w).astype(jnp.bfloat16)
    key_low = typed(shifted_b, key_w).astype(jnp.bfloat16)
    value_low = typed(shifted_b, value_w).astype(jnp.bfloat16)
    kind_low = node_type.astype(jnp.bfloat16)
    q_heads = q_low.reshape(tgt_rows, head_count, head_size).astype(jnp.float32)
    att_f = rel_att.astype(jnp.float32)
    factor = rel_prior / math.sqrt(head_size)
    rel_raw = jnp.einsum("thj,rhjk->rthk", q_heads, att_f, precision=HIGH)
    rel_query = (rel_raw * factor[:, None, :, None]).astype(jnp.bfloat16)
    select = jnp.einsum("tk,ksr->tsr", type_hot, jnp.asarray(relation_table()), precision=HIGH)
    select_low = select.astype(jnp.bfloat16)
    cite_hot = (jnp.arange(rel_count) == 3).astype(jnp.float32)
    q_four = (
        jnp.einsum("tsr,rthd->thsd", select_low, rel_query, preferred_element_type=jnp.float32)
        .astype(jnp.bfloat16)
        .reshape(tgt_rows, head_count, kind_count * head_size)
    )
    q_cite = rel_query[3]

    def block_codes(source):
        return lax.dynamic_slice_in_dim(edge_codes, source * tgt_rows, tgt_rows, 1)

    def forward_block(run_state, kv_blk, qf_part, qc_part, code_blk):
        result = attend_block(run_state, kv_blk, qf_part, qc_part, code_blk, kind_count)
        return result

    def backward_block(kv_blk, qf_part, qc_part, gf_part, gc_part, lse_part, delta_part, code_blk):
        return back_block(
            kv_blk, qf_part, qc_part, gf_part, gc_part, lse_part, delta_part, code_blk, kind_count
        )

    whole_kv = (key_low, value_low, kind_low)

    def forward_turn(step_idx, loop_state):
        run_state, kv_blk = loop_state
        run_state = forward_block(
            run_state, kv_blk, q_four, q_cite, block_codes((my_blk - step_idx) % n_blk)
        )
        kv_blk = from_behind((kv_blk[0], kv_blk[1], kv_blk[2]), "blk", 1)
        return (run_state, kv_blk)

    run_state, kv_last = lax.fori_loop(
        0,
        n_blk,
        forward_turn,
        (
            (
                jnp.full((head_count, tgt_rows), NEG_FILL, jnp.float32),
                jnp.zeros((head_count, tgt_rows), jnp.float32),
                jnp.zeros((tgt_rows, head_count, kind_count * head_size), jnp.float32),
                jnp.zeros((tgt_rows, head_count, head_size), jnp.float32),
            ),
            whole_kv,
        ),
    )
    run_max, run_sum, acc_four, acc_cite = run_state
    floor_sum = jnp.maximum(run_sum, 1.0)
    log_total = run_max + jnp.log(floor_sum)
    norm_t = floor_sum.T[:, :, None]
    u_four = acc_four / norm_t
    u_cite = acc_cite / norm_t
    u_rel = jnp.einsum(
        "tsr,thsd->rthd",
        select,
        u_four.reshape(tgt_rows, head_count, kind_count, head_size),
        precision=HIGH,
    )
    u_rel = u_rel + cite_hot[:, None, None, None] * u_cite[None]
    u_rel_b = u_rel.astype(jnp.bfloat16)
    agg_sum = jnp.einsum(
        "rthd,rhde->the", u_rel_b, rel_msg, preferred_element_type=jnp.float32
    ).reshape(tgt_rows, feat_dim)
    act_full, gelu_back = jax.vjp(jax.nn.gelu, agg_sum)
    act_low = act_full.astype(jnp.bfloat16)
    branch = typed(act_low, out_w)
    skip_all = jax.nn.sigmoid(skip_logit)
    skip_gate = jnp.sum(type_hot * skip_all[None, :], axis=1)[:, None]
    mixed_sum = skip_gate * branch + (1.0 - skip_gate) * x_f
    centered = mixed_sum - jnp.mean(mixed_sum, axis=1, keepdims=True)
    inv_std = lax.rsqrt(jnp.mean(centered * centered, axis=1, keepdims=True) + LN_EPS)
    normed = centered * inv_std
    valid_col = node_valid.astype(jnp.float32)[:, None]
    layer_out = (valid_col * (normed * ln_gain + ln_bias)).astype(jnp.bfloat16)
    grad_y = cotangent.astype(jnp.float32) * valid_col
    gain_grad = jnp.sum(grad_y * normed, axis=0)
    bias_grad = jnp.sum(grad_y, axis=0)
    grad_norm = grad_y * ln_gain
    grad_mix = inv_std * (
        grad_norm
        - jnp.mean(grad_norm, axis=1, keepdims=True)
        - normed * jnp.mean(grad_norm * normed, axis=1, keepdims=True)
    )
    grad_branch = (skip_gate * grad_mix).astype(jnp.bfloat16)
    gate_term = (
        jnp.sum(grad_mix * (branch - x_f), axis=1, keepdims=True) * skip_gate * (1.0 - skip_gate)
    )
    skip_grad = jnp.sum(type_hot * gate_term, axis=0)
    out_grad = typed_grad(act_low, grad_branch)
    grad_agg = gelu_back(typed_back(grad_branch, out_w))[0].astype(jnp.bfloat16)
    grad_agg_heads = grad_agg.reshape(tgt_rows, head_count, head_size)
    msg_grad = jnp.einsum(
        "rthd,the->rhde", u_rel_b, grad_agg_heads, preferred_element_type=jnp.float32
    )
    grad_urel = jnp.einsum(
        "the,rhde->rthd", grad_agg_heads, rel_msg, preferred_element_type=jnp.float32
    ).astype(jnp.bfloat16)
    grad_four = (
        jnp.einsum("tsr,rthd->thsd", select_low, grad_urel, preferred_element_type=jnp.float32)
        .astype(jnp.bfloat16)
        .reshape(tgt_rows, head_count, kind_count * head_size)
    )
    grad_cite = grad_urel[3]
    row_delta = (
        jnp.sum(grad_four.astype(jnp.float32) * u_four, axis=2)
        + jnp.sum(grad_cite.astype(jnp.float32) * u_cite, axis=2)
    ).T
    zero_four = jnp.zeros((tgt_rows, head_count, kind_count * head_size), jnp.float32)
    zero_cite = jnp.zeros((tgt_rows, head_count, head_size), jnp.float32)

    def back_turn(step_idx, loop_state):
        kv_blk, travel, acc_qf, acc_qc = loop_state
        k_grad, v_grad, qf_grad, qc_grad = backward_block(
            kv_blk,
            q_four,
            q_cite,
            grad_four,
            grad_cite,
            log_total,
            row_delta,
            block_codes((my_blk - step_idx) % n_blk),
        )
        travel = (
            from_behind((travel[0] + k_grad).astype(jnp.bfloat16), "blk", 1).astype(jnp.float32),
            from_behind((travel[1] + v_grad).astype(jnp.bfloat16), "blk", 1).astype(jnp.float32),
        )
        kv_blk = from_behind((kv_blk[0], kv_blk[1], kv_blk[2]), "blk", 1)
        return (kv_blk, travel, acc_qf + qf_grad, acc_qc + qc_grad)

    zero_kv = jnp.zeros((tgt_rows, feat_dim), jnp.float32)
    loop_state = lax.fori_loop(
        0, n_blk, back_turn, (whole_kv, (zero_kv, zero_kv), zero_four, zero_cite)
    )
    key_acc, value_acc = loop_state[1]
    acc_qf, acc_qc = (loop_state[2], loop_state[3])
    grad_key = key_acc.astype(jnp.bfloat16)
    grad_value = value_acc.astype(jnp.bfloat16)
    grad_relq = jnp.einsum(
        "tsr,thsd->rthd",
        select,
        acc_qf.reshape(tgt_rows, head_count, kind_count, head_size),
        precision=HIGH,
    )
    grad_relq = (
        (grad_relq + cite_hot[:, None, None, None] * acc_qc[None])
        .astype(jnp.bfloat16)
        .astype(jnp.float32)
    )
    prior_grad = jnp.sum(grad_relq * rel_raw, axis=(1, 3)) / math.sqrt(head_size)
    grad_raw = grad_relq * factor[:, None, :, None]
    att_grad = jnp.einsum("thj,rthk->rhjk", q_heads, grad_raw, precision=HIGH)
    grad_query = (
        jnp.einsum("rthk,rhjk->thj", grad_raw, att_f, precision=HIGH)
        .reshape(tgt_rows, feat_dim)
        .astype(jnp.bfloat16)
    )
    query_grad = typed_grad(features, grad_query)
    key_grad = typed_grad(shifted_b, grad_key)
    value_grad = typed_grad(shifted_b, grad_value)
    grad_shift = typed_back(grad_key, key_w) + typed_back(grad_value, value_w)
    table_grad = jnp.dot(gap_hot.T, grad_shift, precision=HIGH)
    rte_grad = jnp.dot(time_low.T, table_grad, precision=HIGH)
    input_grad = (
        (1.0 - skip_gate) * grad_mix + typed_back(grad_query, query_w) + grad_shift
    ).astype(jnp.bfloat16)
    summed = lax.psum(
        (
            query_grad,
            key_grad,
            value_grad,
            out_grad,
            att_grad,
            msg_grad,
            prior_grad,
            skip_grad,
            rte_grad,
            gain_grad,
            bias_grad,
        ),
        ("blk", "rep"),
    )
    return (
        layer_out,
        input_grad,
        summed[0],
        summed[1],
        summed[2],
        summed[3],
        summed[4],
        summed[5],
        summed[6],
        summed[7],
        summed[8],
        summed[9],
        summed[10],
    )


REL_TAB = relation_table()
HALF = 128
F32 = jnp.float32
LOW = jnp.bfloat16
VMEM_CAP = 65400 * 2**10
PROB_UNROLL = 2


def nn(a, b):
    return lax.dot_general(a, b, (((1,), (0,)), ((), ())), preferred_element_type=F32)


def nt(a, b):
    return lax.dot_general(a, b, (((1,), (1,)), ((), ())), preferred_element_type=F32)


def tn(a, b):
    return lax.dot_general(a, b, (((0,), (0,)), ((), ())), preferred_element_type=F32)


def pick(kinds, kind, value):
    return jnp.where(kinds == kind, value, jnp.zeros_like(value))


def relation_of(kind, slot):
    hit = np.nonzero(REL_TAB[kind, slot])[0]
    return int(hit[0]) if len(hit) else None


def to_slots(rel_rows, kinds, kind_count):
    slots = []
    for slot in range(kind_count):
        rows = jnp.zeros(kinds.shape, F32)
        for kind in range(kind_count):
            rel = relation_of(kind, slot)
            if rel is not None:
                rows = jnp.where(kinds == kind, rel_rows(rel), rows)
        slots.append(rows)
    return slots, pick(kinds, 0, rel_rows(3))


def to_relations(slot_rows, cite_rows, kinds, kind_count, rel_count):
    out = []
    for rel in range(rel_count):
        if rel == 3:
            out.append(pick(kinds, 0, cite_rows))
            continue
        (kind, slot) = [
            (k, s) for k in range(kind_count) for s in range(kind_count) if relation_of(k, s) == rel
        ][0]
        out.append(pick(kinds, kind, slot_rows(slot)))
    return out


def flip(index, mask):
    return sum(((index // bit + mask // bit) % 2) * bit for bit in (1, 2, 4))


def gap_hot(gap_row, levels):
    gaps = jnp.broadcast_to(gap_row, (levels, gap_row.shape[1]))
    return (lax.broadcasted_iota(jnp.int32, gaps.shape, 0) == gaps).astype(F32).astype(LOW)


def remote(src, dst, sends, recvs, send_at, recv_at, device):
    return pltpu.make_async_remote_copy(
        src_ref=src,
        dst_ref=dst,
        send_sem=sends.at[send_at],
        recv_sem=recvs.at[recv_at],
        device_id=device,
        device_id_type=pl.DeviceIdType.MESH,
    )


def greet(devices):
    barrier = pltpu.get_barrier_semaphore()
    for device in devices:
        pl.semaphore_signal(
            barrier, inc=1, device_id=device, device_id_type=pl.DeviceIdType.MESH
        )
    pl.semaphore_wait(barrier, len(devices))


def out_at(k, half):
    return (2 * k + half) * 256


def msg_at(half):
    return 2048 + half * 256


def query_at(k, half):
    return 2560 + (12 * half + k) * 256


def key_at(k, half):
    return 2560 + (12 * half + 4 + k) * 256


def value_at(k, half):
    return 2560 + (12 * half + 8 + k) * 256


def att_at(half):
    return 8704 + half * 256


SUM_PARTS = ((0, (512, 768)), (2560, (768, 768)), (5632, (768, 1024)))
SUM_TICKS = (
    ((0, 0, 1), (2, 0, 2), (3, 0, 3)),
    ((0, 0, 4), (1, 1, 1), (2, 0, 5), (2, 1, 2), (3, 0, 6), (3, 1, 3)),
)
GRAD_ROWS = 9216


def span(start, size):
    return pl.ds(start if isinstance(start, int) else pl.multiple_of(start, 16), size)


def summation(part, refs, places, pack):
    grads, full, core_in, first_in, second_in, line_in, sends, recvs = refs
    (z, y, x, core), by_core, by_x, by_y, by_z = places
    base, streams = SUM_PARTS[part]
    half = sum(streams)
    ahead = sum(sum(SUM_PARTS[before][1]) for before in range(part))
    count = iter(range(32 * part, 32 * part + 32))
    mine = base + core * half
    begin = (mine, mine + streams[0])
    landing = (ahead, ahead + streams[0])
    pending = []

    def send(src, dst, device):
        at = next(count)

        def copy():
            return remote(src(), dst(), sends, recvs, at, at, device)

        copy().start()
        pending.append(copy)

    def settle():
        for copy in pending:
            copy().wait()
        pending.clear()

    def piece(ref, start, size):
        return lambda: ref.at[span(start, size), :]

    def small(ref, at):
        return lambda: ref.at[at]

    def load(ref, start, size):
        return ref[span(start, size), :].astype(F32)

    def add_in(start, size, ref, at):
        value = load(grads, start, size) + load(ref, at, size)
        grads[span(start, size), :] = value.astype(LOW)

    turns = ((x, y), (y, x))
    ways = ((by_x, by_y), (by_y, by_x))
    firsts = [size // 2 for size in streams]
    seconds = [size // 4 for size in streams]
    lines = [size // 16 for size in streams]
    at_first = [begin[s] + turns[s][0] * firsts[s] for s in range(2)]
    at_second = [at_first[s] + turns[s][1] * seconds[s] for s in range(2)]
    at_line = [at_second[s] + z * lines[s] for s in range(2)]
    other_z = [(z + step) % 4 for step in (1, 2, 3)]
    aways = [
        [begin[s] + firsts[s] - turns[s][0] * firsts[s] for s in range(2)],
        [at_first[s] + seconds[s] - turns[s][1] * seconds[s] for s in range(2)],
    ]
    there_core = base + half - core * half
    line_there = [[at_second[s] + other_z[i] * lines[s] for i in range(3)] for s in range(2)]
    line_land = [3 * landing[s] // 16 for s in range(2)]

    def cores():
        send(piece(grads, there_core, half), piece(core_in, ahead, half), by_core)
        if pack:
            send(small(pack[0], 0), small(pack[1], 0), by_core)

    def plane_one():
        settle()
        add_in(mine, half, core_in, ahead)
        for s in range(2):
            send(
                piece(grads, aways[0][s], firsts[s]),
                piece(first_in, landing[s] // 2, firsts[s]),
                ways[s][0],
            )
        if pack:
            pack[0][1] = pack[0][0] + pack[1][0]
            send(small(pack[0], 1), small(pack[1], 1), by_x)

    def plane_two():
        settle()
        for s in range(2):
            add_in(at_first[s], firsts[s], first_in, landing[s] // 2)
        for s in range(2):
            send(
                piece(grads, aways[1][s], seconds[s]),
                piece(second_in, landing[s] // 4, seconds[s]),
                ways[s][1],
            )
        if pack:
            pack[0][2] = pack[0][1] + pack[1][1]
            send(small(pack[0], 2), small(pack[1], 2), by_y)

    def line():
        settle()
        for s in range(2):
            add_in(at_second[s], seconds[s], second_in, landing[s] // 4)
        for step in (2, 3, 1):
            for s in range(2):
                land = line_land[s] + (step - 1) * lines[s]
                send(
                    piece(grads, line_there[s][step - 1], lines[s]),
                    piece(line_in, land, lines[s]),
                    by_z[step - 1],
                )
        if pack:
            pack[0][3] = pack[0][2] + pack[1][2]
            for step in (2, 3, 1):
                send(small(pack[0], 3), small(pack[1], 2 + step), by_z[step - 1])

    def share(start, size, device):
        send(piece(full, start, size), piece(full, start, size), device)

    def line_back():
        settle()
        for s in range(2):
            value = load(grads, at_line[s], lines[s])
            for step in range(3):
                value = value + load(line_in, line_land[s] + step * lines[s], lines[s])
            full[span(at_line[s], lines[s]), :] = value.astype(LOW)
        for step in (2, 3, 1):
            for s in range(2):
                share(at_line[s], lines[s], by_z[step - 1])
        if pack:
            pack[2][...] = pack[0][3] + pack[1][3] + pack[1][4] + pack[1][5]

    def plane_two_back():
        settle()
        for s in range(2):
            share(at_second[s], seconds[s], ways[s][1])

    def plane_one_back():
        settle()
        for s in range(2):
            share(at_first[s], firsts[s], ways[s][0])

    def cores_back():
        settle()
        for s in range(2):
            share(begin[s], streams[s], by_core)

    return [
        cores,
        plane_one,
        plane_two,
        line,
        line_back,
        plane_two_back,
        plane_one_back,
        cores_back,
        settle,
    ]


def layer_kernel(
    x_ref,
    kind_ref,
    gap_ref,
    valid_ref,
    rte_ref,
    time_ref,
    codes_hbm,
    cot_ref,
    qw_hbm,
    kw_hbm,
    vw_hbm,
    ow_hbm,
    att_ref,
    msg_ref,
    prior_ref,
    skip_ref,
    gain_ref,
    bias_ref,
    out_ref,
    input_ref,
    full,
    small_ref,
    att_flat,
    codes,
    qw,
    kw,
    vw,
    ow,
    msg_flat,
    shifted,
    xt,
    base,
    shift_out,
    plane_back,
    line_back,
    load_sem,
    gather_send,
    gather_recv,
    back_send,
    back_recv,
    grads,
    core_in,
    first_in,
    second_in,
    line_in,
    pack,
    pack_in,
    sum_send,
    sum_recv,
    kt,
    vx,
    sbuf,
    probs,
    sm,
    qs,
    tails,
    qt2,
    qh,
    gt2,
    acc,
    two,
    agg,
    grad_even,
    grad_odd,
):
    rows, feat = x_ref.shape
    n_blk = shifted.shape[0]
    levels = time_ref.shape[1]
    kind_count = qw.shape[0]
    rel_count, heads, size = att_ref.shape[:3]
    group = heads // 2
    me = lax.axis_index("blk")
    rep = lax.axis_index("rep")
    loads = [
        pltpu.make_async_copy(src, dst, load_sem.at[at])
        for at, (src, dst) in enumerate(
            ((kw_hbm, kw), (vw_hbm, vw), (qw_hbm, qw), (codes_hbm, codes), (ow_hbm, ow))
        )
    ]
    for load in loads:
        load.start()
    by_core = (me, rep + 1 - 2 * (rep % 2))
    by_x = (me, rep + 2 - 4 * (rep // 2))
    greet([(flip(me, mask), rep) for mask in range(1, n_blk)] + [by_core, by_x])

    x_f = x_ref[...].astype(F32).T
    x_t = x_f.astype(LOW)
    xt[...] = x_t
    table = tn(rte_ref[...], time_ref[...])
    table_hi = table.astype(LOW)
    table_lo = (table - table_hi.astype(F32)).astype(LOW)
    hot = gap_hot(gap_ref[...], levels)
    shifted[me, 0:feat, :] = (x_f + nn(table_hi, hot) + nn(table_lo, hot)).astype(LOW)
    shifted[me, feat:, :] = jnp.concatenate(
        [kind_ref[...].astype(F32), gap_ref[...].astype(F32), jnp.zeros((14, rows), F32)], axis=0
    ).astype(LOW)

    def hand_on(block, mask, send_at):
        return remote(
            shifted.at[block],
            shifted.at[block],
            gather_send,
            gather_recv,
            send_at,
            block,
            (flip(me, mask), rep),
        )

    for mask in (1, 2, 6, 4):
        hand_on(me, mask, mask).start()

    def source_row(j, row):
        return shifted[j, feat : feat + 16, :].astype(F32)[row : row + 1].astype(jnp.int32)

    kinds = jnp.broadcast_to(kind_ref[...], (size, rows))
    kinds_f = jnp.broadcast_to(kind_ref[...], (feat, rows))
    valid_f = jnp.broadcast_to(valid_ref[...], (feat, rows)).astype(F32)
    lane = lax.broadcasted_iota(jnp.int32, (rows, HALF), 1)
    ones_pad = (lax.broadcasted_iota(jnp.int32, (16, rows), 0) < 2).astype(F32).astype(LOW)
    scale = 1.0 / math.sqrt(size)

    def cols(j):
        return pl.ds(pl.multiple_of(j * rows, rows), rows)

    def store_part(start, value):
        grads[pl.ds(start, value.shape[0]), :] = value.astype(LOW)

    for r in range(rel_count):
        for h in range(heads):
            agg[h * size : (h + 1) * size, r * size : (r + 1) * size] = att_ref[r, h].astype(F32)
    att_flat[...] = agg[...].astype(LOW)
    for r in range(rel_count):
        for h in range(heads):
            agg[r * size : (r + 1) * size, h * size : (h + 1) * size] = msg_ref[r, h].astype(F32)
    msg_flat[...] = agg[...].T.astype(LOW)

    def turned(m, k):
        return probs.at[0, 2 * m + k // 2, pl.ds((k % 2) * feat, feat), :]

    for m, (load, ref) in enumerate(((loads[0], kw), (loads[1], vw))):
        load.wait()
        for k in range(kind_count):
            turned(m, k)[...] = ref[k].astype(F32).T.astype(LOW)

    loads[2].wait()
    q_full = jnp.zeros((feat, rows), F32)
    for k in range(kind_count):
        q_full = jnp.where(kinds_f == k, tn(qw[k], x_t), q_full)
    for h in range(heads):
        qh[h] = q_full[h * size : (h + 1) * size].astype(LOW)

    def head_rows(ref, h):
        return ref[pl.ds(pl.multiple_of(h * size, size), size), :]

    def query_head(h, carry):
        raw = tn(head_rows(att_flat, h), qh[h])

        def rel_rows(r):
            part = raw[r * size : (r + 1) * size] * (prior_ref[r, h] * scale)
            return part.astype(LOW).astype(F32)

        slots, cite = to_slots(rel_rows, kinds, kind_count)
        slot_t = jnp.concatenate(slots, axis=0)
        cite_t = jnp.concatenate([cite, jnp.zeros((HALF - size, rows), F32)], axis=0)
        qt2[h, :, 0:rows] = slot_t.astype(LOW)
        qt2[h, :, rows:] = cite_t.astype(LOW)
        qs[h, 0:rows, :] = slot_t.T.astype(LOW)
        qs[h, rows:, :] = cite_t.T.astype(LOW)
        return carry

    lax.fori_loop(0, heads, query_head, 0, unroll=2)
    loads[3].wait()
    acc[:, :, 0:rows] = jnp.full((heads, HALF, rows), NEG_FILL, F32)

    def keep_scores(h, j, both, second, edge):
        val = jnp.where(second, both[rows:], both[:rows])
        val = jnp.where(edge, val, NEG_FILL)
        if h < group:
            sbuf[j, pl.ds(h * rows, rows), :] = val
        else:
            high = val.astype(LOW)
            probs[j, h, 0:rows, :] = high
            probs[j, h, rows:, :] = (val - high.astype(F32)).astype(LOW)
        top = jnp.maximum(val[:, :HALF], val[:, HALF:])
        for part in range(rows // HALF):
            at = slice(part * HALF, (part + 1) * HALF)
            acc[h, :, at] = jnp.maximum(acc[h, :, at], top[at])

    def arrive(i, carry):
        j = flip(me, i)

        @pl.when(i > 0)
        def _():
            hand_on(j, 1, 0).wait_recv()

        @pl.when((i > 0) & (i % 2 == 0))
        def _():
            hand_on(j, 1, i + 1).start()

        src = jnp.broadcast_to(source_row(j, 0), (size, rows))
        block = shifted[j, 0:feat, :]
        for k in range(kind_count):
            key = nn(turned(0, k)[...], block)
            value = nn(turned(1, k)[...], block)
            for h in range(heads):
                part = slice(h * size, (h + 1) * size)
                kt[j, h, pl.ds(k * size, size), :] = pick(src, k, key[part]).astype(LOW)
                vx[j, h, pl.ds(k * size, size), :] = pick(src, k, value[part]).astype(LOW)
        code = codes[:, cols(j)]
        second = code == 2
        edge = code > 0
        two[j] = second.astype(F32).astype(LOW)
        before = None
        for h in range(heads + 1):
            both = nn(qs[h], kt[j, h]) if h < heads else None
            if h > 0:
                keep_scores(h - 1, j, before, second, edge)
            before = both
        return carry

    lax.fori_loop(0, n_blk, arrive, 0)
    for send_at in range(1, n_blk):
        hand_on(me, 1, send_at).wait_send()

    def prob_block(h, j, top, kept):
        if kept:
            val = sbuf[j, pl.ds(pl.multiple_of(h * rows, rows), rows), :]
        else:
            val = probs[j, h, 0:rows, :].astype(F32) + probs[j, h, rows:, :].astype(F32)
        val = jnp.exp(val - top)
        low = val.astype(LOW)
        second = low * two[j]
        probs[j, h, 0:rows, :] = low - second
        probs[j, h, rows:, :] = second
        return val[:, :HALF] + val[:, HALF:]

    sm[...] = jnp.zeros((rows, HALF), F32)

    def prob_head(h, kept):
        top = jnp.concatenate([acc[h, :, 0:HALF], acc[h, :, HALF:rows]], axis=0)
        top = jnp.max(top, axis=1, keepdims=True)
        top = jnp.broadcast_to(jnp.maximum(top, 0.1 * NEG_FILL), (rows, rows))
        value_sum = None
        total = None
        for j in range(n_blk + 1):
            if j < n_blk:
                part = prob_block(h, j, top, kept)
                total = part if total is None else total + part
            if j > 0:
                part = nt(vx[j - 1, h], probs[j - 1, h])
                value_sum = part if value_sum is None else value_sum + part
        acc[h] = value_sum
        total = jnp.sum(total, axis=1, keepdims=True)
        sm[...] = jnp.where(lane == h, jnp.broadcast_to(total, (rows, HALF)), sm[...])

    for kept in (True, False):

        def prob_pair(pair, carry, kept=kept):
            for u in range(PROB_UNROLL):
                prob_head((0 if kept else group) + PROB_UNROLL * pair + u, kept)
            return carry

        lax.fori_loop(0, group // PROB_UNROLL, prob_pair, 0)

    inverse = 1.0 / jnp.maximum(sm[...].T, 1.0)
    sm[0:heads, :] = inverse[0:heads, 0:HALF]
    sm[heads : 2 * heads, :] = inverse[0:heads, HALF:]

    def inv_row(h, count):
        row = jnp.concatenate([sm[pl.ds(h, 1), :], sm[pl.ds(heads + h, 1), :]], axis=1)
        return jnp.broadcast_to(row, (count, rows))

    def rel_part(h):
        return sbuf[h // group, pl.ds((h % group) * feat, feat), :].astype(LOW)

    for h in range(heads):
        inv = inv_row(h, HALF)
        u_slot = acc[h, :, 0:rows] * inv
        u_cite = acc[h, 0:size, rows:] * inv[0:size]
        acc[h, :, 0:rows] = u_slot
        acc[h, 0:size, rows:] = u_cite
        rel = to_relations(
            lambda s: u_slot[s * size : (s + 1) * size], u_cite, kinds, kind_count, rel_count
        )
        rel = jnp.concatenate(rel, axis=0)
        sbuf[h // group, pl.ds((h % group) * feat, feat), :] = rel
        agg[pl.ds(h * size, size), :] = nn(head_rows(msg_flat, h), rel.astype(LOW))
    loads[4].wait()
    agg_t = agg[...]
    slope = 0.7978845608028654
    inner = jnp.tanh(slope * (agg_t + 0.044715 * agg_t * agg_t * agg_t))
    act_t = (0.5 * agg_t * (1.0 + inner)).astype(LOW)
    gelu_back = 0.5 * (1.0 + inner) + 0.5 * agg_t * (1.0 - inner * inner) * slope * (
        1.0 + 3.0 * 0.044715 * agg_t * agg_t
    )
    skip = jnp.zeros((1, rows), F32)
    branch = jnp.zeros((feat, rows), F32)
    for k in range(kind_count):
        skip = jnp.where(kinds[0:1] == k, skip_ref[k], skip)
        branch = jnp.where(kinds_f == k, tn(ow[k], act_t), branch)
    gate_row = 1.0 / (1.0 + jnp.exp(-skip))
    gate = jnp.broadcast_to(gate_row, (feat, rows))
    mixed = gate * branch + (1.0 - gate) * x_f
    centered = mixed - jnp.mean(mixed, axis=0, keepdims=True)
    inv_std = lax.rsqrt(jnp.mean(centered * centered, axis=0, keepdims=True) + LN_EPS)
    normed = centered * inv_std
    affine = jnp.concatenate([gain_ref[...], bias_ref[...], jnp.zeros((HALF - 2, feat), F32)], axis=0).T
    gain = jnp.broadcast_to(affine[:, 0:1], (feat, rows))
    bias = jnp.broadcast_to(affine[:, 1:2], (feat, rows))
    out_ref[...] = (valid_f * (normed * gain + bias)).T.astype(LOW)
    grad_y = cot_ref[...].astype(F32).T * valid_f
    gain_col = jnp.sum(grad_y * normed, axis=1, keepdims=True)
    bias_col = jnp.sum(grad_y, axis=1, keepdims=True)
    grad_norm = grad_y * gain
    grad_mix = inv_std * (
        grad_norm
        - jnp.mean(grad_norm, axis=0, keepdims=True)
        - normed * jnp.mean(grad_norm * normed, axis=0, keepdims=True)
    )
    skip_row = (
        jnp.sum(grad_mix * (branch - x_f), axis=0, keepdims=True) * gate_row * (1.0 - gate_row)
    )
    base[...] = (1.0 - gate) * grad_mix
    grad_branch = gate * grad_mix
    grad_act = jnp.zeros((feat, rows), F32)
    for k in range(kind_count):
        masked = pick(kinds_f, k, grad_branch).astype(LOW)
        out_grad = nt(act_t, masked)
        store_part(out_at(k, 0), out_grad[:, :HALF])
        store_part(out_at(k, 1), out_grad[:, HALF:])
        grad_act = grad_act + nn(ow[k], masked)
    agg[...] = gelu_back * grad_act

    for h in range(heads):
        grad_agg = agg[pl.ds(h * size, size), :].astype(LOW)
        msg_grad = nt(grad_agg, rel_part(h))
        store_part(msg_at(0) + h * size, msg_grad[:, :HALF])
        store_part(msg_at(1) + h * size, msg_grad[:, HALF:])
        inv = inv_row(h, size)
        grad_u = tn(head_rows(msg_flat, h), grad_agg)

        def rel_rows(r):
            return grad_u[r * size : (r + 1) * size] * inv

        slots, cite = to_slots(rel_rows, kinds, kind_count)
        slot_t = jnp.concatenate(slots, axis=0).astype(LOW)
        cite_t = jnp.concatenate([cite, jnp.zeros((HALF - size, rows), F32)], axis=0).astype(LOW)
        gt2[h, :, 0:rows] = slot_t
        gt2[h, :, rows:] = cite_t
        slot_f = slot_t.astype(F32)
        cite_f = cite_t.astype(F32)
        delta = -(
            jnp.sum(slot_f * acc[h, :, 0:rows], axis=0, keepdims=True)
            + jnp.sum(cite_f[0:size] * acc[h, 0:size, rows:], axis=0, keepdims=True)
        )
        delta_hi = delta.astype(LOW).astype(F32)
        tail = jnp.concatenate(
            [delta_hi, delta - delta_hi, jnp.zeros((HALF - 2, rows), F32)], axis=0
        )
        tail_t = tail.T.astype(LOW)
        qs[h, 0:rows, :] = slot_f.T.astype(LOW)
        qs[h, rows:, :] = cite_f.T.astype(LOW)
        tails[h] = tail_t[:, 0:16]
        acc[h] = jnp.zeros(acc.shape[1:], F32)

    refs = (grads, full, core_in, first_in, second_in, line_in, sum_send, sum_recv)
    by_y = (flip(me, 1), rep)
    by_z = [(((me // 2 + step) % 4) * 2 + me % 2, rep) for step in (1, 2, 3)]
    places = ((me // 2, me % 2, rep // 2, rep % 2), by_core, by_x, by_y, by_z)
    sums = [summation(part, refs, places, None) for part in range(2)]
    sums.append(summation(2, refs, places, (pack, pack_in, small_ref)))
    sums[0][0]()

    slot_id = lax.broadcasted_iota(jnp.int32, (HALF, rows), 0) // size
    pack[0] = jnp.zeros(pack.shape[1:], F32)

    def along_y(m):
        return remote(
            shift_out.at[flip(me, m + 1)],
            plane_back.at[m // 2],
            back_send,
            back_recv,
            m // 2,
            m // 2,
            by_y,
        )

    def along_z(m):
        at = n_blk // 2 + m // 2
        return remote(
            shift_out.at[flip(me, m)],
            line_back.at[m // 2],
            back_send,
            back_recv,
            at,
            at,
            (flip(me, m), rep),
        )

    def pass_on(m):
        along_y(m).wait_recv()
        j = flip(me, m)
        total = shift_out[j].astype(F32) + plane_back[m // 2].astype(F32)
        shift_out[j] = total.astype(LOW)
        along_z(m).start()

    grad_bufs = (grad_even, grad_odd)
    for g in range(2):
        half = slice(g * HALF, (g + 1) * HALF)

        def block_pair(pair, carry, g=g, half=half):
            m = n_blk - 2 - 2 * pair
            blocks = (flip(me, m + 1), flip(me, m))
            owns = [slot_id == jnp.broadcast_to(source_row(j, 0), (HALF, rows)) for j in blocks]

            def keep(at, u, kind, part):
                for k in range(kind_count):
                    start = (2 * k + kind) * HALF + u * size
                    sbuf[blocks[at], pl.ds(start, size), :] = part[k * size : (k + 1) * size]

            def score_part(at, u):
                h = g * group + u
                both = jnp.concatenate([tails[h], tails[h]], axis=0)
                left = jnp.concatenate([qs[h], both], axis=1)
                right = jnp.concatenate([vx[blocks[at], h], ones_pad], axis=0)
                grad_bufs[u % 2][...] = probs[blocks[at], h] * nn(left, right).astype(LOW)
                keep(at, u, 1, jnp.where(owns[at], nn(gt2[h], probs[blocks[at], h]), 0.0))

            def key_part(at, u):
                h = g * group + u
                grad = grad_bufs[u % 2][...]
                keep(at, u, 0, jnp.where(owns[at], nn(qt2[h], grad), 0.0))
                acc[h] = acc[h] + nt(kt[blocks[at], h], grad)

            units = [(at, u) for at in range(2) for u in range(group)]
            for i in range(len(units) + 1):
                if i < len(units):
                    score_part(*units[i])
                if i > 0:
                    key_part(*units[i - 1])
            for at in range(2):
                j = blocks[at]
                total = None
                for k in range(kind_count):
                    weights = jnp.concatenate([kw[k, :, half], vw[k, :, half]], axis=1)
                    part = nn(weights, sbuf[j, pl.ds(k * feat, feat), :].astype(LOW))
                    total = part if total is None else total + part
                if g == 1:
                    total = total + shift_out[j].astype(F32)
                low = total.astype(LOW)
                shift_out[j] = low
                if g == 1:
                    gaps = gap_hot(source_row(j, 1), levels)
                    pack[0, 0:levels, :] = pack[0, 0:levels, :] + nt(gaps, low)
                    if at == 0:
                        along_y(m).start()
            if g == 1:

                @pl.when(pair > 0)
                def _():
                    pass_on(m + 2)

            for when, part, step in SUM_TICKS[g]:

                @pl.when(pair == when)
                def _(part=part, step=step):
                    sums[part][step]()

            return carry

        lax.fori_loop(0, n_blk // 2, block_pair, 0)

        for k in range(kind_count):
            total = None
            for j in range(n_blk):
                part = nt(shifted[j, 0:feat, :], sbuf[j, pl.ds(k * feat, feat), :].astype(LOW))
                total = part if total is None else total + part
            store_part(key_at(k, g), total[:, :HALF])
            store_part(value_at(k, g), total[:, HALF:])
        grad_q = []
        for h in range(g * group, (g + 1) * group):
            slot = acc[h, :, 0:rows]
            rel = to_relations(
                lambda s: slot[s * size : (s + 1) * size],
                acc[h, 0:size, rows:],
                kinds,
                kind_count,
                rel_count,
            )
            rel = [part.astype(LOW) for part in rel]
            att_grad = nt(qh[h], jnp.concatenate(rel, axis=0))
            store_part(att_at(0) + h * size, att_grad[:, :HALF])
            store_part(att_at(1) + h * size, att_grad[:, HALF:])
            raw = [
                (part.astype(F32) * (prior_ref[r, h] * scale)).astype(LOW)
                for r, part in enumerate(rel)
            ]
            grad_q.append(nn(head_rows(att_flat, h), jnp.concatenate(raw, axis=0)))
        grad_q = jnp.concatenate(grad_q, axis=0).astype(LOW).astype(F32)
        total = base[...]
        for k in range(kind_count):
            masked = pick(kinds_f[0:HALF], k, grad_q).astype(LOW)
            store_part(query_at(k, g), nt(xt[...], masked))
            total = total + nn(qw[k, :, half], masked)
        base[...] = total
        if g == 0:
            sums[1][0]()

    pair = jnp.where(
        lane == 0,
        jnp.broadcast_to(gain_col, (feat, HALF)),
        jnp.where(lane == 1, jnp.broadcast_to(bias_col, (feat, HALF)), 0.0),
    ).T
    spot = lax.broadcasted_iota(jnp.int32, (1, rows), 1)
    skips = jnp.zeros((1, rows), F32)
    for k in range(kind_count):
        skips = jnp.where(
            spot == k, jnp.sum(pick(kinds[0:1], k, skip_row), axis=1, keepdims=True), skips
        )
    pack[0, levels : levels + 8, :] = jnp.concatenate(
        [pair[0:2], skips, jnp.zeros((5, rows), F32)], axis=0
    )
    sums[2][0]()
    along_y(0).wait_recv()
    total = base[...] + shift_out[me].astype(F32) + plane_back[0].astype(F32)
    sums[0][7]()
    sums[1][4]()
    sums[2][1]()
    for m in (2, 4, 6):
        along_z(m).wait_recv()
        total = total + line_back[m // 2].astype(F32)
    input_ref[...] = total.T.astype(LOW)
    sums[0][8]()
    sums[2][2]()
    sums[1][5]()
    sums[2][3]()
    sums[1][6]()
    sums[2][4]()
    sums[1][7]()
    sums[2][5]()
    sums[1][8]()
    for step in (6, 7, 8):
        sums[2][step]()
    for m in (0, 2, 4, 6):
        along_y(m).wait_send()
        if m > 0:
            along_z(m).wait_send()


def finish_kernel(
    full,
    small_ref,
    att_flat,
    time_ref,
    prior_ref,
    out_in,
    input_in,
    out_ref,
    input_ref,
    qg_ref,
    kg_ref,
    vg_ref,
    og_ref,
    attg_ref,
    msgg_ref,
    priorg_ref,
    skip_ref,
    rte_ref,
    gain_ref,
    bias_ref,
):
    out_ref[...] = out_in[...]
    input_ref[...] = input_in[...]
    kind_count, feat = qg_ref.shape[:2]
    rel_count, heads, width = attg_ref.shape[:3]
    scale = 1.0 / math.sqrt(width)

    def part(start):
        return full[pl.ds(start, feat), :].astype(F32)

    for ref, at in ((qg_ref, query_at), (kg_ref, key_at), (vg_ref, value_at), (og_ref, out_at)):
        for k in range(kind_count):
            for half in range(2):
                ref[k, :, half * HALF : (half + 1) * HALF] = part(at(k, half))
    att = jnp.concatenate([part(att_at(0)), part(att_at(1))], axis=1)
    msg = jnp.concatenate([part(msg_at(0)), part(msg_at(1))], axis=1).T
    for r in range(rel_count):
        for h in range(heads):
            block = (slice(h * width, (h + 1) * width), slice(r * width, (r + 1) * width))
            attg_ref[r, h] = att[block] * (prior_ref[r, h] * scale)
            msgg_ref[r, h] = msg[block[::-1]]
    prod = (att * att_flat[...].astype(F32)).reshape(heads, width, feat)
    prod = jnp.sum(prod, axis=1)
    spread = (
        lax.broadcasted_iota(jnp.int32, (feat, rel_count), 0) // width
        == lax.broadcasted_iota(jnp.int32, (feat, rel_count), 1)
    ).astype(F32).astype(LOW)
    prior = jnp.zeros((rel_count, heads), F32)
    for _ in range(3):
        low = prod.astype(LOW)
        prior = prior + lax.dot_general(
            spread, low, (((0,), (1,)), ((), ())), preferred_element_type=F32
        )
        prod = prod - low.astype(F32)
    priorg_ref[...] = prior * scale
    levels = time_ref.shape[1]
    small = small_ref[...]
    rte = jnp.zeros(rte_ref.shape, F32)
    rest = small[0:levels]
    for _ in range(3):
        low = rest.astype(LOW)
        rte = rte + nn(time_ref[...], low)
        rest = rest - low.astype(F32)
    rte_ref[...] = rte
    gain_ref[...] = small[levels : levels + 1]
    bias_ref[...] = small[levels + 1 : levels + 2]
    skip_ref[...] = small[levels + 2 : levels + 3, 0:kind_count]


def layer_call(n_blk, *args):
    rows, feat = args[0].shape
    kind_count = args[8].shape[0]
    rel_count, heads, size = args[12].shape[:3]
    vmem = pl.BlockSpec(memory_space=pltpu.VMEM)
    smem = pl.BlockSpec(memory_space=pltpu.SMEM)
    hbm = pl.BlockSpec(memory_space=pl.ANY)
    square = (feat, feat)
    weight = pltpu.VMEM((kind_count,) + square, LOW)

    def shape(dims, kind):
        return jax.ShapeDtypeStruct(dims, kind)

    return pl.pallas_call(
        layer_kernel,
        out_shape=[
            shape((rows, feat), LOW),
            shape((rows, feat), LOW),
            shape((GRAD_ROWS, HALF), LOW),
            shape((LEVELS + 8, feat), F32),
            shape(square, LOW),
        ],
        in_specs=[vmem] * 6 + [hbm, vmem] + [hbm] * 4 + [vmem] * 2 + [smem] * 2 + [vmem] * 2,
        out_specs=[vmem] * 5,
        scratch_shapes=[
            pltpu.VMEM((rows, n_blk * rows), jnp.int32),
            weight,
            weight,
            weight,
            weight,
            pltpu.VMEM(square, LOW),
            pltpu.VMEM((n_blk, feat + 16, rows), LOW),
            pltpu.VMEM((feat, rows), LOW),
            pltpu.VMEM((feat, rows), F32),
            pltpu.VMEM((n_blk, feat, rows), LOW),
            pltpu.VMEM((n_blk // 2, feat, rows), LOW),
            pltpu.VMEM((n_blk // 2, feat, rows), LOW),
            pltpu.SemaphoreType.DMA((5,)),
            pltpu.SemaphoreType.DMA((n_blk,)),
            pltpu.SemaphoreType.DMA((n_blk,)),
            pltpu.SemaphoreType.DMA((n_blk,)),
            pltpu.SemaphoreType.DMA((n_blk,)),
            pltpu.VMEM((GRAD_ROWS, HALF), LOW),
            pltpu.VMEM((GRAD_ROWS // 2, HALF), LOW),
            pltpu.VMEM((GRAD_ROWS // 4, HALF), LOW),
            pltpu.VMEM((GRAD_ROWS // 8, HALF), LOW),
            pltpu.VMEM((3 * GRAD_ROWS // 32, HALF), LOW),
            pltpu.VMEM((4, LEVELS + 8, feat), F32),
            pltpu.VMEM((6, LEVELS + 8, feat), F32),
            pltpu.SemaphoreType.DMA((96,)),
            pltpu.SemaphoreType.DMA((96,)),
            pltpu.VMEM((n_blk, heads, HALF, rows), LOW),
            pltpu.VMEM((n_blk, heads, HALF, rows), LOW),
            pltpu.VMEM((n_blk, heads // 2 * rows, rows), F32),
            pltpu.VMEM((n_blk, heads, 2 * rows, rows), LOW),
            pltpu.VMEM((rows, HALF), F32),
            pltpu.VMEM((heads, 2 * rows, HALF), LOW),
            pltpu.VMEM((heads, rows, 16), LOW),
            pltpu.VMEM((heads, HALF, 2 * rows), LOW),
            pltpu.VMEM((heads, size, rows), LOW),
            pltpu.VMEM((heads, HALF, 2 * rows), LOW),
            pltpu.VMEM((heads, HALF, 2 * rows), F32),
            pltpu.VMEM((n_blk, rows, rows), LOW),
            pltpu.VMEM(square, F32),
            pltpu.VMEM((2 * rows, rows), LOW),
            pltpu.VMEM((2 * rows, rows), LOW),
        ],
        compiler_params=pltpu.CompilerParams(
            vmem_limit_bytes=VMEM_CAP, collective_id=0, has_side_effects=True
        ),
        name="layer",
    )(*args)


def time_columns(level_count, feat_width):
    positions = np.arange(level_count, dtype=np.float32)[:, None]
    steps = np.arange(feat_width // 2, dtype=np.float32)[None, :]
    phases = positions / np.power(np.float32(10000.0), np.float32(2.0) * steps / feat_width)
    table = np.stack([np.sin(phases), np.cos(phases)], axis=2).reshape(level_count, feat_width)
    return jnp.asarray(np.ascontiguousarray(table.T), LOW)


def fast_body(
    features,
    node_type,
    time_gap,
    node_valid,
    edge_codes,
    query_w,
    key_w,
    value_w,
    out_w,
    rel_att,
    rel_msg,
    rel_prior,
    skip_logit,
    rte_w,
    ln_gain,
    ln_bias,
    cotangent,
):
    rows, feat = features.shape
    n_blk = lax.axis_size("blk")
    kind_count = query_w.shape[0]
    time_low = time_columns(LEVELS, feat)
    vmem = pl.BlockSpec(memory_space=pltpu.VMEM)
    smem = pl.BlockSpec(memory_space=pltpu.SMEM)
    square = (feat, feat)

    def shape(dims, kind):
        return jax.ShapeDtypeStruct(dims, kind)

    layer_out, input_grad, full, small, att_flat = layer_call(
        n_blk,
        features,
        node_type[None],
        time_gap[None],
        node_valid[None],
        rte_w,
        time_low,
        edge_codes,
        cotangent,
        query_w,
        key_w,
        value_w,
        out_w,
        rel_att,
        rel_msg,
        rel_prior,
        skip_logit,
        ln_gain[None],
        ln_bias[None],
    )
    outs = pl.pallas_call(
        finish_kernel,
        out_shape=[shape(layer_out.shape, LOW), shape(input_grad.shape, LOW)]
        + [shape((kind_count,) + square, F32)] * 4
        + [shape(rel_att.shape, F32)] * 2
        + [
            shape(rel_prior.shape, F32),
            shape((1, kind_count), F32),
            shape(square, F32),
            shape((1, feat), F32),
            shape((1, feat), F32),
        ],
        in_specs=[vmem] * 4 + [smem] + [vmem] * 2,
        out_specs=[vmem] * 13,
        compiler_params=pltpu.CompilerParams(vmem_limit_bytes=VMEM_CAP),
        name="finish",
    )(full, small, att_flat, time_low, rel_prior, layer_out, input_grad)
    return (*outs[:9], outs[9][0], outs[10], outs[11][0], outs[12][0])


def solution(mesh):
    in_specs = (
        P(("blk", "rep"), None),
        P(("blk", "rep")),
        P(("blk", "rep")),
        P(("blk", "rep")),
        P(("blk", "rep"), None),
        P(),
        P(),
        P(),
        P(),
        P(),
        P(),
        P(),
        P(),
        P(),
        P(),
        P(),
        P(("blk", "rep"), None),
    )
    out_specs = (
        P(("blk", "rep"), None),
        P(("blk", "rep"), None),
        P(),
        P(),
        P(),
        P(),
        P(),
        P(),
        P(),
        P(),
        P(),
        P(),
        P(),
    )
    plan = fast_body if tuple(mesh.shape.values()) == (8, 4) else body
    return jax.shard_map(plan, mesh=mesh, in_specs=in_specs, out_specs=out_specs, check_vma=False)
```

```python
import math

import jax
import jax.numpy as jnp
import numpy as np
from jax import lax
from jax.experimental import pallas as pl
from jax.experimental.pallas import tpu as pltpu
from jax.sharding import PartitionSpec as P

LEVELS = 16


NEG_FILL = -1e30
LN_EPS = 1e-05
HIGH = lax.Precision.HIGHEST


def from_behind(block, axis, distance):
    devices = range(lax.axis_size(axis))
    route = [((i - distance) % len(devices), i) for i in devices]
    return lax.ppermute(block, axis, route)


def relation_table():
    rel_tab = np.zeros((4, 4, 8), np.float32)
    rel_tab[0, 1, 0] = 1.0
    rel_tab[1, 0, 1] = 1.0
    rel_tab[0, 0, 2] = 1.0
    rel_tab[2, 0, 4] = 1.0
    rel_tab[0, 2, 5] = 1.0
    rel_tab[3, 1, 6] = 1.0
    rel_tab[1, 3, 7] = 1.0
    return rel_tab


def time_table(level_count, feat_width):
    positions = jnp.arange(level_count, dtype=jnp.float32)[:, None]
    freq_idx = jnp.arange(feat_width // 2, dtype=jnp.float32)[None, :]
    phases = positions / jnp.power(10000.0, 2.0 * freq_idx / feat_width)
    return jnp.stack([jnp.sin(phases), jnp.cos(phases)], axis=2).reshape(level_count, feat_width)


def slot_spread(heads_arr, kind_hot):
    spread_out = heads_arr[:, :, None, :] * kind_hot[:, None, :, None]
    return spread_out.reshape(heads_arr.shape[0], heads_arr.shape[1], -1)


def slot_collapse(slot_arr, kind_hot):
    src_rows, head_count = (slot_arr.shape[0], slot_arr.shape[1])
    kind_count = kind_hot.shape[1]
    shaped = slot_arr.reshape(src_rows, head_count, kind_count, -1)
    return jnp.sum(shaped * kind_hot.astype(jnp.float32)[:, None, :, None], axis=2)


def block_scores(kv_blk, q_four, q_cite, code_blk, kind_count):
    key_blk, value_blk, kind_blk = kv_blk
    src_rows = key_blk.shape[0]
    head_count = q_four.shape[1]
    key_heads = key_blk.reshape(src_rows, head_count, -1)
    value_heads = value_blk.reshape(src_rows, head_count, -1)
    kind_hot = (kind_blk[:, None] == jnp.arange(kind_count).astype(jnp.bfloat16)[None, :]).astype(
        jnp.bfloat16
    )
    key_four = slot_spread(key_heads, kind_hot)
    value_four = slot_spread(value_heads, kind_hot)
    is_one = (code_blk == 1)[None]
    is_two = (code_blk == 2)[None]
    slot_dot = jnp.einsum("thc,shc->hts", q_four, key_four, preferred_element_type=jnp.float32)
    cite_dot = jnp.einsum("thd,shd->hts", q_cite, key_heads, preferred_element_type=jnp.float32)
    scores = jnp.where(is_one, slot_dot, jnp.where(is_two, cite_dot, NEG_FILL))
    return (scores, is_one, is_two, key_heads, value_heads, key_four, value_four, kind_hot)


def attend_block(run_state, kv_blk, q_four, q_cite, code_blk, kind_count):
    run_max, run_sum, acc_four, acc_cite = run_state
    scores, is_one, is_two, key_heads, value_heads, key_four, value_four, kind_hot = block_scores(
        kv_blk, q_four, q_cite, code_blk, kind_count
    )
    new_max = jnp.maximum(run_max, jnp.max(scores, axis=2))
    expd = jnp.where((code_blk > 0)[None], jnp.exp(scores - new_max[:, :, None]), 0.0)
    rescale = jnp.exp(run_max - new_max)
    run_sum = run_sum * rescale + jnp.sum(expd, axis=2)
    prob_low = expd.astype(jnp.bfloat16)
    zero_low = jnp.zeros_like(prob_low)
    p_one = jnp.where(is_one, prob_low, zero_low)
    p_two = jnp.where(is_two, prob_low, zero_low)
    rescale_t = rescale.T[:, :, None]
    acc_four = acc_four * rescale_t + jnp.einsum(
        "hts,shc->thc", p_one, value_four, preferred_element_type=jnp.float32
    )
    acc_cite = acc_cite * rescale_t + jnp.einsum(
        "hts,shd->thd", p_two, value_heads, preferred_element_type=jnp.float32
    )
    return (new_max, run_sum, acc_four, acc_cite)


def back_block(
    kv_blk, q_four, q_cite, grad_four, grad_cite, log_total, row_delta, code_blk, kind_count
):
    scores, is_one, is_two, key_heads, value_heads, key_four, value_four, kind_hot = block_scores(
        kv_blk, q_four, q_cite, code_blk, kind_count
    )
    prob_full = jnp.where((code_blk > 0)[None], jnp.exp(scores - log_total[:, :, None]), 0.0)
    prob_low = prob_full.astype(jnp.bfloat16)
    zero_low = jnp.zeros_like(prob_low)
    p_one = jnp.where(is_one, prob_low, zero_low)
    p_two = jnp.where(is_two, prob_low, zero_low)
    grad_slot = jnp.einsum(
        "thc,shc->hts", grad_four, value_four, preferred_element_type=jnp.float32
    )
    grad_other = jnp.einsum(
        "thd,shd->hts", grad_cite, value_heads, preferred_element_type=jnp.float32
    )
    grad_probs = jnp.where(is_one, grad_slot, jnp.where(is_two, grad_other, 0.0))
    grad_scores = (prob_full * (grad_probs - row_delta[:, :, None])).astype(jnp.bfloat16)
    d_one = jnp.where(is_one, grad_scores, zero_low)
    d_two = jnp.where(is_two, grad_scores, zero_low)
    qf_grad = jnp.einsum("hts,shc->thc", d_one, key_four, preferred_element_type=jnp.float32)
    qc_grad = jnp.einsum("hts,shd->thd", d_two, key_heads, preferred_element_type=jnp.float32)
    k_grad = slot_collapse(
        jnp.einsum("hts,thc->shc", d_one, q_four, preferred_element_type=jnp.float32), kind_hot
    )
    k_grad = k_grad + jnp.einsum("hts,thd->shd", d_two, q_cite, preferred_element_type=jnp.float32)
    v_grad = slot_collapse(
        jnp.einsum("hts,thc->shc", p_one, grad_four, preferred_element_type=jnp.float32), kind_hot
    )
    v_grad = v_grad + jnp.einsum(
        "hts,thd->shd", p_two, grad_cite, preferred_element_type=jnp.float32
    )
    src_rows = k_grad.shape[0]
    return (k_grad.reshape(src_rows, -1), v_grad.reshape(src_rows, -1), qf_grad, qc_grad)


def body(
    features,
    node_type,
    time_gap,
    node_valid,
    edge_codes,
    query_w,
    key_w,
    value_w,
    out_w,
    rel_att,
    rel_msg,
    rel_prior,
    skip_logit,
    rte_w,
    ln_gain,
    ln_bias,
    cotangent,
):
    tgt_rows, feat_dim = features.shape
    kind_count = query_w.shape[0]
    rel_count = rel_att.shape[0]
    head_count = rel_att.shape[1]
    head_size = rel_att.shape[2]
    n_blk = lax.axis_size("blk")
    my_blk = lax.axis_index("blk")
    type_hot = (node_type[:, None] == jnp.arange(kind_count)[None, :]).astype(jnp.float32)
    type_low = type_hot.astype(jnp.bfloat16)
    gap_hot = (time_gap[:, None] == jnp.arange(LEVELS)[None, :]).astype(jnp.float32)
    time_low = time_table(LEVELS, feat_dim).astype(jnp.bfloat16).astype(jnp.float32)
    rte_table = jnp.dot(time_low, rte_w.astype(jnp.float32), precision=HIGH)
    x_f = features.astype(jnp.float32)
    shifted = x_f + jnp.dot(gap_hot, rte_table, precision=HIGH)
    shifted_b = shifted.astype(jnp.bfloat16)

    def typed(inp, weights):
        parts = jnp.einsum("th,khd->tkd", inp, weights, preferred_element_type=jnp.float32)
        return jnp.sum(parts * type_hot[:, :, None], axis=1)

    def typed_grad(inp, grad_low):
        masked = inp[:, None, :] * type_low[:, :, None]
        return jnp.einsum("tkh,td->khd", masked, grad_low, preferred_element_type=jnp.float32)

    def typed_back(grad_low, weights):
        parts = jnp.einsum("td,khd->tkh", grad_low, weights, preferred_element_type=jnp.float32)
        return jnp.sum(parts * type_hot[:, :, None], axis=1)

    q_low = typed(features, query_w).astype(jnp.bfloat16)
    key_low = typed(shifted_b, key_w).astype(jnp.bfloat16)
    value_low = typed(shifted_b, value_w).astype(jnp.bfloat16)
    kind_low = node_type.astype(jnp.bfloat16)
    q_heads = q_low.reshape(tgt_rows, head_count, head_size).astype(jnp.float32)
    att_f = rel_att.astype(jnp.float32)
    factor = rel_prior / math.sqrt(head_size)
    rel_raw = jnp.einsum("thj,rhjk->rthk", q_heads, att_f, precision=HIGH)
    rel_query = (rel_raw * factor[:, None, :, None]).astype(jnp.bfloat16)
    select = jnp.einsum("tk,ksr->tsr", type_hot, jnp.asarray(relation_table()), precision=HIGH)
    select_low = select.astype(jnp.bfloat16)
    cite_hot = (jnp.arange(rel_count) == 3).astype(jnp.float32)
    q_four = (
        jnp.einsum("tsr,rthd->thsd", select_low, rel_query, preferred_element_type=jnp.float32)
        .astype(jnp.bfloat16)
        .reshape(tgt_rows, head_count, kind_count * head_size)
    )
    q_cite = rel_query[3]

    def block_codes(source):
        return lax.dynamic_slice_in_dim(edge_codes, source * tgt_rows, tgt_rows, 1)

    def forward_block(run_state, kv_blk, qf_part, qc_part, code_blk):
        result = attend_block(run_state, kv_blk, qf_part, qc_part, code_blk, kind_count)
        return result

    def backward_block(kv_blk, qf_part, qc_part, gf_part, gc_part, lse_part, delta_part, code_blk):
        return back_block(
            kv_blk, qf_part, qc_part, gf_part, gc_part, lse_part, delta_part, code_blk, kind_count
        )

    whole_kv = (key_low, value_low, kind_low)

    def forward_turn(step_idx, loop_state):
        run_state, kv_blk = loop_state
        run_state = forward_block(
            run_state, kv_blk, q_four, q_cite, block_codes((my_blk - step_idx) % n_blk)
        )
        kv_blk = from_behind((kv_blk[0], kv_blk[1], kv_blk[2]), "blk", 1)
        return (run_state, kv_blk)

    run_state, kv_last = lax.fori_loop(
        0,
        n_blk,
        forward_turn,
        (
            (
                jnp.full((head_count, tgt_rows), NEG_FILL, jnp.float32),
                jnp.zeros((head_count, tgt_rows), jnp.float32),
                jnp.zeros((tgt_rows, head_count, kind_count * head_size), jnp.float32),
                jnp.zeros((tgt_rows, head_count, head_size), jnp.float32),
            ),
            whole_kv,
        ),
    )
    run_max, run_sum, acc_four, acc_cite = run_state
    floor_sum = jnp.maximum(run_sum, 1.0)
    log_total = run_max + jnp.log(floor_sum)
    norm_t = floor_sum.T[:, :, None]
    u_four = acc_four / norm_t
    u_cite = acc_cite / norm_t
    u_rel = jnp.einsum(
        "tsr,thsd->rthd",
        select,
        u_four.reshape(tgt_rows, head_count, kind_count, head_size),
        precision=HIGH,
    )
    u_rel = u_rel + cite_hot[:, None, None, None] * u_cite[None]
    u_rel_b = u_rel.astype(jnp.bfloat16)
    agg_sum = jnp.einsum(
        "rthd,rhde->the", u_rel_b, rel_msg, preferred_element_type=jnp.float32
    ).reshape(tgt_rows, feat_dim)
    act_full, gelu_back = jax.vjp(jax.nn.gelu, agg_sum)
    act_low = act_full.astype(jnp.bfloat16)
    branch = typed(act_low, out_w)
    skip_all = jax.nn.sigmoid(skip_logit)
    skip_gate = jnp.sum(type_hot * skip_all[None, :], axis=1)[:, None]
    mixed_sum = skip_gate * branch + (1.0 - skip_gate) * x_f
    centered = mixed_sum - jnp.mean(mixed_sum, axis=1, keepdims=True)
    inv_std = lax.rsqrt(jnp.mean(centered * centered, axis=1, keepdims=True) + LN_EPS)
    normed = centered * inv_std
    valid_col = node_valid.astype(jnp.float32)[:, None]
    layer_out = (valid_col * (normed * ln_gain + ln_bias)).astype(jnp.bfloat16)
    grad_y = cotangent.astype(jnp.float32) * valid_col
    gain_grad = jnp.sum(grad_y * normed, axis=0)
    bias_grad = jnp.sum(grad_y, axis=0)
    grad_norm = grad_y * ln_gain
    grad_mix = inv_std * (
        grad_norm
        - jnp.mean(grad_norm, axis=1, keepdims=True)
        - normed * jnp.mean(grad_norm * normed, axis=1, keepdims=True)
    )
    grad_branch = (skip_gate * grad_mix).astype(jnp.bfloat16)
    gate_term = (
        jnp.sum(grad_mix * (branch - x_f), axis=1, keepdims=True) * skip_gate * (1.0 - skip_gate)
    )
    skip_grad = jnp.sum(type_hot * gate_term, axis=0)
    out_grad = typed_grad(act_low, grad_branch)
    grad_agg = gelu_back(typed_back(grad_branch, out_w))[0].astype(jnp.bfloat16)
    grad_agg_heads = grad_agg.reshape(tgt_rows, head_count, head_size)
    msg_grad = jnp.einsum(
        "rthd,the->rhde", u_rel_b, grad_agg_heads, preferred_element_type=jnp.float32
    )
    grad_urel = jnp.einsum(
        "the,rhde->rthd", grad_agg_heads, rel_msg, preferred_element_type=jnp.float32
    ).astype(jnp.bfloat16)
    grad_four = (
        jnp.einsum("tsr,rthd->thsd", select_low, grad_urel, preferred_element_type=jnp.float32)
        .astype(jnp.bfloat16)
        .reshape(tgt_rows, head_count, kind_count * head_size)
    )
    grad_cite = grad_urel[3]
    row_delta = (
        jnp.sum(grad_four.astype(jnp.float32) * u_four, axis=2)
        + jnp.sum(grad_cite.astype(jnp.float32) * u_cite, axis=2)
    ).T
    zero_four = jnp.zeros((tgt_rows, head_count, kind_count * head_size), jnp.float32)
    zero_cite = jnp.zeros((tgt_rows, head_count, head_size), jnp.float32)

    def back_turn(step_idx, loop_state):
        kv_blk, travel, acc_qf, acc_qc = loop_state
        k_grad, v_grad, qf_grad, qc_grad = backward_block(
            kv_blk,
            q_four,
            q_cite,
            grad_four,
            grad_cite,
            log_total,
            row_delta,
            block_codes((my_blk - step_idx) % n_blk),
        )
        travel = (
            from_behind((travel[0] + k_grad).astype(jnp.bfloat16), "blk", 1).astype(jnp.float32),
            from_behind((travel[1] + v_grad).astype(jnp.bfloat16), "blk", 1).astype(jnp.float32),
        )
        kv_blk = from_behind((kv_blk[0], kv_blk[1], kv_blk[2]), "blk", 1)
        return (kv_blk, travel, acc_qf + qf_grad, acc_qc + qc_grad)

    zero_kv = jnp.zeros((tgt_rows, feat_dim), jnp.float32)
    loop_state = lax.fori_loop(
        0, n_blk, back_turn, (whole_kv, (zero_kv, zero_kv), zero_four, zero_cite)
    )
    key_acc, value_acc = loop_state[1]
    acc_qf, acc_qc = (loop_state[2], loop_state[3])
    grad_key = key_acc.astype(jnp.bfloat16)
    grad_value = value_acc.astype(jnp.bfloat16)
    grad_relq = jnp.einsum(
        "tsr,thsd->rthd",
        select,
        acc_qf.reshape(tgt_rows, head_count, kind_count, head_size),
        precision=HIGH,
    )
    grad_relq = (
        (grad_relq + cite_hot[:, None, None, None] * acc_qc[None])
        .astype(jnp.bfloat16)
        .astype(jnp.float32)
    )
    prior_grad = jnp.sum(grad_relq * rel_raw, axis=(1, 3)) / math.sqrt(head_size)
    grad_raw = grad_relq * factor[:, None, :, None]
    att_grad = jnp.einsum("thj,rthk->rhjk", q_heads, grad_raw, precision=HIGH)
    grad_query = (
        jnp.einsum("rthk,rhjk->thj", grad_raw, att_f, precision=HIGH)
        .reshape(tgt_rows, feat_dim)
        .astype(jnp.bfloat16)
    )
    query_grad = typed_grad(features, grad_query)
    key_grad = typed_grad(shifted_b, grad_key)
    value_grad = typed_grad(shifted_b, grad_value)
    grad_shift = typed_back(grad_key, key_w) + typed_back(grad_value, value_w)
    table_grad = jnp.dot(gap_hot.T, grad_shift, precision=HIGH)
    rte_grad = jnp.dot(time_low.T, table_grad, precision=HIGH)
    input_grad = (
        (1.0 - skip_gate) * grad_mix + typed_back(grad_query, query_w) + grad_shift
    ).astype(jnp.bfloat16)
    summed = lax.psum(
        (
            query_grad,
            key_grad,
            value_grad,
            out_grad,
            att_grad,
            msg_grad,
            prior_grad,
            skip_grad,
            rte_grad,
            gain_grad,
            bias_grad,
        ),
        ("blk", "rep"),
    )
    return (
        layer_out,
        input_grad,
        summed[0],
        summed[1],
        summed[2],
        summed[3],
        summed[4],
        summed[5],
        summed[6],
        summed[7],
        summed[8],
        summed[9],
        summed[10],
    )


REL_TAB = relation_table()
HALF = 128
F32 = jnp.float32
LOW = jnp.bfloat16
VMEM_CAP = 65400 * 2**10
PROB_UNROLL = 2
GATHER_CUTS = 2


def nn(a, b):
    return lax.dot_general(a, b, (((1,), (0,)), ((), ())), preferred_element_type=F32)


def nt(a, b):
    return lax.dot_general(a, b, (((1,), (1,)), ((), ())), preferred_element_type=F32)


def tn(a, b):
    return lax.dot_general(a, b, (((0,), (0,)), ((), ())), preferred_element_type=F32)


def pick(kinds, kind, value):
    return jnp.where(kinds == kind, value, jnp.zeros_like(value))


def relation_of(kind, slot):
    hit = np.nonzero(REL_TAB[kind, slot])[0]
    return int(hit[0]) if len(hit) else None


def to_slots(rel_rows, kinds, kind_count):
    slots = []
    for slot in range(kind_count):
        rows = jnp.zeros(kinds.shape, F32)
        for kind in range(kind_count):
            rel = relation_of(kind, slot)
            if rel is not None:
                rows = jnp.where(kinds == kind, rel_rows(rel), rows)
        slots.append(rows)
    return slots, pick(kinds, 0, rel_rows(3))


def to_relations(slot_rows, cite_rows, kinds, kind_count, rel_count):
    out = []
    for rel in range(rel_count):
        if rel == 3:
            out.append(pick(kinds, 0, cite_rows))
            continue
        (kind, slot) = [
            (k, s) for k in range(kind_count) for s in range(kind_count) if relation_of(k, s) == rel
        ][0]
        out.append(pick(kinds, kind, slot_rows(slot)))
    return out


def flip(index, mask):
    return sum(((index // bit + mask // bit) % 2) * bit for bit in (1, 2, 4))


def gap_hot(gap_row, levels):
    gaps = jnp.broadcast_to(gap_row, (levels, gap_row.shape[1]))
    return (lax.broadcasted_iota(jnp.int32, gaps.shape, 0) == gaps).astype(F32).astype(LOW)


def remote(src, dst, sends, recvs, send_at, recv_at, device):
    return pltpu.make_async_remote_copy(
        src_ref=src,
        dst_ref=dst,
        send_sem=sends.at[send_at],
        recv_sem=recvs.at[recv_at],
        device_id=device,
        device_id_type=pl.DeviceIdType.MESH,
    )


def greet(device):
    pl.semaphore_signal(
        pltpu.get_barrier_semaphore(),
        inc=1,
        device_id=device,
        device_id_type=pl.DeviceIdType.MESH,
    )


def out_at(k, half):
    return (2 * k + half) * 256


def msg_at(half):
    return 2048 + half * 256


def key_at(k, half):
    return 2560 + 3072 * half + k * 256


def value_at(k, half):
    return 2560 + 3072 * half + (4 + k) * 256


def query_at(k, half):
    return 2560 + 3072 * half + (8 + k) * 256


def att_at(half):
    return 8704 + half * 256


SUM_PARTS = ((0, (512, 768)), (2560, (768, 768)), (5632, (512, 512)), (7680, (256, 512)))
SUM_TICKS = (
    ((0, 0, 1), (2, 0, 2), (3, 0, 3)),
    ((0, 0, 4), (1, 1, 1), (2, 0, 5), (2, 1, 2), (3, 0, 6), (3, 1, 3)),
)
SUM_TAIL = (
    ((0, 8), (1, 5), (2, 2), (3, 2), (1, 6), (2, 3), (3, 3), (1, 7), (2, 4), (3, 4), (1, 8))
    + tuple((part, step) for step in (5, 6, 7, 8) for part in (2, 3))
)
GRAD_ROWS = 9216


def span(start, size):
    return pl.ds(start if isinstance(start, int) else pl.multiple_of(start, 16), size)


def summation(part, refs, places, pack):
    grads, full, core_in, first_in, second_in, line_in, sends, recvs = refs
    (z, y, x, core), by_core, by_x, by_y, by_z = places
    base, streams = SUM_PARTS[part]
    half = sum(streams)
    ahead = sum(sum(SUM_PARTS[before][1]) for before in range(part))
    count = iter(range(32 * part, 32 * part + 32))
    mine = base + core * half
    begin = (mine, mine + streams[0])
    landing = (ahead, ahead + streams[0])
    pending = []

    def send(src, dst, device):
        at = next(count)

        def copy():
            return remote(src(), dst(), sends, recvs, at, at, device)

        copy().start()
        pending.append(copy)

    def settle():
        for copy in pending:
            copy().wait()
        pending.clear()

    def piece(ref, start, size):
        return lambda: ref.at[span(start, size), :]

    def small(ref, at):
        return lambda: ref.at[at]

    def load(ref, start, size):
        return ref[span(start, size), :].astype(F32)

    def add_in(start, size, ref, at):
        value = load(grads, start, size) + load(ref, at, size)
        grads[span(start, size), :] = value.astype(LOW)

    turns = ((x, y), (y, x))
    ways = ((by_x, by_y), (by_y, by_x))
    firsts = [size // 2 for size in streams]
    seconds = [size // 4 for size in streams]
    lines = [size // 16 for size in streams]
    at_first = [begin[s] + turns[s][0] * firsts[s] for s in range(2)]
    at_second = [at_first[s] + turns[s][1] * seconds[s] for s in range(2)]
    at_line = [at_second[s] + z * lines[s] for s in range(2)]
    other_z = [(z + step) % 4 for step in (1, 2, 3)]
    aways = [
        [begin[s] + firsts[s] - turns[s][0] * firsts[s] for s in range(2)],
        [at_first[s] + seconds[s] - turns[s][1] * seconds[s] for s in range(2)],
    ]
    there_core = base + half - core * half
    line_there = [[at_second[s] + other_z[i] * lines[s] for i in range(3)] for s in range(2)]
    line_land = [3 * landing[s] // 16 for s in range(2)]

    def cores():
        send(piece(grads, there_core, half), piece(core_in, ahead, half), by_core)
        if pack:
            send(small(pack[0], 0), small(pack[1], 0), by_core)

    def plane_one():
        settle()
        add_in(mine, half, core_in, ahead)
        for s in range(2):
            send(
                piece(grads, aways[0][s], firsts[s]),
                piece(first_in, landing[s] // 2, firsts[s]),
                ways[s][0],
            )
        if pack:
            pack[0][1] = pack[0][0] + pack[1][0]
            send(small(pack[0], 1), small(pack[1], 1), by_x)

    def plane_two():
        settle()
        for s in range(2):
            add_in(at_first[s], firsts[s], first_in, landing[s] // 2)
        for s in range(2):
            send(
                piece(grads, aways[1][s], seconds[s]),
                piece(second_in, landing[s] // 4, seconds[s]),
                ways[s][1],
            )
        if pack:
            pack[0][2] = pack[0][1] + pack[1][1]
            send(small(pack[0], 2), small(pack[1], 2), by_y)

    def line():
        settle()
        for s in range(2):
            add_in(at_second[s], seconds[s], second_in, landing[s] // 4)
        for step in (2, 3, 1):
            for s in range(2):
                land = line_land[s] + (step - 1) * lines[s]
                send(
                    piece(grads, line_there[s][step - 1], lines[s]),
                    piece(line_in, land, lines[s]),
                    by_z[step - 1],
                )
        if pack:
            pack[0][3] = pack[0][2] + pack[1][2]
            for step in (2, 3, 1):
                send(small(pack[0], 3), small(pack[1], 2 + step), by_z[step - 1])

    def share(start, size, device):
        send(piece(full, start, size), piece(full, start, size), device)

    def line_back():
        settle()
        for s in range(2):
            value = load(grads, at_line[s], lines[s])
            for step in range(3):
                value = value + load(line_in, line_land[s] + step * lines[s], lines[s])
            full[span(at_line[s], lines[s]), :] = value.astype(LOW)
        for step in (2, 3, 1):
            for s in range(2):
                share(at_line[s], lines[s], by_z[step - 1])
        if pack:
            pack[2][...] = pack[0][3] + pack[1][3] + pack[1][4] + pack[1][5]

    def plane_two_back():
        settle()
        for s in range(2):
            share(at_second[s], seconds[s], ways[s][1])

    def plane_one_back():
        settle()
        for s in range(2):
            share(at_first[s], firsts[s], ways[s][0])

    def cores_back():
        settle()
        for s in range(2):
            share(begin[s], streams[s], by_core)

    return [
        cores,
        plane_one,
        plane_two,
        line,
        line_back,
        plane_two_back,
        plane_one_back,
        cores_back,
        settle,
    ]


def layer_kernel(
    x_ref,
    kind_ref,
    gap_ref,
    valid_ref,
    rte_ref,
    time_ref,
    codes_hbm,
    cot_hbm,
    qw_hbm,
    kw_hbm,
    vw_hbm,
    ow_hbm,
    att_hbm,
    msg_hbm,
    prior_ref,
    skip_ref,
    gain_ref,
    bias_ref,
    out_ref,
    input_ref,
    full,
    small_ref,
    att_flat,
    att_ref,
    msg_ref,
    cot_ref,
    codes,
    qw,
    kw,
    vw,
    ow,
    msg_flat,
    shifted,
    xt,
    base,
    shift_out,
    plane_back,
    line_back,
    load_sem,
    gather_send,
    gather_recv,
    back_send,
    back_recv,
    grads,
    core_in,
    first_in,
    second_in,
    line_in,
    pack,
    pack_in,
    sum_send,
    sum_recv,
    kt,
    vx,
    sbuf,
    probs,
    sm,
    qs,
    tails,
    qt2,
    qh,
    gt2,
    acc,
    two,
    agg,
    grad_even,
    grad_odd,
):
    rows, feat = x_ref.shape
    n_blk = shifted.shape[0]
    levels = time_ref.shape[1]
    kind_count = qw.shape[0]
    rel_count, heads, size = att_ref.shape[:3]
    group = heads // 2
    me = lax.axis_index("blk")
    rep = lax.axis_index("rep")
    z, y = me // 2, me % 2
    inner = ((z + 1) // 2) % 2
    by_y = (flip(me, 1), rep)
    by_core = (me, rep + 1 - 2 * (rep % 2))
    by_x = (me, rep + 2 - 4 * (rep // 2))
    for device in (by_y, by_core, by_x):
        greet(device)

    @pl.when(z < 3)
    def _():
        greet((me + 2, rep))

    @pl.when(z > 0)
    def _():
        greet((me - 2, rep))

    loads = [
        pltpu.make_async_copy(src, dst, load_sem.at[at])
        for at, (src, dst) in enumerate(
            (
                (att_hbm, att_ref),
                (msg_hbm, msg_ref),
                (kw_hbm, kw),
                (vw_hbm, vw),
                (qw_hbm, qw),
                (codes_hbm, codes),
                (ow_hbm, ow),
                (cot_hbm, cot_ref),
            )
        )
    ]

    x_f = x_ref[...].astype(F32).T
    x_t = x_f.astype(LOW)
    xt[...] = x_t
    table = tn(rte_ref[...], time_ref[...])
    table_hi = table.astype(LOW)
    table_lo = (table - table_hi.astype(F32)).astype(LOW)
    hot = gap_hot(gap_ref[...], levels)
    shifted[me, 0:feat, :] = (x_f + nn(table_hi, hot) + nn(table_lo, hot)).astype(LOW)
    shifted[me, feat:, :] = jnp.concatenate(
        [kind_ref[...].astype(F32), gap_ref[...].astype(F32), jnp.zeros((14, rows), F32)], axis=0
    ).astype(LOW)

    edges = [feat * c // GATHER_CUTS for c in range(GATHER_CUTS)] + [feat + 16]

    def move(block, cut, send_at, device):
        at = pl.ds(edges[cut], edges[cut + 1] - edges[cut])
        return remote(
            shifted.at[block, at, :],
            shifted.at[block, at, :],
            gather_send,
            gather_recv,
            send_at * GATHER_CUTS + cut,
            block * GATHER_CUTS + cut,
            device,
        )

    def other_z(n):
        order = ((1, 2, 1, 2), (2, 0, 3, 1), (3, 3, 0, 0))
        table = sum(row[i] * 4 ** (4 * r + i) for r, row in enumerate(order) for i in range(4))
        power = (1 + 3 * (z % 2)) * (1 + 15 * (z // 2)) * (1 + 255 * (n // 2)) * (1 + 255 * (n // 3))
        own = (3 - n) // 3
        return own * z + (1 - own) * ((table // power) % 4)

    def own_moves(act):
        for cut in range(GATHER_CUTS):

            @pl.when(z < 3)
            def _():
                act(move(me, cut, 0, (me + 2, rep)))

            @pl.when(z > 0)
            def _():
                act(move(me, cut, 1, (me - 2, rep)))

            act(move(me, cut, 2, by_y))

    def hand_on(n, act, wait):
        there = other_z(n)
        step = 2 * ((z - there + 3) // 4) - 1
        block = 2 * there + y
        for cut in range(GATHER_CUTS):
            if wait:
                move(block, cut, 0, by_y).wait_recv()
            act(move(block, cut, 2 + n, by_y))

            @pl.when((z + step >= 0) & (z + step <= 3))
            def _():
                act(move(block, cut, 5 + n, (me + 2 * step, rep)))

    pl.semaphore_wait(pltpu.get_barrier_semaphore(), 4 + inner)
    own_moves(lambda copy: copy.start())
    for load in loads:
        load.start()

    def source_row(j, row):
        return shifted[j, feat : feat + 16, :].astype(F32)[row : row + 1].astype(jnp.int32)

    kinds = jnp.broadcast_to(kind_ref[...], (size, rows))
    kinds_f = jnp.broadcast_to(kind_ref[...], (feat, rows))
    valid_f = jnp.broadcast_to(valid_ref[...], (feat, rows)).astype(F32)
    lane = lax.broadcasted_iota(jnp.int32, (rows, HALF), 1)
    ones_pad = (lax.broadcasted_iota(jnp.int32, (16, rows), 0) < 2).astype(F32).astype(LOW)
    scale = 1.0 / math.sqrt(size)

    def cols(j):
        return pl.ds(pl.multiple_of(j * rows, rows), rows)

    def store_part(start, value):
        grads[pl.ds(start, value.shape[0]), :] = value.astype(LOW)

    loads[0].wait()
    loads[1].wait()
    for r in range(rel_count):
        for h in range(heads):
            agg[h * size : (h + 1) * size, r * size : (r + 1) * size] = att_ref[r, h].astype(F32)
    att_flat[...] = agg[...].astype(LOW)
    for r in range(rel_count):
        for h in range(heads):
            agg[r * size : (r + 1) * size, h * size : (h + 1) * size] = msg_ref[r, h].astype(F32)
    msg_flat[...] = agg[...].T.astype(LOW)

    def turned(m, k):
        return probs.at[0, 2 * m + k // 2, pl.ds((k % 2) * feat, feat), :]

    for m, (load, ref) in enumerate(((loads[2], kw), (loads[3], vw))):
        load.wait()
        for k in range(kind_count):
            turned(m, k)[...] = ref[k].astype(F32).T.astype(LOW)

    loads[4].wait()
    q_full = jnp.zeros((feat, rows), F32)
    for k in range(kind_count):
        q_full = jnp.where(kinds_f == k, tn(qw[k], x_t), q_full)
    for h in range(heads):
        qh[h] = q_full[h * size : (h + 1) * size].astype(LOW)

    def head_rows(ref, h):
        return ref[pl.ds(pl.multiple_of(h * size, size), size), :]

    def query_head(h, carry):
        raw = tn(head_rows(att_flat, h), qh[h])

        def rel_rows(r):
            part = raw[r * size : (r + 1) * size] * (prior_ref[r, h] * scale)
            return part.astype(LOW).astype(F32)

        slots, cite = to_slots(rel_rows, kinds, kind_count)
        slot_t = jnp.concatenate(slots, axis=0)
        cite_t = jnp.concatenate([cite, jnp.zeros((HALF - size, rows), F32)], axis=0)
        qt2[h, :, 0:rows] = slot_t.astype(LOW)
        qt2[h, :, rows:] = cite_t.astype(LOW)
        qs[h, 0:rows, :] = slot_t.T.astype(LOW)
        qs[h, rows:, :] = cite_t.T.astype(LOW)
        return carry

    lax.fori_loop(0, heads, query_head, 0, unroll=2)
    loads[5].wait()
    acc[:, :, 0:rows] = jnp.full((heads, HALF, rows), NEG_FILL, F32)

    def keep_scores(h, j, both, second, edge):
        val = jnp.where(second, both[rows:], both[:rows])
        val = jnp.where(edge, val, NEG_FILL)
        if h < group:
            sbuf[j, pl.ds(h * rows, rows), :] = val
        else:
            high = val.astype(LOW)
            probs[j, h, 0:rows, :] = high
            probs[j, h, rows:, :] = (val - high.astype(F32)).astype(LOW)
        top = jnp.maximum(val[:, :HALF], val[:, HALF:])
        for part in range(rows // HALF):
            at = slice(part * HALF, (part + 1) * HALF)
            acc[h, :, at] = jnp.maximum(acc[h, :, at], top[at])

    def arrive(j):
        src = jnp.broadcast_to(source_row(j, 0), (size, rows))
        block = shifted[j, 0:feat, :]
        for k in range(kind_count):
            key = nn(turned(0, k)[...], block)
            value = nn(turned(1, k)[...], block)
            for h in range(heads):
                part = slice(h * size, (h + 1) * size)
                kt[j, h, pl.ds(k * size, size), :] = pick(src, k, key[part]).astype(LOW)
                vx[j, h, pl.ds(k * size, size), :] = pick(src, k, value[part]).astype(LOW)
        code = codes[:, cols(j)]
        second = code == 2
        edge = code > 0
        two[j] = second.astype(F32).astype(LOW)
        before = None
        for h in range(heads + 1):
            both = nn(qs[h], kt[j, h]) if h < heads else None
            if h > 0:
                keep_scores(h - 1, j, before, second, edge)
            before = both

    def start(copy):
        copy.start()

    def two_blocks(n, carry):
        there = other_z(n)

        def one(line, inside):
            block = 2 * there + (y + line) % 2

            @pl.when(line == 1)
            def _():
                @pl.when(n == 0)
                def _():
                    hand_on(1, start, True)

                @pl.when((n == 0) & (inner == 1))
                def _():
                    hand_on(2, start, True)

                @pl.when(n == 1)
                def _():
                    hand_on(2 + inner, start, True)

                @pl.when((n == 2) & (inner == 0))
                def _():
                    hand_on(3, start, True)

                for cut in range(GATHER_CUTS):
                    move(block, cut, 0, by_y).wait_recv()

            arrive(block)
            return inside

        return lax.fori_loop(0, 2, one, carry)

    lax.fori_loop(0, n_blk // 2, two_blocks, 0)
    own_moves(lambda copy: copy.wait_send())
    for n in range(1, n_blk // 2):
        hand_on(n, lambda copy: copy.wait_send(), False)

    def prob_block(h, j, top, kept):
        if kept:
            val = sbuf[j, pl.ds(pl.multiple_of(h * rows, rows), rows), :]
        else:
            val = probs[j, h, 0:rows, :].astype(F32) + probs[j, h, rows:, :].astype(F32)
        val = jnp.exp(val - top)
        low = val.astype(LOW)
        second = low * two[j]
        probs[j, h, 0:rows, :] = low - second
        probs[j, h, rows:, :] = second
        return val[:, :HALF] + val[:, HALF:]

    sm[...] = jnp.zeros((rows, HALF), F32)

    def prob_head(h, kept):
        top = jnp.concatenate([acc[h, :, 0:HALF], acc[h, :, HALF:rows]], axis=0)
        top = jnp.max(top, axis=1, keepdims=True)
        top = jnp.broadcast_to(jnp.maximum(top, 0.1 * NEG_FILL), (rows, rows))
        value_sum = None
        total = None
        for j in range(n_blk + 1):
            if j < n_blk:
                part = prob_block(h, j, top, kept)
                total = part if total is None else total + part
            if j > 0:
                part = nt(vx[j - 1, h], probs[j - 1, h])
                value_sum = part if value_sum is None else value_sum + part
        acc[h] = value_sum
        total = jnp.sum(total, axis=1, keepdims=True)
        sm[...] = jnp.where(lane == h, jnp.broadcast_to(total, (rows, HALF)), sm[...])

    for kept in (True, False):

        def prob_pair(pair, carry, kept=kept):
            for u in range(PROB_UNROLL):
                prob_head((0 if kept else group) + PROB_UNROLL * pair + u, kept)
            return carry

        lax.fori_loop(0, group // PROB_UNROLL, prob_pair, 0)

    inverse = 1.0 / jnp.maximum(sm[...].T, 1.0)
    sm[0:heads, :] = inverse[0:heads, 0:HALF]
    sm[heads : 2 * heads, :] = inverse[0:heads, HALF:]

    def inv_row(h, count):
        row = jnp.concatenate([sm[pl.ds(h, 1), :], sm[pl.ds(heads + h, 1), :]], axis=1)
        return jnp.broadcast_to(row, (count, rows))

    def rel_part(h):
        return sbuf[h // group, pl.ds((h % group) * feat, feat), :].astype(LOW)

    for h in range(heads):
        inv = inv_row(h, HALF)
        u_slot = acc[h, :, 0:rows] * inv
        u_cite = acc[h, 0:size, rows:] * inv[0:size]
        acc[h, :, 0:rows] = u_slot
        acc[h, 0:size, rows:] = u_cite
        rel = to_relations(
            lambda s: u_slot[s * size : (s + 1) * size], u_cite, kinds, kind_count, rel_count
        )
        rel = jnp.concatenate(rel, axis=0)
        sbuf[h // group, pl.ds((h % group) * feat, feat), :] = rel
        agg[pl.ds(h * size, size), :] = nn(head_rows(msg_flat, h), rel.astype(LOW))
    loads[6].wait()
    loads[7].wait()
    agg_t = agg[...]
    slope = 0.7978845608028654
    inner = jnp.tanh(slope * (agg_t + 0.044715 * agg_t * agg_t * agg_t))
    act_t = (0.5 * agg_t * (1.0 + inner)).astype(LOW)
    gelu_back = 0.5 * (1.0 + inner) + 0.5 * agg_t * (1.0 - inner * inner) * slope * (
        1.0 + 3.0 * 0.044715 * agg_t * agg_t
    )
    skip = jnp.zeros((1, rows), F32)
    branch = jnp.zeros((feat, rows), F32)
    for k in range(kind_count):
        skip = jnp.where(kinds[0:1] == k, skip_ref[k], skip)
        branch = jnp.where(kinds_f == k, tn(ow[k], act_t), branch)
    gate_row = 1.0 / (1.0 + jnp.exp(-skip))
    gate = jnp.broadcast_to(gate_row, (feat, rows))
    mixed = gate * branch + (1.0 - gate) * x_f
    centered = mixed - jnp.mean(mixed, axis=0, keepdims=True)
    inv_std = lax.rsqrt(jnp.mean(centered * centered, axis=0, keepdims=True) + LN_EPS)
    normed = centered * inv_std
    affine = jnp.concatenate([gain_ref[...], bias_ref[...], jnp.zeros((HALF - 2, feat), F32)], axis=0).T
    gain = jnp.broadcast_to(affine[:, 0:1], (feat, rows))
    bias = jnp.broadcast_to(affine[:, 1:2], (feat, rows))
    out_ref[...] = (valid_f * (normed * gain + bias)).T.astype(LOW)
    grad_y = cot_ref[...].astype(F32).T * valid_f
    gain_col = jnp.sum(grad_y * normed, axis=1, keepdims=True)
    bias_col = jnp.sum(grad_y, axis=1, keepdims=True)
    grad_norm = grad_y * gain
    grad_mix = inv_std * (
        grad_norm
        - jnp.mean(grad_norm, axis=0, keepdims=True)
        - normed * jnp.mean(grad_norm * normed, axis=0, keepdims=True)
    )
    skip_row = (
        jnp.sum(grad_mix * (branch - x_f), axis=0, keepdims=True) * gate_row * (1.0 - gate_row)
    )
    base[...] = (1.0 - gate) * grad_mix
    grad_branch = gate * grad_mix
    grad_act = jnp.zeros((feat, rows), F32)
    for k in range(kind_count):
        masked = pick(kinds_f, k, grad_branch).astype(LOW)
        out_grad = nt(act_t, masked)
        store_part(out_at(k, 0), out_grad[:, :HALF])
        store_part(out_at(k, 1), out_grad[:, HALF:])
        grad_act = grad_act + nn(ow[k], masked)
    agg[...] = gelu_back * grad_act

    for h in range(heads):
        grad_agg = agg[pl.ds(h * size, size), :].astype(LOW)
        msg_grad = nt(grad_agg, rel_part(h))
        store_part(msg_at(0) + h * size, msg_grad[:, :HALF])
        store_part(msg_at(1) + h * size, msg_grad[:, HALF:])
        inv = inv_row(h, size)
        grad_u = tn(head_rows(msg_flat, h), grad_agg)

        def rel_rows(r):
            return grad_u[r * size : (r + 1) * size] * inv

        slots, cite = to_slots(rel_rows, kinds, kind_count)
        slot_t = jnp.concatenate(slots, axis=0).astype(LOW)
        cite_t = jnp.concatenate([cite, jnp.zeros((HALF - size, rows), F32)], axis=0).astype(LOW)
        gt2[h, :, 0:rows] = slot_t
        gt2[h, :, rows:] = cite_t
        slot_f = slot_t.astype(F32)
        cite_f = cite_t.astype(F32)
        delta = -(
            jnp.sum(slot_f * acc[h, :, 0:rows], axis=0, keepdims=True)
            + jnp.sum(cite_f[0:size] * acc[h, 0:size, rows:], axis=0, keepdims=True)
        )
        delta_hi = delta.astype(LOW).astype(F32)
        tail = jnp.concatenate(
            [delta_hi, delta - delta_hi, jnp.zeros((HALF - 2, rows), F32)], axis=0
        )
        tail_t = tail.T.astype(LOW)
        qs[h, 0:rows, :] = slot_f.T.astype(LOW)
        qs[h, rows:, :] = cite_f.T.astype(LOW)
        tails[h] = tail_t[:, 0:16]
        acc[h] = jnp.zeros(acc.shape[1:], F32)

    refs = (grads, full, core_in, first_in, second_in, line_in, sum_send, sum_recv)
    by_z = [(((me // 2 + step) % 4) * 2 + me % 2, rep) for step in (1, 2, 3)]
    places = ((me // 2, me % 2, rep // 2, rep % 2), by_core, by_x, by_y, by_z)
    sums = [summation(part, refs, places, None) for part in range(3)]
    sums.append(summation(3, refs, places, (pack, pack_in, small_ref)))
    sums[0][0]()

    slot_id = lax.broadcasted_iota(jnp.int32, (HALF, rows), 0) // size
    pack[0] = jnp.zeros(pack.shape[1:], F32)

    def along_y(m):
        return remote(
            shift_out.at[flip(me, m + 1)],
            plane_back.at[m // 2],
            back_send,
            back_recv,
            m // 2,
            m // 2,
            by_y,
        )

    def along_z(m):
        at = n_blk // 2 + m // 2
        return remote(
            shift_out.at[flip(me, m)],
            line_back.at[m // 2],
            back_send,
            back_recv,
            at,
            at,
            (flip(me, m), rep),
        )

    def pass_on(m):
        along_y(m).wait_recv()
        j = flip(me, m)
        total = shift_out[j].astype(F32) + plane_back[m // 2].astype(F32)
        shift_out[j] = total.astype(LOW)
        along_z(m).start()

    grad_bufs = (grad_even, grad_odd)
    for g in range(2):
        half = slice(g * HALF, (g + 1) * HALF)

        def block_pair(pair, carry, g=g, half=half):
            m = n_blk - 2 - 2 * pair
            blocks = (flip(me, m + 1), flip(me, m))
            owns = [slot_id == jnp.broadcast_to(source_row(j, 0), (HALF, rows)) for j in blocks]

            def keep(at, u, kind, part):
                for k in range(kind_count):
                    start = (2 * k + kind) * HALF + u * size
                    sbuf[blocks[at], pl.ds(start, size), :] = part[k * size : (k + 1) * size]

            def score_part(at, u):
                h = g * group + u
                both = jnp.concatenate([tails[h], tails[h]], axis=0)
                left = jnp.concatenate([qs[h], both], axis=1)
                right = jnp.concatenate([vx[blocks[at], h], ones_pad], axis=0)
                grad_bufs[u % 2][...] = probs[blocks[at], h] * nn(left, right).astype(LOW)
                keep(at, u, 1, jnp.where(owns[at], nn(gt2[h], probs[blocks[at], h]), 0.0))

            def key_part(at, u):
                h = g * group + u
                grad = grad_bufs[u % 2][...]
                keep(at, u, 0, jnp.where(owns[at], nn(qt2[h], grad), 0.0))
                acc[h] = acc[h] + nt(kt[blocks[at], h], grad)

            units = [(at, u) for at in range(2) for u in range(group)]
            for i in range(len(units) + 1):
                if i < len(units):
                    score_part(*units[i])
                if i > 0:
                    key_part(*units[i - 1])
            for at in range(2):
                j = blocks[at]
                total = None
                for k in range(kind_count):
                    weights = jnp.concatenate([kw[k, :, half], vw[k, :, half]], axis=1)
                    part = nn(weights, sbuf[j, pl.ds(k * feat, feat), :].astype(LOW))
                    total = part if total is None else total + part
                if g == 1:
                    total = total + shift_out[j].astype(F32)
                low = total.astype(LOW)
                shift_out[j] = low
                if g == 1:
                    gaps = gap_hot(source_row(j, 1), levels)
                    pack[0, 0:levels, :] = pack[0, 0:levels, :] + nt(gaps, low)
                    if at == 0:
                        along_y(m).start()
            if g == 1:

                @pl.when(pair > 0)
                def _():
                    pass_on(m + 2)

            for when, part, step in SUM_TICKS[g]:

                @pl.when(pair == when)
                def _(part=part, step=step):
                    sums[part][step]()

            return carry

        lax.fori_loop(0, n_blk // 2, block_pair, 0)

        for k in range(kind_count):
            total = None
            for j in range(n_blk):
                part = nt(shifted[j, 0:feat, :], sbuf[j, pl.ds(k * feat, feat), :].astype(LOW))
                total = part if total is None else total + part
            store_part(key_at(k, g), total[:, :HALF])
            store_part(value_at(k, g), total[:, HALF:])
        if g == 1:
            sums[2][0]()
        grad_q = []
        for h in range(g * group, (g + 1) * group):
            slot = acc[h, :, 0:rows]
            rel = to_relations(
                lambda s: slot[s * size : (s + 1) * size],
                acc[h, 0:size, rows:],
                kinds,
                kind_count,
                rel_count,
            )
            rel = [part.astype(LOW) for part in rel]
            att_grad = nt(qh[h], jnp.concatenate(rel, axis=0))
            store_part(att_at(0) + h * size, att_grad[:, :HALF])
            store_part(att_at(1) + h * size, att_grad[:, HALF:])
            raw = [
                (part.astype(F32) * (prior_ref[r, h] * scale)).astype(LOW)
                for r, part in enumerate(rel)
            ]
            grad_q.append(nn(head_rows(att_flat, h), jnp.concatenate(raw, axis=0)))
        grad_q = jnp.concatenate(grad_q, axis=0).astype(LOW).astype(F32)
        total = base[...]
        for k in range(kind_count):
            masked = pick(kinds_f[0:HALF], k, grad_q).astype(LOW)
            store_part(query_at(k, g), nt(xt[...], masked))
            total = total + nn(qw[k, :, half], masked)
        base[...] = total
        if g == 0:
            sums[1][0]()

    pair = jnp.where(
        lane == 0,
        jnp.broadcast_to(gain_col, (feat, HALF)),
        jnp.where(lane == 1, jnp.broadcast_to(bias_col, (feat, HALF)), 0.0),
    ).T
    spot = lax.broadcasted_iota(jnp.int32, (1, rows), 1)
    skips = jnp.zeros((1, rows), F32)
    for k in range(kind_count):
        skips = jnp.where(
            spot == k, jnp.sum(pick(kinds[0:1], k, skip_row), axis=1, keepdims=True), skips
        )
    pack[0, levels : levels + 8, :] = jnp.concatenate(
        [pair[0:2], skips, jnp.zeros((5, rows), F32)], axis=0
    )
    sums[3][0]()
    sums[0][7]()
    sums[1][4]()
    sums[2][1]()
    sums[3][1]()
    along_y(0).wait_recv()
    total = base[...] + shift_out[me].astype(F32) + plane_back[0].astype(F32)
    for m in (2, 4, 6):
        along_z(m).wait_recv()
        total = total + line_back[m // 2].astype(F32)
    input_ref[...] = total.T.astype(LOW)
    for part, step in SUM_TAIL:
        sums[part][step]()
    for m in (0, 2, 4, 6):
        along_y(m).wait_send()
        if m > 0:
            along_z(m).wait_send()


def finish_kernel(
    full,
    small_ref,
    att_flat,
    time_ref,
    prior_ref,
    out_in,
    input_in,
    out_ref,
    input_ref,
    qg_ref,
    kg_ref,
    vg_ref,
    og_ref,
    attg_ref,
    msgg_ref,
    priorg_ref,
    skip_ref,
    rte_ref,
    gain_ref,
    bias_ref,
):
    out_ref[...] = out_in[...]
    input_ref[...] = input_in[...]
    kind_count, feat = qg_ref.shape[:2]
    rel_count, heads, width = attg_ref.shape[:3]
    scale = 1.0 / math.sqrt(width)

    def part(start):
        return full[pl.ds(start, feat), :].astype(F32)

    for ref, at in ((qg_ref, query_at), (kg_ref, key_at), (vg_ref, value_at), (og_ref, out_at)):
        for k in range(kind_count):
            for half in range(2):
                ref[k, :, half * HALF : (half + 1) * HALF] = part(at(k, half))
    att = jnp.concatenate([part(att_at(0)), part(att_at(1))], axis=1)
    msg = jnp.concatenate([part(msg_at(0)), part(msg_at(1))], axis=1).T
    for r in range(rel_count):
        for h in range(heads):
            block = (slice(h * width, (h + 1) * width), slice(r * width, (r + 1) * width))
            attg_ref[r, h] = att[block] * (prior_ref[r, h] * scale)
            msgg_ref[r, h] = msg[block[::-1]]
    prod = (att * att_flat[...].astype(F32)).reshape(heads, width, feat)
    prod = jnp.sum(prod, axis=1)
    spread = (
        lax.broadcasted_iota(jnp.int32, (feat, rel_count), 0) // width
        == lax.broadcasted_iota(jnp.int32, (feat, rel_count), 1)
    ).astype(F32).astype(LOW)
    prior = jnp.zeros((rel_count, heads), F32)
    for _ in range(3):
        low = prod.astype(LOW)
        prior = prior + lax.dot_general(
            spread, low, (((0,), (1,)), ((), ())), preferred_element_type=F32
        )
        prod = prod - low.astype(F32)
    priorg_ref[...] = prior * scale
    levels = time_ref.shape[1]
    small = small_ref[...]
    rte = jnp.zeros(rte_ref.shape, F32)
    rest = small[0:levels]
    for _ in range(3):
        low = rest.astype(LOW)
        rte = rte + nn(time_ref[...], low)
        rest = rest - low.astype(F32)
    rte_ref[...] = rte
    gain_ref[...] = small[levels : levels + 1]
    bias_ref[...] = small[levels + 1 : levels + 2]
    skip_ref[...] = small[levels + 2 : levels + 3, 0:kind_count]


def layer_call(n_blk, *args):
    rows, feat = args[0].shape
    kind_count = args[8].shape[0]
    rel_count, heads, size = args[12].shape[:3]
    vmem = pl.BlockSpec(memory_space=pltpu.VMEM)
    smem = pl.BlockSpec(memory_space=pltpu.SMEM)
    hbm = pl.BlockSpec(memory_space=pl.ANY)
    square = (feat, feat)
    weight = pltpu.VMEM((kind_count,) + square, LOW)

    def shape(dims, kind):
        return jax.ShapeDtypeStruct(dims, kind)

    return pl.pallas_call(
        layer_kernel,
        out_shape=[
            shape((rows, feat), LOW),
            shape((rows, feat), LOW),
            shape((GRAD_ROWS, HALF), LOW),
            shape((LEVELS + 8, feat), F32),
            shape(square, LOW),
        ],
        in_specs=[vmem] * 6 + [hbm] * 8 + [smem] * 2 + [vmem] * 2,
        out_specs=[vmem] * 5,
        scratch_shapes=[
            pltpu.VMEM((rel_count, heads, size, size), LOW),
            pltpu.VMEM((rel_count, heads, size, size), LOW),
            pltpu.VMEM((rows, feat), LOW),
            pltpu.VMEM((rows, n_blk * rows), jnp.int32),
            weight,
            weight,
            weight,
            weight,
            pltpu.VMEM(square, LOW),
            pltpu.VMEM((n_blk, feat + 16, rows), LOW),
            pltpu.VMEM((feat, rows), LOW),
            pltpu.VMEM((feat, rows), F32),
            pltpu.VMEM((n_blk, feat, rows), LOW),
            pltpu.VMEM((n_blk // 2, feat, rows), LOW),
            pltpu.VMEM((n_blk // 2, feat, rows), LOW),
            pltpu.SemaphoreType.DMA((8,)),
            pltpu.SemaphoreType.DMA((9 * GATHER_CUTS,)),
            pltpu.SemaphoreType.DMA((n_blk * GATHER_CUTS,)),
            pltpu.SemaphoreType.DMA((n_blk,)),
            pltpu.SemaphoreType.DMA((n_blk,)),
            pltpu.VMEM((GRAD_ROWS, HALF), LOW),
            pltpu.VMEM((GRAD_ROWS // 2, HALF), LOW),
            pltpu.VMEM((GRAD_ROWS // 4, HALF), LOW),
            pltpu.VMEM((GRAD_ROWS // 8, HALF), LOW),
            pltpu.VMEM((3 * GRAD_ROWS // 32, HALF), LOW),
            pltpu.VMEM((4, LEVELS + 8, feat), F32),
            pltpu.VMEM((6, LEVELS + 8, feat), F32),
            pltpu.SemaphoreType.DMA((128,)),
            pltpu.SemaphoreType.DMA((128,)),
            pltpu.VMEM((n_blk, heads, HALF, rows), LOW),
            pltpu.VMEM((n_blk, heads, HALF, rows), LOW),
            pltpu.VMEM((n_blk, heads // 2 * rows, rows), F32),
            pltpu.VMEM((n_blk, heads, 2 * rows, rows), LOW),
            pltpu.VMEM((rows, HALF), F32),
            pltpu.VMEM((heads, 2 * rows, HALF), LOW),
            pltpu.VMEM((heads, rows, 16), LOW),
            pltpu.VMEM((heads, HALF, 2 * rows), LOW),
            pltpu.VMEM((heads, size, rows), LOW),
            pltpu.VMEM((heads, HALF, 2 * rows), LOW),
            pltpu.VMEM((heads, HALF, 2 * rows), F32),
            pltpu.VMEM((n_blk, rows, rows), LOW),
            pltpu.VMEM(square, F32),
            pltpu.VMEM((2 * rows, rows), LOW),
            pltpu.VMEM((2 * rows, rows), LOW),
        ],
        compiler_params=pltpu.CompilerParams(
            vmem_limit_bytes=VMEM_CAP, collective_id=0, has_side_effects=True
        ),
        name="layer",
    )(*args)


def time_columns(level_count, feat_width):
    positions = np.arange(level_count, dtype=np.float32)[:, None]
    steps = np.arange(feat_width // 2, dtype=np.float32)[None, :]
    phases = positions / np.power(np.float32(10000.0), np.float32(2.0) * steps / feat_width)
    table = np.stack([np.sin(phases), np.cos(phases)], axis=2).reshape(level_count, feat_width)
    return jnp.asarray(np.ascontiguousarray(table.T), LOW)


def fast_body(
    features,
    node_type,
    time_gap,
    node_valid,
    edge_codes,
    query_w,
    key_w,
    value_w,
    out_w,
    rel_att,
    rel_msg,
    rel_prior,
    skip_logit,
    rte_w,
    ln_gain,
    ln_bias,
    cotangent,
):
    rows, feat = features.shape
    n_blk = lax.axis_size("blk")
    kind_count = query_w.shape[0]
    time_low = time_columns(LEVELS, feat)
    vmem = pl.BlockSpec(memory_space=pltpu.VMEM)
    smem = pl.BlockSpec(memory_space=pltpu.SMEM)
    square = (feat, feat)

    def shape(dims, kind):
        return jax.ShapeDtypeStruct(dims, kind)

    layer_out, input_grad, full, small, att_flat = layer_call(
        n_blk,
        features,
        node_type[None],
        time_gap[None],
        node_valid[None],
        rte_w,
        time_low,
        edge_codes,
        cotangent,
        query_w,
        key_w,
        value_w,
        out_w,
        rel_att,
        rel_msg,
        rel_prior,
        skip_logit,
        ln_gain[None],
        ln_bias[None],
    )
    outs = pl.pallas_call(
        finish_kernel,
        out_shape=[shape(layer_out.shape, LOW), shape(input_grad.shape, LOW)]
        + [shape((kind_count,) + square, F32)] * 4
        + [shape(rel_att.shape, F32)] * 2
        + [
            shape(rel_prior.shape, F32),
            shape((1, kind_count), F32),
            shape(square, F32),
            shape((1, feat), F32),
            shape((1, feat), F32),
        ],
        in_specs=[vmem] * 4 + [smem] + [vmem] * 2,
        out_specs=[vmem] * 13,
        compiler_params=pltpu.CompilerParams(vmem_limit_bytes=VMEM_CAP),
        name="finish",
    )(full, small, att_flat, time_low, rel_prior, layer_out, input_grad)
    return (*outs[:9], outs[9][0], outs[10], outs[11][0], outs[12][0])


def solution(mesh):
    in_specs = (
        P(("blk", "rep"), None),
        P(("blk", "rep")),
        P(("blk", "rep")),
        P(("blk", "rep")),
        P(("blk", "rep"), None),
        P(),
        P(),
        P(),
        P(),
        P(),
        P(),
        P(),
        P(),
        P(),
        P(),
        P(),
        P(("blk", "rep"), None),
    )
    out_specs = (
        P(("blk", "rep"), None),
        P(("blk", "rep"), None),
        P(),
        P(),
        P(),
        P(),
        P(),
        P(),
        P(),
        P(),
        P(),
        P(),
        P(),
    )
    plan = fast_body if tuple(mesh.shape.values()) == (8, 4) else body
    return jax.shard_map(plan, mesh=mesh, in_specs=in_specs, out_specs=out_specs, check_vma=False)
```

```python
import math

import jax
import jax.numpy as jnp
import numpy as np
from jax import lax
from jax.experimental import pallas as pl
from jax.experimental.pallas import tpu as pltpu
from jax.sharding import PartitionSpec as P

LEVELS = 16


NEG_FILL = -1e30
LN_EPS = 1e-05
HIGH = lax.Precision.HIGHEST


def from_behind(block, axis, distance):
    devices = range(lax.axis_size(axis))
    route = [((i - distance) % len(devices), i) for i in devices]
    return lax.ppermute(block, axis, route)


def relation_table():
    rel_tab = np.zeros((4, 4, 8), np.float32)
    rel_tab[0, 1, 0] = 1.0
    rel_tab[1, 0, 1] = 1.0
    rel_tab[0, 0, 2] = 1.0
    rel_tab[2, 0, 4] = 1.0
    rel_tab[0, 2, 5] = 1.0
    rel_tab[3, 1, 6] = 1.0
    rel_tab[1, 3, 7] = 1.0
    return rel_tab


def time_table(level_count, feat_width):
    positions = jnp.arange(level_count, dtype=jnp.float32)[:, None]
    freq_idx = jnp.arange(feat_width // 2, dtype=jnp.float32)[None, :]
    phases = positions / jnp.power(10000.0, 2.0 * freq_idx / feat_width)
    return jnp.stack([jnp.sin(phases), jnp.cos(phases)], axis=2).reshape(level_count, feat_width)


def slot_spread(heads_arr, kind_hot):
    spread_out = heads_arr[:, :, None, :] * kind_hot[:, None, :, None]
    return spread_out.reshape(heads_arr.shape[0], heads_arr.shape[1], -1)


def slot_collapse(slot_arr, kind_hot):
    src_rows, head_count = (slot_arr.shape[0], slot_arr.shape[1])
    kind_count = kind_hot.shape[1]
    shaped = slot_arr.reshape(src_rows, head_count, kind_count, -1)
    return jnp.sum(shaped * kind_hot.astype(jnp.float32)[:, None, :, None], axis=2)


def block_scores(kv_blk, q_four, q_cite, code_blk, kind_count):
    key_blk, value_blk, kind_blk = kv_blk
    src_rows = key_blk.shape[0]
    head_count = q_four.shape[1]
    key_heads = key_blk.reshape(src_rows, head_count, -1)
    value_heads = value_blk.reshape(src_rows, head_count, -1)
    kind_hot = (kind_blk[:, None] == jnp.arange(kind_count).astype(jnp.bfloat16)[None, :]).astype(
        jnp.bfloat16
    )
    key_four = slot_spread(key_heads, kind_hot)
    value_four = slot_spread(value_heads, kind_hot)
    is_one = (code_blk == 1)[None]
    is_two = (code_blk == 2)[None]
    slot_dot = jnp.einsum("thc,shc->hts", q_four, key_four, preferred_element_type=jnp.float32)
    cite_dot = jnp.einsum("thd,shd->hts", q_cite, key_heads, preferred_element_type=jnp.float32)
    scores = jnp.where(is_one, slot_dot, jnp.where(is_two, cite_dot, NEG_FILL))
    return (scores, is_one, is_two, key_heads, value_heads, key_four, value_four, kind_hot)


def attend_block(run_state, kv_blk, q_four, q_cite, code_blk, kind_count):
    run_max, run_sum, acc_four, acc_cite = run_state
    scores, is_one, is_two, key_heads, value_heads, key_four, value_four, kind_hot = block_scores(
        kv_blk, q_four, q_cite, code_blk, kind_count
    )
    new_max = jnp.maximum(run_max, jnp.max(scores, axis=2))
    expd = jnp.where((code_blk > 0)[None], jnp.exp(scores - new_max[:, :, None]), 0.0)
    rescale = jnp.exp(run_max - new_max)
    run_sum = run_sum * rescale + jnp.sum(expd, axis=2)
    prob_low = expd.astype(jnp.bfloat16)
    zero_low = jnp.zeros_like(prob_low)
    p_one = jnp.where(is_one, prob_low, zero_low)
    p_two = jnp.where(is_two, prob_low, zero_low)
    rescale_t = rescale.T[:, :, None]
    acc_four = acc_four * rescale_t + jnp.einsum(
        "hts,shc->thc", p_one, value_four, preferred_element_type=jnp.float32
    )
    acc_cite = acc_cite * rescale_t + jnp.einsum(
        "hts,shd->thd", p_two, value_heads, preferred_element_type=jnp.float32
    )
    return (new_max, run_sum, acc_four, acc_cite)


def back_block(
    kv_blk, q_four, q_cite, grad_four, grad_cite, log_total, row_delta, code_blk, kind_count
):
    scores, is_one, is_two, key_heads, value_heads, key_four, value_four, kind_hot = block_scores(
        kv_blk, q_four, q_cite, code_blk, kind_count
    )
    prob_full = jnp.where((code_blk > 0)[None], jnp.exp(scores - log_total[:, :, None]), 0.0)
    prob_low = prob_full.astype(jnp.bfloat16)
    zero_low = jnp.zeros_like(prob_low)
    p_one = jnp.where(is_one, prob_low, zero_low)
    p_two = jnp.where(is_two, prob_low, zero_low)
    grad_slot = jnp.einsum(
        "thc,shc->hts", grad_four, value_four, preferred_element_type=jnp.float32
    )
    grad_other = jnp.einsum(
        "thd,shd->hts", grad_cite, value_heads, preferred_element_type=jnp.float32
    )
    grad_probs = jnp.where(is_one, grad_slot, jnp.where(is_two, grad_other, 0.0))
    grad_scores = (prob_full * (grad_probs - row_delta[:, :, None])).astype(jnp.bfloat16)
    d_one = jnp.where(is_one, grad_scores, zero_low)
    d_two = jnp.where(is_two, grad_scores, zero_low)
    qf_grad = jnp.einsum("hts,shc->thc", d_one, key_four, preferred_element_type=jnp.float32)
    qc_grad = jnp.einsum("hts,shd->thd", d_two, key_heads, preferred_element_type=jnp.float32)
    k_grad = slot_collapse(
        jnp.einsum("hts,thc->shc", d_one, q_four, preferred_element_type=jnp.float32), kind_hot
    )
    k_grad = k_grad + jnp.einsum("hts,thd->shd", d_two, q_cite, preferred_element_type=jnp.float32)
    v_grad = slot_collapse(
        jnp.einsum("hts,thc->shc", p_one, grad_four, preferred_element_type=jnp.float32), kind_hot
    )
    v_grad = v_grad + jnp.einsum(
        "hts,thd->shd", p_two, grad_cite, preferred_element_type=jnp.float32
    )
    src_rows = k_grad.shape[0]
    return (k_grad.reshape(src_rows, -1), v_grad.reshape(src_rows, -1), qf_grad, qc_grad)


def body(
    features,
    node_type,
    time_gap,
    node_valid,
    edge_codes,
    query_w,
    key_w,
    value_w,
    out_w,
    rel_att,
    rel_msg,
    rel_prior,
    skip_logit,
    rte_w,
    ln_gain,
    ln_bias,
    cotangent,
):
    tgt_rows, feat_dim = features.shape
    kind_count = query_w.shape[0]
    rel_count = rel_att.shape[0]
    head_count = rel_att.shape[1]
    head_size = rel_att.shape[2]
    n_blk = lax.axis_size("blk")
    my_blk = lax.axis_index("blk")
    type_hot = (node_type[:, None] == jnp.arange(kind_count)[None, :]).astype(jnp.float32)
    type_low = type_hot.astype(jnp.bfloat16)
    gap_hot = (time_gap[:, None] == jnp.arange(LEVELS)[None, :]).astype(jnp.float32)
    time_low = time_table(LEVELS, feat_dim).astype(jnp.bfloat16).astype(jnp.float32)
    rte_table = jnp.dot(time_low, rte_w.astype(jnp.float32), precision=HIGH)
    x_f = features.astype(jnp.float32)
    shifted = x_f + jnp.dot(gap_hot, rte_table, precision=HIGH)
    shifted_b = shifted.astype(jnp.bfloat16)

    def typed(inp, weights):
        parts = jnp.einsum("th,khd->tkd", inp, weights, preferred_element_type=jnp.float32)
        return jnp.sum(parts * type_hot[:, :, None], axis=1)

    def typed_grad(inp, grad_low):
        masked = inp[:, None, :] * type_low[:, :, None]
        return jnp.einsum("tkh,td->khd", masked, grad_low, preferred_element_type=jnp.float32)

    def typed_back(grad_low, weights):
        parts = jnp.einsum("td,khd->tkh", grad_low, weights, preferred_element_type=jnp.float32)
        return jnp.sum(parts * type_hot[:, :, None], axis=1)

    q_low = typed(features, query_w).astype(jnp.bfloat16)
    key_low = typed(shifted_b, key_w).astype(jnp.bfloat16)
    value_low = typed(shifted_b, value_w).astype(jnp.bfloat16)
    kind_low = node_type.astype(jnp.bfloat16)
    q_heads = q_low.reshape(tgt_rows, head_count, head_size).astype(jnp.float32)
    att_f = rel_att.astype(jnp.float32)
    factor = rel_prior / math.sqrt(head_size)
    rel_raw = jnp.einsum("thj,rhjk->rthk", q_heads, att_f, precision=HIGH)
    rel_query = (rel_raw * factor[:, None, :, None]).astype(jnp.bfloat16)
    select = jnp.einsum("tk,ksr->tsr", type_hot, jnp.asarray(relation_table()), precision=HIGH)
    select_low = select.astype(jnp.bfloat16)
    cite_hot = (jnp.arange(rel_count) == 3).astype(jnp.float32)
    q_four = (
        jnp.einsum("tsr,rthd->thsd", select_low, rel_query, preferred_element_type=jnp.float32)
        .astype(jnp.bfloat16)
        .reshape(tgt_rows, head_count, kind_count * head_size)
    )
    q_cite = rel_query[3]

    def block_codes(source):
        return lax.dynamic_slice_in_dim(edge_codes, source * tgt_rows, tgt_rows, 1)

    def forward_block(run_state, kv_blk, qf_part, qc_part, code_blk):
        result = attend_block(run_state, kv_blk, qf_part, qc_part, code_blk, kind_count)
        return result

    def backward_block(kv_blk, qf_part, qc_part, gf_part, gc_part, lse_part, delta_part, code_blk):
        return back_block(
            kv_blk, qf_part, qc_part, gf_part, gc_part, lse_part, delta_part, code_blk, kind_count
        )

    whole_kv = (key_low, value_low, kind_low)

    def forward_turn(step_idx, loop_state):
        run_state, kv_blk = loop_state
        run_state = forward_block(
            run_state, kv_blk, q_four, q_cite, block_codes((my_blk - step_idx) % n_blk)
        )
        kv_blk = from_behind((kv_blk[0], kv_blk[1], kv_blk[2]), "blk", 1)
        return (run_state, kv_blk)

    run_state, kv_last = lax.fori_loop(
        0,
        n_blk,
        forward_turn,
        (
            (
                jnp.full((head_count, tgt_rows), NEG_FILL, jnp.float32),
                jnp.zeros((head_count, tgt_rows), jnp.float32),
                jnp.zeros((tgt_rows, head_count, kind_count * head_size), jnp.float32),
                jnp.zeros((tgt_rows, head_count, head_size), jnp.float32),
            ),
            whole_kv,
        ),
    )
    run_max, run_sum, acc_four, acc_cite = run_state
    floor_sum = jnp.maximum(run_sum, 1.0)
    log_total = run_max + jnp.log(floor_sum)
    norm_t = floor_sum.T[:, :, None]
    u_four = acc_four / norm_t
    u_cite = acc_cite / norm_t
    u_rel = jnp.einsum(
        "tsr,thsd->rthd",
        select,
        u_four.reshape(tgt_rows, head_count, kind_count, head_size),
        precision=HIGH,
    )
    u_rel = u_rel + cite_hot[:, None, None, None] * u_cite[None]
    u_rel_b = u_rel.astype(jnp.bfloat16)
    agg_sum = jnp.einsum(
        "rthd,rhde->the", u_rel_b, rel_msg, preferred_element_type=jnp.float32
    ).reshape(tgt_rows, feat_dim)
    act_full, gelu_back = jax.vjp(jax.nn.gelu, agg_sum)
    act_low = act_full.astype(jnp.bfloat16)
    branch = typed(act_low, out_w)
    skip_all = jax.nn.sigmoid(skip_logit)
    skip_gate = jnp.sum(type_hot * skip_all[None, :], axis=1)[:, None]
    mixed_sum = skip_gate * branch + (1.0 - skip_gate) * x_f
    centered = mixed_sum - jnp.mean(mixed_sum, axis=1, keepdims=True)
    inv_std = lax.rsqrt(jnp.mean(centered * centered, axis=1, keepdims=True) + LN_EPS)
    normed = centered * inv_std
    valid_col = node_valid.astype(jnp.float32)[:, None]
    layer_out = (valid_col * (normed * ln_gain + ln_bias)).astype(jnp.bfloat16)
    grad_y = cotangent.astype(jnp.float32) * valid_col
    gain_grad = jnp.sum(grad_y * normed, axis=0)
    bias_grad = jnp.sum(grad_y, axis=0)
    grad_norm = grad_y * ln_gain
    grad_mix = inv_std * (
        grad_norm
        - jnp.mean(grad_norm, axis=1, keepdims=True)
        - normed * jnp.mean(grad_norm * normed, axis=1, keepdims=True)
    )
    grad_branch = (skip_gate * grad_mix).astype(jnp.bfloat16)
    gate_term = (
        jnp.sum(grad_mix * (branch - x_f), axis=1, keepdims=True) * skip_gate * (1.0 - skip_gate)
    )
    skip_grad = jnp.sum(type_hot * gate_term, axis=0)
    out_grad = typed_grad(act_low, grad_branch)
    grad_agg = gelu_back(typed_back(grad_branch, out_w))[0].astype(jnp.bfloat16)
    grad_agg_heads = grad_agg.reshape(tgt_rows, head_count, head_size)
    msg_grad = jnp.einsum(
        "rthd,the->rhde", u_rel_b, grad_agg_heads, preferred_element_type=jnp.float32
    )
    grad_urel = jnp.einsum(
        "the,rhde->rthd", grad_agg_heads, rel_msg, preferred_element_type=jnp.float32
    ).astype(jnp.bfloat16)
    grad_four = (
        jnp.einsum("tsr,rthd->thsd", select_low, grad_urel, preferred_element_type=jnp.float32)
        .astype(jnp.bfloat16)
        .reshape(tgt_rows, head_count, kind_count * head_size)
    )
    grad_cite = grad_urel[3]
    row_delta = (
        jnp.sum(grad_four.astype(jnp.float32) * u_four, axis=2)
        + jnp.sum(grad_cite.astype(jnp.float32) * u_cite, axis=2)
    ).T
    zero_four = jnp.zeros((tgt_rows, head_count, kind_count * head_size), jnp.float32)
    zero_cite = jnp.zeros((tgt_rows, head_count, head_size), jnp.float32)

    def back_turn(step_idx, loop_state):
        kv_blk, travel, acc_qf, acc_qc = loop_state
        k_grad, v_grad, qf_grad, qc_grad = backward_block(
            kv_blk,
            q_four,
            q_cite,
            grad_four,
            grad_cite,
            log_total,
            row_delta,
            block_codes((my_blk - step_idx) % n_blk),
        )
        travel = (
            from_behind((travel[0] + k_grad).astype(jnp.bfloat16), "blk", 1).astype(jnp.float32),
            from_behind((travel[1] + v_grad).astype(jnp.bfloat16), "blk", 1).astype(jnp.float32),
        )
        kv_blk = from_behind((kv_blk[0], kv_blk[1], kv_blk[2]), "blk", 1)
        return (kv_blk, travel, acc_qf + qf_grad, acc_qc + qc_grad)

    zero_kv = jnp.zeros((tgt_rows, feat_dim), jnp.float32)
    loop_state = lax.fori_loop(
        0, n_blk, back_turn, (whole_kv, (zero_kv, zero_kv), zero_four, zero_cite)
    )
    key_acc, value_acc = loop_state[1]
    acc_qf, acc_qc = (loop_state[2], loop_state[3])
    grad_key = key_acc.astype(jnp.bfloat16)
    grad_value = value_acc.astype(jnp.bfloat16)
    grad_relq = jnp.einsum(
        "tsr,thsd->rthd",
        select,
        acc_qf.reshape(tgt_rows, head_count, kind_count, head_size),
        precision=HIGH,
    )
    grad_relq = (
        (grad_relq + cite_hot[:, None, None, None] * acc_qc[None])
        .astype(jnp.bfloat16)
        .astype(jnp.float32)
    )
    prior_grad = jnp.sum(grad_relq * rel_raw, axis=(1, 3)) / math.sqrt(head_size)
    grad_raw = grad_relq * factor[:, None, :, None]
    att_grad = jnp.einsum("thj,rthk->rhjk", q_heads, grad_raw, precision=HIGH)
    grad_query = (
        jnp.einsum("rthk,rhjk->thj", grad_raw, att_f, precision=HIGH)
        .reshape(tgt_rows, feat_dim)
        .astype(jnp.bfloat16)
    )
    query_grad = typed_grad(features, grad_query)
    key_grad = typed_grad(shifted_b, grad_key)
    value_grad = typed_grad(shifted_b, grad_value)
    grad_shift = typed_back(grad_key, key_w) + typed_back(grad_value, value_w)
    table_grad = jnp.dot(gap_hot.T, grad_shift, precision=HIGH)
    rte_grad = jnp.dot(time_low.T, table_grad, precision=HIGH)
    input_grad = (
        (1.0 - skip_gate) * grad_mix + typed_back(grad_query, query_w) + grad_shift
    ).astype(jnp.bfloat16)
    summed = lax.psum(
        (
            query_grad,
            key_grad,
            value_grad,
            out_grad,
            att_grad,
            msg_grad,
            prior_grad,
            skip_grad,
            rte_grad,
            gain_grad,
            bias_grad,
        ),
        ("blk", "rep"),
    )
    return (
        layer_out,
        input_grad,
        summed[0],
        summed[1],
        summed[2],
        summed[3],
        summed[4],
        summed[5],
        summed[6],
        summed[7],
        summed[8],
        summed[9],
        summed[10],
    )


REL_TAB = relation_table()
HALF = 128
F32 = jnp.float32
LOW = jnp.bfloat16
VMEM_CAP = 65400 * 2**10
PROB_UNROLL = 2
GATHER_CUTS = 2


def nn(a, b):
    return lax.dot_general(a, b, (((1,), (0,)), ((), ())), preferred_element_type=F32)


def nt(a, b):
    return lax.dot_general(a, b, (((1,), (1,)), ((), ())), preferred_element_type=F32)


def tn(a, b):
    return lax.dot_general(a, b, (((0,), (0,)), ((), ())), preferred_element_type=F32)


def pick(kinds, kind, value):
    return jnp.where(kinds == kind, value, jnp.zeros_like(value))


def relation_of(kind, slot):
    hit = np.nonzero(REL_TAB[kind, slot])[0]
    return int(hit[0]) if len(hit) else None


def to_slots(rel_rows, kinds, kind_count):
    slots = []
    for slot in range(kind_count):
        rows = jnp.zeros(kinds.shape, F32)
        for kind in range(kind_count):
            rel = relation_of(kind, slot)
            if rel is not None:
                rows = jnp.where(kinds == kind, rel_rows(rel), rows)
        slots.append(rows)
    return slots, pick(kinds, 0, rel_rows(3))


def to_relations(slot_rows, cite_rows, kinds, kind_count, rel_count):
    out = []
    for rel in range(rel_count):
        if rel == 3:
            out.append(pick(kinds, 0, cite_rows))
            continue
        (kind, slot) = [
            (k, s) for k in range(kind_count) for s in range(kind_count) if relation_of(k, s) == rel
        ][0]
        out.append(pick(kinds, kind, slot_rows(slot)))
    return out


def flip(index, mask):
    return sum(((index // bit + mask // bit) % 2) * bit for bit in (1, 2, 4))


def gap_hot(gap_row, levels):
    gaps = jnp.broadcast_to(gap_row, (levels, gap_row.shape[1]))
    return (lax.broadcasted_iota(jnp.int32, gaps.shape, 0) == gaps).astype(F32).astype(LOW)


def remote(src, dst, sends, recvs, send_at, recv_at, device):
    return pltpu.make_async_remote_copy(
        src_ref=src,
        dst_ref=dst,
        send_sem=sends.at[send_at],
        recv_sem=recvs.at[recv_at],
        device_id=device,
        device_id_type=pl.DeviceIdType.MESH,
    )


def greet(device):
    pl.semaphore_signal(
        pltpu.get_barrier_semaphore(),
        inc=1,
        device_id=device,
        device_id_type=pl.DeviceIdType.MESH,
    )


def out_at(k, half):
    return (2 * k + half) * 256


def msg_at(half):
    return 2048 + half * 256


def key_at(k, half):
    return 2560 + 3072 * half + k * 256


def value_at(k, half):
    return 2560 + 3072 * half + (4 + k) * 256


def query_at(k, half):
    return 2560 + 3072 * half + (8 + k) * 256


def att_at(half):
    return 8704 + half * 256


SUM_PARTS = ((0, 2560, False), (2560, 3072, False), (5632, 2048, True), (7680, 1536, True))
SUM_TICKS = (
    ((0, 0, 1), (2, 0, 2), (3, 0, 3)),
    ((0, 0, 4), (0, 1, 1), (2, 0, 5), (2, 1, 2), (3, 0, 6), (3, 1, 3)),
)
SUM_NEXT = ((0, 7), (1, 4), (2, 1), (3, 1))
SUM_TAIL = ((0, 8), (1, 5), (2, 2), (3, 2), (1, 6), (2, 3), (3, 3), (1, 7), (2, 4), (3, 4), (1, 8), (2, 5), (3, 5), (2, 6), (3, 6))
GRAD_ROWS = 9216


def span(start, size):
    return pl.ds(start if isinstance(start, int) else pl.multiple_of(start, 16), size)


def summation(part, refs, places, pack):
    grads, full, core_in, plane_in, line_in, sends, recvs = refs
    (z, y, x, core), by_core, by_plane, by_z, by_y = places
    base, rows, at_once = SUM_PARTS[part]
    half, quarter, chunk = rows // 2, rows // 8, rows // 32
    count = iter(range(24 * part, 24 * part + 24))
    mine = base + core * half
    there_core = base + half - core * half
    spots = [(2 * x + y + step) % 4 for step in range(4)]
    plane_at = [mine + spot * quarter for spot in spots]
    own_x = mine + x * 2 * quarter
    other_x = mine + (1 - x) * 2 * quarter
    other_y = own_x + (1 - y) * quarter
    by_x = by_plane[1]
    line_at = [plane_at[0] + ((z + step) % 4) * chunk for step in range(4)]
    core_land, plane_land, line_land = base // 2, 3 * base // 8, 3 * base // 32
    pending = []

    def send(src, dst, device):
        at = next(count)

        def copy():
            return remote(src(), dst(), sends, recvs, at, at, device)

        copy().start()
        pending.append(copy)

    def settle():
        for copy in pending:
            copy().wait()
        pending.clear()

    def piece(ref, start, size):
        return lambda: ref.at[span(start, size), :]

    def small(ref, at):
        return lambda: ref.at[at]

    def load(ref, start, size):
        return ref[span(start, size), :].astype(F32)

    def add_in(start, size, *others):
        value = load(grads, start, size)
        for ref, at in others:
            value = value + load(ref, at, size)
        grads[span(start, size), :] = value.astype(LOW)

    def cores():
        send(piece(grads, there_core, half), piece(core_in, core_land, half), by_core)
        if pack:
            send(small(pack[0], 0), small(pack[1], 0), by_core)

    def plane():
        settle()
        for step in (2, 1, 3, 0):
            add_in(plane_at[step], quarter, (core_in, plane_at[step] - mine + core_land))
            if step:
                land = plane_land + (step - 1) * quarter
                send(
                    piece(grads, plane_at[step], quarter),
                    piece(plane_in, land, quarter),
                    by_plane[step - 1],
                )
        if pack:
            pack[0][1] = pack[0][0] + pack[1][0]
            for step in (1, 2, 3):
                send(small(pack[0], 1), small(pack[1], step), by_plane[step - 1])

    def along_x():
        settle()
        for start in (other_x, own_x):
            add_in(start, 2 * quarter, (core_in, start - mine + core_land))
            if start is other_x:
                send(
                    piece(grads, start, 2 * quarter),
                    piece(plane_in, plane_land, 2 * quarter),
                    by_x,
                )

    def along_y():
        settle()
        for start in (other_y, plane_at[0]):
            add_in(start, quarter, (plane_in, start - own_x + plane_land))
            if start is other_y:
                land = plane_land + 2 * quarter
                send(piece(grads, start, quarter), piece(plane_in, land, quarter), by_y)

    def line():
        settle()
        lands = range(3) if at_once else (2,)
        for step in (2, 3, 1, 0):
            within = line_at[step] - plane_at[0] + plane_land
            add_in(line_at[step], chunk, *[(plane_in, within + i * quarter) for i in lands])
            if step:
                land = line_land + (step - 1) * chunk
                send(
                    piece(grads, line_at[step], chunk),
                    piece(line_in, land, chunk),
                    by_z[step - 1],
                )
        if pack:
            pack[0][2] = pack[0][1] + pack[1][1] + pack[1][2] + pack[1][3]
            for step in (2, 3, 1):
                send(small(pack[0], 2), small(pack[1], 3 + step), by_z[step - 1])

    def share(start, size, device):
        send(piece(full, start, size), piece(full, start, size), device)

    def line_back():
        settle()
        value = load(grads, line_at[0], chunk)
        for step in range(3):
            value = value + load(line_in, line_land + step * chunk, chunk)
        full[span(line_at[0], chunk), :] = value.astype(LOW)
        for step in (2, 3, 1):
            share(line_at[0], chunk, by_z[step - 1])
        if pack:
            pack[2][...] = pack[0][2] + pack[1][4] + pack[1][5] + pack[1][6]

    def plane_back():
        settle()
        for step in (2, 1, 3):
            share(plane_at[0], quarter, by_plane[step - 1])

    def back_y():
        settle()
        share(plane_at[0], quarter, by_y)

    def back_x():
        settle()
        share(own_x, 2 * quarter, by_x)

    def cores_back():
        settle()
        share(mine, half, by_core)

    if at_once:
        return [cores, plane, line, line_back, plane_back, cores_back, settle]
    return [cores, along_x, along_y, line, line_back, back_y, back_x, cores_back, settle]


def layer_kernel(
    x_ref,
    kind_ref,
    gap_ref,
    valid_ref,
    rte_ref,
    time_ref,
    codes_hbm,
    cot_hbm,
    qw_hbm,
    kw_hbm,
    vw_hbm,
    ow_hbm,
    att_hbm,
    msg_hbm,
    prior_ref,
    skip_ref,
    gain_ref,
    bias_ref,
    out_ref,
    input_ref,
    full,
    small_ref,
    att_flat,
    att_ref,
    msg_ref,
    cot_ref,
    codes,
    qw,
    kw,
    vw,
    ow,
    msg_flat,
    shifted,
    xt,
    base,
    shift_out,
    plane_back,
    line_back,
    load_sem,
    gather_send,
    gather_recv,
    back_send,
    back_recv,
    grads,
    core_in,
    plane_in,
    line_in,
    pack,
    pack_in,
    sum_send,
    sum_recv,
    kt,
    vx,
    sbuf,
    probs,
    sm,
    qs,
    tails,
    qt2,
    qh,
    gt2,
    acc,
    two,
    agg,
    grad_even,
    grad_odd,
):
    rows, feat = x_ref.shape
    n_blk = shifted.shape[0]
    levels = time_ref.shape[1]
    kind_count = qw.shape[0]
    rel_count, heads, size = att_ref.shape[:3]
    group = heads // 2
    me = lax.axis_index("blk")
    rep = lax.axis_index("rep")
    z, y = me // 2, me % 2
    inner = ((z + 1) // 2) % 2
    by_y = (flip(me, 1), rep)
    by_core = (me, rep + 1 - 2 * (rep % 2))
    by_x = (me, rep + 2 - 4 * (rep // 2))
    for device in (by_y, by_core, by_x):
        greet(device)

    @pl.when(z < 3)
    def _():
        greet((me + 2, rep))

    @pl.when(z > 0)
    def _():
        greet((me - 2, rep))

    loads = [
        pltpu.make_async_copy(src, dst, load_sem.at[at])
        for at, (src, dst) in enumerate(
            (
                (att_hbm, att_ref),
                (msg_hbm, msg_ref),
                (kw_hbm, kw),
                (vw_hbm, vw),
                (qw_hbm, qw),
                (codes_hbm, codes),
                (ow_hbm, ow),
                (cot_hbm, cot_ref),
            )
        )
    ]

    x_f = x_ref[...].astype(F32).T
    x_t = x_f.astype(LOW)
    xt[...] = x_t
    table = tn(rte_ref[...], time_ref[...])
    table_hi = table.astype(LOW)
    table_lo = (table - table_hi.astype(F32)).astype(LOW)
    hot = gap_hot(gap_ref[...], levels)
    shifted[me, 0:feat, :] = (x_f + nn(table_hi, hot) + nn(table_lo, hot)).astype(LOW)
    shifted[me, feat:, :] = jnp.concatenate(
        [kind_ref[...].astype(F32), gap_ref[...].astype(F32), jnp.zeros((14, rows), F32)], axis=0
    ).astype(LOW)

    edges = [feat * c // GATHER_CUTS for c in range(GATHER_CUTS)] + [feat + 16]

    def move(block, cut, send_at, device):
        at = pl.ds(edges[cut], edges[cut + 1] - edges[cut])
        return remote(
            shifted.at[block, at, :],
            shifted.at[block, at, :],
            gather_send,
            gather_recv,
            send_at * GATHER_CUTS + cut,
            block * GATHER_CUTS + cut,
            device,
        )

    def other_z(n):
        order = ((1, 2, 1, 2), (2, 0, 3, 1), (3, 3, 0, 0))
        table = sum(row[i] * 4 ** (4 * r + i) for r, row in enumerate(order) for i in range(4))
        power = (1 + 3 * (z % 2)) * (1 + 15 * (z // 2)) * (1 + 255 * (n // 2)) * (1 + 255 * (n // 3))
        own = (3 - n) // 3
        return own * z + (1 - own) * ((table // power) % 4)

    def own_moves(act):
        for cut in range(GATHER_CUTS):

            @pl.when(z < 3)
            def _():
                act(move(me, cut, 0, (me + 2, rep)))

            @pl.when(z > 0)
            def _():
                act(move(me, cut, 1, (me - 2, rep)))

            act(move(me, cut, 2, by_y))

    def hand_on(n, act, wait):
        there = other_z(n)
        step = 2 * ((z - there + 3) // 4) - 1
        block = 2 * there + y
        for cut in range(GATHER_CUTS):
            if wait:
                move(block, cut, 0, by_y).wait_recv()
            act(move(block, cut, 2 + n, by_y))

            @pl.when((z + step >= 0) & (z + step <= 3))
            def _():
                act(move(block, cut, 5 + n, (me + 2 * step, rep)))

    pl.semaphore_wait(pltpu.get_barrier_semaphore(), 4 + inner)
    own_moves(lambda copy: copy.start())
    for load in loads:
        load.start()

    def source_row(j, row):
        return shifted[j, feat : feat + 16, :].astype(F32)[row : row + 1].astype(jnp.int32)

    kinds = jnp.broadcast_to(kind_ref[...], (size, rows))
    kinds_f = jnp.broadcast_to(kind_ref[...], (feat, rows))
    valid_f = jnp.broadcast_to(valid_ref[...], (feat, rows)).astype(F32)
    lane = lax.broadcasted_iota(jnp.int32, (rows, HALF), 1)
    ones_pad = (lax.broadcasted_iota(jnp.int32, (16, rows), 0) < 2).astype(F32).astype(LOW)
    scale = 1.0 / math.sqrt(size)

    def cols(j):
        return pl.ds(pl.multiple_of(j * rows, rows), rows)

    def store_part(start, value):
        grads[pl.ds(start, value.shape[0]), :] = value.astype(LOW)

    loads[0].wait()
    loads[1].wait()
    for r in range(rel_count):
        for h in range(heads):
            agg[h * size : (h + 1) * size, r * size : (r + 1) * size] = att_ref[r, h].astype(F32)
    att_flat[...] = agg[...].astype(LOW)
    for r in range(rel_count):
        for h in range(heads):
            agg[r * size : (r + 1) * size, h * size : (h + 1) * size] = msg_ref[r, h].astype(F32)
    msg_flat[...] = agg[...].T.astype(LOW)

    def turned(m, k):
        return probs.at[0, 2 * m + k // 2, pl.ds((k % 2) * feat, feat), :]

    for m, (load, ref) in enumerate(((loads[2], kw), (loads[3], vw))):
        load.wait()
        for k in range(kind_count):
            turned(m, k)[...] = ref[k].astype(F32).T.astype(LOW)

    loads[4].wait()
    q_full = jnp.zeros((feat, rows), F32)
    for k in range(kind_count):
        q_full = jnp.where(kinds_f == k, tn(qw[k], x_t), q_full)
    for h in range(heads):
        qh[h] = q_full[h * size : (h + 1) * size].astype(LOW)

    def head_rows(ref, h):
        return ref[pl.ds(pl.multiple_of(h * size, size), size), :]

    def query_head(h, carry):
        raw = tn(head_rows(att_flat, h), qh[h])

        def rel_rows(r):
            part = raw[r * size : (r + 1) * size] * (prior_ref[r, h] * scale)
            return part.astype(LOW).astype(F32)

        slots, cite = to_slots(rel_rows, kinds, kind_count)
        slot_t = jnp.concatenate(slots, axis=0)
        cite_t = jnp.concatenate([cite, jnp.zeros((HALF - size, rows), F32)], axis=0)
        qt2[h, :, 0:rows] = slot_t.astype(LOW)
        qt2[h, :, rows:] = cite_t.astype(LOW)
        qs[h, 0:rows, :] = slot_t.T.astype(LOW)
        qs[h, rows:, :] = cite_t.T.astype(LOW)
        return carry

    lax.fori_loop(0, heads, query_head, 0, unroll=2)
    loads[5].wait()
    acc[:, 0:rows, :] = jnp.full((heads, rows, HALF), NEG_FILL, F32)

    def keep_scores(h, j, both, second, edge):
        val = jnp.where(second, both[rows:], both[:rows])
        val = jnp.where(edge, val, NEG_FILL)
        if h < group:
            sbuf[j, pl.ds(h * rows, rows), :] = val
        else:
            high = val.astype(LOW)
            probs[j, h, 0:rows, :] = high
            probs[j, h, rows:, :] = (val - high.astype(F32)).astype(LOW)
        top = jnp.maximum(val[:, :HALF], val[:, HALF:])
        acc[h, 0:rows, :] = jnp.maximum(acc[h, 0:rows, :], top)

    def arrive(j):
        src = jnp.broadcast_to(source_row(j, 0), (size, rows))
        block = shifted[j, 0:feat, :]
        for k in range(kind_count):
            key = nn(turned(0, k)[...], block)
            value = nn(turned(1, k)[...], block)
            for h in range(heads):
                part = slice(h * size, (h + 1) * size)
                kt[j, h, pl.ds(k * size, size), :] = pick(src, k, key[part]).astype(LOW)
                vx[j, h, pl.ds(k * size, size), :] = pick(src, k, value[part]).astype(LOW)
        code = codes[:, cols(j)]
        second = code == 2
        edge = code > 0
        two[j] = second.astype(F32).astype(LOW)
        before = None
        for h in range(heads + 1):
            both = nn(qs[h], kt[j, h]) if h < heads else None
            if h > 0:
                keep_scores(h - 1, j, before, second, edge)
            before = both

    def start(copy):
        copy.start()

    def two_blocks(n, carry):
        there = other_z(n)

        def one(line, inside):
            block = 2 * there + (y + line) % 2

            @pl.when(line == 1)
            def _():
                @pl.when(n == 0)
                def _():
                    hand_on(1, start, True)

                @pl.when((n == 0) & (inner == 1))
                def _():
                    hand_on(2, start, True)

                @pl.when(n == 1)
                def _():
                    hand_on(2 + inner, start, True)

                @pl.when((n == 2) & (inner == 0))
                def _():
                    hand_on(3, start, True)

                for cut in range(GATHER_CUTS):
                    move(block, cut, 0, by_y).wait_recv()

            arrive(block)
            return inside

        return lax.fori_loop(0, 2, one, carry)

    lax.fori_loop(0, n_blk // 2, two_blocks, 0)
    own_moves(lambda copy: copy.wait_send())
    for n in range(1, n_blk // 2):
        hand_on(n, lambda copy: copy.wait_send(), False)

    def prob_block(h, j, top, kept):
        if kept:
            val = sbuf[j, pl.ds(pl.multiple_of(h * rows, rows), rows), :]
        else:
            val = probs[j, h, 0:rows, :].astype(F32) + probs[j, h, rows:, :].astype(F32)
        val = jnp.exp(val - top)
        low = val.astype(LOW)
        second = low * two[j]
        probs[j, h, 0:rows, :] = low - second
        probs[j, h, rows:, :] = second
        return val[:, :HALF] + val[:, HALF:], jnp.concatenate([low - second, second], axis=0)

    sm[...] = jnp.zeros((rows, HALF), F32)

    def prob_head(h, kept):
        top = jnp.max(acc[h, 0:rows, :], axis=1, keepdims=True)
        top = jnp.broadcast_to(jnp.maximum(top, 0.1 * NEG_FILL), (rows, rows))
        value_sum = None
        total = None
        for j in range(n_blk + 1):
            if j < n_blk:
                part, now = prob_block(h, j, top, kept)
                total = part if total is None else total + part
            if j > 0:
                part = nt(before, vx[j - 1, h])
                value_sum = part if value_sum is None else value_sum + part
            before = now
        acc[h] = value_sum
        total = jnp.sum(total, axis=1, keepdims=True)
        sm[...] = jnp.where(lane == h, jnp.broadcast_to(total, (rows, HALF)), sm[...])

    for kept in (True, False):

        def prob_pair(pair, carry, kept=kept):
            for u in range(PROB_UNROLL):
                prob_head((0 if kept else group) + PROB_UNROLL * pair + u, kept)
            return carry

        lax.fori_loop(0, group // PROB_UNROLL, prob_pair, 0)

    inverse = 1.0 / jnp.maximum(sm[...].T, 1.0)
    sm[0:heads, :] = inverse[0:heads, 0:HALF]
    sm[heads : 2 * heads, :] = inverse[0:heads, HALF:]

    def inv_row(h, count):
        row = jnp.concatenate([sm[pl.ds(h, 1), :], sm[pl.ds(heads + h, 1), :]], axis=1)
        return jnp.broadcast_to(row, (count, rows))

    def rel_part(h):
        return sbuf[h // group, pl.ds((h % group) * feat, feat), :].astype(LOW)

    for h in range(heads):
        inv = inv_row(h, HALF)
        u_turned = acc[h].T
        u_slot = u_turned[:, 0:rows] * inv
        u_cite = u_turned[0:size, rows:] * inv[0:size]
        sbuf[2 + h // group, pl.ds((h % group) * feat, HALF), :] = u_slot
        sbuf[2 + h // group, pl.ds((h % group) * feat + HALF, size), :] = u_cite
        rel = to_relations(
            lambda s: u_slot[s * size : (s + 1) * size], u_cite, kinds, kind_count, rel_count
        )
        rel = jnp.concatenate(rel, axis=0)
        sbuf[h // group, pl.ds((h % group) * feat, feat), :] = rel
        agg[pl.ds(h * size, size), :] = nn(head_rows(msg_flat, h), rel.astype(LOW))
    loads[6].wait()
    loads[7].wait()
    agg_t = agg[...]
    slope = 0.7978845608028654
    inner = jnp.tanh(slope * (agg_t + 0.044715 * agg_t * agg_t * agg_t))
    act_t = (0.5 * agg_t * (1.0 + inner)).astype(LOW)
    gelu_back = 0.5 * (1.0 + inner) + 0.5 * agg_t * (1.0 - inner * inner) * slope * (
        1.0 + 3.0 * 0.044715 * agg_t * agg_t
    )
    skip = jnp.zeros((1, rows), F32)
    branch = jnp.zeros((feat, rows), F32)
    for k in range(kind_count):
        skip = jnp.where(kinds[0:1] == k, skip_ref[k], skip)
        branch = jnp.where(kinds_f == k, tn(ow[k], act_t), branch)
    gate_row = 1.0 / (1.0 + jnp.exp(-skip))
    gate = jnp.broadcast_to(gate_row, (feat, rows))
    mixed = gate * branch + (1.0 - gate) * x_f
    centered = mixed - jnp.mean(mixed, axis=0, keepdims=True)
    inv_std = lax.rsqrt(jnp.mean(centered * centered, axis=0, keepdims=True) + LN_EPS)
    normed = centered * inv_std
    affine = jnp.concatenate([gain_ref[...], bias_ref[...], jnp.zeros((HALF - 2, feat), F32)], axis=0).T
    gain = jnp.broadcast_to(affine[:, 0:1], (feat, rows))
    bias = jnp.broadcast_to(affine[:, 1:2], (feat, rows))
    out_ref[...] = (valid_f * (normed * gain + bias)).T.astype(LOW)
    grad_y = cot_ref[...].astype(F32).T * valid_f
    gain_col = jnp.sum(grad_y * normed, axis=1, keepdims=True)
    bias_col = jnp.sum(grad_y, axis=1, keepdims=True)
    grad_norm = grad_y * gain
    grad_mix = inv_std * (
        grad_norm
        - jnp.mean(grad_norm, axis=0, keepdims=True)
        - normed * jnp.mean(grad_norm * normed, axis=0, keepdims=True)
    )
    skip_row = (
        jnp.sum(grad_mix * (branch - x_f), axis=0, keepdims=True) * gate_row * (1.0 - gate_row)
    )
    base[...] = (1.0 - gate) * grad_mix
    grad_branch = gate * grad_mix
    grad_act = jnp.zeros((feat, rows), F32)
    for k in range(kind_count):
        masked = pick(kinds_f, k, grad_branch).astype(LOW)
        out_grad = nt(act_t, masked)
        store_part(out_at(k, 0), out_grad[:, :HALF])
        store_part(out_at(k, 1), out_grad[:, HALF:])
        grad_act = grad_act + nn(ow[k], masked)
    agg[...] = gelu_back * grad_act

    for h in range(heads):
        grad_agg = agg[pl.ds(h * size, size), :].astype(LOW)
        msg_grad = nt(grad_agg, rel_part(h))
        store_part(msg_at(0) + h * size, msg_grad[:, :HALF])
        store_part(msg_at(1) + h * size, msg_grad[:, HALF:])
        inv = inv_row(h, size)
        grad_u = tn(head_rows(msg_flat, h), grad_agg)

        def rel_rows(r):
            return grad_u[r * size : (r + 1) * size] * inv

        slots, cite = to_slots(rel_rows, kinds, kind_count)
        slot_t = jnp.concatenate(slots, axis=0).astype(LOW)
        cite_t = jnp.concatenate([cite, jnp.zeros((HALF - size, rows), F32)], axis=0).astype(LOW)
        gt2[h, :, 0:rows] = slot_t
        gt2[h, :, rows:] = cite_t
        slot_f = slot_t.astype(F32)
        cite_f = cite_t.astype(F32)
        u_at = (h % group) * feat
        delta = -(
            jnp.sum(slot_f * sbuf[2 + h // group, pl.ds(u_at, HALF), :], axis=0, keepdims=True)
            + jnp.sum(
                cite_f[0:size] * sbuf[2 + h // group, pl.ds(u_at + HALF, size), :],
                axis=0,
                keepdims=True,
            )
        )
        delta_hi = delta.astype(LOW).astype(F32)
        tail = jnp.concatenate(
            [delta_hi, delta - delta_hi, jnp.zeros((HALF - 2, rows), F32)], axis=0
        )
        tail_t = tail.T.astype(LOW)
        qs[h, 0:rows, :] = slot_f.T.astype(LOW)
        qs[h, rows:, :] = cite_f.T.astype(LOW)
        tails[h] = tail_t[:, 0:16]
        acc[h] = jnp.zeros(acc.shape[1:], F32)

    refs = (grads, full, core_in, plane_in, line_in, sum_send, sum_recv)
    by_z = [(((me // 2 + step) % 4) * 2 + me % 2, rep) for step in (1, 2, 3)]
    spots = [(2 * (rep // 2) + y + step) % 4 for step in (1, 2, 3)]
    by_plane = [(2 * z + spot % 2, 2 * (spot // 2) + rep % 2) for spot in spots]
    places = ((z, y, rep // 2, rep % 2), by_core, by_plane, by_z, by_y)
    sums = [summation(part, refs, places, None) for part in range(3)]
    sums.append(summation(3, refs, places, (pack, pack_in, small_ref)))
    sums[0][0]()

    slot_id = lax.broadcasted_iota(jnp.int32, (HALF, rows), 0) // size
    pack[0] = jnp.zeros(pack.shape[1:], F32)

    def along_y(m):
        return remote(
            shift_out.at[flip(me, m + 1)],
            plane_back.at[m // 2],
            back_send,
            back_recv,
            m // 2,
            m // 2,
            by_y,
        )

    def along_z(m):
        at = n_blk // 2 + m // 2
        return remote(
            shift_out.at[flip(me, m)],
            line_back.at[m // 2],
            back_send,
            back_recv,
            at,
            at,
            (flip(me, m), rep),
        )

    def pass_on(m):
        along_y(m).wait_recv()
        j = flip(me, m)
        total = shift_out[j].astype(F32) + plane_back[m // 2].astype(F32)
        shift_out[j] = total.astype(LOW)
        along_z(m).start()

    grad_bufs = (grad_even, grad_odd)
    for g in range(2):
        half = slice(g * HALF, (g + 1) * HALF)

        def block_pair(pair, carry, g=g, half=half):
            m = n_blk - 2 - 2 * pair
            blocks = (flip(me, m + 1), flip(me, m))
            owns = [slot_id == jnp.broadcast_to(source_row(j, 0), (HALF, rows)) for j in blocks]

            def keep(at, u, kind, part):
                for k in range(kind_count):
                    start = (2 * k + kind) * HALF + u * size
                    sbuf[blocks[at], pl.ds(start, size), :] = part[k * size : (k + 1) * size]

            def score_part(at, u):
                h = g * group + u
                both = jnp.concatenate([tails[h], tails[h]], axis=0)
                left = jnp.concatenate([qs[h], both], axis=1)
                right = jnp.concatenate([vx[blocks[at], h], ones_pad], axis=0)
                grad_bufs[u % 2][:, at * rows : (at + 1) * rows] = probs[blocks[at], h] * nn(
                    left, right
                ).astype(LOW)
                keep(at, u, 1, jnp.where(owns[at], nn(gt2[h], probs[blocks[at], h]), 0.0))

            def key_part(at, u):
                h = g * group + u
                grad = grad_bufs[u % 2][:, at * rows : (at + 1) * rows]
                keep(at, u, 0, jnp.where(owns[at], nn(qt2[h], grad), 0.0))
                if at == 1:
                    keys = jnp.concatenate([kt[j, h] for j in blocks], axis=1)
                    acc[h] = acc[h] + nt(grad_bufs[u % 2][...], keys)

            units = [(at, u) for u in range(group) for at in range(2)]
            for i in range(len(units) + 2):
                if i < len(units):
                    score_part(*units[i])
                if i > 1:
                    key_part(*units[i - 2])
            for at in range(2):
                j = blocks[at]
                total = None
                for k in range(kind_count):
                    weights = jnp.concatenate([kw[k, :, half], vw[k, :, half]], axis=1)
                    part = nn(weights, sbuf[j, pl.ds(k * feat, feat), :].astype(LOW))
                    total = part if total is None else total + part
                if g == 1:
                    total = total + shift_out[j].astype(F32)
                low = total.astype(LOW)
                shift_out[j] = low
                if g == 1:
                    gaps = gap_hot(source_row(j, 1), levels)
                    pack[0, 0:levels, :] = pack[0, 0:levels, :] + nt(gaps, low)
                    if at == 0:
                        along_y(m).start()
            if g == 1:

                @pl.when(pair > 0)
                def _():
                    pass_on(m + 2)

            for when, part, step in SUM_TICKS[g]:

                @pl.when(pair == when)
                def _(part=part, step=step):
                    sums[part][step]()

            return carry

        lax.fori_loop(0, n_blk // 2, block_pair, 0)

        for k in range(kind_count):
            total = None
            for j in range(n_blk):
                part = nt(shifted[j, 0:feat, :], sbuf[j, pl.ds(k * feat, feat), :].astype(LOW))
                total = part if total is None else total + part
            store_part(key_at(k, g), total[:, :HALF])
            store_part(value_at(k, g), total[:, HALF:])
        if g == 1:
            sums[2][0]()
        grad_q = []
        for h in range(g * group, (g + 1) * group):
            slot = acc[h].T
            rel = to_relations(
                lambda s: slot[s * size : (s + 1) * size, 0:rows],
                slot[0:size, rows:],
                kinds,
                kind_count,
                rel_count,
            )
            rel = [part.astype(LOW) for part in rel]
            att_grad = nt(qh[h], jnp.concatenate(rel, axis=0))
            store_part(att_at(0) + h * size, att_grad[:, :HALF])
            store_part(att_at(1) + h * size, att_grad[:, HALF:])
            raw = [
                (part.astype(F32) * (prior_ref[r, h] * scale)).astype(LOW)
                for r, part in enumerate(rel)
            ]
            grad_q.append(nn(head_rows(att_flat, h), jnp.concatenate(raw, axis=0)))
        grad_q = jnp.concatenate(grad_q, axis=0).astype(LOW).astype(F32)
        total = base[...]
        for k in range(kind_count):
            masked = pick(kinds_f[0:HALF], k, grad_q).astype(LOW)
            store_part(query_at(k, g), nt(xt[...], masked))
            total = total + nn(qw[k, :, half], masked)
        base[...] = total
        if g == 0:
            sums[1][0]()

    pair = jnp.where(
        lane == 0,
        jnp.broadcast_to(gain_col, (feat, HALF)),
        jnp.where(lane == 1, jnp.broadcast_to(bias_col, (feat, HALF)), 0.0),
    ).T
    spot = lax.broadcasted_iota(jnp.int32, (1, rows), 1)
    skips = jnp.zeros((1, rows), F32)
    for k in range(kind_count):
        skips = jnp.where(
            spot == k, jnp.sum(pick(kinds[0:1], k, skip_row), axis=1, keepdims=True), skips
        )
    pack[0, levels : levels + 8, :] = jnp.concatenate(
        [pair[0:2], skips, jnp.zeros((5, rows), F32)], axis=0
    )
    sums[3][0]()
    for part, step in SUM_NEXT:
        sums[part][step]()
    along_y(0).wait_recv()
    total = base[...] + shift_out[me].astype(F32) + plane_back[0].astype(F32)
    for m in (2, 4, 6):
        along_z(m).wait_recv()
        total = total + line_back[m // 2].astype(F32)
    input_ref[...] = total.T.astype(LOW)
    for part, step in SUM_TAIL:
        sums[part][step]()
    for m in (0, 2, 4, 6):
        along_y(m).wait_send()
        if m > 0:
            along_z(m).wait_send()


def finish_kernel(
    full,
    small_ref,
    att_flat,
    time_ref,
    prior_ref,
    out_in,
    input_in,
    out_ref,
    input_ref,
    qg_ref,
    kg_ref,
    vg_ref,
    og_ref,
    attg_ref,
    msgg_ref,
    priorg_ref,
    skip_ref,
    rte_ref,
    gain_ref,
    bias_ref,
):
    out_ref[...] = out_in[...]
    input_ref[...] = input_in[...]
    kind_count, feat = qg_ref.shape[:2]
    rel_count, heads, width = attg_ref.shape[:3]
    scale = 1.0 / math.sqrt(width)

    def part(start):
        return full[pl.ds(start, feat), :].astype(F32)

    for ref, at in ((qg_ref, query_at), (kg_ref, key_at), (vg_ref, value_at), (og_ref, out_at)):
        for k in range(kind_count):
            for half in range(2):
                ref[k, :, half * HALF : (half + 1) * HALF] = part(at(k, half))
    att = jnp.concatenate([part(att_at(0)), part(att_at(1))], axis=1)
    msg = jnp.concatenate([part(msg_at(0)), part(msg_at(1))], axis=1).T
    for r in range(rel_count):
        for h in range(heads):
            block = (slice(h * width, (h + 1) * width), slice(r * width, (r + 1) * width))
            attg_ref[r, h] = att[block] * (prior_ref[r, h] * scale)
            msgg_ref[r, h] = msg[block[::-1]]
    prod = (att * att_flat[...].astype(F32)).reshape(heads, width, feat)
    prod = jnp.sum(prod, axis=1)
    spread = (
        lax.broadcasted_iota(jnp.int32, (feat, rel_count), 0) // width
        == lax.broadcasted_iota(jnp.int32, (feat, rel_count), 1)
    ).astype(F32).astype(LOW)
    prior = jnp.zeros((rel_count, heads), F32)
    for _ in range(3):
        low = prod.astype(LOW)
        prior = prior + lax.dot_general(
            spread, low, (((0,), (1,)), ((), ())), preferred_element_type=F32
        )
        prod = prod - low.astype(F32)
    priorg_ref[...] = prior * scale
    levels = time_ref.shape[1]
    small = small_ref[...]
    rte = jnp.zeros(rte_ref.shape, F32)
    rest = small[0:levels]
    for _ in range(3):
        low = rest.astype(LOW)
        rte = rte + nn(time_ref[...], low)
        rest = rest - low.astype(F32)
    rte_ref[...] = rte
    gain_ref[...] = small[levels : levels + 1]
    bias_ref[...] = small[levels + 1 : levels + 2]
    skip_ref[...] = small[levels + 2 : levels + 3, 0:kind_count]


def layer_call(n_blk, *args):
    rows, feat = args[0].shape
    kind_count = args[8].shape[0]
    rel_count, heads, size = args[12].shape[:3]
    vmem = pl.BlockSpec(memory_space=pltpu.VMEM)
    smem = pl.BlockSpec(memory_space=pltpu.SMEM)
    hbm = pl.BlockSpec(memory_space=pl.ANY)
    square = (feat, feat)
    weight = pltpu.VMEM((kind_count,) + square, LOW)

    def shape(dims, kind):
        return jax.ShapeDtypeStruct(dims, kind)

    return pl.pallas_call(
        layer_kernel,
        out_shape=[
            shape((rows, feat), LOW),
            shape((rows, feat), LOW),
            shape((GRAD_ROWS, HALF), LOW),
            shape((LEVELS + 8, feat), F32),
            shape(square, LOW),
        ],
        in_specs=[vmem] * 6 + [hbm] * 8 + [smem] * 2 + [vmem] * 2,
        out_specs=[vmem] * 5,
        scratch_shapes=[
            pltpu.VMEM((rel_count, heads, size, size), LOW),
            pltpu.VMEM((rel_count, heads, size, size), LOW),
            pltpu.VMEM((rows, feat), LOW),
            pltpu.VMEM((rows, n_blk * rows), jnp.int32),
            weight,
            weight,
            weight,
            weight,
            pltpu.VMEM(square, LOW),
            pltpu.VMEM((n_blk, feat + 16, rows), LOW),
            pltpu.VMEM((feat, rows), LOW),
            pltpu.VMEM((feat, rows), F32),
            pltpu.VMEM((n_blk, feat, rows), LOW),
            pltpu.VMEM((n_blk // 2, feat, rows), LOW),
            pltpu.VMEM((n_blk // 2, feat, rows), LOW),
            pltpu.SemaphoreType.DMA((8,)),
            pltpu.SemaphoreType.DMA((9 * GATHER_CUTS,)),
            pltpu.SemaphoreType.DMA((n_blk * GATHER_CUTS,)),
            pltpu.SemaphoreType.DMA((n_blk,)),
            pltpu.SemaphoreType.DMA((n_blk,)),
            pltpu.VMEM((GRAD_ROWS, HALF), LOW),
            pltpu.VMEM((GRAD_ROWS // 2, HALF), LOW),
            pltpu.VMEM((3 * GRAD_ROWS // 8, HALF), LOW),
            pltpu.VMEM((3 * GRAD_ROWS // 32, HALF), LOW),
            pltpu.VMEM((3, LEVELS + 8, feat), F32),
            pltpu.VMEM((7, LEVELS + 8, feat), F32),
            pltpu.SemaphoreType.DMA((96,)),
            pltpu.SemaphoreType.DMA((96,)),
            pltpu.VMEM((n_blk, heads, HALF, rows), LOW),
            pltpu.VMEM((n_blk, heads, HALF, rows), LOW),
            pltpu.VMEM((n_blk, heads // 2 * rows, rows), F32),
            pltpu.VMEM((n_blk, heads, 2 * rows, rows), LOW),
            pltpu.VMEM((rows, HALF), F32),
            pltpu.VMEM((heads, 2 * rows, HALF), LOW),
            pltpu.VMEM((heads, rows, 16), LOW),
            pltpu.VMEM((heads, HALF, 2 * rows), LOW),
            pltpu.VMEM((heads, size, rows), LOW),
            pltpu.VMEM((heads, HALF, 2 * rows), LOW),
            pltpu.VMEM((heads, 2 * rows, HALF), F32),
            pltpu.VMEM((n_blk, rows, rows), LOW),
            pltpu.VMEM(square, F32),
            pltpu.VMEM((2 * rows, 2 * rows), LOW),
            pltpu.VMEM((2 * rows, 2 * rows), LOW),
        ],
        compiler_params=pltpu.CompilerParams(
            vmem_limit_bytes=VMEM_CAP, collective_id=0, has_side_effects=True
        ),
        name="layer",
    )(*args)


def time_columns(level_count, feat_width):
    positions = np.arange(level_count, dtype=np.float32)[:, None]
    steps = np.arange(feat_width // 2, dtype=np.float32)[None, :]
    phases = positions / np.power(np.float32(10000.0), np.float32(2.0) * steps / feat_width)
    table = np.stack([np.sin(phases), np.cos(phases)], axis=2).reshape(level_count, feat_width)
    return jnp.asarray(np.ascontiguousarray(table.T), LOW)


def fast_body(
    features,
    node_type,
    time_gap,
    node_valid,
    edge_codes,
    query_w,
    key_w,
    value_w,
    out_w,
    rel_att,
    rel_msg,
    rel_prior,
    skip_logit,
    rte_w,
    ln_gain,
    ln_bias,
    cotangent,
):
    rows, feat = features.shape
    n_blk = lax.axis_size("blk")
    kind_count = query_w.shape[0]
    time_low = time_columns(LEVELS, feat)
    vmem = pl.BlockSpec(memory_space=pltpu.VMEM)
    smem = pl.BlockSpec(memory_space=pltpu.SMEM)
    square = (feat, feat)

    def shape(dims, kind):
        return jax.ShapeDtypeStruct(dims, kind)

    layer_out, input_grad, full, small, att_flat = layer_call(
        n_blk,
        features,
        node_type[None],
        time_gap[None],
        node_valid[None],
        rte_w,
        time_low,
        edge_codes,
        cotangent,
        query_w,
        key_w,
        value_w,
        out_w,
        rel_att,
        rel_msg,
        rel_prior,
        skip_logit,
        ln_gain[None],
        ln_bias[None],
    )
    outs = pl.pallas_call(
        finish_kernel,
        out_shape=[shape(layer_out.shape, LOW), shape(input_grad.shape, LOW)]
        + [shape((kind_count,) + square, F32)] * 4
        + [shape(rel_att.shape, F32)] * 2
        + [
            shape(rel_prior.shape, F32),
            shape((1, kind_count), F32),
            shape(square, F32),
            shape((1, feat), F32),
            shape((1, feat), F32),
        ],
        in_specs=[vmem] * 4 + [smem] + [vmem] * 2,
        out_specs=[vmem] * 13,
        compiler_params=pltpu.CompilerParams(vmem_limit_bytes=VMEM_CAP),
        name="finish",
    )(full, small, att_flat, time_low, rel_prior, layer_out, input_grad)
    return (*outs[:9], outs[9][0], outs[10], outs[11][0], outs[12][0])


def solution(mesh):
    in_specs = (
        P(("blk", "rep"), None),
        P(("blk", "rep")),
        P(("blk", "rep")),
        P(("blk", "rep")),
        P(("blk", "rep"), None),
        P(),
        P(),
        P(),
        P(),
        P(),
        P(),
        P(),
        P(),
        P(),
        P(),
        P(),
        P(("blk", "rep"), None),
    )
    out_specs = (
        P(("blk", "rep"), None),
        P(("blk", "rep"), None),
        P(),
        P(),
        P(),
        P(),
        P(),
        P(),
        P(),
        P(),
        P(),
        P(),
        P(),
    )
    plan = fast_body if tuple(mesh.shape.values()) == (8, 4) else body
    return jax.shard_map(plan, mesh=mesh, in_specs=in_specs, out_specs=out_specs, check_vma=False)
```

```python
import math

import jax
import jax.numpy as jnp
import numpy as np
from jax import lax
from jax.experimental import pallas as pl
from jax.experimental.pallas import tpu as pltpu
from jax.sharding import PartitionSpec as P

LEVELS = 16


NEG_FILL = -1e30
LOG2_E = 1.4426950408889634
LN_EPS = 1e-05
HIGH = lax.Precision.HIGHEST


def from_behind(block, axis, distance):
    devices = range(lax.axis_size(axis))
    route = [((i - distance) % len(devices), i) for i in devices]
    return lax.ppermute(block, axis, route)


def relation_table():
    rel_tab = np.zeros((4, 4, 8), np.float32)
    rel_tab[0, 1, 0] = 1.0
    rel_tab[1, 0, 1] = 1.0
    rel_tab[0, 0, 2] = 1.0
    rel_tab[2, 0, 4] = 1.0
    rel_tab[0, 2, 5] = 1.0
    rel_tab[3, 1, 6] = 1.0
    rel_tab[1, 3, 7] = 1.0
    return rel_tab


def time_table(level_count, feat_width):
    positions = jnp.arange(level_count, dtype=jnp.float32)[:, None]
    freq_idx = jnp.arange(feat_width // 2, dtype=jnp.float32)[None, :]
    phases = positions / jnp.power(10000.0, 2.0 * freq_idx / feat_width)
    return jnp.stack([jnp.sin(phases), jnp.cos(phases)], axis=2).reshape(level_count, feat_width)


def slot_spread(heads_arr, kind_hot):
    spread_out = heads_arr[:, :, None, :] * kind_hot[:, None, :, None]
    return spread_out.reshape(heads_arr.shape[0], heads_arr.shape[1], -1)


def slot_collapse(slot_arr, kind_hot):
    src_rows, head_count = (slot_arr.shape[0], slot_arr.shape[1])
    kind_count = kind_hot.shape[1]
    shaped = slot_arr.reshape(src_rows, head_count, kind_count, -1)
    return jnp.sum(shaped * kind_hot.astype(jnp.float32)[:, None, :, None], axis=2)


def block_scores(kv_blk, q_four, q_cite, code_blk, kind_count):
    key_blk, value_blk, kind_blk = kv_blk
    src_rows = key_blk.shape[0]
    head_count = q_four.shape[1]
    key_heads = key_blk.reshape(src_rows, head_count, -1)
    value_heads = value_blk.reshape(src_rows, head_count, -1)
    kind_hot = (kind_blk[:, None] == jnp.arange(kind_count).astype(jnp.bfloat16)[None, :]).astype(
        jnp.bfloat16
    )
    key_four = slot_spread(key_heads, kind_hot)
    value_four = slot_spread(value_heads, kind_hot)
    is_one = (code_blk == 1)[None]
    is_two = (code_blk == 2)[None]
    slot_dot = jnp.einsum("thc,shc->hts", q_four, key_four, preferred_element_type=jnp.float32)
    cite_dot = jnp.einsum("thd,shd->hts", q_cite, key_heads, preferred_element_type=jnp.float32)
    scores = jnp.where(is_one, slot_dot, jnp.where(is_two, cite_dot, NEG_FILL))
    return (scores, is_one, is_two, key_heads, value_heads, key_four, value_four, kind_hot)


def attend_block(run_state, kv_blk, q_four, q_cite, code_blk, kind_count):
    run_max, run_sum, acc_four, acc_cite = run_state
    scores, is_one, is_two, key_heads, value_heads, key_four, value_four, kind_hot = block_scores(
        kv_blk, q_four, q_cite, code_blk, kind_count
    )
    new_max = jnp.maximum(run_max, jnp.max(scores, axis=2))
    expd = jnp.where((code_blk > 0)[None], jnp.exp(scores - new_max[:, :, None]), 0.0)
    rescale = jnp.exp(run_max - new_max)
    run_sum = run_sum * rescale + jnp.sum(expd, axis=2)
    prob_low = expd.astype(jnp.bfloat16)
    zero_low = jnp.zeros_like(prob_low)
    p_one = jnp.where(is_one, prob_low, zero_low)
    p_two = jnp.where(is_two, prob_low, zero_low)
    rescale_t = rescale.T[:, :, None]
    acc_four = acc_four * rescale_t + jnp.einsum(
        "hts,shc->thc", p_one, value_four, preferred_element_type=jnp.float32
    )
    acc_cite = acc_cite * rescale_t + jnp.einsum(
        "hts,shd->thd", p_two, value_heads, preferred_element_type=jnp.float32
    )
    return (new_max, run_sum, acc_four, acc_cite)


def back_block(
    kv_blk, q_four, q_cite, grad_four, grad_cite, log_total, row_delta, code_blk, kind_count
):
    scores, is_one, is_two, key_heads, value_heads, key_four, value_four, kind_hot = block_scores(
        kv_blk, q_four, q_cite, code_blk, kind_count
    )
    prob_full = jnp.where((code_blk > 0)[None], jnp.exp(scores - log_total[:, :, None]), 0.0)
    prob_low = prob_full.astype(jnp.bfloat16)
    zero_low = jnp.zeros_like(prob_low)
    p_one = jnp.where(is_one, prob_low, zero_low)
    p_two = jnp.where(is_two, prob_low, zero_low)
    grad_slot = jnp.einsum(
        "thc,shc->hts", grad_four, value_four, preferred_element_type=jnp.float32
    )
    grad_other = jnp.einsum(
        "thd,shd->hts", grad_cite, value_heads, preferred_element_type=jnp.float32
    )
    grad_probs = jnp.where(is_one, grad_slot, jnp.where(is_two, grad_other, 0.0))
    grad_scores = (prob_full * (grad_probs - row_delta[:, :, None])).astype(jnp.bfloat16)
    d_one = jnp.where(is_one, grad_scores, zero_low)
    d_two = jnp.where(is_two, grad_scores, zero_low)
    qf_grad = jnp.einsum("hts,shc->thc", d_one, key_four, preferred_element_type=jnp.float32)
    qc_grad = jnp.einsum("hts,shd->thd", d_two, key_heads, preferred_element_type=jnp.float32)
    k_grad = slot_collapse(
        jnp.einsum("hts,thc->shc", d_one, q_four, preferred_element_type=jnp.float32), kind_hot
    )
    k_grad = k_grad + jnp.einsum("hts,thd->shd", d_two, q_cite, preferred_element_type=jnp.float32)
    v_grad = slot_collapse(
        jnp.einsum("hts,thc->shc", p_one, grad_four, preferred_element_type=jnp.float32), kind_hot
    )
    v_grad = v_grad + jnp.einsum(
        "hts,thd->shd", p_two, grad_cite, preferred_element_type=jnp.float32
    )
    src_rows = k_grad.shape[0]
    return (k_grad.reshape(src_rows, -1), v_grad.reshape(src_rows, -1), qf_grad, qc_grad)


def body(
    features,
    node_type,
    time_gap,
    node_valid,
    edge_codes,
    query_w,
    key_w,
    value_w,
    out_w,
    rel_att,
    rel_msg,
    rel_prior,
    skip_logit,
    rte_w,
    ln_gain,
    ln_bias,
    cotangent,
):
    tgt_rows, feat_dim = features.shape
    kind_count = query_w.shape[0]
    rel_count = rel_att.shape[0]
    head_count = rel_att.shape[1]
    head_size = rel_att.shape[2]
    n_blk = lax.axis_size("blk")
    my_blk = lax.axis_index("blk")
    type_hot = (node_type[:, None] == jnp.arange(kind_count)[None, :]).astype(jnp.float32)
    type_low = type_hot.astype(jnp.bfloat16)
    gap_hot = (time_gap[:, None] == jnp.arange(LEVELS)[None, :]).astype(jnp.float32)
    time_low = time_table(LEVELS, feat_dim).astype(jnp.bfloat16).astype(jnp.float32)
    rte_table = jnp.dot(time_low, rte_w.astype(jnp.float32), precision=HIGH)
    x_f = features.astype(jnp.float32)
    shifted = x_f + jnp.dot(gap_hot, rte_table, precision=HIGH)
    shifted_b = shifted.astype(jnp.bfloat16)

    def typed(inp, weights):
        parts = jnp.einsum("th,khd->tkd", inp, weights, preferred_element_type=jnp.float32)
        return jnp.sum(parts * type_hot[:, :, None], axis=1)

    def typed_grad(inp, grad_low):
        masked = inp[:, None, :] * type_low[:, :, None]
        return jnp.einsum("tkh,td->khd", masked, grad_low, preferred_element_type=jnp.float32)

    def typed_back(grad_low, weights):
        parts = jnp.einsum("td,khd->tkh", grad_low, weights, preferred_element_type=jnp.float32)
        return jnp.sum(parts * type_hot[:, :, None], axis=1)

    q_low = typed(features, query_w).astype(jnp.bfloat16)
    key_low = typed(shifted_b, key_w).astype(jnp.bfloat16)
    value_low = typed(shifted_b, value_w).astype(jnp.bfloat16)
    kind_low = node_type.astype(jnp.bfloat16)
    q_heads = q_low.reshape(tgt_rows, head_count, head_size).astype(jnp.float32)
    att_f = rel_att.astype(jnp.float32)
    factor = rel_prior / math.sqrt(head_size)
    rel_raw = jnp.einsum("thj,rhjk->rthk", q_heads, att_f, precision=HIGH)
    rel_query = (rel_raw * factor[:, None, :, None]).astype(jnp.bfloat16)
    select = jnp.einsum("tk,ksr->tsr", type_hot, jnp.asarray(relation_table()), precision=HIGH)
    select_low = select.astype(jnp.bfloat16)
    cite_hot = (jnp.arange(rel_count) == 3).astype(jnp.float32)
    q_four = (
        jnp.einsum("tsr,rthd->thsd", select_low, rel_query, preferred_element_type=jnp.float32)
        .astype(jnp.bfloat16)
        .reshape(tgt_rows, head_count, kind_count * head_size)
    )
    q_cite = rel_query[3]

    def block_codes(source):
        return lax.dynamic_slice_in_dim(edge_codes, source * tgt_rows, tgt_rows, 1)

    def forward_block(run_state, kv_blk, qf_part, qc_part, code_blk):
        result = attend_block(run_state, kv_blk, qf_part, qc_part, code_blk, kind_count)
        return result

    def backward_block(kv_blk, qf_part, qc_part, gf_part, gc_part, lse_part, delta_part, code_blk):
        return back_block(
            kv_blk, qf_part, qc_part, gf_part, gc_part, lse_part, delta_part, code_blk, kind_count
        )

    whole_kv = (key_low, value_low, kind_low)

    def forward_turn(step_idx, loop_state):
        run_state, kv_blk = loop_state
        run_state = forward_block(
            run_state, kv_blk, q_four, q_cite, block_codes((my_blk - step_idx) % n_blk)
        )
        kv_blk = from_behind((kv_blk[0], kv_blk[1], kv_blk[2]), "blk", 1)
        return (run_state, kv_blk)

    run_state, kv_last = lax.fori_loop(
        0,
        n_blk,
        forward_turn,
        (
            (
                jnp.full((head_count, tgt_rows), NEG_FILL, jnp.float32),
                jnp.zeros((head_count, tgt_rows), jnp.float32),
                jnp.zeros((tgt_rows, head_count, kind_count * head_size), jnp.float32),
                jnp.zeros((tgt_rows, head_count, head_size), jnp.float32),
            ),
            whole_kv,
        ),
    )
    run_max, run_sum, acc_four, acc_cite = run_state
    floor_sum = jnp.maximum(run_sum, 1.0)
    log_total = run_max + jnp.log(floor_sum)
    norm_t = floor_sum.T[:, :, None]
    u_four = acc_four / norm_t
    u_cite = acc_cite / norm_t
    u_rel = jnp.einsum(
        "tsr,thsd->rthd",
        select,
        u_four.reshape(tgt_rows, head_count, kind_count, head_size),
        precision=HIGH,
    )
    u_rel = u_rel + cite_hot[:, None, None, None] * u_cite[None]
    u_rel_b = u_rel.astype(jnp.bfloat16)
    agg_sum = jnp.einsum(
        "rthd,rhde->the", u_rel_b, rel_msg, preferred_element_type=jnp.float32
    ).reshape(tgt_rows, feat_dim)
    act_full, gelu_back = jax.vjp(jax.nn.gelu, agg_sum)
    act_low = act_full.astype(jnp.bfloat16)
    branch = typed(act_low, out_w)
    skip_all = jax.nn.sigmoid(skip_logit)
    skip_gate = jnp.sum(type_hot * skip_all[None, :], axis=1)[:, None]
    mixed_sum = skip_gate * branch + (1.0 - skip_gate) * x_f
    centered = mixed_sum - jnp.mean(mixed_sum, axis=1, keepdims=True)
    inv_std = lax.rsqrt(jnp.mean(centered * centered, axis=1, keepdims=True) + LN_EPS)
    normed = centered * inv_std
    valid_col = node_valid.astype(jnp.float32)[:, None]
    layer_out = (valid_col * (normed * ln_gain + ln_bias)).astype(jnp.bfloat16)
    grad_y = cotangent.astype(jnp.float32) * valid_col
    gain_grad = jnp.sum(grad_y * normed, axis=0)
    bias_grad = jnp.sum(grad_y, axis=0)
    grad_norm = grad_y * ln_gain
    grad_mix = inv_std * (
        grad_norm
        - jnp.mean(grad_norm, axis=1, keepdims=True)
        - normed * jnp.mean(grad_norm * normed, axis=1, keepdims=True)
    )
    grad_branch = (skip_gate * grad_mix).astype(jnp.bfloat16)
    gate_term = (
        jnp.sum(grad_mix * (branch - x_f), axis=1, keepdims=True) * skip_gate * (1.0 - skip_gate)
    )
    skip_grad = jnp.sum(type_hot * gate_term, axis=0)
    out_grad = typed_grad(act_low, grad_branch)
    grad_agg = gelu_back(typed_back(grad_branch, out_w))[0].astype(jnp.bfloat16)
    grad_agg_heads = grad_agg.reshape(tgt_rows, head_count, head_size)
    msg_grad = jnp.einsum(
        "rthd,the->rhde", u_rel_b, grad_agg_heads, preferred_element_type=jnp.float32
    )
    grad_urel = jnp.einsum(
        "the,rhde->rthd", grad_agg_heads, rel_msg, preferred_element_type=jnp.float32
    ).astype(jnp.bfloat16)
    grad_four = (
        jnp.einsum("tsr,rthd->thsd", select_low, grad_urel, preferred_element_type=jnp.float32)
        .astype(jnp.bfloat16)
        .reshape(tgt_rows, head_count, kind_count * head_size)
    )
    grad_cite = grad_urel[3]
    row_delta = (
        jnp.sum(grad_four.astype(jnp.float32) * u_four, axis=2)
        + jnp.sum(grad_cite.astype(jnp.float32) * u_cite, axis=2)
    ).T
    zero_four = jnp.zeros((tgt_rows, head_count, kind_count * head_size), jnp.float32)
    zero_cite = jnp.zeros((tgt_rows, head_count, head_size), jnp.float32)

    def back_turn(step_idx, loop_state):
        kv_blk, travel, acc_qf, acc_qc = loop_state
        k_grad, v_grad, qf_grad, qc_grad = backward_block(
            kv_blk,
            q_four,
            q_cite,
            grad_four,
            grad_cite,
            log_total,
            row_delta,
            block_codes((my_blk - step_idx) % n_blk),
        )
        travel = (
            from_behind((travel[0] + k_grad).astype(jnp.bfloat16), "blk", 1).astype(jnp.float32),
            from_behind((travel[1] + v_grad).astype(jnp.bfloat16), "blk", 1).astype(jnp.float32),
        )
        kv_blk = from_behind((kv_blk[0], kv_blk[1], kv_blk[2]), "blk", 1)
        return (kv_blk, travel, acc_qf + qf_grad, acc_qc + qc_grad)

    zero_kv = jnp.zeros((tgt_rows, feat_dim), jnp.float32)
    loop_state = lax.fori_loop(
        0, n_blk, back_turn, (whole_kv, (zero_kv, zero_kv), zero_four, zero_cite)
    )
    key_acc, value_acc = loop_state[1]
    acc_qf, acc_qc = (loop_state[2], loop_state[3])
    grad_key = key_acc.astype(jnp.bfloat16)
    grad_value = value_acc.astype(jnp.bfloat16)
    grad_relq = jnp.einsum(
        "tsr,thsd->rthd",
        select,
        acc_qf.reshape(tgt_rows, head_count, kind_count, head_size),
        precision=HIGH,
    )
    grad_relq = (
        (grad_relq + cite_hot[:, None, None, None] * acc_qc[None])
        .astype(jnp.bfloat16)
        .astype(jnp.float32)
    )
    prior_grad = jnp.sum(grad_relq * rel_raw, axis=(1, 3)) / math.sqrt(head_size)
    grad_raw = grad_relq * factor[:, None, :, None]
    att_grad = jnp.einsum("thj,rthk->rhjk", q_heads, grad_raw, precision=HIGH)
    grad_query = (
        jnp.einsum("rthk,rhjk->thj", grad_raw, att_f, precision=HIGH)
        .reshape(tgt_rows, feat_dim)
        .astype(jnp.bfloat16)
    )
    query_grad = typed_grad(features, grad_query)
    key_grad = typed_grad(shifted_b, grad_key)
    value_grad = typed_grad(shifted_b, grad_value)
    grad_shift = typed_back(grad_key, key_w) + typed_back(grad_value, value_w)
    table_grad = jnp.dot(gap_hot.T, grad_shift, precision=HIGH)
    rte_grad = jnp.dot(time_low.T, table_grad, precision=HIGH)
    input_grad = (
        (1.0 - skip_gate) * grad_mix + typed_back(grad_query, query_w) + grad_shift
    ).astype(jnp.bfloat16)
    summed = lax.psum(
        (
            query_grad,
            key_grad,
            value_grad,
            out_grad,
            att_grad,
            msg_grad,
            prior_grad,
            skip_grad,
            rte_grad,
            gain_grad,
            bias_grad,
        ),
        ("blk", "rep"),
    )
    return (
        layer_out,
        input_grad,
        summed[0],
        summed[1],
        summed[2],
        summed[3],
        summed[4],
        summed[5],
        summed[6],
        summed[7],
        summed[8],
        summed[9],
        summed[10],
    )


REL_TAB = relation_table()
HALF = 128
F32 = jnp.float32
LOW = jnp.bfloat16
VMEM_CAP = 65400 * 2**10
PROB_UNROLL = 2
GATHER_CUTS = 2


def nn(a, b):
    return lax.dot_general(a, b, (((1,), (0,)), ((), ())), preferred_element_type=F32)


def nt(a, b):
    return lax.dot_general(a, b, (((1,), (1,)), ((), ())), preferred_element_type=F32)


def tn(a, b):
    return lax.dot_general(a, b, (((0,), (0,)), ((), ())), preferred_element_type=F32)


def pick(kinds, kind, value):
    return jnp.where(kinds == kind, value, jnp.zeros_like(value))


def relation_of(kind, slot):
    hit = np.nonzero(REL_TAB[kind, slot])[0]
    return int(hit[0]) if len(hit) else None


def to_slots(rel_rows, kinds, kind_count):
    slots = []
    for slot in range(kind_count):
        rows = jnp.zeros(kinds.shape, F32)
        for kind in range(kind_count):
            rel = relation_of(kind, slot)
            if rel is not None:
                rows = jnp.where(kinds == kind, rel_rows(rel), rows)
        slots.append(rows)
    return slots, pick(kinds, 0, rel_rows(3))


def to_relations(slot_rows, cite_rows, kinds, kind_count, rel_count):
    out = []
    for rel in range(rel_count):
        if rel == 3:
            out.append(pick(kinds, 0, cite_rows))
            continue
        (kind, slot) = [
            (k, s) for k in range(kind_count) for s in range(kind_count) if relation_of(k, s) == rel
        ][0]
        out.append(pick(kinds, kind, slot_rows(slot)))
    return out


def flip(index, mask):
    return sum(((index // bit + mask // bit) % 2) * bit for bit in (1, 2, 4))


def gap_hot(gap_row, levels):
    gaps = jnp.broadcast_to(gap_row, (levels, gap_row.shape[1]))
    return (lax.broadcasted_iota(jnp.int32, gaps.shape, 0) == gaps).astype(F32).astype(LOW)


def remote(src, dst, sends, recvs, send_at, recv_at, device):
    return pltpu.make_async_remote_copy(
        src_ref=src,
        dst_ref=dst,
        send_sem=sends.at[send_at],
        recv_sem=recvs.at[recv_at],
        device_id=device,
        device_id_type=pl.DeviceIdType.MESH,
    )


def greet(device):
    pl.semaphore_signal(
        pltpu.get_barrier_semaphore(),
        inc=1,
        device_id=device,
        device_id_type=pl.DeviceIdType.MESH,
    )


def out_at(k, half):
    return (2 * k + half) * 256


def msg_at(half):
    return 2048 + half * 256


def key_at(k, half):
    return 2560 + 3072 * half + k * 256


def value_at(k, half):
    return 2560 + 3072 * half + (4 + k) * 256


def query_at(k, half):
    return 2560 + 3072 * half + (8 + k) * 256


def att_at(half):
    return 8704 + half * 256


SUM_PARTS = ((0, 2560, False), (2560, 3072, False), (5632, 2048, True), (7680, 1536, True))
SUM_TICKS = (
    ((0, 0, 1), (2, 0, 2), (3, 0, 3)),
    ((0, 0, 4), (0, 1, 1), (2, 0, 5), (2, 1, 2), (3, 0, 6), (3, 1, 3)),
)
SUM_NEXT = ((0, 7), (1, 4), (2, 1), (3, 1))
SUM_TAIL = ((0, 8), (1, 5), (2, 2), (3, 2), (1, 6), (2, 3), (3, 3), (1, 7), (2, 4), (3, 4), (1, 8), (2, 5), (3, 5), (2, 6), (3, 6))
GRAD_ROWS = 9216


def span(start, size):
    return pl.ds(start if isinstance(start, int) else pl.multiple_of(start, 16), size)


def summation(part, refs, places, pack):
    grads, full, core_in, plane_in, line_in, sends, recvs = refs
    (z, y, x, core), by_core, by_plane, by_z, by_y = places
    base, rows, at_once = SUM_PARTS[part]
    half, quarter, chunk = rows // 2, rows // 8, rows // 32
    count = iter(range(24 * part, 24 * part + 24))
    mine = base + core * half
    there_core = base + half - core * half
    spots = [(2 * x + y + step) % 4 for step in range(4)]
    plane_at = [mine + spot * quarter for spot in spots]
    own_x = mine + x * 2 * quarter
    other_x = mine + (1 - x) * 2 * quarter
    other_y = own_x + (1 - y) * quarter
    by_x = by_plane[1]
    line_at = [plane_at[0] + ((z + step) % 4) * chunk for step in range(4)]
    core_land, plane_land, line_land = base // 2, 3 * base // 8, 3 * base // 32
    pending = []

    def send(src, dst, device):
        at = next(count)

        def copy():
            return remote(src(), dst(), sends, recvs, at, at, device)

        copy().start()
        pending.append(copy)

    def settle():
        for copy in pending:
            copy().wait()
        pending.clear()

    def piece(ref, start, size):
        return lambda: ref.at[span(start, size), :]

    def small(ref, at):
        return lambda: ref.at[at]

    def load(ref, start, size):
        return ref[span(start, size), :].astype(F32)

    def add_in(start, size, *others):
        value = load(grads, start, size)
        for ref, at in others:
            value = value + load(ref, at, size)
        grads[span(start, size), :] = value.astype(LOW)

    def cores():
        send(piece(grads, there_core, half), piece(core_in, core_land, half), by_core)
        if pack:
            send(small(pack[0], 0), small(pack[1], 0), by_core)

    def plane():
        settle()
        for step in (2, 1, 3, 0):
            add_in(plane_at[step], quarter, (core_in, plane_at[step] - mine + core_land))
            if step:
                land = plane_land + (step - 1) * quarter
                send(
                    piece(grads, plane_at[step], quarter),
                    piece(plane_in, land, quarter),
                    by_plane[step - 1],
                )
        if pack:
            pack[0][1] = pack[0][0] + pack[1][0]
            for step in (1, 2, 3):
                send(small(pack[0], 1), small(pack[1], step), by_plane[step - 1])

    def along_x():
        settle()
        for start in (other_x, own_x):
            add_in(start, 2 * quarter, (core_in, start - mine + core_land))
            if start is other_x:
                send(
                    piece(grads, start, 2 * quarter),
                    piece(plane_in, plane_land, 2 * quarter),
                    by_x,
                )

    def along_y():
        settle()
        for start in (other_y, plane_at[0]):
            add_in(start, quarter, (plane_in, start - own_x + plane_land))
            if start is other_y:
                land = plane_land + 2 * quarter
                send(piece(grads, start, quarter), piece(plane_in, land, quarter), by_y)

    def line():
        settle()
        lands = range(3) if at_once else (2,)
        for step in (2, 3, 1, 0):
            within = line_at[step] - plane_at[0] + plane_land
            add_in(line_at[step], chunk, *[(plane_in, within + i * quarter) for i in lands])
            if step:
                land = line_land + (step - 1) * chunk
                send(
                    piece(grads, line_at[step], chunk),
                    piece(line_in, land, chunk),
                    by_z[step - 1],
                )
        if pack:
            pack[0][2] = pack[0][1] + pack[1][1] + pack[1][2] + pack[1][3]
            for step in (2, 3, 1):
                send(small(pack[0], 2), small(pack[1], 3 + step), by_z[step - 1])

    def share(start, size, device):
        send(piece(full, start, size), piece(full, start, size), device)

    def line_back():
        settle()
        value = load(grads, line_at[0], chunk)
        for step in range(3):
            value = value + load(line_in, line_land + step * chunk, chunk)
        full[span(line_at[0], chunk), :] = value.astype(LOW)
        for step in (2, 3, 1):
            share(line_at[0], chunk, by_z[step - 1])
        if pack:
            pack[2][...] = pack[0][2] + pack[1][4] + pack[1][5] + pack[1][6]

    def plane_back():
        settle()
        for step in (2, 1, 3):
            share(plane_at[0], quarter, by_plane[step - 1])

    def back_y():
        settle()
        share(plane_at[0], quarter, by_y)

    def back_x():
        settle()
        share(own_x, 2 * quarter, by_x)

    def cores_back():
        settle()
        share(mine, half, by_core)

    if at_once:
        return [cores, plane, line, line_back, plane_back, cores_back, settle]
    return [cores, along_x, along_y, line, line_back, back_y, back_x, cores_back, settle]


def layer_kernel(
    x_ref,
    kind_ref,
    gap_ref,
    valid_ref,
    rte_ref,
    time_ref,
    codes_hbm,
    cot_hbm,
    qw_hbm,
    kw_hbm,
    vw_hbm,
    ow_hbm,
    att_hbm,
    msg_hbm,
    prior_ref,
    skip_ref,
    gain_ref,
    bias_ref,
    out_ref,
    input_ref,
    full,
    small_ref,
    att_flat,
    att_ref,
    msg_ref,
    cot_ref,
    codes,
    qw,
    kw,
    vw,
    ow,
    msg_flat,
    shifted,
    xt,
    base,
    shift_out,
    plane_back,
    line_back,
    load_sem,
    gather_send,
    gather_recv,
    back_send,
    back_recv,
    grads,
    core_in,
    plane_in,
    line_in,
    pack,
    pack_in,
    sum_send,
    sum_recv,
    kt,
    vx,
    sbuf,
    probs,
    sm,
    qs,
    tails,
    qt2,
    qh,
    gt2,
    acc,
    two,
    agg,
    grad_even,
    grad_odd,
):
    rows, feat = x_ref.shape
    n_blk = shifted.shape[0]
    levels = time_ref.shape[1]
    kind_count = qw.shape[0]
    rel_count, heads, size = att_ref.shape[:3]
    group = heads // 2
    me = lax.axis_index("blk")
    rep = lax.axis_index("rep")
    z, y = me // 2, me % 2
    inner = ((z + 1) // 2) % 2
    by_y = (flip(me, 1), rep)
    by_core = (me, rep + 1 - 2 * (rep % 2))
    by_x = (me, rep + 2 - 4 * (rep // 2))
    for device in (by_y, by_core, by_x):
        greet(device)

    @pl.when(z < 3)
    def _():
        greet((me + 2, rep))

    @pl.when(z > 0)
    def _():
        greet((me - 2, rep))

    loads = [
        pltpu.make_async_copy(src, dst, load_sem.at[at])
        for at, (src, dst) in enumerate(
            (
                (att_hbm, att_ref),
                (msg_hbm, msg_ref),
                (kw_hbm, kw),
                (vw_hbm, vw),
                (qw_hbm, qw),
                (codes_hbm, codes),
                (ow_hbm, ow),
                (cot_hbm, cot_ref),
            )
        )
    ]

    x_f = x_ref[...].astype(F32).T
    x_t = x_f.astype(LOW)
    xt[...] = x_t
    table = tn(rte_ref[...], time_ref[...])
    table_hi = table.astype(LOW)
    table_lo = (table - table_hi.astype(F32)).astype(LOW)
    hot = gap_hot(gap_ref[...], levels)
    shifted[me, 0:feat, :] = (x_f + nn(table_hi, hot) + nn(table_lo, hot)).astype(LOW)
    shifted[me, feat:, :] = jnp.concatenate(
        [kind_ref[...].astype(F32), gap_ref[...].astype(F32), jnp.zeros((14, rows), F32)], axis=0
    ).astype(LOW)

    edges = [feat * c // GATHER_CUTS for c in range(GATHER_CUTS)] + [feat + 16]

    def move(block, cut, send_at, device):
        at = pl.ds(edges[cut], edges[cut + 1] - edges[cut])
        return remote(
            shifted.at[block, at, :],
            shifted.at[block, at, :],
            gather_send,
            gather_recv,
            send_at * GATHER_CUTS + cut,
            block * GATHER_CUTS + cut,
            device,
        )

    def other_z(n):
        order = ((1, 2, 1, 2), (2, 0, 3, 1), (3, 3, 0, 0))
        table = sum(row[i] * 4 ** (4 * r + i) for r, row in enumerate(order) for i in range(4))
        power = (1 + 3 * (z % 2)) * (1 + 15 * (z // 2)) * (1 + 255 * (n // 2)) * (1 + 255 * (n // 3))
        own = (3 - n) // 3
        return own * z + (1 - own) * ((table // power) % 4)

    def own_moves(act):
        for cut in range(GATHER_CUTS):

            @pl.when(z < 3)
            def _():
                act(move(me, cut, 0, (me + 2, rep)))

            @pl.when(z > 0)
            def _():
                act(move(me, cut, 1, (me - 2, rep)))

            act(move(me, cut, 2, by_y))

    def hand_on(n, act, wait):
        there = other_z(n)
        step = 2 * ((z - there + 3) // 4) - 1
        block = 2 * there + y
        for cut in range(GATHER_CUTS):
            if wait:
                move(block, cut, 0, by_y).wait_recv()
            act(move(block, cut, 2 + n, by_y))

            @pl.when((z + step >= 0) & (z + step <= 3))
            def _():
                act(move(block, cut, 5 + n, (me + 2 * step, rep)))

    pl.semaphore_wait(pltpu.get_barrier_semaphore(), 4 + inner)
    own_moves(lambda copy: copy.start())
    for load in loads:
        load.start()

    def source_row(j, row):
        return shifted[j, feat : feat + 16, :].astype(F32)[row : row + 1].astype(jnp.int32)

    kinds = jnp.broadcast_to(kind_ref[...], (size, rows))
    kinds_f = jnp.broadcast_to(kind_ref[...], (feat, rows))
    valid_f = jnp.broadcast_to(valid_ref[...], (feat, rows)).astype(F32)
    lane = lax.broadcasted_iota(jnp.int32, (rows, HALF), 1)
    ones_pad = (lax.broadcasted_iota(jnp.int32, (16, rows), 0) < 2).astype(F32).astype(LOW)
    scale = 1.0 / math.sqrt(size)

    def cols(j):
        return pl.ds(pl.multiple_of(j * rows, rows), rows)

    def store_part(start, value):
        grads[pl.ds(start, value.shape[0]), :] = value.astype(LOW)

    loads[0].wait()
    loads[1].wait()
    for r in range(rel_count):
        for h in range(heads):
            agg[h * size : (h + 1) * size, r * size : (r + 1) * size] = att_ref[r, h].astype(F32)
    att_flat[...] = agg[...].astype(LOW)
    for r in range(rel_count):
        for h in range(heads):
            agg[r * size : (r + 1) * size, h * size : (h + 1) * size] = msg_ref[r, h].astype(F32)
    msg_flat[...] = agg[...].T.astype(LOW)

    def turned(m, k):
        return probs.at[0, 2 * m + k // 2, pl.ds((k % 2) * feat, feat), :]

    for m, (load, ref) in enumerate(((loads[2], kw), (loads[3], vw))):
        load.wait()
        for k in range(kind_count):
            turned(m, k)[...] = ref[k].astype(F32).T.astype(LOW)

    loads[4].wait()
    q_full = jnp.zeros((feat, rows), F32)
    for k in range(kind_count):
        q_full = jnp.where(kinds_f == k, tn(qw[k], x_t), q_full)
    for h in range(heads):
        qh[h] = q_full[h * size : (h + 1) * size].astype(LOW)

    def head_rows(ref, h):
        return ref[pl.ds(pl.multiple_of(h * size, size), size), :]

    def query_head(h, carry):
        raw = tn(head_rows(att_flat, h), qh[h])

        def rel_rows(r):
            part = raw[r * size : (r + 1) * size] * (prior_ref[r, h] * scale)
            return part.astype(LOW).astype(F32)

        slots, cite = to_slots(rel_rows, kinds, kind_count)
        slot_t = jnp.concatenate(slots, axis=0)
        cite_t = jnp.concatenate([cite, jnp.zeros((HALF - size, rows), F32)], axis=0)
        qt2[h, :, 0:rows] = slot_t.astype(LOW)
        qt2[h, :, rows:] = cite_t.astype(LOW)
        qs[h, 0:rows, :] = slot_t.T.astype(LOW)
        qs[h, rows:, :] = cite_t.T.astype(LOW)
        return carry

    lax.fori_loop(0, heads, query_head, 0, unroll=2)
    loads[5].wait()
    acc[:, 0:rows, :] = jnp.full((heads, rows, HALF), NEG_FILL, F32)

    def keep_scores(h, j, both, second, edge):
        val = jnp.where(second, both[rows:], both[:rows]) * LOG2_E
        val = jnp.where(edge, val, NEG_FILL)
        if h < group:
            sbuf[j, pl.ds(h * rows, rows), :] = val
        else:
            high = val.astype(LOW)
            probs[j, h, 0:rows, :] = high
            probs[j, h, rows:, :] = (val - high.astype(F32)).astype(LOW)
        top = jnp.maximum(val[:, :HALF], val[:, HALF:])
        acc[h, 0:rows, :] = jnp.maximum(acc[h, 0:rows, :], top)

    def arrive(j):
        src = jnp.broadcast_to(source_row(j, 0), (size, rows))
        block = shifted[j, 0:feat, :]
        for k in range(kind_count):
            key = nn(turned(0, k)[...], block)
            value = nn(turned(1, k)[...], block)
            for h in range(heads):
                part = slice(h * size, (h + 1) * size)
                kt[j, h, pl.ds(k * size, size), :] = pick(src, k, key[part]).astype(LOW)
                vx[j, h, pl.ds(k * size, size), :] = pick(src, k, value[part]).astype(LOW)
        code = codes[:, cols(j)]
        second = code == 2
        edge = code > 0
        two[j] = second.astype(F32).astype(LOW)
        before = None
        for h in range(heads + 1):
            both = nn(qs[h], kt[j, h]) if h < heads else None
            if h > 0:
                keep_scores(h - 1, j, before, second, edge)
            before = both

    def start(copy):
        copy.start()

    def two_blocks(n, carry):
        there = other_z(n)

        def one(line, inside):
            block = 2 * there + (y + line) % 2

            @pl.when(line == 1)
            def _():
                @pl.when(n == 0)
                def _():
                    hand_on(1, start, True)

                @pl.when((n == 0) & (inner == 1))
                def _():
                    hand_on(2, start, True)

                @pl.when(n == 1)
                def _():
                    hand_on(2 + inner, start, True)

                @pl.when((n == 2) & (inner == 0))
                def _():
                    hand_on(3, start, True)

                for cut in range(GATHER_CUTS):
                    move(block, cut, 0, by_y).wait_recv()

            arrive(block)
            return inside

        return lax.fori_loop(0, 2, one, carry)

    lax.fori_loop(0, n_blk // 2, two_blocks, 0)
    own_moves(lambda copy: copy.wait_send())
    for n in range(1, n_blk // 2):
        hand_on(n, lambda copy: copy.wait_send(), False)

    def prob_block(h, j, top, kept):
        if kept:
            val = sbuf[j, pl.ds(pl.multiple_of(h * rows, rows), rows), :]
        else:
            val = probs[j, h, 0:rows, :].astype(F32) + probs[j, h, rows:, :].astype(F32)
        val = jnp.exp2(val - top)
        low = val.astype(LOW)
        second = low * two[j]
        probs[j, h, 0:rows, :] = low - second
        probs[j, h, rows:, :] = second
        return val[:, :HALF] + val[:, HALF:], jnp.concatenate([low - second, second], axis=0)

    sm[...] = jnp.zeros((rows, HALF), F32)

    def prob_head(h, kept):
        top = jnp.max(acc[h, 0:rows, :], axis=1, keepdims=True)
        top = jnp.broadcast_to(jnp.maximum(top, 0.1 * NEG_FILL), (rows, rows))
        value_sum = None
        total = None
        for j in range(n_blk + 1):
            if j < n_blk:
                part, now = prob_block(h, j, top, kept)
                total = part if total is None else total + part
            if j > 0:
                part = nt(before, vx[j - 1, h])
                value_sum = part if value_sum is None else value_sum + part
            before = now
        acc[h] = value_sum
        total = jnp.sum(total, axis=1, keepdims=True)
        sm[...] = jnp.where(lane == h, jnp.broadcast_to(total, (rows, HALF)), sm[...])

    for kept in (True, False):

        def prob_pair(pair, carry, kept=kept):
            for u in range(PROB_UNROLL):
                prob_head((0 if kept else group) + PROB_UNROLL * pair + u, kept)
            return carry

        lax.fori_loop(0, group // PROB_UNROLL, prob_pair, 0)

    inverse = 1.0 / jnp.maximum(sm[...].T, 1.0)
    sm[0:heads, :] = inverse[0:heads, 0:HALF]
    sm[heads : 2 * heads, :] = inverse[0:heads, HALF:]

    def inv_row(h, count):
        row = jnp.concatenate([sm[pl.ds(h, 1), :], sm[pl.ds(heads + h, 1), :]], axis=1)
        return jnp.broadcast_to(row, (count, rows))

    def rel_part(h):
        return sbuf[h // group, pl.ds((h % group) * feat, feat), :].astype(LOW)

    for h in range(heads):
        inv = inv_row(h, HALF)
        u_turned = acc[h].T
        u_slot = u_turned[:, 0:rows] * inv
        u_cite = u_turned[0:size, rows:] * inv[0:size]
        sbuf[2 + h // group, pl.ds((h % group) * feat, HALF), :] = u_slot
        sbuf[2 + h // group, pl.ds((h % group) * feat + HALF, size), :] = u_cite
        rel = to_relations(
            lambda s: u_slot[s * size : (s + 1) * size], u_cite, kinds, kind_count, rel_count
        )
        rel = jnp.concatenate(rel, axis=0)
        sbuf[h // group, pl.ds((h % group) * feat, feat), :] = rel
        agg[pl.ds(h * size, size), :] = nn(head_rows(msg_flat, h), rel.astype(LOW))
    loads[6].wait()
    loads[7].wait()
    agg_t = agg[...]
    slope = 0.7978845608028654
    inner = jnp.tanh(slope * (agg_t + 0.044715 * agg_t * agg_t * agg_t))
    act_t = (0.5 * agg_t * (1.0 + inner)).astype(LOW)
    gelu_back = 0.5 * (1.0 + inner) + 0.5 * agg_t * (1.0 - inner * inner) * slope * (
        1.0 + 3.0 * 0.044715 * agg_t * agg_t
    )
    skip = jnp.zeros((1, rows), F32)
    branch = jnp.zeros((feat, rows), F32)
    for k in range(kind_count):
        skip = jnp.where(kinds[0:1] == k, skip_ref[k], skip)
        branch = jnp.where(kinds_f == k, tn(ow[k], act_t), branch)
    gate_row = 1.0 / (1.0 + jnp.exp(-skip))
    gate = jnp.broadcast_to(gate_row, (feat, rows))
    mixed = gate * branch + (1.0 - gate) * x_f
    centered = mixed - jnp.mean(mixed, axis=0, keepdims=True)
    inv_std = lax.rsqrt(jnp.mean(centered * centered, axis=0, keepdims=True) + LN_EPS)
    normed = centered * inv_std
    affine = jnp.concatenate([gain_ref[...], bias_ref[...], jnp.zeros((HALF - 2, feat), F32)], axis=0).T
    gain = jnp.broadcast_to(affine[:, 0:1], (feat, rows))
    bias = jnp.broadcast_to(affine[:, 1:2], (feat, rows))
    out_ref[...] = (valid_f * (normed * gain + bias)).T.astype(LOW)
    grad_y = cot_ref[...].astype(F32).T * valid_f
    gain_col = jnp.sum(grad_y * normed, axis=1, keepdims=True)
    bias_col = jnp.sum(grad_y, axis=1, keepdims=True)
    grad_norm = grad_y * gain
    grad_mix = inv_std * (
        grad_norm
        - jnp.mean(grad_norm, axis=0, keepdims=True)
        - normed * jnp.mean(grad_norm * normed, axis=0, keepdims=True)
    )
    skip_row = (
        jnp.sum(grad_mix * (branch - x_f), axis=0, keepdims=True) * gate_row * (1.0 - gate_row)
    )
    base[...] = (1.0 - gate) * grad_mix
    grad_branch = gate * grad_mix
    grad_act = jnp.zeros((feat, rows), F32)
    for k in range(kind_count):
        masked = pick(kinds_f, k, grad_branch).astype(LOW)
        out_grad = nt(act_t, masked)
        store_part(out_at(k, 0), out_grad[:, :HALF])
        store_part(out_at(k, 1), out_grad[:, HALF:])
        grad_act = grad_act + nn(ow[k], masked)
    agg[...] = gelu_back * grad_act

    for h in range(heads):
        grad_agg = agg[pl.ds(h * size, size), :].astype(LOW)
        msg_grad = nt(grad_agg, rel_part(h))
        store_part(msg_at(0) + h * size, msg_grad[:, :HALF])
        store_part(msg_at(1) + h * size, msg_grad[:, HALF:])
        inv = inv_row(h, size)
        grad_u = tn(head_rows(msg_flat, h), grad_agg)

        def rel_rows(r):
            return grad_u[r * size : (r + 1) * size] * inv

        slots, cite = to_slots(rel_rows, kinds, kind_count)
        slot_t = jnp.concatenate(slots, axis=0).astype(LOW)
        cite_t = jnp.concatenate([cite, jnp.zeros((HALF - size, rows), F32)], axis=0).astype(LOW)
        gt2[h, :, 0:rows] = slot_t
        gt2[h, :, rows:] = cite_t
        slot_f = slot_t.astype(F32)
        cite_f = cite_t.astype(F32)
        u_at = (h % group) * feat
        delta = -(
            jnp.sum(slot_f * sbuf[2 + h // group, pl.ds(u_at, HALF), :], axis=0, keepdims=True)
            + jnp.sum(
                cite_f[0:size] * sbuf[2 + h // group, pl.ds(u_at + HALF, size), :],
                axis=0,
                keepdims=True,
            )
        )
        delta_hi = delta.astype(LOW).astype(F32)
        tail = jnp.concatenate(
            [delta_hi, delta - delta_hi, jnp.zeros((HALF - 2, rows), F32)], axis=0
        )
        tail_t = tail.T.astype(LOW)
        qs[h, 0:rows, :] = slot_f.T.astype(LOW)
        qs[h, rows:, :] = cite_f.T.astype(LOW)
        tails[h] = tail_t[:, 0:16]
        acc[h] = jnp.zeros(acc.shape[1:], F32)

    refs = (grads, full, core_in, plane_in, line_in, sum_send, sum_recv)
    by_z = [(((me // 2 + step) % 4) * 2 + me % 2, rep) for step in (1, 2, 3)]
    spots = [(2 * (rep // 2) + y + step) % 4 for step in (1, 2, 3)]
    by_plane = [(2 * z + spot % 2, 2 * (spot // 2) + rep % 2) for spot in spots]
    places = ((z, y, rep // 2, rep % 2), by_core, by_plane, by_z, by_y)
    sums = [summation(part, refs, places, None) for part in range(3)]
    sums.append(summation(3, refs, places, (pack, pack_in, small_ref)))
    sums[0][0]()

    slot_id = lax.broadcasted_iota(jnp.int32, (HALF, rows), 0) // size
    pack[0] = jnp.zeros(pack.shape[1:], F32)

    def along_y(m):
        return remote(
            shift_out.at[flip(me, m + 1)],
            plane_back.at[m // 2],
            back_send,
            back_recv,
            m // 2,
            m // 2,
            by_y,
        )

    def along_z(m):
        at = n_blk // 2 + m // 2
        return remote(
            shift_out.at[flip(me, m)],
            line_back.at[m // 2],
            back_send,
            back_recv,
            at,
            at,
            (flip(me, m), rep),
        )

    def pass_on(m):
        along_y(m).wait_recv()
        j = flip(me, m)
        total = shift_out[j].astype(F32) + plane_back[m // 2].astype(F32)
        shift_out[j] = total.astype(LOW)
        along_z(m).start()

    grad_bufs = (grad_even, grad_odd)
    for g in range(2):
        half = slice(g * HALF, (g + 1) * HALF)

        def block_pair(pair, carry, g=g, half=half):
            m = n_blk - 2 - 2 * pair
            blocks = (flip(me, m + 1), flip(me, m))
            owns = [slot_id == jnp.broadcast_to(source_row(j, 0), (HALF, rows)) for j in blocks]

            def keep(at, u, kind, part):
                for k in range(kind_count):
                    start = (2 * k + kind) * HALF + u * size
                    sbuf[blocks[at], pl.ds(start, size), :] = part[k * size : (k + 1) * size]

            def score_part(at, u):
                h = g * group + u
                both = jnp.concatenate([tails[h], tails[h]], axis=0)
                left = jnp.concatenate([qs[h], both], axis=1)
                right = jnp.concatenate([vx[blocks[at], h], ones_pad], axis=0)
                grad_bufs[u % 2][:, at * rows : (at + 1) * rows] = probs[blocks[at], h] * nn(
                    left, right
                ).astype(LOW)
                keep(at, u, 1, jnp.where(owns[at], nn(gt2[h], probs[blocks[at], h]), 0.0))

            def key_part(at, u):
                h = g * group + u
                grad = grad_bufs[u % 2][:, at * rows : (at + 1) * rows]
                keep(at, u, 0, jnp.where(owns[at], nn(qt2[h], grad), 0.0))
                if at == 1:
                    keys = jnp.concatenate([kt[j, h] for j in blocks], axis=1)
                    acc[h] = acc[h] + nt(grad_bufs[u % 2][...], keys)

            units = [(at, u) for u in range(group) for at in range(2)]
            for i in range(len(units) + 2):
                if i < len(units):
                    score_part(*units[i])
                if i > 1:
                    key_part(*units[i - 2])
            for at in range(2):
                j = blocks[at]
                total = None
                for k in range(kind_count):
                    weights = jnp.concatenate([kw[k, :, half], vw[k, :, half]], axis=1)
                    part = nn(weights, sbuf[j, pl.ds(k * feat, feat), :].astype(LOW))
                    total = part if total is None else total + part
                if g == 1:
                    total = total + shift_out[j].astype(F32)
                low = total.astype(LOW)
                shift_out[j] = low
                if g == 1:
                    gaps = gap_hot(source_row(j, 1), levels)
                    pack[0, 0:levels, :] = pack[0, 0:levels, :] + nt(gaps, low)
                    if at == 0:
                        along_y(m).start()
            if g == 1:

                @pl.when(pair > 0)
                def _():
                    pass_on(m + 2)

            for when, part, step in SUM_TICKS[g]:

                @pl.when(pair == when)
                def _(part=part, step=step):
                    sums[part][step]()

            return carry

        lax.fori_loop(0, n_blk // 2, block_pair, 0)

        for k in range(kind_count):
            total = None
            for j in range(n_blk):
                part = nt(shifted[j, 0:feat, :], sbuf[j, pl.ds(k * feat, feat), :].astype(LOW))
                total = part if total is None else total + part
            store_part(key_at(k, g), total[:, :HALF])
            store_part(value_at(k, g), total[:, HALF:])
        if g == 1:
            sums[2][0]()
        grad_q = []
        for h in range(g * group, (g + 1) * group):
            slot = acc[h].T
            rel = to_relations(
                lambda s: slot[s * size : (s + 1) * size, 0:rows],
                slot[0:size, rows:],
                kinds,
                kind_count,
                rel_count,
            )
            rel = [part.astype(LOW) for part in rel]
            att_grad = nt(qh[h], jnp.concatenate(rel, axis=0))
            store_part(att_at(0) + h * size, att_grad[:, :HALF])
            store_part(att_at(1) + h * size, att_grad[:, HALF:])
            raw = [
                (part.astype(F32) * (prior_ref[r, h] * scale)).astype(LOW)
                for r, part in enumerate(rel)
            ]
            grad_q.append(nn(head_rows(att_flat, h), jnp.concatenate(raw, axis=0)))
        grad_q = jnp.concatenate(grad_q, axis=0).astype(LOW).astype(F32)
        total = base[...]
        for k in range(kind_count):
            masked = pick(kinds_f[0:HALF], k, grad_q).astype(LOW)
            store_part(query_at(k, g), nt(xt[...], masked))
            total = total + nn(qw[k, :, half], masked)
        base[...] = total
        if g == 0:
            sums[1][0]()

    pair = jnp.where(
        lane == 0,
        jnp.broadcast_to(gain_col, (feat, HALF)),
        jnp.where(lane == 1, jnp.broadcast_to(bias_col, (feat, HALF)), 0.0),
    ).T
    spot = lax.broadcasted_iota(jnp.int32, (1, rows), 1)
    skips = jnp.zeros((1, rows), F32)
    for k in range(kind_count):
        skips = jnp.where(
            spot == k, jnp.sum(pick(kinds[0:1], k, skip_row), axis=1, keepdims=True), skips
        )
    pack[0, levels : levels + 8, :] = jnp.concatenate(
        [pair[0:2], skips, jnp.zeros((5, rows), F32)], axis=0
    )
    sums[3][0]()
    for part, step in SUM_NEXT:
        sums[part][step]()
    along_y(0).wait_recv()
    total = base[...] + shift_out[me].astype(F32) + plane_back[0].astype(F32)
    for m in (2, 4, 6):
        along_z(m).wait_recv()
        total = total + line_back[m // 2].astype(F32)
    input_ref[...] = total.T.astype(LOW)
    for part, step in SUM_TAIL:
        sums[part][step]()
    for m in (0, 2, 4, 6):
        along_y(m).wait_send()
        if m > 0:
            along_z(m).wait_send()


def finish_kernel(
    full,
    small_ref,
    att_flat,
    time_ref,
    prior_ref,
    out_in,
    input_in,
    out_ref,
    input_ref,
    qg_ref,
    kg_ref,
    vg_ref,
    og_ref,
    attg_ref,
    msgg_ref,
    priorg_ref,
    skip_ref,
    rte_ref,
    gain_ref,
    bias_ref,
):
    out_ref[...] = out_in[...]
    input_ref[...] = input_in[...]
    kind_count, feat = qg_ref.shape[:2]
    rel_count, heads, width = attg_ref.shape[:3]
    scale = 1.0 / math.sqrt(width)

    def part(start):
        return full[pl.ds(start, feat), :].astype(F32)

    for ref, at in ((qg_ref, query_at), (kg_ref, key_at), (vg_ref, value_at), (og_ref, out_at)):
        for k in range(kind_count):
            for half in range(2):
                ref[k, :, half * HALF : (half + 1) * HALF] = part(at(k, half))
    att = jnp.concatenate([part(att_at(0)), part(att_at(1))], axis=1)
    msg = jnp.concatenate([part(msg_at(0)), part(msg_at(1))], axis=1).T
    for r in range(rel_count):
        for h in range(heads):
            block = (slice(h * width, (h + 1) * width), slice(r * width, (r + 1) * width))
            attg_ref[r, h] = att[block] * (prior_ref[r, h] * scale)
            msgg_ref[r, h] = msg[block[::-1]]
    prod = (att * att_flat[...].astype(F32)).reshape(heads, width, feat)
    prod = jnp.sum(prod, axis=1)
    spread = (
        lax.broadcasted_iota(jnp.int32, (feat, rel_count), 0) // width
        == lax.broadcasted_iota(jnp.int32, (feat, rel_count), 1)
    ).astype(F32).astype(LOW)
    prior = jnp.zeros((rel_count, heads), F32)
    for _ in range(3):
        low = prod.astype(LOW)
        prior = prior + lax.dot_general(
            spread, low, (((0,), (1,)), ((), ())), preferred_element_type=F32
        )
        prod = prod - low.astype(F32)
    priorg_ref[...] = prior * scale
    levels = time_ref.shape[1]
    small = small_ref[...]
    rte = jnp.zeros(rte_ref.shape, F32)
    rest = small[0:levels]
    for _ in range(3):
        low = rest.astype(LOW)
        rte = rte + nn(time_ref[...], low)
        rest = rest - low.astype(F32)
    rte_ref[...] = rte
    gain_ref[...] = small[levels : levels + 1]
    bias_ref[...] = small[levels + 1 : levels + 2]
    skip_ref[...] = small[levels + 2 : levels + 3, 0:kind_count]


def layer_call(n_blk, *args):
    rows, feat = args[0].shape
    kind_count = args[8].shape[0]
    rel_count, heads, size = args[12].shape[:3]
    vmem = pl.BlockSpec(memory_space=pltpu.VMEM)
    smem = pl.BlockSpec(memory_space=pltpu.SMEM)
    hbm = pl.BlockSpec(memory_space=pl.ANY)
    square = (feat, feat)
    weight = pltpu.VMEM((kind_count,) + square, LOW)

    def shape(dims, kind):
        return jax.ShapeDtypeStruct(dims, kind)

    return pl.pallas_call(
        layer_kernel,
        out_shape=[
            shape((rows, feat), LOW),
            shape((rows, feat), LOW),
            shape((GRAD_ROWS, HALF), LOW),
            shape((LEVELS + 8, feat), F32),
            shape(square, LOW),
        ],
        in_specs=[vmem] * 6 + [hbm] * 8 + [smem] * 2 + [vmem] * 2,
        out_specs=[vmem] * 5,
        scratch_shapes=[
            pltpu.VMEM((rel_count, heads, size, size), LOW),
            pltpu.VMEM((rel_count, heads, size, size), LOW),
            pltpu.VMEM((rows, feat), LOW),
            pltpu.VMEM((rows, n_blk * rows), jnp.int32),
            weight,
            weight,
            weight,
            weight,
            pltpu.VMEM(square, LOW),
            pltpu.VMEM((n_blk, feat + 16, rows), LOW),
            pltpu.VMEM((feat, rows), LOW),
            pltpu.VMEM((feat, rows), F32),
            pltpu.VMEM((n_blk, feat, rows), LOW),
            pltpu.VMEM((n_blk // 2, feat, rows), LOW),
            pltpu.VMEM((n_blk // 2, feat, rows), LOW),
            pltpu.SemaphoreType.DMA((8,)),
            pltpu.SemaphoreType.DMA((9 * GATHER_CUTS,)),
            pltpu.SemaphoreType.DMA((n_blk * GATHER_CUTS,)),
            pltpu.SemaphoreType.DMA((n_blk,)),
            pltpu.SemaphoreType.DMA((n_blk,)),
            pltpu.VMEM((GRAD_ROWS, HALF), LOW),
            pltpu.VMEM((GRAD_ROWS // 2, HALF), LOW),
            pltpu.VMEM((3 * GRAD_ROWS // 8, HALF), LOW),
            pltpu.VMEM((3 * GRAD_ROWS // 32, HALF), LOW),
            pltpu.VMEM((3, LEVELS + 8, feat), F32),
            pltpu.VMEM((7, LEVELS + 8, feat), F32),
            pltpu.SemaphoreType.DMA((96,)),
            pltpu.SemaphoreType.DMA((96,)),
            pltpu.VMEM((n_blk, heads, HALF, rows), LOW),
            pltpu.VMEM((n_blk, heads, HALF, rows), LOW),
            pltpu.VMEM((n_blk, heads // 2 * rows, rows), F32),
            pltpu.VMEM((n_blk, heads, 2 * rows, rows), LOW),
            pltpu.VMEM((rows, HALF), F32),
            pltpu.VMEM((heads, 2 * rows, HALF), LOW),
            pltpu.VMEM((heads, rows, 16), LOW),
            pltpu.VMEM((heads, HALF, 2 * rows), LOW),
            pltpu.VMEM((heads, size, rows), LOW),
            pltpu.VMEM((heads, HALF, 2 * rows), LOW),
            pltpu.VMEM((heads, 2 * rows, HALF), F32),
            pltpu.VMEM((n_blk, rows, rows), LOW),
            pltpu.VMEM(square, F32),
            pltpu.VMEM((2 * rows, 2 * rows), LOW),
            pltpu.VMEM((2 * rows, 2 * rows), LOW),
        ],
        compiler_params=pltpu.CompilerParams(
            vmem_limit_bytes=VMEM_CAP, collective_id=0, has_side_effects=True
        ),
        name="layer",
    )(*args)


def time_columns(level_count, feat_width):
    positions = np.arange(level_count, dtype=np.float32)[:, None]
    steps = np.arange(feat_width // 2, dtype=np.float32)[None, :]
    phases = positions / np.power(np.float32(10000.0), np.float32(2.0) * steps / feat_width)
    table = np.stack([np.sin(phases), np.cos(phases)], axis=2).reshape(level_count, feat_width)
    return jnp.asarray(np.ascontiguousarray(table.T), LOW)


def fast_body(
    features,
    node_type,
    time_gap,
    node_valid,
    edge_codes,
    query_w,
    key_w,
    value_w,
    out_w,
    rel_att,
    rel_msg,
    rel_prior,
    skip_logit,
    rte_w,
    ln_gain,
    ln_bias,
    cotangent,
):
    rows, feat = features.shape
    n_blk = lax.axis_size("blk")
    kind_count = query_w.shape[0]
    time_low = time_columns(LEVELS, feat)
    vmem = pl.BlockSpec(memory_space=pltpu.VMEM)
    smem = pl.BlockSpec(memory_space=pltpu.SMEM)
    square = (feat, feat)

    def shape(dims, kind):
        return jax.ShapeDtypeStruct(dims, kind)

    layer_out, input_grad, full, small, att_flat = layer_call(
        n_blk,
        features,
        node_type[None],
        time_gap[None],
        node_valid[None],
        rte_w,
        time_low,
        edge_codes,
        cotangent,
        query_w,
        key_w,
        value_w,
        out_w,
        rel_att,
        rel_msg,
        rel_prior,
        skip_logit,
        ln_gain[None],
        ln_bias[None],
    )
    outs = pl.pallas_call(
        finish_kernel,
        out_shape=[shape(layer_out.shape, LOW), shape(input_grad.shape, LOW)]
        + [shape((kind_count,) + square, F32)] * 4
        + [shape(rel_att.shape, F32)] * 2
        + [
            shape(rel_prior.shape, F32),
            shape((1, kind_count), F32),
            shape(square, F32),
            shape((1, feat), F32),
            shape((1, feat), F32),
        ],
        in_specs=[vmem] * 4 + [smem] + [vmem] * 2,
        out_specs=[vmem] * 13,
        compiler_params=pltpu.CompilerParams(vmem_limit_bytes=VMEM_CAP),
        name="finish",
    )(full, small, att_flat, time_low, rel_prior, layer_out, input_grad)
    return (*outs[:9], outs[9][0], outs[10], outs[11][0], outs[12][0])


def solution(mesh):
    in_specs = (
        P(("blk", "rep"), None),
        P(("blk", "rep")),
        P(("blk", "rep")),
        P(("blk", "rep")),
        P(("blk", "rep"), None),
        P(),
        P(),
        P(),
        P(),
        P(),
        P(),
        P(),
        P(),
        P(),
        P(),
        P(),
        P(("blk", "rep"), None),
    )
    out_specs = (
        P(("blk", "rep"), None),
        P(("blk", "rep"), None),
        P(),
        P(),
        P(),
        P(),
        P(),
        P(),
        P(),
        P(),
        P(),
        P(),
        P(),
    )
    plan = fast_body if tuple(mesh.shape.values()) == (8, 4) else body
    return jax.shard_map(plan, mesh=mesh, in_specs=in_specs, out_specs=out_specs, check_vma=False)
```

```python
import math

import jax
import jax.numpy as jnp
import numpy as np
from jax import lax
from jax.experimental import pallas as pl
from jax.experimental.pallas import tpu as pltpu
from jax.sharding import PartitionSpec as P

LEVELS = 16


NEG_FILL = -1e30
LOG2_E = 1.4426950408889634
LN_EPS = 1e-05
HIGH = lax.Precision.HIGHEST


def from_behind(block, axis, distance):
    devices = range(lax.axis_size(axis))
    route = [((i - distance) % len(devices), i) for i in devices]
    return lax.ppermute(block, axis, route)


def relation_table():
    rel_tab = np.zeros((4, 4, 8), np.float32)
    rel_tab[0, 1, 0] = 1.0
    rel_tab[1, 0, 1] = 1.0
    rel_tab[0, 0, 2] = 1.0
    rel_tab[2, 0, 4] = 1.0
    rel_tab[0, 2, 5] = 1.0
    rel_tab[3, 1, 6] = 1.0
    rel_tab[1, 3, 7] = 1.0
    return rel_tab


def time_table(level_count, feat_width):
    positions = jnp.arange(level_count, dtype=jnp.float32)[:, None]
    freq_idx = jnp.arange(feat_width // 2, dtype=jnp.float32)[None, :]
    phases = positions / jnp.power(10000.0, 2.0 * freq_idx / feat_width)
    return jnp.stack([jnp.sin(phases), jnp.cos(phases)], axis=2).reshape(level_count, feat_width)


def slot_spread(heads_arr, kind_hot):
    spread_out = heads_arr[:, :, None, :] * kind_hot[:, None, :, None]
    return spread_out.reshape(heads_arr.shape[0], heads_arr.shape[1], -1)


def slot_collapse(slot_arr, kind_hot):
    src_rows, head_count = (slot_arr.shape[0], slot_arr.shape[1])
    kind_count = kind_hot.shape[1]
    shaped = slot_arr.reshape(src_rows, head_count, kind_count, -1)
    return jnp.sum(shaped * kind_hot.astype(jnp.float32)[:, None, :, None], axis=2)


def block_scores(kv_blk, q_four, q_cite, code_blk, kind_count):
    key_blk, value_blk, kind_blk = kv_blk
    src_rows = key_blk.shape[0]
    head_count = q_four.shape[1]
    key_heads = key_blk.reshape(src_rows, head_count, -1)
    value_heads = value_blk.reshape(src_rows, head_count, -1)
    kind_hot = (kind_blk[:, None] == jnp.arange(kind_count).astype(jnp.bfloat16)[None, :]).astype(
        jnp.bfloat16
    )
    key_four = slot_spread(key_heads, kind_hot)
    value_four = slot_spread(value_heads, kind_hot)
    is_one = (code_blk == 1)[None]
    is_two = (code_blk == 2)[None]
    slot_dot = jnp.einsum("thc,shc->hts", q_four, key_four, preferred_element_type=jnp.float32)
    cite_dot = jnp.einsum("thd,shd->hts", q_cite, key_heads, preferred_element_type=jnp.float32)
    scores = jnp.where(is_one, slot_dot, jnp.where(is_two, cite_dot, NEG_FILL))
    return (scores, is_one, is_two, key_heads, value_heads, key_four, value_four, kind_hot)


def attend_block(run_state, kv_blk, q_four, q_cite, code_blk, kind_count):
    run_max, run_sum, acc_four, acc_cite = run_state
    scores, is_one, is_two, key_heads, value_heads, key_four, value_four, kind_hot = block_scores(
        kv_blk, q_four, q_cite, code_blk, kind_count
    )
    new_max = jnp.maximum(run_max, jnp.max(scores, axis=2))
    expd = jnp.where((code_blk > 0)[None], jnp.exp(scores - new_max[:, :, None]), 0.0)
    rescale = jnp.exp(run_max - new_max)
    run_sum = run_sum * rescale + jnp.sum(expd, axis=2)
    prob_low = expd.astype(jnp.bfloat16)
    zero_low = jnp.zeros_like(prob_low)
    p_one = jnp.where(is_one, prob_low, zero_low)
    p_two = jnp.where(is_two, prob_low, zero_low)
    rescale_t = rescale.T[:, :, None]
    acc_four = acc_four * rescale_t + jnp.einsum(
        "hts,shc->thc", p_one, value_four, preferred_element_type=jnp.float32
    )
    acc_cite = acc_cite * rescale_t + jnp.einsum(
        "hts,shd->thd", p_two, value_heads, preferred_element_type=jnp.float32
    )
    return (new_max, run_sum, acc_four, acc_cite)


def back_block(
    kv_blk, q_four, q_cite, grad_four, grad_cite, log_total, row_delta, code_blk, kind_count
):
    scores, is_one, is_two, key_heads, value_heads, key_four, value_four, kind_hot = block_scores(
        kv_blk, q_four, q_cite, code_blk, kind_count
    )
    prob_full = jnp.where((code_blk > 0)[None], jnp.exp(scores - log_total[:, :, None]), 0.0)
    prob_low = prob_full.astype(jnp.bfloat16)
    zero_low = jnp.zeros_like(prob_low)
    p_one = jnp.where(is_one, prob_low, zero_low)
    p_two = jnp.where(is_two, prob_low, zero_low)
    grad_slot = jnp.einsum(
        "thc,shc->hts", grad_four, value_four, preferred_element_type=jnp.float32
    )
    grad_other = jnp.einsum(
        "thd,shd->hts", grad_cite, value_heads, preferred_element_type=jnp.float32
    )
    grad_probs = jnp.where(is_one, grad_slot, jnp.where(is_two, grad_other, 0.0))
    grad_scores = (prob_full * (grad_probs - row_delta[:, :, None])).astype(jnp.bfloat16)
    d_one = jnp.where(is_one, grad_scores, zero_low)
    d_two = jnp.where(is_two, grad_scores, zero_low)
    qf_grad = jnp.einsum("hts,shc->thc", d_one, key_four, preferred_element_type=jnp.float32)
    qc_grad = jnp.einsum("hts,shd->thd", d_two, key_heads, preferred_element_type=jnp.float32)
    k_grad = slot_collapse(
        jnp.einsum("hts,thc->shc", d_one, q_four, preferred_element_type=jnp.float32), kind_hot
    )
    k_grad = k_grad + jnp.einsum("hts,thd->shd", d_two, q_cite, preferred_element_type=jnp.float32)
    v_grad = slot_collapse(
        jnp.einsum("hts,thc->shc", p_one, grad_four, preferred_element_type=jnp.float32), kind_hot
    )
    v_grad = v_grad + jnp.einsum(
        "hts,thd->shd", p_two, grad_cite, preferred_element_type=jnp.float32
    )
    src_rows = k_grad.shape[0]
    return (k_grad.reshape(src_rows, -1), v_grad.reshape(src_rows, -1), qf_grad, qc_grad)


def body(
    features,
    node_type,
    time_gap,
    node_valid,
    edge_codes,
    query_w,
    key_w,
    value_w,
    out_w,
    rel_att,
    rel_msg,
    rel_prior,
    skip_logit,
    rte_w,
    ln_gain,
    ln_bias,
    cotangent,
):
    tgt_rows, feat_dim = features.shape
    kind_count = query_w.shape[0]
    rel_count = rel_att.shape[0]
    head_count = rel_att.shape[1]
    head_size = rel_att.shape[2]
    n_blk = lax.axis_size("blk")
    my_blk = lax.axis_index("blk")
    type_hot = (node_type[:, None] == jnp.arange(kind_count)[None, :]).astype(jnp.float32)
    type_low = type_hot.astype(jnp.bfloat16)
    gap_hot = (time_gap[:, None] == jnp.arange(LEVELS)[None, :]).astype(jnp.float32)
    time_low = time_table(LEVELS, feat_dim).astype(jnp.bfloat16).astype(jnp.float32)
    rte_table = jnp.dot(time_low, rte_w.astype(jnp.float32), precision=HIGH)
    x_f = features.astype(jnp.float32)
    shifted = x_f + jnp.dot(gap_hot, rte_table, precision=HIGH)
    shifted_b = shifted.astype(jnp.bfloat16)

    def typed(inp, weights):
        parts = jnp.einsum("th,khd->tkd", inp, weights, preferred_element_type=jnp.float32)
        return jnp.sum(parts * type_hot[:, :, None], axis=1)

    def typed_grad(inp, grad_low):
        masked = inp[:, None, :] * type_low[:, :, None]
        return jnp.einsum("tkh,td->khd", masked, grad_low, preferred_element_type=jnp.float32)

    def typed_back(grad_low, weights):
        parts = jnp.einsum("td,khd->tkh", grad_low, weights, preferred_element_type=jnp.float32)
        return jnp.sum(parts * type_hot[:, :, None], axis=1)

    q_low = typed(features, query_w).astype(jnp.bfloat16)
    key_low = typed(shifted_b, key_w).astype(jnp.bfloat16)
    value_low = typed(shifted_b, value_w).astype(jnp.bfloat16)
    kind_low = node_type.astype(jnp.bfloat16)
    q_heads = q_low.reshape(tgt_rows, head_count, head_size).astype(jnp.float32)
    att_f = rel_att.astype(jnp.float32)
    factor = rel_prior / math.sqrt(head_size)
    rel_raw = jnp.einsum("thj,rhjk->rthk", q_heads, att_f, precision=HIGH)
    rel_query = (rel_raw * factor[:, None, :, None]).astype(jnp.bfloat16)
    select = jnp.einsum("tk,ksr->tsr", type_hot, jnp.asarray(relation_table()), precision=HIGH)
    select_low = select.astype(jnp.bfloat16)
    cite_hot = (jnp.arange(rel_count) == 3).astype(jnp.float32)
    q_four = (
        jnp.einsum("tsr,rthd->thsd", select_low, rel_query, preferred_element_type=jnp.float32)
        .astype(jnp.bfloat16)
        .reshape(tgt_rows, head_count, kind_count * head_size)
    )
    q_cite = rel_query[3]

    def block_codes(source):
        return lax.dynamic_slice_in_dim(edge_codes, source * tgt_rows, tgt_rows, 1)

    def forward_block(run_state, kv_blk, qf_part, qc_part, code_blk):
        result = attend_block(run_state, kv_blk, qf_part, qc_part, code_blk, kind_count)
        return result

    def backward_block(kv_blk, qf_part, qc_part, gf_part, gc_part, lse_part, delta_part, code_blk):
        return back_block(
            kv_blk, qf_part, qc_part, gf_part, gc_part, lse_part, delta_part, code_blk, kind_count
        )

    whole_kv = (key_low, value_low, kind_low)

    def forward_turn(step_idx, loop_state):
        run_state, kv_blk = loop_state
        run_state = forward_block(
            run_state, kv_blk, q_four, q_cite, block_codes((my_blk - step_idx) % n_blk)
        )
        kv_blk = from_behind((kv_blk[0], kv_blk[1], kv_blk[2]), "blk", 1)
        return (run_state, kv_blk)

    run_state, kv_last = lax.fori_loop(
        0,
        n_blk,
        forward_turn,
        (
            (
                jnp.full((head_count, tgt_rows), NEG_FILL, jnp.float32),
                jnp.zeros((head_count, tgt_rows), jnp.float32),
                jnp.zeros((tgt_rows, head_count, kind_count * head_size), jnp.float32),
                jnp.zeros((tgt_rows, head_count, head_size), jnp.float32),
            ),
            whole_kv,
        ),
    )
    run_max, run_sum, acc_four, acc_cite = run_state
    floor_sum = jnp.maximum(run_sum, 1.0)
    log_total = run_max + jnp.log(floor_sum)
    norm_t = floor_sum.T[:, :, None]
    u_four = acc_four / norm_t
    u_cite = acc_cite / norm_t
    u_rel = jnp.einsum(
        "tsr,thsd->rthd",
        select,
        u_four.reshape(tgt_rows, head_count, kind_count, head_size),
        precision=HIGH,
    )
    u_rel = u_rel + cite_hot[:, None, None, None] * u_cite[None]
    u_rel_b = u_rel.astype(jnp.bfloat16)
    agg_sum = jnp.einsum(
        "rthd,rhde->the", u_rel_b, rel_msg, preferred_element_type=jnp.float32
    ).reshape(tgt_rows, feat_dim)
    act_full, gelu_back = jax.vjp(jax.nn.gelu, agg_sum)
    act_low = act_full.astype(jnp.bfloat16)
    branch = typed(act_low, out_w)
    skip_all = jax.nn.sigmoid(skip_logit)
    skip_gate = jnp.sum(type_hot * skip_all[None, :], axis=1)[:, None]
    mixed_sum = skip_gate * branch + (1.0 - skip_gate) * x_f
    centered = mixed_sum - jnp.mean(mixed_sum, axis=1, keepdims=True)
    inv_std = lax.rsqrt(jnp.mean(centered * centered, axis=1, keepdims=True) + LN_EPS)
    normed = centered * inv_std
    valid_col = node_valid.astype(jnp.float32)[:, None]
    layer_out = (valid_col * (normed * ln_gain + ln_bias)).astype(jnp.bfloat16)
    grad_y = cotangent.astype(jnp.float32) * valid_col
    gain_grad = jnp.sum(grad_y * normed, axis=0)
    bias_grad = jnp.sum(grad_y, axis=0)
    grad_norm = grad_y * ln_gain
    grad_mix = inv_std * (
        grad_norm
        - jnp.mean(grad_norm, axis=1, keepdims=True)
        - normed * jnp.mean(grad_norm * normed, axis=1, keepdims=True)
    )
    grad_branch = (skip_gate * grad_mix).astype(jnp.bfloat16)
    gate_term = (
        jnp.sum(grad_mix * (branch - x_f), axis=1, keepdims=True) * skip_gate * (1.0 - skip_gate)
    )
    skip_grad = jnp.sum(type_hot * gate_term, axis=0)
    out_grad = typed_grad(act_low, grad_branch)
    grad_agg = gelu_back(typed_back(grad_branch, out_w))[0].astype(jnp.bfloat16)
    grad_agg_heads = grad_agg.reshape(tgt_rows, head_count, head_size)
    msg_grad = jnp.einsum(
        "rthd,the->rhde", u_rel_b, grad_agg_heads, preferred_element_type=jnp.float32
    )
    grad_urel = jnp.einsum(
        "the,rhde->rthd", grad_agg_heads, rel_msg, preferred_element_type=jnp.float32
    ).astype(jnp.bfloat16)
    grad_four = (
        jnp.einsum("tsr,rthd->thsd", select_low, grad_urel, preferred_element_type=jnp.float32)
        .astype(jnp.bfloat16)
        .reshape(tgt_rows, head_count, kind_count * head_size)
    )
    grad_cite = grad_urel[3]
    row_delta = (
        jnp.sum(grad_four.astype(jnp.float32) * u_four, axis=2)
        + jnp.sum(grad_cite.astype(jnp.float32) * u_cite, axis=2)
    ).T
    zero_four = jnp.zeros((tgt_rows, head_count, kind_count * head_size), jnp.float32)
    zero_cite = jnp.zeros((tgt_rows, head_count, head_size), jnp.float32)

    def back_turn(step_idx, loop_state):
        kv_blk, travel, acc_qf, acc_qc = loop_state
        k_grad, v_grad, qf_grad, qc_grad = backward_block(
            kv_blk,
            q_four,
            q_cite,
            grad_four,
            grad_cite,
            log_total,
            row_delta,
            block_codes((my_blk - step_idx) % n_blk),
        )
        travel = (
            from_behind((travel[0] + k_grad).astype(jnp.bfloat16), "blk", 1).astype(jnp.float32),
            from_behind((travel[1] + v_grad).astype(jnp.bfloat16), "blk", 1).astype(jnp.float32),
        )
        kv_blk = from_behind((kv_blk[0], kv_blk[1], kv_blk[2]), "blk", 1)
        return (kv_blk, travel, acc_qf + qf_grad, acc_qc + qc_grad)

    zero_kv = jnp.zeros((tgt_rows, feat_dim), jnp.float32)
    loop_state = lax.fori_loop(
        0, n_blk, back_turn, (whole_kv, (zero_kv, zero_kv), zero_four, zero_cite)
    )
    key_acc, value_acc = loop_state[1]
    acc_qf, acc_qc = (loop_state[2], loop_state[3])
    grad_key = key_acc.astype(jnp.bfloat16)
    grad_value = value_acc.astype(jnp.bfloat16)
    grad_relq = jnp.einsum(
        "tsr,thsd->rthd",
        select,
        acc_qf.reshape(tgt_rows, head_count, kind_count, head_size),
        precision=HIGH,
    )
    grad_relq = (
        (grad_relq + cite_hot[:, None, None, None] * acc_qc[None])
        .astype(jnp.bfloat16)
        .astype(jnp.float32)
    )
    prior_grad = jnp.sum(grad_relq * rel_raw, axis=(1, 3)) / math.sqrt(head_size)
    grad_raw = grad_relq * factor[:, None, :, None]
    att_grad = jnp.einsum("thj,rthk->rhjk", q_heads, grad_raw, precision=HIGH)
    grad_query = (
        jnp.einsum("rthk,rhjk->thj", grad_raw, att_f, precision=HIGH)
        .reshape(tgt_rows, feat_dim)
        .astype(jnp.bfloat16)
    )
    query_grad = typed_grad(features, grad_query)
    key_grad = typed_grad(shifted_b, grad_key)
    value_grad = typed_grad(shifted_b, grad_value)
    grad_shift = typed_back(grad_key, key_w) + typed_back(grad_value, value_w)
    table_grad = jnp.dot(gap_hot.T, grad_shift, precision=HIGH)
    rte_grad = jnp.dot(time_low.T, table_grad, precision=HIGH)
    input_grad = (
        (1.0 - skip_gate) * grad_mix + typed_back(grad_query, query_w) + grad_shift
    ).astype(jnp.bfloat16)
    summed = lax.psum(
        (
            query_grad,
            key_grad,
            value_grad,
            out_grad,
            att_grad,
            msg_grad,
            prior_grad,
            skip_grad,
            rte_grad,
            gain_grad,
            bias_grad,
        ),
        ("blk", "rep"),
    )
    return (
        layer_out,
        input_grad,
        summed[0],
        summed[1],
        summed[2],
        summed[3],
        summed[4],
        summed[5],
        summed[6],
        summed[7],
        summed[8],
        summed[9],
        summed[10],
    )


REL_TAB = relation_table()
HALF = 128
F32 = jnp.float32
LOW = jnp.bfloat16
VMEM_CAP = 65400 * 2**10
PROB_UNROLL = 2
GATHER_CUTS = 2


def nn(a, b):
    return lax.dot_general(a, b, (((1,), (0,)), ((), ())), preferred_element_type=F32)


def nt(a, b):
    return lax.dot_general(a, b, (((1,), (1,)), ((), ())), preferred_element_type=F32)


def tn(a, b):
    return lax.dot_general(a, b, (((0,), (0,)), ((), ())), preferred_element_type=F32)


def pick(kinds, kind, value):
    return jnp.where(kinds == kind, value, jnp.zeros_like(value))


def relation_of(kind, slot):
    hit = np.nonzero(REL_TAB[kind, slot])[0]
    return int(hit[0]) if len(hit) else None


def to_slots(rel_rows, kinds, kind_count):
    slots = []
    for slot in range(kind_count):
        rows = jnp.zeros(kinds.shape, F32)
        for kind in range(kind_count):
            rel = relation_of(kind, slot)
            if rel is not None:
                rows = jnp.where(kinds == kind, rel_rows(rel), rows)
        slots.append(rows)
    return slots, pick(kinds, 0, rel_rows(3))


def to_relations(slot_rows, cite_rows, kinds, kind_count, rel_count):
    out = []
    for rel in range(rel_count):
        if rel == 3:
            out.append(pick(kinds, 0, cite_rows))
            continue
        (kind, slot) = [
            (k, s) for k in range(kind_count) for s in range(kind_count) if relation_of(k, s) == rel
        ][0]
        out.append(pick(kinds, kind, slot_rows(slot)))
    return out


def flip(index, mask):
    return sum(((index // bit + mask // bit) % 2) * bit for bit in (1, 2, 4))


def gap_hot(gap_row, levels):
    gaps = jnp.broadcast_to(gap_row, (levels, gap_row.shape[1]))
    return (lax.broadcasted_iota(jnp.int32, gaps.shape, 0) == gaps).astype(F32).astype(LOW)


def remote(src, dst, sends, recvs, send_at, recv_at, device):
    return pltpu.make_async_remote_copy(
        src_ref=src,
        dst_ref=dst,
        send_sem=sends.at[send_at],
        recv_sem=recvs.at[recv_at],
        device_id=device,
        device_id_type=pl.DeviceIdType.MESH,
    )


def greet(device):
    pl.semaphore_signal(
        pltpu.get_barrier_semaphore(),
        inc=1,
        device_id=device,
        device_id_type=pl.DeviceIdType.MESH,
    )


def out_at(k, half):
    return (2 * k + half) * 256


def msg_at(half):
    return 2048 + half * 256


def key_at(k, half):
    return 2560 + 3072 * half + k * 256


def value_at(k, half):
    return 2560 + 3072 * half + (4 + k) * 256


def query_at(k, half):
    return 2560 + 3072 * half + (8 + k) * 256


def att_at(half):
    return 8704 + half * 256


SUM_PARTS = ((0, 2560, False), (2560, 3072, False), (5632, 2048, True), (7680, 1536, True))
SUM_TICKS = (
    ((0, 0, 1), (2, 0, 2), (3, 0, 3)),
    ((0, 0, 4), (0, 1, 1), (2, 0, 5), (2, 1, 2), (3, 0, 6), (3, 1, 3)),
)
SUM_NEXT = ((0, 7), (1, 4), (2, 1), (3, 1))
SUM_TAIL = ((0, 8), (1, 5), (2, 2), (3, 2), (1, 6), (2, 3), (3, 3), (1, 7), (2, 4), (3, 4), (1, 8), (2, 5), (3, 5), (2, 6), (3, 6))
GRAD_ROWS = 9216


def span(start, size):
    return pl.ds(start if isinstance(start, int) else pl.multiple_of(start, 16), size)


def summation(part, refs, places, pack):
    grads, full, core_in, plane_in, line_in, sends, recvs = refs
    (z, y, x, core), by_core, by_plane, by_z, by_y = places
    base, rows, at_once = SUM_PARTS[part]
    half, quarter, chunk = rows // 2, rows // 8, rows // 32
    count = iter(range(24 * part, 24 * part + 24))
    mine = base + core * half
    there_core = base + half - core * half
    spots = [(2 * x + y + step) % 4 for step in range(4)]
    plane_at = [mine + spot * quarter for spot in spots]
    own_x = mine + x * 2 * quarter
    other_x = mine + (1 - x) * 2 * quarter
    other_y = own_x + (1 - y) * quarter
    by_x = by_plane[1]
    line_at = [plane_at[0] + ((z + step) % 4) * chunk for step in range(4)]
    core_land, plane_land, line_land = base // 2, 3 * base // 8, 3 * base // 32
    pending = []

    def send(src, dst, device):
        at = next(count)

        def copy():
            return remote(src(), dst(), sends, recvs, at, at, device)

        copy().start()
        pending.append(copy)

    def settle():
        for copy in pending:
            copy().wait()
        pending.clear()

    def piece(ref, start, size):
        return lambda: ref.at[span(start, size), :]

    def small(ref, at):
        return lambda: ref.at[at]

    def load(ref, start, size):
        return ref[span(start, size), :].astype(F32)

    def add_in(start, size, *others):
        value = load(grads, start, size)
        for ref, at in others:
            value = value + load(ref, at, size)
        grads[span(start, size), :] = value.astype(LOW)

    def cores():
        send(piece(grads, there_core, half), piece(core_in, core_land, half), by_core)
        if pack:
            send(small(pack[0], 0), small(pack[1], 0), by_core)

    def plane():
        settle()
        for step in (2, 1, 3, 0):
            add_in(plane_at[step], quarter, (core_in, plane_at[step] - mine + core_land))
            if step:
                land = plane_land + (step - 1) * quarter
                send(
                    piece(grads, plane_at[step], quarter),
                    piece(plane_in, land, quarter),
                    by_plane[step - 1],
                )
        if pack:
            pack[0][1] = pack[0][0] + pack[1][0]
            for step in (1, 2, 3):
                send(small(pack[0], 1), small(pack[1], step), by_plane[step - 1])

    def along_x():
        settle()
        for start in (other_x, own_x):
            add_in(start, 2 * quarter, (core_in, start - mine + core_land))
            if start is other_x:
                send(
                    piece(grads, start, 2 * quarter),
                    piece(plane_in, plane_land, 2 * quarter),
                    by_x,
                )

    def along_y():
        settle()
        for start in (other_y, plane_at[0]):
            add_in(start, quarter, (plane_in, start - own_x + plane_land))
            if start is other_y:
                land = plane_land + 2 * quarter
                send(piece(grads, start, quarter), piece(plane_in, land, quarter), by_y)

    def line():
        settle()
        lands = range(3) if at_once else (2,)
        for step in (2, 3, 1, 0):
            within = line_at[step] - plane_at[0] + plane_land
            add_in(line_at[step], chunk, *[(plane_in, within + i * quarter) for i in lands])
            if step:
                land = line_land + (step - 1) * chunk
                send(
                    piece(grads, line_at[step], chunk),
                    piece(line_in, land, chunk),
                    by_z[step - 1],
                )
        if pack:
            pack[0][2] = pack[0][1] + pack[1][1] + pack[1][2] + pack[1][3]
            for step in (2, 3, 1):
                send(small(pack[0], 2), small(pack[1], 3 + step), by_z[step - 1])

    def share(start, size, device):
        send(piece(full, start, size), piece(full, start, size), device)

    def line_back():
        settle()
        value = load(grads, line_at[0], chunk)
        for step in range(3):
            value = value + load(line_in, line_land + step * chunk, chunk)
        full[span(line_at[0], chunk), :] = value.astype(LOW)
        for step in (2, 3, 1):
            share(line_at[0], chunk, by_z[step - 1])
        if pack:
            pack[2][...] = pack[0][2] + pack[1][4] + pack[1][5] + pack[1][6]

    def plane_back():
        settle()
        for step in (2, 1, 3):
            share(plane_at[0], quarter, by_plane[step - 1])

    def back_y():
        settle()
        share(plane_at[0], quarter, by_y)

    def back_x():
        settle()
        share(own_x, 2 * quarter, by_x)

    def cores_back():
        settle()
        share(mine, half, by_core)

    if at_once:
        return [cores, plane, line, line_back, plane_back, cores_back, settle]
    return [cores, along_x, along_y, line, line_back, back_y, back_x, cores_back, settle]


def layer_kernel(
    x_ref,
    kind_ref,
    gap_ref,
    valid_ref,
    rte_ref,
    time_ref,
    codes_hbm,
    cot_hbm,
    qw_hbm,
    kw_hbm,
    vw_hbm,
    ow_hbm,
    att_hbm,
    msg_hbm,
    prior_ref,
    skip_ref,
    gain_ref,
    bias_ref,
    out_ref,
    input_ref,
    full,
    small_ref,
    att_flat,
    att_ref,
    msg_ref,
    cot_ref,
    codes,
    qw,
    kw,
    vw,
    ow,
    msg_flat,
    shifted,
    xt,
    base,
    shift_out,
    plane_back,
    line_back,
    load_sem,
    gather_send,
    gather_recv,
    back_send,
    back_recv,
    grads,
    core_in,
    plane_in,
    line_in,
    pack,
    pack_in,
    sum_send,
    sum_recv,
    kt,
    vx,
    sbuf,
    probs,
    sm,
    qs,
    tails,
    qt2,
    qh,
    gt2,
    acc,
    two,
    agg,
    grad_even,
    grad_odd,
):
    rows, feat = x_ref.shape
    n_blk = shifted.shape[0]
    levels = time_ref.shape[1]
    kind_count = qw.shape[0]
    rel_count, heads, size = att_ref.shape[:3]
    group = heads // 2
    me = lax.axis_index("blk")
    rep = lax.axis_index("rep")
    z, y = me // 2, me % 2
    inner = ((z + 1) // 2) % 2
    by_y = (flip(me, 1), rep)
    by_core = (me, rep + 1 - 2 * (rep % 2))
    by_x = (me, rep + 2 - 4 * (rep // 2))
    for device in (by_y, by_core, by_x):
        greet(device)

    @pl.when(z < 3)
    def _():
        greet((me + 2, rep))

    @pl.when(z > 0)
    def _():
        greet((me - 2, rep))

    loads = [
        pltpu.make_async_copy(src, dst, load_sem.at[at])
        for at, (src, dst) in enumerate(
            (
                (att_hbm, att_ref),
                (msg_hbm, msg_ref),
                (kw_hbm, kw),
                (vw_hbm, vw),
                (qw_hbm, qw),
                (codes_hbm, codes),
                (ow_hbm, ow),
                (cot_hbm, cot_ref),
            )
        )
    ]

    x_f = x_ref[...].astype(F32).T
    x_t = x_f.astype(LOW)
    xt[...] = x_t
    table = tn(rte_ref[...], time_ref[...])
    table_hi = table.astype(LOW)
    table_lo = (table - table_hi.astype(F32)).astype(LOW)
    hot = gap_hot(gap_ref[...], levels)
    shifted[me, 0:feat, :] = (x_f + nn(table_hi, hot) + nn(table_lo, hot)).astype(LOW)
    shifted[me, feat:, :] = jnp.concatenate(
        [kind_ref[...].astype(F32), gap_ref[...].astype(F32), jnp.zeros((14, rows), F32)], axis=0
    ).astype(LOW)

    edges = [feat * c // GATHER_CUTS for c in range(GATHER_CUTS)] + [feat + 16]

    def move(block, cut, send_at, device):
        at = pl.ds(edges[cut], edges[cut + 1] - edges[cut])
        return remote(
            shifted.at[block, at, :],
            shifted.at[block, at, :],
            gather_send,
            gather_recv,
            send_at * GATHER_CUTS + cut,
            block * GATHER_CUTS + cut,
            device,
        )

    def other_z(n):
        order = ((1, 2, 1, 2), (2, 0, 3, 1), (3, 3, 0, 0))
        table = sum(row[i] * 4 ** (4 * r + i) for r, row in enumerate(order) for i in range(4))
        power = (1 + 3 * (z % 2)) * (1 + 15 * (z // 2)) * (1 + 255 * (n // 2)) * (1 + 255 * (n // 3))
        own = (3 - n) // 3
        return own * z + (1 - own) * ((table // power) % 4)

    def own_moves(act):
        for cut in range(GATHER_CUTS):

            @pl.when(z < 3)
            def _():
                act(move(me, cut, 0, (me + 2, rep)))

            @pl.when(z > 0)
            def _():
                act(move(me, cut, 1, (me - 2, rep)))

            act(move(me, cut, 2, by_y))

    def hand_on(n, act, wait):
        there = other_z(n)
        step = 2 * ((z - there + 3) // 4) - 1
        block = 2 * there + y
        for cut in range(GATHER_CUTS):
            if wait:
                move(block, cut, 0, by_y).wait_recv()
            act(move(block, cut, 2 + n, by_y))

            @pl.when((z + step >= 0) & (z + step <= 3))
            def _():
                act(move(block, cut, 5 + n, (me + 2 * step, rep)))

    pl.semaphore_wait(pltpu.get_barrier_semaphore(), 4 + inner)
    own_moves(lambda copy: copy.start())
    for load in loads:
        load.start()

    def source_row(j, row):
        return shifted[j, feat : feat + 16, :].astype(F32)[row : row + 1].astype(jnp.int32)

    kinds = jnp.broadcast_to(kind_ref[...], (size, rows))
    kinds_f = jnp.broadcast_to(kind_ref[...], (feat, rows))
    valid_f = jnp.broadcast_to(valid_ref[...], (feat, rows)).astype(F32)
    lane = lax.broadcasted_iota(jnp.int32, (rows, HALF), 1)
    ones_pad = (lax.broadcasted_iota(jnp.int32, (16, rows), 0) < 2).astype(F32).astype(LOW)
    scale = 1.0 / math.sqrt(size)

    def cols(j):
        return pl.ds(pl.multiple_of(j * rows, rows), rows)

    def store_part(start, value):
        grads[pl.ds(start, value.shape[0]), :] = value.astype(LOW)

    loads[0].wait()
    loads[1].wait()
    for r in range(rel_count):
        for h in range(heads):
            agg[h * size : (h + 1) * size, r * size : (r + 1) * size] = att_ref[r, h].astype(F32)
    att_flat[...] = agg[...].astype(LOW)
    for r in range(rel_count):
        for h in range(heads):
            agg[r * size : (r + 1) * size, h * size : (h + 1) * size] = msg_ref[r, h].astype(F32)
    msg_flat[...] = agg[...].T.astype(LOW)

    def turned(m, k):
        return probs.at[0, 2 * m + k // 2, pl.ds((k % 2) * feat, feat), :]

    for m, (load, ref) in enumerate(((loads[2], kw), (loads[3], vw))):
        load.wait()
        for k in range(kind_count):
            turned(m, k)[...] = ref[k].astype(F32).T.astype(LOW)

    loads[4].wait()
    q_full = jnp.zeros((feat, rows), F32)
    for k in range(kind_count):
        q_full = jnp.where(kinds_f == k, tn(qw[k], x_t), q_full)
    for h in range(heads):
        qh[h] = q_full[h * size : (h + 1) * size].astype(LOW)

    def head_rows(ref, h):
        return ref[pl.ds(pl.multiple_of(h * size, size), size), :]

    def query_head(h, carry):
        raw = tn(head_rows(att_flat, h), qh[h])

        def rel_rows(r):
            part = raw[r * size : (r + 1) * size] * (prior_ref[r, h] * scale)
            return part.astype(LOW).astype(F32)

        slots, cite = to_slots(rel_rows, kinds, kind_count)
        slot_t = jnp.concatenate(slots, axis=0)
        cite_t = jnp.concatenate([cite, jnp.zeros((HALF - size, rows), F32)], axis=0)
        qt2[h, :, 0:rows] = slot_t.astype(LOW)
        qt2[h, :, rows:] = cite_t.astype(LOW)
        qs[h, 0:rows, :] = slot_t.T.astype(LOW)
        qs[h, rows:, :] = cite_t.T.astype(LOW)
        return carry

    lax.fori_loop(0, heads, query_head, 0, unroll=2)
    loads[5].wait()
    acc[:, 0:rows, :] = jnp.full((heads, rows, HALF), NEG_FILL, F32)

    def keep_scores(h, j, both, second, edge):
        val = jnp.where(second, both[rows:], both[:rows]) * LOG2_E
        val = jnp.where(edge, val, NEG_FILL)
        if h < group:
            sbuf[j, pl.ds(h * rows, rows), :] = val
        else:
            high = val.astype(LOW)
            probs[j, h, 0:rows, :] = high
            probs[j, h, rows:, :] = (val - high.astype(F32)).astype(LOW)
        top = jnp.maximum(val[:, :HALF], val[:, HALF:])
        acc[h, 0:rows, :] = jnp.maximum(acc[h, 0:rows, :], top)

    def arrive(j):
        src = jnp.broadcast_to(source_row(j, 0), (size, rows))
        block = shifted[j, 0:feat, :]
        for k in range(kind_count):
            key = nn(turned(0, k)[...], block)
            value = nn(turned(1, k)[...], block)
            for h in range(heads):
                part = slice(h * size, (h + 1) * size)
                kt[j, h, pl.ds(k * size, size), :] = pick(src, k, key[part]).astype(LOW)
                vx[j, h, pl.ds(k * size, size), :] = pick(src, k, value[part]).astype(LOW)
        code = codes[:, cols(j)]
        second = code == 2
        edge = code > 0
        two[j] = second.astype(F32).astype(LOW)
        before = None
        for h in range(heads + 1):
            both = nn(qs[h], kt[j, h]) if h < heads else None
            if h > 0:
                keep_scores(h - 1, j, before, second, edge)
            before = both

    def start(copy):
        copy.start()

    def two_blocks(n, carry):
        there = other_z(n)

        def one(line, inside):
            block = 2 * there + (y + line) % 2

            @pl.when(line == 1)
            def _():
                @pl.when(n == 0)
                def _():
                    hand_on(1, start, True)

                @pl.when((n == 0) & (inner == 1))
                def _():
                    hand_on(2, start, True)

                @pl.when(n == 1)
                def _():
                    hand_on(2 + inner, start, True)

                @pl.when((n == 2) & (inner == 0))
                def _():
                    hand_on(3, start, True)

                for cut in range(GATHER_CUTS):
                    move(block, cut, 0, by_y).wait_recv()

            arrive(block)
            return inside

        return lax.fori_loop(0, 2, one, carry)

    lax.fori_loop(0, n_blk // 2, two_blocks, 0)
    own_moves(lambda copy: copy.wait_send())
    for n in range(1, n_blk // 2):
        hand_on(n, lambda copy: copy.wait_send(), False)

    def prob_block(h, j, top, kept):
        if kept:
            val = sbuf[j, pl.ds(pl.multiple_of(h * rows, rows), rows), :]
        else:
            val = probs[j, h, 0:rows, :].astype(F32) + probs[j, h, rows:, :].astype(F32)
        val = jnp.exp2(val - top)
        low = val.astype(LOW)
        second = low * two[j]
        probs[j, h, 0:rows, :] = low - second
        probs[j, h, rows:, :] = second
        return val[:, :HALF] + val[:, HALF:], jnp.concatenate([low - second, second], axis=0)

    sm[...] = jnp.zeros((rows, HALF), F32)

    def prob_head(h, kept):
        top = jnp.max(acc[h, 0:rows, :], axis=1, keepdims=True)
        top = jnp.broadcast_to(jnp.maximum(top, 0.1 * NEG_FILL), (rows, rows))
        value_sum = None
        total = None
        for j in range(n_blk + 1):
            if j < n_blk:
                part, now = prob_block(h, j, top, kept)
                total = part if total is None else total + part
            if j > 0:
                part = nt(before, vx[j - 1, h])
                value_sum = part if value_sum is None else value_sum + part
            before = now
        acc[h] = value_sum
        total = jnp.sum(total, axis=1, keepdims=True)
        sm[...] = jnp.where(lane == h, jnp.broadcast_to(total, (rows, HALF)), sm[...])

    for kept in (True, False):

        def prob_pair(pair, carry, kept=kept):
            for u in range(PROB_UNROLL):
                prob_head((0 if kept else group) + PROB_UNROLL * pair + u, kept)
            return carry

        lax.fori_loop(0, group // PROB_UNROLL, prob_pair, 0)

    inverse = 1.0 / jnp.maximum(sm[...].T, 1.0)
    sm[0:heads, :] = inverse[0:heads, 0:HALF]
    sm[heads : 2 * heads, :] = inverse[0:heads, HALF:]

    def inv_row(h, count):
        row = jnp.concatenate([sm[pl.ds(h, 1), :], sm[pl.ds(heads + h, 1), :]], axis=1)
        return jnp.broadcast_to(row, (count, rows))

    def rel_part(h):
        return sbuf[h // group, pl.ds((h % group) * feat, feat), :].astype(LOW)

    for h in range(heads):
        inv = inv_row(h, HALF)
        u_turned = acc[h].T
        u_slot = u_turned[:, 0:rows] * inv
        u_cite = u_turned[0:size, rows:] * inv[0:size]
        sbuf[2 + h // group, pl.ds((h % group) * feat, HALF), :] = u_slot
        sbuf[2 + h // group, pl.ds((h % group) * feat + HALF, size), :] = u_cite
        rel = to_relations(
            lambda s: u_slot[s * size : (s + 1) * size], u_cite, kinds, kind_count, rel_count
        )
        rel = jnp.concatenate(rel, axis=0)
        sbuf[h // group, pl.ds((h % group) * feat, feat), :] = rel
        agg[pl.ds(h * size, size), :] = nn(head_rows(msg_flat, h), rel.astype(LOW))
    loads[6].wait()
    loads[7].wait()
    agg_t = agg[...]
    slope = 0.7978845608028654
    inner = jnp.tanh(slope * (agg_t + 0.044715 * agg_t * agg_t * agg_t))
    act_t = (0.5 * agg_t * (1.0 + inner)).astype(LOW)
    gelu_back = 0.5 * (1.0 + inner) + 0.5 * agg_t * (1.0 - inner * inner) * slope * (
        1.0 + 3.0 * 0.044715 * agg_t * agg_t
    )
    skip = jnp.zeros((1, rows), F32)
    branch = jnp.zeros((feat, rows), F32)
    for k in range(kind_count):
        skip = jnp.where(kinds[0:1] == k, skip_ref[k], skip)
        branch = jnp.where(kinds_f == k, tn(ow[k], act_t), branch)
    gate_row = 1.0 / (1.0 + jnp.exp(-skip))
    gate = jnp.broadcast_to(gate_row, (feat, rows))
    mixed = gate * branch + (1.0 - gate) * x_f
    centered = mixed - jnp.mean(mixed, axis=0, keepdims=True)
    inv_std = lax.rsqrt(jnp.mean(centered * centered, axis=0, keepdims=True) + LN_EPS)
    normed = centered * inv_std
    affine = jnp.concatenate([gain_ref[...], bias_ref[...], jnp.zeros((HALF - 2, feat), F32)], axis=0).T
    gain = jnp.broadcast_to(affine[:, 0:1], (feat, rows))
    bias = jnp.broadcast_to(affine[:, 1:2], (feat, rows))
    out_ref[...] = (valid_f * (normed * gain + bias)).T.astype(LOW)
    grad_y = cot_ref[...].astype(F32).T * valid_f
    gain_col = jnp.sum(grad_y * normed, axis=1, keepdims=True)
    bias_col = jnp.sum(grad_y, axis=1, keepdims=True)
    grad_norm = grad_y * gain
    grad_mix = inv_std * (
        grad_norm
        - jnp.mean(grad_norm, axis=0, keepdims=True)
        - normed * jnp.mean(grad_norm * normed, axis=0, keepdims=True)
    )
    skip_row = (
        jnp.sum(grad_mix * (branch - x_f), axis=0, keepdims=True) * gate_row * (1.0 - gate_row)
    )
    base[...] = (1.0 - gate) * grad_mix
    grad_branch = gate * grad_mix
    grad_act = jnp.zeros((feat, rows), F32)
    for k in range(kind_count):
        masked = pick(kinds_f, k, grad_branch).astype(LOW)
        out_grad = nt(act_t, masked)
        store_part(out_at(k, 0), out_grad[:, :HALF])
        store_part(out_at(k, 1), out_grad[:, HALF:])
        grad_act = grad_act + nn(ow[k], masked)
    agg[...] = gelu_back * grad_act

    for h in range(heads):
        grad_agg = agg[pl.ds(h * size, size), :].astype(LOW)
        msg_grad = nt(grad_agg, rel_part(h))
        store_part(msg_at(0) + h * size, msg_grad[:, :HALF])
        store_part(msg_at(1) + h * size, msg_grad[:, HALF:])
        inv = inv_row(h, size)
        grad_u = tn(head_rows(msg_flat, h), grad_agg)

        def rel_rows(r):
            return grad_u[r * size : (r + 1) * size] * inv

        slots, cite = to_slots(rel_rows, kinds, kind_count)
        slot_t = jnp.concatenate(slots, axis=0).astype(LOW)
        cite_t = jnp.concatenate([cite, jnp.zeros((HALF - size, rows), F32)], axis=0).astype(LOW)
        gt2[h, :, 0:rows] = slot_t
        gt2[h, :, rows:] = cite_t
        slot_f = slot_t.astype(F32)
        cite_f = cite_t.astype(F32)
        u_at = (h % group) * feat
        delta = -(
            jnp.sum(slot_f * sbuf[2 + h // group, pl.ds(u_at, HALF), :], axis=0, keepdims=True)
            + jnp.sum(
                cite_f[0:size] * sbuf[2 + h // group, pl.ds(u_at + HALF, size), :],
                axis=0,
                keepdims=True,
            )
        )
        delta_hi = delta.astype(LOW).astype(F32)
        tail = jnp.concatenate(
            [delta_hi, delta - delta_hi, jnp.zeros((HALF - 2, rows), F32)], axis=0
        )
        tail_t = tail.T.astype(LOW)
        qs[h, 0:rows, :] = slot_f.T.astype(LOW)
        qs[h, rows:, :] = cite_f.T.astype(LOW)
        tails[h] = tail_t[:, 0:16]
        acc[h] = jnp.zeros(acc.shape[1:], F32)

    refs = (grads, full, core_in, plane_in, line_in, sum_send, sum_recv)
    by_z = [(((me // 2 + step) % 4) * 2 + me % 2, rep) for step in (1, 2, 3)]
    spots = [(2 * (rep // 2) + y + step) % 4 for step in (1, 2, 3)]
    by_plane = [(2 * z + spot % 2, 2 * (spot // 2) + rep % 2) for spot in spots]
    places = ((z, y, rep // 2, rep % 2), by_core, by_plane, by_z, by_y)
    sums = [summation(part, refs, places, None) for part in range(3)]
    sums.append(summation(3, refs, places, (pack, pack_in, small_ref)))
    sums[0][0]()

    slot_id = lax.broadcasted_iota(jnp.int32, (HALF, rows), 0) // size
    pack[0] = jnp.zeros(pack.shape[1:], F32)
    pair = jnp.where(
        lane == 0,
        jnp.broadcast_to(gain_col, (feat, HALF)),
        jnp.where(lane == 1, jnp.broadcast_to(bias_col, (feat, HALF)), 0.0),
    ).T
    spot = lax.broadcasted_iota(jnp.int32, (1, rows), 1)
    skips = jnp.zeros((1, rows), F32)
    for k in range(kind_count):
        skips = jnp.where(
            spot == k, jnp.sum(pick(kinds[0:1], k, skip_row), axis=1, keepdims=True), skips
        )
    pack[0, levels : levels + 8, :] = jnp.concatenate(
        [pair[0:2], skips, jnp.zeros((5, rows), F32)], axis=0
    )

    def along_y(m):
        return remote(
            shift_out.at[flip(me, m + 1)],
            plane_back.at[m // 2],
            back_send,
            back_recv,
            m // 2,
            m // 2,
            by_y,
        )

    def along_z(m):
        at = n_blk // 2 + m // 2
        return remote(
            shift_out.at[flip(me, m)],
            line_back.at[m // 2],
            back_send,
            back_recv,
            at,
            at,
            (flip(me, m), rep),
        )

    def pass_on(m):
        along_y(m).wait_recv()
        j = flip(me, m)
        total = shift_out[j].astype(F32) + plane_back[m // 2].astype(F32)
        shift_out[j] = total.astype(LOW)
        along_z(m).start()

    grad_bufs = (grad_even, grad_odd)
    for g in range(2):
        half = slice(g * HALF, (g + 1) * HALF)

        def block_pair(pair, carry, g=g, half=half):
            m = n_blk - 2 - 2 * pair
            blocks = (flip(me, m + 1), flip(me, m))
            owns = [slot_id == jnp.broadcast_to(source_row(j, 0), (HALF, rows)) for j in blocks]

            def keep(at, u, kind, part):
                for k in range(kind_count):
                    start = (2 * k + kind) * HALF + u * size
                    sbuf[blocks[at], pl.ds(start, size), :] = part[k * size : (k + 1) * size]

            def score_part(at, u):
                h = g * group + u
                both = jnp.concatenate([tails[h], tails[h]], axis=0)
                left = jnp.concatenate([qs[h], both], axis=1)
                right = jnp.concatenate([vx[blocks[at], h], ones_pad], axis=0)
                grad_bufs[u % 2][:, at * rows : (at + 1) * rows] = probs[blocks[at], h] * nn(
                    left, right
                ).astype(LOW)
                keep(at, u, 1, jnp.where(owns[at], nn(gt2[h], probs[blocks[at], h]), 0.0))

            def key_part(at, u):
                h = g * group + u
                grad = grad_bufs[u % 2][:, at * rows : (at + 1) * rows]
                keep(at, u, 0, jnp.where(owns[at], nn(qt2[h], grad), 0.0))
                if at == 1:
                    keys = jnp.concatenate([kt[j, h] for j in blocks], axis=1)
                    acc[h] = acc[h] + nt(grad_bufs[u % 2][...], keys)

            units = [(at, u) for u in range(group) for at in range(2)]
            for i in range(len(units) + 2):
                if i < len(units):
                    score_part(*units[i])
                if i > 1:
                    key_part(*units[i - 2])
            for at in range(2):
                j = blocks[at]
                total = None
                for k in range(kind_count):
                    weights = jnp.concatenate([kw[k, :, half], vw[k, :, half]], axis=1)
                    part = nn(weights, sbuf[j, pl.ds(k * feat, feat), :].astype(LOW))
                    total = part if total is None else total + part
                if g == 1:
                    total = total + shift_out[j].astype(F32)
                low = total.astype(LOW)
                shift_out[j] = low
                if g == 1:
                    gaps = gap_hot(source_row(j, 1), levels)
                    pack[0, 0:levels, :] = pack[0, 0:levels, :] + nt(gaps, low)
                    if at == 0:
                        along_y(m).start()
            if g == 1:

                @pl.when(pair > 0)
                def _():
                    pass_on(m + 2)

            for when, part, step in SUM_TICKS[g]:

                @pl.when(pair == when)
                def _(part=part, step=step):
                    sums[part][step]()

            return carry

        lax.fori_loop(0, n_blk // 2, block_pair, 0)

        for k in range(kind_count):
            total = None
            for j in range(n_blk):
                part = nt(shifted[j, 0:feat, :], sbuf[j, pl.ds(k * feat, feat), :].astype(LOW))
                total = part if total is None else total + part
            store_part(key_at(k, g), total[:, :HALF])
            store_part(value_at(k, g), total[:, HALF:])
        if g == 1:
            sums[2][0]()
        grad_q = []
        for h in range(g * group, (g + 1) * group):
            slot = acc[h].T
            rel = to_relations(
                lambda s: slot[s * size : (s + 1) * size, 0:rows],
                slot[0:size, rows:],
                kinds,
                kind_count,
                rel_count,
            )
            rel = [part.astype(LOW) for part in rel]
            att_grad = nt(qh[h], jnp.concatenate(rel, axis=0))
            store_part(att_at(0) + h * size, att_grad[:, :HALF])
            store_part(att_at(1) + h * size, att_grad[:, HALF:])
            raw = [
                (part.astype(F32) * (prior_ref[r, h] * scale)).astype(LOW)
                for r, part in enumerate(rel)
            ]
            grad_q.append(nn(head_rows(att_flat, h), jnp.concatenate(raw, axis=0)))
        grad_q = jnp.concatenate(grad_q, axis=0).astype(LOW).astype(F32)
        masked = [pick(kinds_f[0:HALF], k, grad_q).astype(LOW) for k in range(kind_count)]
        for k in range(kind_count):
            store_part(query_at(k, g), nt(xt[...], masked[k]))
        if g == 1:
            sums[3][0]()
        total = base[...]
        for k in range(kind_count):
            total = total + nn(qw[k, :, half], masked[k])
        base[...] = total
        if g == 0:
            sums[1][0]()

    for part, step in SUM_NEXT:
        sums[part][step]()
    along_y(0).wait_recv()
    total = base[...] + shift_out[me].astype(F32) + plane_back[0].astype(F32)
    for m in (2, 4, 6):
        along_z(m).wait_recv()
        total = total + line_back[m // 2].astype(F32)
    input_ref[...] = total.T.astype(LOW)
    for part, step in SUM_TAIL:
        sums[part][step]()
    for m in (0, 2, 4, 6):
        along_y(m).wait_send()
        if m > 0:
            along_z(m).wait_send()


def finish_kernel(
    full,
    small_ref,
    att_flat,
    time_ref,
    prior_ref,
    out_in,
    input_in,
    out_ref,
    input_ref,
    qg_ref,
    kg_ref,
    vg_ref,
    og_ref,
    attg_ref,
    msgg_ref,
    priorg_ref,
    skip_ref,
    rte_ref,
    gain_ref,
    bias_ref,
):
    out_ref[...] = out_in[...]
    input_ref[...] = input_in[...]
    kind_count, feat = qg_ref.shape[:2]
    rel_count, heads, width = attg_ref.shape[:3]
    scale = 1.0 / math.sqrt(width)

    def part(start):
        return full[pl.ds(start, feat), :].astype(F32)

    for ref, at in ((qg_ref, query_at), (kg_ref, key_at), (vg_ref, value_at), (og_ref, out_at)):
        for k in range(kind_count):
            for half in range(2):
                ref[k, :, half * HALF : (half + 1) * HALF] = part(at(k, half))
    att = jnp.concatenate([part(att_at(0)), part(att_at(1))], axis=1)
    msg = jnp.concatenate([part(msg_at(0)), part(msg_at(1))], axis=1).T
    for r in range(rel_count):
        for h in range(heads):
            block = (slice(h * width, (h + 1) * width), slice(r * width, (r + 1) * width))
            attg_ref[r, h] = att[block] * (prior_ref[r, h] * scale)
            msgg_ref[r, h] = msg[block[::-1]]
    prod = (att * att_flat[...].astype(F32)).reshape(heads, width, feat)
    prod = jnp.sum(prod, axis=1)
    spread = (
        lax.broadcasted_iota(jnp.int32, (feat, rel_count), 0) // width
        == lax.broadcasted_iota(jnp.int32, (feat, rel_count), 1)
    ).astype(F32).astype(LOW)
    prior = jnp.zeros((rel_count, heads), F32)
    for _ in range(3):
        low = prod.astype(LOW)
        prior = prior + lax.dot_general(
            spread, low, (((0,), (1,)), ((), ())), preferred_element_type=F32
        )
        prod = prod - low.astype(F32)
    priorg_ref[...] = prior * scale
    levels = time_ref.shape[1]
    small = small_ref[...]
    rte = jnp.zeros(rte_ref.shape, F32)
    rest = small[0:levels]
    for _ in range(3):
        low = rest.astype(LOW)
        rte = rte + nn(time_ref[...], low)
        rest = rest - low.astype(F32)
    rte_ref[...] = rte
    gain_ref[...] = small[levels : levels + 1]
    bias_ref[...] = small[levels + 1 : levels + 2]
    skip_ref[...] = small[levels + 2 : levels + 3, 0:kind_count]


def layer_call(n_blk, *args):
    rows, feat = args[0].shape
    kind_count = args[8].shape[0]
    rel_count, heads, size = args[12].shape[:3]
    vmem = pl.BlockSpec(memory_space=pltpu.VMEM)
    smem = pl.BlockSpec(memory_space=pltpu.SMEM)
    hbm = pl.BlockSpec(memory_space=pl.ANY)
    square = (feat, feat)
    weight = pltpu.VMEM((kind_count,) + square, LOW)

    def shape(dims, kind):
        return jax.ShapeDtypeStruct(dims, kind)

    return pl.pallas_call(
        layer_kernel,
        out_shape=[
            shape((rows, feat), LOW),
            shape((rows, feat), LOW),
            shape((GRAD_ROWS, HALF), LOW),
            shape((LEVELS + 8, feat), F32),
            shape(square, LOW),
        ],
        in_specs=[vmem] * 6 + [hbm] * 8 + [smem] * 2 + [vmem] * 2,
        out_specs=[vmem] * 5,
        scratch_shapes=[
            pltpu.VMEM((rel_count, heads, size, size), LOW),
            pltpu.VMEM((rel_count, heads, size, size), LOW),
            pltpu.VMEM((rows, feat), LOW),
            pltpu.VMEM((rows, n_blk * rows), jnp.int32),
            weight,
            weight,
            weight,
            weight,
            pltpu.VMEM(square, LOW),
            pltpu.VMEM((n_blk, feat + 16, rows), LOW),
            pltpu.VMEM((feat, rows), LOW),
            pltpu.VMEM((feat, rows), F32),
            pltpu.VMEM((n_blk, feat, rows), LOW),
            pltpu.VMEM((n_blk // 2, feat, rows), LOW),
            pltpu.VMEM((n_blk // 2, feat, rows), LOW),
            pltpu.SemaphoreType.DMA((8,)),
            pltpu.SemaphoreType.DMA((9 * GATHER_CUTS,)),
            pltpu.SemaphoreType.DMA((n_blk * GATHER_CUTS,)),
            pltpu.SemaphoreType.DMA((n_blk,)),
            pltpu.SemaphoreType.DMA((n_blk,)),
            pltpu.VMEM((GRAD_ROWS, HALF), LOW),
            pltpu.VMEM((GRAD_ROWS // 2, HALF), LOW),
            pltpu.VMEM((3 * GRAD_ROWS // 8, HALF), LOW),
            pltpu.VMEM((3 * GRAD_ROWS // 32, HALF), LOW),
            pltpu.VMEM((3, LEVELS + 8, feat), F32),
            pltpu.VMEM((7, LEVELS + 8, feat), F32),
            pltpu.SemaphoreType.DMA((96,)),
            pltpu.SemaphoreType.DMA((96,)),
            pltpu.VMEM((n_blk, heads, HALF, rows), LOW),
            pltpu.VMEM((n_blk, heads, HALF, rows), LOW),
            pltpu.VMEM((n_blk, heads // 2 * rows, rows), F32),
            pltpu.VMEM((n_blk, heads, 2 * rows, rows), LOW),
            pltpu.VMEM((rows, HALF), F32),
            pltpu.VMEM((heads, 2 * rows, HALF), LOW),
            pltpu.VMEM((heads, rows, 16), LOW),
            pltpu.VMEM((heads, HALF, 2 * rows), LOW),
            pltpu.VMEM((heads, size, rows), LOW),
            pltpu.VMEM((heads, HALF, 2 * rows), LOW),
            pltpu.VMEM((heads, 2 * rows, HALF), F32),
            pltpu.VMEM((n_blk, rows, rows), LOW),
            pltpu.VMEM(square, F32),
            pltpu.VMEM((2 * rows, 2 * rows), LOW),
            pltpu.VMEM((2 * rows, 2 * rows), LOW),
        ],
        compiler_params=pltpu.CompilerParams(
            vmem_limit_bytes=VMEM_CAP, collective_id=0, has_side_effects=True
        ),
        name="layer",
    )(*args)


def time_columns(level_count, feat_width):
    positions = np.arange(level_count, dtype=np.float32)[:, None]
    steps = np.arange(feat_width // 2, dtype=np.float32)[None, :]
    phases = positions / np.power(np.float32(10000.0), np.float32(2.0) * steps / feat_width)
    table = np.stack([np.sin(phases), np.cos(phases)], axis=2).reshape(level_count, feat_width)
    return jnp.asarray(np.ascontiguousarray(table.T), LOW)


def fast_body(
    features,
    node_type,
    time_gap,
    node_valid,
    edge_codes,
    query_w,
    key_w,
    value_w,
    out_w,
    rel_att,
    rel_msg,
    rel_prior,
    skip_logit,
    rte_w,
    ln_gain,
    ln_bias,
    cotangent,
):
    rows, feat = features.shape
    n_blk = lax.axis_size("blk")
    kind_count = query_w.shape[0]
    time_low = time_columns(LEVELS, feat)
    vmem = pl.BlockSpec(memory_space=pltpu.VMEM)
    smem = pl.BlockSpec(memory_space=pltpu.SMEM)
    square = (feat, feat)

    def shape(dims, kind):
        return jax.ShapeDtypeStruct(dims, kind)

    layer_out, input_grad, full, small, att_flat = layer_call(
        n_blk,
        features,
        node_type[None],
        time_gap[None],
        node_valid[None],
        rte_w,
        time_low,
        edge_codes,
        cotangent,
        query_w,
        key_w,
        value_w,
        out_w,
        rel_att,
        rel_msg,
        rel_prior,
        skip_logit,
        ln_gain[None],
        ln_bias[None],
    )
    outs = pl.pallas_call(
        finish_kernel,
        out_shape=[shape(layer_out.shape, LOW), shape(input_grad.shape, LOW)]
        + [shape((kind_count,) + square, F32)] * 4
        + [shape(rel_att.shape, F32)] * 2
        + [
            shape(rel_prior.shape, F32),
            shape((1, kind_count), F32),
            shape(square, F32),
            shape((1, feat), F32),
            shape((1, feat), F32),
        ],
        in_specs=[vmem] * 4 + [smem] + [vmem] * 2,
        out_specs=[vmem] * 13,
        compiler_params=pltpu.CompilerParams(vmem_limit_bytes=VMEM_CAP),
        name="finish",
    )(full, small, att_flat, time_low, rel_prior, layer_out, input_grad)
    return (*outs[:9], outs[9][0], outs[10], outs[11][0], outs[12][0])


def solution(mesh):
    in_specs = (
        P(("blk", "rep"), None),
        P(("blk", "rep")),
        P(("blk", "rep")),
        P(("blk", "rep")),
        P(("blk", "rep"), None),
        P(),
        P(),
        P(),
        P(),
        P(),
        P(),
        P(),
        P(),
        P(),
        P(),
        P(),
        P(("blk", "rep"), None),
    )
    out_specs = (
        P(("blk", "rep"), None),
        P(("blk", "rep"), None),
        P(),
        P(),
        P(),
        P(),
        P(),
        P(),
        P(),
        P(),
        P(),
        P(),
        P(),
    )
    plan = fast_body if tuple(mesh.shape.values()) == (8, 4) else body
    return jax.shard_map(plan, mesh=mesh, in_specs=in_specs, out_specs=out_specs, check_vma=False)
```
